32 devices in a mesh: dp: 8 (over z, x), mp: 4 (over y, core).
Axes of the slice: x: 2, y: 2, z: 4, core: 2. Of those that a mesh axis runs over, the one named last changes fastest.
Arguments:
- pixels_in: bfloat16 [6400, 320], P('dp', 'mp'), may hold values from -6 to 6
- cotangent: bfloat16 [6400, 320], P('dp'), may hold values from -6 to 6
- pixel_mask: int32 [6400], P('dp'), may hold values from 0 to 1, as said below
- tile_slot: int32 [8, 2], replicated, may hold values from 0 to 7, as said below
- ln1_gain: float32 [320], replicated, may hold values from 0.5 to 1.5
- ln1_bias: float32 [320], replicated, may hold values from -2 to 2
- w_query: bfloat16 [320, 320], replicated, may hold values from -0.3125 to 0.3125
- b_query: float32 [320], replicated, may hold values from -2 to 2
- w_key: bfloat16 [320, 320], replicated, may hold values from -0.3125 to 0.3125
- w_value: bfloat16 [320, 320], replicated, may hold values from -0.3125 to 0.3125
- b_value: float32 [320], replicated, may hold values from -2 to 2
- w_reduce: bfloat16 [1280, 320], replicated, may hold values from -0.15625 to 0.15625
- b_reduce: float32 [320], replicated, may hold values from -2 to 2
- lnr_gain: float32 [320], replicated, may hold values from 0.5 to 1.5
- lnr_bias: float32 [320], replicated, may hold values from -2 to 2
- w_out: bfloat16 [320, 320], replicated, may hold values from -2.5 to 2.5
- b_out: float32 [320], replicated, may hold values from -2 to 2
- ln2_gain: float32 [320], replicated, may hold values from 0.5 to 1.5
- ln2_bias: float32 [320], replicated, may hold values from -2 to 2
- w_fc1: bfloat16 [320, 1280], P(None, 'mp'), may hold values from -0.3125 to 0.3125
- b_fc1: float32 [1280], P('mp'), may hold values from -2 to 2
- w_depth: float32 [9, 1280], P(None, 'mp'), may hold values from -2 to 2
- b_depth: float32 [1280], P('mp'), may hold values from -2 to 2
- w_fc2: bfloat16 [1280, 320], P('mp'), may hold values from -0.3125 to 0.3125
- b_fc2: float32 [320], replicated, may hold values from -2 to 2
Outputs:
- block_out: bfloat16 [6400, 320], P('dp', 'mp')
- grad_pixels_in: float32 [6400, 320], P('dp', 'mp')
- grad_ln1_gain: float32 [320], replicated
- grad_ln1_bias: float32 [320], replicated
- grad_w_query: float32 [320, 320], replicated
- grad_b_query: float32 [320], replicated
- grad_w_key: float32 [320, 320], replicated
- grad_w_value: float32 [320, 320], replicated
- grad_b_value: float32 [320], replicated
- grad_w_reduce: float32 [1280, 320], replicated
- grad_b_reduce: float32 [320], replicated
- grad_lnr_gain: float32 [320], replicated
- grad_lnr_bias: float32 [320], replicated
- output_weight_gradient: float32 [320, 320], replicated
- grad_b_out: float32 [320], replicated
- grad_ln2_gain: float32 [320], replicated
- grad_ln2_bias: float32 [320], replicated
- grad_w_fc1: float32 [320, 1280], P(None, 'mp')
- grad_b_fc1: float32 [1280], P('mp')
- grad_w_depth: float32 [9, 1280], P(None, 'mp')
- grad_b_depth: float32 [1280], P('mp')
- grad_w_fc2: float32 [1280, 320], P('mp')
- grad_b_fc2: float32 [320], replicated
The draws below stay inside these ranges and needn't reach their ends.
Inputs may be any that keep to these rules, and one draw needn't show every extreme that they name: `tile_slot`: row d names the crop (below 1) and tile (below 8) of device d; every pair of crop and tile appears exactly once. `pixel_mask`: 1 exactly inside the crop's square of side 64 or 80 at the frame's top-left corner.
All inputs are finite; a program needn't handle non-finite values.
Results may differ from the reference program's by a relative error of at most 0.024.
Values may be sent and summed in bfloat16 or wider, within the bound.
A program may use at most 128 MiB of HBM per device.

```python
import jax
import jax.numpy as jnp
from jax import lax

D = 320
HEADS = 5
HEAD_FEATURES = 64
FF = 1280
FRAME = 80
SIDE_SMALL = 64
TILE_ROWS = 8
TILES_COL = 1
TR = 10
TC = 80
TPF = 8
CROPS = 1
KC = 1600
TOKENS = 6400
N_DP = 8


def tile_layout(key):
    first, second = jax.random.split(key)
    device_ids = jnp.arange(N_DP, dtype=jnp.int32)
    scores = jax.random.randint(first, (N_DP,), 0, 2 ** 20, dtype=jnp.int32) * N_DP + device_ids
    special = (device_ids == 0) | (device_ids == N_DP // 2) | (device_ids == N_DP - 1)
    scores = jnp.where(special, scores - 2 ** 28, scores)
    ranked = jnp.argsort(jnp.argsort(scores)).astype(jnp.int32)
    crop = ranked // TPF
    tile = ranked % TPF
    coin = jax.random.randint(second, (CROPS,), 0, 2, dtype=jnp.int32)
    sides = jnp.where((jnp.arange(CROPS, dtype=jnp.int32) > 0) & (coin == 1), FRAME, SIDE_SMALL)
    return (crop, tile, sides.astype(jnp.int32))


def draw_tile_slot(key, part):
    crop, tile, sides = tile_layout(key)
    return jnp.stack([crop, tile], axis=1).astype(jnp.int32)


def draw_pixel_mask(key, part):
    crop, tile, sides = tile_layout(key)
    row_index = (tile // TILES_COL)[:, None, None] * TR + jnp.arange(TR, dtype=jnp.int32)[None, :, None]
    col_index = (tile % TILES_COL)[:, None, None] * TC + jnp.arange(TC, dtype=jnp.int32)[None, None, :]
    side = jnp.sum(jnp.where(crop[:, None] == jnp.arange(CROPS, dtype=jnp.int32)[None, :], sides[None, :], 0), axis=1)
    inside = (row_index < side[:, None, None]) & (col_index < side[:, None, None])
    return inside.astype(jnp.int32).reshape(-1)


def block_levels(stream_key, dims, cuts, low, high):
    loudness = 1.0
    for axis_at, parts in cuts:
        steps = jax.random.uniform(jax.random.fold_in(jax.random.fold_in(stream_key, 6), axis_at), (parts,), jnp.float32, low / len(cuts), high / len(cuts))
        loudness = loudness * jnp.repeat(jnp.exp(steps), dims[axis_at] // parts).reshape((-1,) + (1,) * (len(dims) - 1 - axis_at))
    return loudness


def gaussian(rng, dims, deviation, bound, shards=(), kind=jnp.bfloat16):
    array = deviation * jax.random.normal(rng, dims, jnp.float32)
    if shards:
        array = array * block_levels(rng, dims, shards, -0.22, 0.18)
    return jnp.clip(array, -bound, bound).astype(kind)


def setup_inputs(seed: int = 0) -> dict:
    streams_of = jax.random.split(jax.random.key(seed), 26)
    return {
        "pixels_in": gaussian(streams_of[0], (TOKENS, D), 1.0, 6.0, ((0, 8), (1, 4))),
        "cotangent": gaussian(streams_of[1], (TOKENS, D), 1.0, 6.0, ((0, 8),)),
        "pixel_mask": draw_pixel_mask(jax.random.fold_in(streams_of[25], 71), 0),
        "tile_slot": draw_tile_slot(jax.random.fold_in(streams_of[25], 71), 0),
        "ln1_gain": jnp.clip(jax.random.uniform(streams_of[4], (D,), jnp.float32, 0.5, 1.5), 0.5, 1.5),
        "ln1_bias": gaussian(streams_of[5], (D,), 0.3, 2.0, (), jnp.float32),
        "w_query": gaussian(streams_of[6], (D, D), D ** -0.5, 0.3125),
        "b_query": gaussian(streams_of[7], (D,), 0.3, 2.0, (), jnp.float32),
        "w_key": gaussian(streams_of[8], (D, D), D ** -0.5, 0.3125),
        "w_value": gaussian(streams_of[9], (D, D), D ** -0.5, 0.3125),
        "b_value": gaussian(streams_of[10], (D,), 0.3, 2.0, (), jnp.float32),
        "w_reduce": gaussian(streams_of[11], (4 * D, D), (4 * D) ** -0.5, 0.15625),
        "b_reduce": gaussian(streams_of[12], (D,), 0.3, 2.0, (), jnp.float32),
        "lnr_gain": jnp.clip(jax.random.uniform(streams_of[13], (D,), jnp.float32, 0.5, 1.5), 0.5, 1.5),
        "lnr_bias": gaussian(streams_of[14], (D,), 0.3, 2.0, (), jnp.float32),
        "w_out": gaussian(streams_of[15], (D, D), (max(D // 64, 1)) ** -0.5, 2.5),
        "b_out": gaussian(streams_of[16], (D,), 0.3, 2.0, (), jnp.float32),
        "ln2_gain": jnp.clip(jax.random.uniform(streams_of[17], (D,), jnp.float32, 0.5, 1.5), 0.5, 1.5),
        "ln2_bias": gaussian(streams_of[18], (D,), 0.3, 2.0, (), jnp.float32),
        "w_fc1": gaussian(streams_of[19], (D, FF), D ** -0.5, 0.3125, ((1, 4),)),
        "b_fc1": gaussian(streams_of[20], (FF,), 0.3, 2.0, ((0, 4),), jnp.float32),
        "w_depth": gaussian(streams_of[21], (9, FF), 9 ** -0.5, 2.0, ((1, 4),), jnp.float32),
        "b_depth": gaussian(streams_of[22], (FF,), 0.3, 2.0, ((0, 4),), jnp.float32),
        "w_fc2": gaussian(streams_of[23], (FF, D), (FF // 4) ** -0.5, 0.3125, ((0, 4),)),
        "b_fc2": gaussian(streams_of[24], (D,), 0.3, 2.0, (), jnp.float32),
    }


@jax.custom_vjp
def low(v):
    return lax.optimization_barrier(v.astype(jnp.bfloat16)).astype(jnp.float32)

@jax.custom_vjp
def low_back(v):
    return v

def low_keep(v):
    return (low(v), None)

def low_pass(kept, gradient_value):
    return (gradient_value,)

def back_keep(v):
    return (v, None)

def back_low(kept, gradient_value):
    return (low(gradient_value),)
low.defvjp(low_keep, low_pass)
low_back.defvjp(back_keep, back_low)
HIGH = lax.Precision.HIGHEST
NEG = -1e+30
EPS = 1e-05

def matmul(left, right):
    return jnp.dot(left, right, precision=HIGH, preferred_element_type=jnp.float32)

def layer_norm(value, gain, shift):
    mean = lax.optimization_barrier(jnp.mean(value, axis=-1, keepdims=True))
    centred = value - mean
    spread = lax.optimization_barrier(jnp.mean(centred * centred, axis=-1, keepdims=True))
    return centred * lax.rsqrt(spread + EPS) * gain + shift

def to_frames(value, dev_at):
    tiles = value.reshape(N_DP, TR, TC, -1)[dev_at]
    tiles = tiles.reshape(CROPS, TILE_ROWS, TILES_COL, TR, TC, -1)
    return tiles.transpose(0, 1, 3, 2, 4, 5).reshape(CROPS, FRAME, FRAME, -1)

def from_frames(value, place):
    tiles = value.reshape(CROPS, TILE_ROWS, TR, TILES_COL, TC, -1).transpose(0, 1, 3, 2, 4, 5)
    return tiles.reshape(N_DP, TR, TC, -1)[place].reshape(TOKENS, -1)

def attend_block(queries, keys, values, usable):
    raw = jnp.einsum('qhd,khd->hqk', queries, keys, precision=HIGH) * HEAD_FEATURES ** (-0.5)
    scores = jnp.where(usable[None, None, :] > 0.5, low_back(raw), NEG)
    total = jax.nn.logsumexp(scores, axis=-1)
    weights = low(jnp.exp(scores - total[..., None]))
    return jnp.einsum('hqk,khd->qhd', weights, values, precision=HIGH)

def attend_crop(args):
    queries, keys, values, usable = args
    blocks = queries.reshape(4, -1, HEADS, HEAD_FEATURES)

    def one_block(block_queries):
        return attend_block(block_queries, keys, values, usable)
    outs = lax.map(jax.checkpoint(one_block), blocks)
    return outs.reshape(-1, HEADS, HEAD_FEATURES)

def block(inputs, ln1_gain, ln1_bias, w_query, b_query, w_key, w_value, b_value, w_reduce, b_reduce, lnr_gain, lnr_bias, w_out, b_out, ln2_gain, ln2_bias, w_fc1, b_fc1, w_depth, b_depth, w_fc2, b_fc2, maskf, keyok, place, dev_at):
    column = maskf[:, None]
    xm = inputs * column
    n1 = low(layer_norm(xm, ln1_gain, ln1_bias))
    query = low(low_back(matmul(n1, w_query) + b_query))
    frames = to_frames(n1, dev_at)
    patches = frames.reshape(CROPS, FRAME // 2, 2, FRAME // 2, 2, D).transpose(0, 1, 3, 2, 4, 5)
    patches = patches.reshape(CROPS * KC, 4 * D)
    reduced = low_back(matmul(patches, w_reduce) + b_reduce)
    normed = low(layer_norm(reduced, lnr_gain, lnr_bias))
    keys = low(low_back(matmul(normed, w_key))).reshape(CROPS, KC, HEADS, HEAD_FEATURES)
    values = low(low_back(matmul(normed, w_value) + b_value)).reshape(CROPS, KC, HEADS, HEAD_FEATURES)
    queries = to_frames(query, dev_at).reshape(CROPS, FRAME * FRAME, HEADS, HEAD_FEATURES)
    attended = lax.map(attend_crop, (queries, keys, values, keyok))
    attended = low(low_back(attended))
    mixed = from_frames(attended.reshape(CROPS, FRAME, FRAME, D), place)
    branch = low_back(matmul(mixed, w_out)) + b_out
    h1 = xm + branch * column
    n2 = low(layer_norm(h1, ln2_gain, ln2_bias))
    hidden = low(low_back((matmul(n2, w_fc1) + b_fc1) * column))
    padded = jnp.pad(to_frames(hidden, dev_at), ((0, 0), (1, 1), (1, 1), (0, 0)))
    conv = jnp.zeros((CROPS, FRAME, FRAME, FF), jnp.float32) + b_depth
    for row_off in range(3):
        for col_off in range(3):
            conv = conv + w_depth[3 * row_off + col_off] * padded[:, row_off:row_off + FRAME, col_off:col_off + FRAME]
    act = low(low_back(jax.nn.gelu(conv, approximate=False)))
    ffn = low_back(matmul(from_frames(act, place), w_fc2)) + b_fc2
    return h1 + ffn * column

def reference(pixels_in, cotangent, pixel_mask, tile_slot, ln1_gain, ln1_bias, w_query, b_query, w_key, w_value, b_value, w_reduce, b_reduce, lnr_gain, lnr_bias, w_out, b_out, ln2_gain, ln2_bias, w_fc1, b_fc1, w_depth, b_depth, w_fc2, b_fc2):
    place = (tile_slot[:, 0] * TPF + tile_slot[:, 1]).astype(jnp.int32)
    dev_at = jnp.zeros((N_DP,), jnp.int32).at[place].set(jnp.arange(N_DP, dtype=jnp.int32))
    maskf = pixel_mask.astype(jnp.float32)
    mask_frames = to_frames(maskf[:, None], dev_at)[..., 0]
    keyok = mask_frames[:, ::2, ::2].reshape(CROPS, KC)
    params = (pixels_in.astype(jnp.float32), ln1_gain, ln1_bias, w_query.astype(jnp.float32), b_query, w_key.astype(jnp.float32), w_value.astype(jnp.float32), b_value, w_reduce.astype(jnp.float32), b_reduce, lnr_gain, lnr_bias, w_out.astype(jnp.float32), b_out, ln2_gain, ln2_bias, w_fc1.astype(jnp.float32), b_fc1, w_depth, b_depth, w_fc2.astype(jnp.float32), b_fc2)

    def forward(*values):
        return block(*values, maskf, keyok, place, dev_at)
    result, pull = jax.vjp(forward, *params)
    grads = pull(cotangent.astype(jnp.float32))
    return (result.astype(jnp.bfloat16), grads[0], grads[1], grads[2], grads[3], grads[4], grads[5], grads[6], grads[7], grads[8], grads[9], grads[10], grads[11], grads[12], grads[13], grads[14], grads[15], grads[16], grads[17], grads[18], grads[19], grads[20], grads[21])
```

```python
import functools

import jax
import jax.numpy as jnp
from jax import lax
from jax.experimental import pallas as pl
from jax.experimental.pallas import tpu as pltpu
from jax.sharding import PartitionSpec as P

HEADS = 5
HEAD_FEATURES = 64
FRAME = 80
TILE_ROWS = 8


EPS = 1e-05
NEG = -1e30


def layer_norm(value, gain, shift):
    mean = jnp.mean(value, axis=-1, keepdims=True)
    centred = value - mean
    spread = jnp.mean(centred * centred, axis=-1, keepdims=True)
    return centred * lax.rsqrt(spread + EPS) * gain + shift


def depth_gelu(padded, kernel, shift):
    rows = padded.shape[0] - 2
    cols = padded.shape[1] - 2
    total = jnp.zeros((rows, cols, padded.shape[2]), jnp.float32) + shift
    for row_off in range(3):
        for col_off in range(3):
            total = (
                total
                + kernel[3 * row_off + col_off]
                * padded[row_off : row_off + rows, col_off : col_off + cols]
            )
    return jax.nn.gelu(total, approximate=False)


def mat(left, right):
    return jnp.dot(left, right, preferred_element_type=jnp.float32)


def pick(weights, table):
    return jnp.einsum(
        "j,jab->ab", weights.astype(table.dtype), table, preferred_element_type=jnp.float32
    )


def head_columns(weight_matrix, select_where):
    wide_layout = weight_matrix.astype(jnp.float32).reshape(
        weight_matrix.shape[0], HEADS, HEAD_FEATURES
    )
    return (
        jnp.einsum("uzx,nz->unx", wide_layout, select_where)
        .reshape(weight_matrix.shape[0], -1)
        .astype(jnp.bfloat16)
    )


def head_rows(weight_matrix, select_where):
    wide_layout = weight_matrix.astype(jnp.float32).reshape(
        HEADS, HEAD_FEATURES, weight_matrix.shape[1]
    )
    return (
        jnp.einsum("hed,sh->sed", wide_layout, select_where)
        .reshape(-1, weight_matrix.shape[1])
        .astype(jnp.bfloat16)
    )


def head_vector(vector_entries, select_where):
    return jnp.einsum(
        "he,sh->se", vector_entries.reshape(HEADS, HEAD_FEATURES), select_where
    ).reshape(-1)


def spread_columns(gradient_value, select_where):
    return jnp.einsum(
        "tvm,vq->tqm",
        gradient_value.reshape(gradient_value.shape[0], -1, HEAD_FEATURES),
        select_where,
    ).reshape(gradient_value.shape[0], -1)


def spread_rows(gradient_value, select_where):
    return jnp.einsum(
        "sed,sh->hed",
        gradient_value.reshape(-1, HEAD_FEATURES, gradient_value.shape[1]),
        select_where,
    ).reshape(-1, gradient_value.shape[1])


def spread_vector(gradient_value, select_where):
    return jnp.einsum("se,sh->he", gradient_value.reshape(-1, HEAD_FEATURES), select_where).reshape(
        -1
    )


def on_device(
    pixels_in,
    cotangent,
    pixel_mask,
    tile_slot,
    ln1_gain,
    ln1_bias,
    w_query,
    b_query,
    w_key,
    w_value,
    b_value,
    w_reduce,
    b_reduce,
    lnr_gain,
    lnr_bias,
    w_out,
    b_out,
    ln2_gain,
    ln2_bias,
    w_fc1,
    b_fc1,
    w_depth,
    b_depth,
    w_fc2,
    b_fc2,
):
    n_dp = lax.axis_size("dp")
    n_mp = lax.axis_size("mp")
    device = lax.axis_index("dp")
    part = lax.axis_index("mp")
    rows = FRAME // TILE_ROWS
    tokens = pixels_in.shape[0]
    cols = tokens // rows
    tiles_col = FRAME // cols
    per_frame = TILE_ROWS * tiles_col
    width = ln1_gain.shape[0]
    share = width // n_mp
    slots = -(-HEADS // n_mp)
    scale = HEAD_FEATURES ** (-0.5)
    maskf = pixel_mask.astype(jnp.float32)[:, None]
    head_ids = part + n_mp * jnp.arange(slots)
    select_where = (head_ids[:, None] == jnp.arange(HEADS)[None, :]).astype(jnp.float32)
    crops = tile_slot[:, 0]
    tiles = tile_slot[:, 1]
    is_me = jnp.arange(n_dp) == device
    own_crop = jnp.sum(jnp.where(is_me, crops, 0))
    own_tile = jnp.sum(jnp.where(is_me, tiles, 0))
    own_row = own_tile // tiles_col
    own_col = own_tile % tiles_col
    tile_row = tiles // tiles_col
    tile_col = tiles % tiles_col

    def beside(drow, dcol):
        hit = (crops == own_crop) & (tile_row == own_row + drow) & (tile_col == own_col + dcol)
        return hit.astype(jnp.float32)

    member = (crops[None, :] == own_crop) & (tiles[None, :] == jnp.arange(per_frame)[:, None])
    crop_devices = jnp.sum(jnp.where(member, jnp.arange(n_dp)[None, :], 0), axis=1)
    whole = lax.all_gather(pixels_in, "mp", axis=1, tiled=True)
    xm = whole.astype(jnp.float32) * maskf
    n1, first_norm_backward = jax.vjp(layer_norm, xm, ln1_gain, ln1_bias)
    n1b = n1.astype(jnp.bfloat16)
    wq = head_columns(w_query, select_where)
    wk = head_columns(w_key, select_where)
    wv = head_columns(w_value, select_where)
    wo = head_rows(w_out, select_where)
    qb = (mat(n1b, wq) + head_vector(b_query, select_where)).astype(jnp.bfloat16)
    patches = (
        n1b.reshape(rows // 2, 2, cols // 2, 2, width)
        .transpose(0, 2, 1, 3, 4)
        .reshape(-1, 4 * width)
    )
    reduced = mat(patches, w_reduce) + b_reduce
    xr, lnr_back = jax.vjp(layer_norm, reduced, lnr_gain, lnr_bias)
    xrb = xr.astype(jnp.bfloat16)
    kb = mat(xrb, wk).astype(jnp.bfloat16)
    vb = (mat(xrb, wv) + head_vector(b_value, select_where)).astype(jnp.bfloat16)
    kmask = (
        pixel_mask.reshape(rows // 2, 2, cols // 2, 2)[:, 0, :, 0].reshape(-1).astype(jnp.bfloat16)
    )
    keys_all, values_all, kmask_all = (
        lax.all_gather(kb, "dp", axis=0, tiled=True),
        lax.all_gather(vb, "dp", axis=0, tiled=True),
        lax.all_gather(kmask, "dp", axis=0, tiled=True),
    )
    per_key = kb.shape[0]
    keys_crop = keys_all.reshape(n_dp, per_key, -1)[crop_devices]
    values_crop = values_all.reshape(n_dp, per_key, -1)[crop_devices]
    usable_crop = kmask_all.reshape(n_dp, per_key)[crop_devices].astype(jnp.float32) > 0.5
    n_blocks = 4
    key_blocks = keys_crop.reshape(n_blocks, -1, slots, HEAD_FEATURES)
    value_blocks = values_crop.reshape(n_blocks, -1, slots, HEAD_FEATURES)
    usable_blocks = usable_crop.reshape(n_blocks, -1)
    queries = qb.reshape(tokens, slots, HEAD_FEATURES)

    def block_scores(key_block, usable_block):
        raw = (
            jnp.einsum("qsd,ksd->sqk", queries, key_block, preferred_element_type=jnp.float32)
            * scale
        )
        return jnp.where(usable_block[None, None, :], raw, NEG)

    def top_step(carry, blocks):
        top, total = carry
        key_block, usable_block = blocks
        scores = block_scores(key_block, usable_block)
        new_top = jnp.maximum(top, jnp.max(scores, axis=-1))
        total = total * jnp.exp(top - new_top) + jnp.sum(
            jnp.exp(scores - new_top[..., None]), axis=-1
        )
        return ((new_top, total), None)

    start = (jnp.full((slots, tokens), NEG, jnp.float32), jnp.zeros((slots, tokens), jnp.float32))
    (top, total), _ = lax.scan(top_step, start, (key_blocks, usable_blocks))
    lse = top + jnp.log(total)

    def out_step(acc, blocks):
        key_block, value_block, usable_block = blocks
        prob = jnp.exp(block_scores(key_block, usable_block) - lse[..., None])
        acc = acc + jnp.einsum(
            "sqk,ksd->qsd",
            prob.astype(jnp.bfloat16),
            value_block,
            preferred_element_type=jnp.float32,
        )
        return (acc, None)

    empty = jnp.zeros((tokens, slots, HEAD_FEATURES), jnp.float32)
    acc, _ = lax.scan(out_step, empty, (key_blocks, value_blocks, usable_blocks))
    ob = acc.reshape(tokens, -1).astype(jnp.bfloat16)
    branch = lax.psum(mat(ob, wo).astype(jnp.bfloat16), "mp").astype(jnp.float32) + b_out
    h1 = xm + branch * maskf
    n2, ln2_back = jax.vjp(layer_norm, h1, ln2_gain, ln2_bias)
    n2b = n2.astype(jnp.bfloat16)
    ub = ((mat(n2b, w_fc1) + b_fc1) * maskf).astype(jnp.bfloat16)
    channels = ub.shape[1]
    tile_u = ub.reshape(rows, cols, channels)
    lines, sides = (
        lax.all_gather(jnp.stack([tile_u[0], tile_u[-1]]), "dp", axis=0, tiled=True),
        lax.all_gather(jnp.stack([tile_u[:, 0], tile_u[:, -1]]), "dp", axis=0, tiled=True),
    )
    lines = lines.reshape(n_dp, 2, cols, channels)
    sides = sides.reshape(n_dp, 2, rows, channels)
    top_lines = lines[:, 0]
    bottom_lines = lines[:, 1]
    left_sides = sides[:, 0]
    right_sides = sides[:, 1]
    upper = jnp.concatenate(
        [
            pick(beside(-1, -1), bottom_lines[:, -1:]),
            pick(beside(-1, 0), bottom_lines),
            pick(beside(-1, 1), bottom_lines[:, :1]),
        ],
        axis=0,
    )
    lower = jnp.concatenate(
        [
            pick(beside(1, -1), top_lines[:, -1:]),
            pick(beside(1, 0), top_lines),
            pick(beside(1, 1), top_lines[:, :1]),
        ],
        axis=0,
    )
    middle = jnp.concatenate(
        [
            pick(beside(0, -1), right_sides)[:, None],
            tile_u.astype(jnp.float32),
            pick(beside(0, 1), left_sides)[:, None],
        ],
        axis=1,
    )
    padded = jnp.concatenate([upper[None], middle, lower[None]], axis=0)
    act, depth_back = jax.vjp(depth_gelu, padded, w_depth, b_depth)
    gb = act.reshape(tokens, channels).astype(jnp.bfloat16)
    ffn_mine = lax.psum_scatter(
        mat(gb, w_fc2).astype(jnp.bfloat16), "mp", scatter_dimension=1, tiled=True
    ).astype(jnp.float32)
    h1_mine = lax.dynamic_slice_in_dim(h1, part * share, share, 1)
    bias_mine = lax.dynamic_slice_in_dim(b_fc2, part * share, share, 0)
    block_result = (h1_mine + (ffn_mine + bias_mine) * maskf).astype(jnp.bfloat16)
    dy = cotangent.astype(jnp.float32)
    dff = dy * maskf
    grad_b_fc2 = jnp.sum(dff, axis=0)
    dfb = dff.astype(jnp.bfloat16)
    grad_w_fc2 = mat(gb.T, dfb)
    dgr = mat(dfb, w_fc2.T).astype(jnp.bfloat16).astype(jnp.float32).reshape(rows, cols, channels)
    dpad, grad_w_depth, grad_b_depth = depth_back(dgr)
    grad_lines, grad_sides = (
        lax.all_gather(
            jnp.stack([dpad[0], dpad[-1]]).astype(jnp.bfloat16), "dp", axis=0, tiled=True
        ).astype(jnp.float32),
        lax.all_gather(
            jnp.stack([dpad[1:-1, 0], dpad[1:-1, -1]]).astype(jnp.bfloat16),
            "dp",
            axis=0,
            tiled=True,
        ).astype(jnp.float32),
    )
    grad_lines = grad_lines.reshape(n_dp, 2, cols + 2, channels)
    grad_sides = grad_sides.reshape(n_dp, 2, rows, channels)
    top_grads = grad_lines[:, 0]
    bottom_grads = grad_lines[:, 1]
    dtile = dpad[1:-1, 1:-1]
    dtile = dtile.at[0].add(pick(beside(-1, 0), bottom_grads[:, 1:-1]))
    dtile = dtile.at[0, 0].add(pick(beside(-1, -1), bottom_grads[:, -1:])[0])
    dtile = dtile.at[0, -1].add(pick(beside(-1, 1), bottom_grads[:, :1])[0])
    dtile = dtile.at[-1].add(pick(beside(1, 0), top_grads[:, 1:-1]))
    dtile = dtile.at[-1, 0].add(pick(beside(1, -1), top_grads[:, -1:])[0])
    dtile = dtile.at[-1, -1].add(pick(beside(1, 1), top_grads[:, :1])[0])
    dtile = dtile.at[:, 0].add(pick(beside(0, -1), grad_sides[:, 1]))
    dtile = dtile.at[:, -1].add(pick(beside(0, 1), grad_sides[:, 0]))
    dub = (dtile.reshape(tokens, channels).astype(jnp.bfloat16).astype(jnp.float32) * maskf).astype(
        jnp.bfloat16
    )
    grad_b_fc1 = jnp.sum(dub.astype(jnp.float32), axis=0)
    grad_w_fc1 = mat(n2b.T, dub)
    dn2_part = mat(dub, w_fc1.T)
    zero_vector = jnp.zeros((width,), jnp.float32)
    dn2 = lax.psum(dn2_part.astype(jnp.bfloat16), "mp").astype(jnp.float32)
    dh1_norm, shared_gain, shared_bias = ln2_back(dn2)
    dh1 = dy + dh1_norm
    split_gain = zero_vector
    split_bias = zero_vector
    dattn = dh1 * maskf
    grad_b_out = jnp.sum(dattn, axis=0)
    dab = dattn.astype(jnp.bfloat16)
    grad_wo = mat(ob.T, dab)
    dob = mat(dab, wo.T).astype(jnp.bfloat16)
    dout = dob.reshape(tokens, slots, HEAD_FEATURES)
    drow = jnp.sum(dout.astype(jnp.float32) * acc, axis=-1).T

    def back_step(dq_acc, blocks):
        key_block, value_block, usable_block = blocks
        prob = jnp.exp(block_scores(key_block, usable_block) - lse[..., None])
        dv_block = jnp.einsum(
            "sqk,qsd->ksd", prob.astype(jnp.bfloat16), dout, preferred_element_type=jnp.float32
        )
        dprob = jnp.einsum("qsd,ksd->sqk", dout, value_block, preferred_element_type=jnp.float32)
        dscore = (prob * (dprob - drow[..., None])).astype(jnp.bfloat16)
        dq_acc = dq_acc + jnp.einsum(
            "sqk,ksd->qsd", dscore, key_block, preferred_element_type=jnp.float32
        )
        dk_block = (
            jnp.einsum("sqk,qsd->ksd", dscore, queries, preferred_element_type=jnp.float32) * scale
        )
        return (dq_acc, (dk_block, dv_block))

    dq_acc, (dk_blocks, dv_blocks) = lax.scan(
        back_step, empty, (key_blocks, value_blocks, usable_blocks)
    )
    zero_keys = jnp.zeros((n_dp, per_key, slots * HEAD_FEATURES), jnp.float32)
    dk_full = (
        zero_keys.at[crop_devices]
        .set(dk_blocks.reshape(per_frame, per_key, -1))
        .reshape(n_dp * per_key, -1)
    )
    dv_full = (
        zero_keys.at[crop_devices]
        .set(dv_blocks.reshape(per_frame, per_key, -1))
        .reshape(n_dp * per_key, -1)
    )
    dk_mine, dv_mine = (
        lax.psum_scatter(dk_full, "dp", scatter_dimension=0, tiled=True),
        lax.psum_scatter(dv_full, "dp", scatter_dimension=0, tiled=True),
    )
    dkb = dk_mine.astype(jnp.bfloat16)
    dvb = dv_mine.astype(jnp.bfloat16)
    dqb = (dq_acc * scale).reshape(tokens, -1).astype(jnp.bfloat16)
    grad_wq = mat(n1b.T, dqb)
    grad_bq = jnp.sum(dqb.astype(jnp.float32), axis=0)
    grad_wk = mat(xrb.T, dkb)
    grad_wv = mat(xrb.T, dvb)
    grad_bv = jnp.sum(dvb.astype(jnp.float32), axis=0)
    dxr, dn1_query = (
        lax.psum((mat(dkb, wk.T) + mat(dvb, wv.T)).astype(jnp.bfloat16), "mp").astype(jnp.float32),
        lax.psum(mat(dqb, wq.T).astype(jnp.bfloat16), "mp").astype(jnp.float32),
    )
    dreduced, grad_lnr_gain, grad_lnr_bias = lnr_back(dxr)
    drb = dreduced.astype(jnp.bfloat16)
    grad_w_reduce = mat(patches.T, drb)
    grad_b_reduce = jnp.sum(drb.astype(jnp.float32), axis=0)
    dpatch = (
        mat(drb, w_reduce.T)
        .reshape(rows // 2, cols // 2, 2, 2, width)
        .transpose(0, 2, 1, 3, 4)
        .reshape(tokens, width)
    )
    dxm, grad_ln1_gain, grad_ln1_bias = first_norm_backward(dn1_query + dpatch)
    grad_whole = (dxm + dh1) * maskf
    grad_input = lax.dynamic_slice_in_dim(grad_whole, part * share, share, 1)
    (
        grad_w_reduce,
        grad_b_reduce,
        grad_lnr_gain,
        grad_lnr_bias,
        grad_ln1_gain,
        grad_ln1_bias,
        shared_gain,
        shared_bias,
        grad_b_out,
        grad_b_fc2,
        grad_w_fc1,
        grad_b_fc1,
        grad_w_depth,
        grad_b_depth,
        grad_w_fc2,
    ) = lax.psum(
        (
            grad_w_reduce,
            grad_b_reduce,
            grad_lnr_gain,
            grad_lnr_bias,
            grad_ln1_gain,
            grad_ln1_bias,
            shared_gain,
            shared_bias,
            grad_b_out,
            grad_b_fc2,
            grad_w_fc1,
            grad_b_fc1,
            grad_w_depth,
            grad_b_depth,
            grad_w_fc2,
        ),
        "dp",
    )
    (
        grad_w_query,
        grad_b_query,
        grad_w_key,
        grad_w_value,
        grad_b_value,
        output_weight_gradient,
        split_gain,
        split_bias,
    ) = lax.psum(
        (
            spread_columns(grad_wq, select_where),
            spread_vector(grad_bq, select_where),
            spread_columns(grad_wk, select_where),
            spread_columns(grad_wv, select_where),
            spread_vector(grad_bv, select_where),
            spread_rows(grad_wo, select_where),
            split_gain,
            split_bias,
        ),
        ("dp", "mp"),
    )
    grad_ln2_gain = shared_gain + split_gain
    grad_ln2_bias = shared_bias + split_bias
    return (
        block_result,
        grad_input,
        grad_ln1_gain,
        grad_ln1_bias,
        grad_w_query,
        grad_b_query,
        grad_w_key,
        grad_w_value,
        grad_b_value,
        grad_w_reduce,
        grad_b_reduce,
        grad_lnr_gain,
        grad_lnr_bias,
        output_weight_gradient,
        grad_b_out,
        grad_ln2_gain,
        grad_ln2_bias,
        grad_w_fc1,
        grad_b_fc1,
        grad_w_depth,
        grad_b_depth,
        grad_w_fc2,
        grad_b_fc2,
    )


BF = jnp.bfloat16
F32 = jnp.float32
LANES = 128
SIDE_SMALL = 64


def nn(a, b):
    return lax.dot_general(a, b, (((1,), (0,)), ((), ())), preferred_element_type=F32)


def nt(a, b):
    return lax.dot_general(a, b, (((1,), (1,)), ((), ())), preferred_element_type=F32)


def tn(a, b):
    return lax.dot_general(a, b, (((0,), (0,)), ((), ())), preferred_element_type=F32)


def iota(shape, axis):
    return lax.broadcasted_iota(jnp.int32, shape, axis)


def hot(cond):
    return jnp.where(cond, 1.0, 0.0).astype(BF)


def spread(value):
    mean = jnp.sum(value, axis=-1, keepdims=True) * (1.0 / value.shape[-1])
    centred = value - mean
    var = jnp.sum(centred * centred, axis=-1, keepdims=True) * (1.0 / value.shape[-1])
    rstd = lax.rsqrt(var + EPS)
    return centred * rstd, rstd


def norm_back(dn, gain, xhat, rstd):
    e = dn * gain
    scale = 1.0 / dn.shape[-1]
    mean_e = jnp.sum(e, axis=-1, keepdims=True) * scale
    mean_ex = jnp.sum(e * xhat, axis=-1, keepdims=True) * scale
    return rstd * (e - mean_e - xhat * mean_ex)


def rowsum(value):
    return jnp.sum(value, axis=0, keepdims=True)


class Sizes:
    def __init__(self, n_dp, n_mp, tokens, width, hidden):
        self.n_dp, self.n_mp = n_dp, n_mp
        self.tokens, self.width, self.hidden = tokens, width, hidden
        self.share = width // n_mp
        self.rows = FRAME // TILE_ROWS
        self.cols = tokens // self.rows
        self.pa, self.pb = self.rows // 2, self.cols // 2
        self.keys = self.pa * self.pb
        self.plane = -(-self.keys // 16) * 16
        self.all = 4 * self.plane
        self.step = self.plane // 16 // n_mp * 16
        self.quarter = self.plane - (n_mp - 1) * self.step
        self.wide = -(-width // LANES) * LANES
        self.kvrows = self.plane + self.quarter
        self.top = 8 + self.pb
        self.ext = self.top + self.keys + self.pb
        self.erows = 2 * hidden + 2 * HEAD_FEATURES
        self.echunk = self.erows // n_dp
        self.lrows = 2 * width
        self.lchunk = self.lrows // n_dp


def fused_body(
    sz,
    mask_ref, slot_ref, pix_ref, cot_ref, ln1g_ref, ln1b_ref, wq_ref, bq_ref, wk_ref, wv_ref,
    bv_ref, wr_ref, br_ref, lnrg_ref, lnrb_ref, wo_ref, bo_ref, ln2g_ref, ln2b_ref, w1_ref, b1_ref,
    wd_ref, bd_ref, w2_ref, b2_ref,
    blk_ref, gp_ref, eg_ref, wog_ref, lg_ref, veg_ref, vlg_ref,
    x32, c32a, c32b, c32c, xg, dfm, dyh_s, dyh, dyh_g, xm_r, n1_r, xhr_r, rsr_r, xr_r, kva, qa_r, qb_r,
    sbuf, ebuf, e5buf, lse_r, og, row_r, h1_r, n2_r, hal_s, hal, hal_g, ux, ul, ur, dgx, dzx, dzl, dzr,
    g_r, du_r, dn2_s, dn2_r, dh1_r, dos, do_all, dabg, ff_s, ff_r, dks, dkr, dkvg, dqs, dq_all, dqt, dqt5,
    e_s, e_r, l_s, l_r, ve_s, ve_r, vl_s, vl_r, gps,
    ssem, rsem,
):
    D, HF, PB, PA, KEYS, PL, T = sz.width, HEAD_FEATURES, sz.pb, sz.pa, sz.keys, sz.plane, sz.all
    C, FS = sz.hidden, sz.share
    d = lax.axis_index("dp")
    m = lax.axis_index("mp")
    last = sz.n_mp * HF

    def mpx(k):
        if k == 1:
            return m + 1 - 2 * lax.rem(m, 2)
        if k == 2:
            return lax.rem(m + 2, 4)
        return 3 - m

    def dpx(k):
        z, x = d // 2, lax.rem(d, 2)
        if k & 1:
            x = 1 - x
        kz = k >> 1
        if kz == 1:
            z = z + 1 - 2 * lax.rem(z, 2)
        elif kz == 2:
            z = lax.rem(z + 2, 4)
        elif kz == 3:
            z = 3 - z
        return 2 * z + x

    counter = [0]
    pending = []

    def take(n):
        first = counter[0]
        counter[0] += n
        return first

    def copy(src, dst, sem, dev):
        return pltpu.make_async_remote_copy(
            src_ref=src, dst_ref=dst, send_sem=ssem.at[sem], recv_sem=rsem.at[sem],
            device_id=dev, device_id_type=pl.DeviceIdType.MESH,
        )

    def send(src, dst, sem, dev):
        c = copy(src, dst, sem, dev)
        c.start()
        pending.append(c)

    def arrived(ref, sem):
        copy(ref, ref, sem, (d, m)).wait_recv()

    def mp_start(buf):
        base = take(3)
        send(buf.at[m], buf.at[m], base, (d, mpx(1)))
        send(buf.at[m], buf.at[m], base + 1, (d, mpx(2)))
        return base

    def mp_finish(buf, base):
        arrived(buf.at[mpx(2)], base + 1)
        send(buf.at[mpx(2)], buf.at[mpx(2)], base + 2, (d, mpx(1)))
        arrived(buf.at[mpx(1)], base)
        arrived(buf.at[mpx(3)], base + 2)

    def dp_start(buf):
        base = take(7)
        for kz in (3, 2, 1):
            send(buf.at[d], buf.at[d], base + kz, (dpx(2 * kz), m))
        send(buf.at[d], buf.at[d], base, (dpx(1), m))
        return base

    def dp_finish(buf, base, each=None):
        def got(k, sem):
            arrived(buf.at[dpx(k)], sem)
            if each is not None:
                each(k)
        for kz in (1, 2, 3):
            arrived(buf.at[dpx(2 * kz)], base + kz)
            send(buf.at[dpx(2 * kz)], buf.at[dpx(2 * kz)], base + 3 + kz, (dpx(1), m))
            if each is not None:
                each(2 * kz)
        got(1, base)
        for kz in (1, 2, 3):
            got(2 * kz + 1, base + 3 + kz)

    def mp_scatter(block, dst):
        base = take(4)
        for k in (2, 3, 1):
            send(block(mpx(k)), dst(k), base + k, (d, mpx(k)))
        return base

    def dp_scatter(block, dst):
        base = take(8)
        for k in (6, 7, 4, 5, 2, 3, 1):
            send(block(dpx(k)), dst(k), base + k, (dpx(k), m))
        return base

    side = jnp.where(mask_ref[sz.cols - 1] > 0, FRAME, SIDE_SMALL)
    tile = slot_ref[d, 1]
    tiles = [slot_ref[k, 1] for k in range(sz.n_dp)]
    above = sum(jnp.where(tiles[k] == tile - 1, k, 0) for k in range(sz.n_dp))
    below = sum(jnp.where(tiles[k] == tile + 1, k, 0) for k in range(sz.n_dp))

    def place(p, count):
        a = sum(jnp.where(p >= PB * k, 1, 0) for k in range(1, count))
        return a, p - PB * a

    def token_mask(i, j):
        p = iota((PL, 1), 0)
        a, b = place(p, PA)
        inside = (p < KEYS) & (sz.rows * tile + 2 * a + i < side) & (2 * b + j < side)
        return jnp.where(inside, 1.0, 0.0)

    def halo_mask(i, j, a):
        b = iota((PB, 1), 0)
        row = sz.rows * tile + 2 * a + i
        inside = (row >= 0) & (row < side) & (2 * b + j < side)
        return jnp.where(inside, 1.0, 0.0)

    def key_bias(p, tile_at, limit):
        a, b = place(p, PA)
        usable = (p < limit) & (sz.rows * tile_at + 2 * a < side) & (2 * b < side)
        return jnp.where(usable, 0.0, NEG)

    def vec(ref):
        return ref[...].reshape(1, ref.shape[0])

    def own_head(row):
        return sum(
            jnp.where(m == h, 1.0, 0.0) * row[:, HF * h : HF * (h + 1)] for h in range(sz.n_mp)
        )

    def plane_rows(ref, start):
        return ref[pl.ds(pl.multiple_of(start, 16), PL), :]

    peers = [(d, mpx(k)) for k in (1, 2, 3)] + [(dpx(k), m) for k in range(1, 8)]
    bar = pltpu.get_barrier_semaphore()
    for dev in peers:
        pl.semaphore_signal(bar, inc=1, device_id=dev, device_id_type=pl.DeviceIdType.MESH)

    x32[...] = pix_ref[...].astype(F32)
    for i in range(2):
        for j in range(2):
            p = 2 * i + j
            parts = [
                x32[pl.ds((2 * a + i) * sz.cols + j, PB, stride=2), :] for a in range(PA)
            ] + [jnp.zeros((PL - KEYS, FS), F32)]
            block = jnp.concatenate(parts, axis=0)
            block = jnp.concatenate([block, jnp.zeros((PL, LANES - FS), F32)], axis=1)
            xg[m, PL * p : PL * (p + 1), :] = block.astype(BF)
    pl.semaphore_wait(bar, len(peers))
    x_at = mp_start(xg)

    c32a[...] = cot_ref[:, 0:128].astype(F32)
    c32b[...] = cot_ref[:, 128:256].astype(F32)
    c32c[...] = cot_ref[:, 256:D].astype(F32)
    for i in range(2):
        for j in range(2):
            p = 2 * i + j
            lanes = []
            for ref in (c32a, c32b, c32c):
                parts = [
                    ref[pl.ds((2 * a + i) * sz.cols + j, PB, stride=2), :] for a in range(PA)
                ] + [jnp.zeros((PL - KEYS, ref.shape[1]), F32)]
                lanes.append(jnp.concatenate(parts, axis=0))
            dfm[PL * p : PL * (p + 1), :] = (
                jnp.concatenate(lanes, axis=1) * token_mask(i, j)
            ).astype(BF)
    dyh_s[:, :D] = dfm[pl.ds(pl.multiple_of(PL * m + (KEYS - PB) * (m // 2), 16), 48), :]
    dyh_s[:, D:] = jnp.zeros((48, sz.wide - D), BF)
    dyh[d] = dyh_s[...]
    dy_at = dp_start(dyh)

    r2, c2 = iota((D, LANES), 0), iota((D, LANES), 1)
    own_lo = hot((c2 < HF) & (r2 == HF * m + c2))
    own_hi = hot((c2 >= HF) & (r2 == HF * m + c2 - HF))
    last_lo = hot((c2 < HF) & (r2 == last + c2))
    last_hi = hot((c2 >= HF) & (r2 == last + c2 - HF))
    wq, wk, wv = wq_ref[...], wk_ref[...], wv_ref[...]
    wq2 = nn(wq, own_lo + last_hi).astype(BF)
    wkv = (nn(wk, own_lo) + nn(wv, own_hi)).astype(BF)
    wkv5 = (nn(wk, last_lo) + nn(wv, last_hi)).astype(BF)
    bq, bv = vec(bq_ref), vec(bv_ref)
    bq2 = jnp.concatenate([own_head(bq), bq[:, last:]], axis=1)
    nil = jnp.zeros((1, HF), F32)
    bkv = jnp.concatenate([nil, own_head(bv)], axis=1)
    bkv5 = jnp.concatenate([nil, bv[:, last:]], axis=1)

    dgx[...] = jnp.zeros_like(dgx)
    dzx[...] = jnp.zeros_like(dzx)
    for p in range(4):
        dgx[p, sz.top : sz.top + PL, :] = (
            nt(dfm[PL * p : PL * (p + 1), :], w2_ref[...]).astype(BF).astype(F32)
        )

    rp, cp = iota((4 * LANES, D), 0), iota((4 * LANES, D), 1)
    place_in = hot(((rp & (LANES - 1)) < FS) & (cp == FS * (rp >> 7) + (rp & (LANES - 1))))
    mp_finish(xg, x_at)
    for p in range(4):
        pieces = jnp.concatenate([xg[h, PL * p : PL * (p + 1), :] for h in range(4)], axis=1)
        xm = nn(pieces, place_in) * token_mask(p // 2, p % 2)
        xm_r[PL * p : PL * (p + 1), :] = xm.astype(BF)
        xhat, _ = spread(xm)
        n1_r[PL * p : PL * (p + 1), :] = (xhat * vec(ln1g_ref) + vec(ln1b_ref)).astype(BF)

    red = sum(
        nn(n1_r[PL * p : PL * (p + 1), :], wr_ref[D * p : D * (p + 1), :]) for p in range(4)
    ) + vec(br_ref)
    xhr, rsr = spread(red)
    xhr_r[...] = xhr
    rsr_r[...] = jnp.broadcast_to(rsr, (PL, LANES))
    xr_r[...] = (xhr * vec(lnrg_ref) + vec(lnrb_ref)).astype(BF)
    kva[d, 0:PL, :] = (nn(xr_r[...], wkv) + bkv).astype(BF)
    part = xr_r[pl.ds(pl.multiple_of(sz.step * m, 16), sz.quarter), :]
    kva[d, PL:, :] = (nn(part, wkv5) + bkv5).astype(BF)
    kv_at = dp_start(kva)

    q2t = ((nn(n1_r[...], wq2) + bq2).astype(BF).astype(F32) * HF ** (-0.5)).T
    half = jnp.zeros((HF, T), F32)
    qa_r[...] = jnp.concatenate([q2t[0:HF], half], axis=0).astype(BF)
    qb_r[...] = jnp.concatenate([q2t[HF:], half], axis=0).astype(BF)

    dp_finish(dyh, dy_at)
    from_above = jnp.where(m >= 2, above, below)
    dyh_g[m] = dyh[from_above]
    dyg_at = mp_start(dyh_g)
    dp_finish(kva, kv_at)

    limit5 = jnp.where(m == sz.n_mp - 1, KEYS - sz.step * m, sz.step)
    pk = iota((sz.quarter, 1), 0)
    bias5 = jnp.concatenate(
        [
            jnp.where(pk < limit5, key_bias(pk + sz.step * m, tiles[k], KEYS), NEG)
            for k in range(sz.n_dp)
        ],
        axis=0,
    )
    kv5 = kva[:, PL:, :].reshape(sz.n_dp * sz.quarter, LANES)
    s5 = nn(kv5, qb_r[...]) + bias5
    m5 = jnp.max(s5, axis=0, keepdims=True)
    e5 = jnp.exp(s5 - m5)
    l5 = rowsum(e5)
    e5b = e5.astype(BF)
    e5buf[...] = e5b.reshape(sz.n_dp, sz.quarter, T)
    o5t = tn(kv5, e5b)
    lse_r[m] = jnp.broadcast_to(m5 + jnp.log(l5), (8, T))
    lse_at = mp_scatter(lambda h: lse_r.at[m], lambda k: lse_r.at[m])

    pk = iota((PL, 1), 0)

    def score_step(j, top):
        s = nn(kva[j, 0:PL, :], qa_r[...]) + key_bias(pk, slot_ref[j, 1], KEYS)
        sbuf[j] = s
        return jnp.maximum(top, jnp.max(s, axis=0, keepdims=True))

    top = lax.fori_loop(0, sz.n_dp, score_step, jnp.full((1, T), NEG, F32))

    def exp_step(j, total):
        e = jnp.exp(sbuf[j] - top)
        ebuf[j] = e.astype(BF)
        return total + rowsum(e)

    total = lax.fori_loop(0, sz.n_dp, exp_step, jnp.zeros((1, T), F32))
    ot = tn(
        kva[:, 0:PL, :].reshape(sz.n_dp * PL, LANES), ebuf[...].reshape(sz.n_dp * PL, T)
    )
    inv = 1.0 / total
    for k in (1, 2, 3):
        arrived(lse_r.at[mpx(k)], lse_at + k)
    lses = [lse_r[h][0:1] for h in range(4)]
    lmax = jnp.maximum(jnp.maximum(lses[0], lses[1]), jnp.maximum(lses[2], lses[3]))
    lse5 = lmax + jnp.log(sum(jnp.exp(v - lmax) for v in lses))
    f5 = jnp.exp(m5 - lse5)
    row_r[0:1, :] = inv
    row_r[1:2, :] = f5
    o2t = jnp.concatenate([ot[HF:] * inv, o5t[HF:] * f5], axis=0)
    og[m] = o2t.T.astype(BF)
    og_at = mp_start(og)

    mp_finish(dyh_g, dyg_at)
    for p in range(4):
        i, j = p // 2, p % 2
        start = sz.top - PB if i == 1 else sz.top + KEYS
        rows = dyh_g[p][:, :D].astype(F32)[0:PB] if i == 0 else dyh_g[p][:, :D].astype(F32)[0:PB]
        rows = rows * halo_mask(i, j, -1 if i == 1 else PA)
        dgx[p, start : start + PB, :] = nt(rows.astype(BF), w2_ref[...]).astype(BF).astype(F32)

    wo = wo_ref[...]
    wo_cat = jnp.concatenate(
        [b for h in range(4) for b in (wo[HF * h : HF * (h + 1)], wo[last:])], axis=0
    )
    mp_finish(og, og_at)
    for p in range(4):
        oc = jnp.concatenate([og[h, PL * p : PL * (p + 1), :] for h in range(4)], axis=1)
        h1 = xm_r[PL * p : PL * (p + 1), :].astype(F32) + token_mask(p // 2, p % 2) * (
            nn(oc, wo_cat) + vec(bo_ref)
        )
        h1_r[PL * p : PL * (p + 1), :] = h1
        xhat, _ = spread(h1)
        n2_r[PL * p : PL * (p + 1), :] = (xhat * vec(ln2g_ref) + vec(ln2b_ref)).astype(BF)

    mine = plane_rows(n2_r, PL * m).astype(F32)
    hal_s[:, :D] = jnp.concatenate([mine[0:PB], mine[KEYS - PB : KEYS]], axis=0).astype(BF)
    hal_s[:, D:] = jnp.zeros((2 * PB, sz.wide - D), BF)
    hal[d] = hal_s[...]
    hal_at = dp_start(hal)

    def hidden(rows, mask):
        return ((nn(rows, w1_ref[...]) + vec(b1_ref)) * mask).astype(BF).astype(F32)

    for p in range(4):
        ux[p, 0 : sz.top, :] = jnp.zeros((sz.top, C), F32)
        ux[p, sz.top : sz.top + PL, :] = hidden(
            n2_r[PL * p : PL * (p + 1), :], token_mask(p // 2, p % 2)
        )
    dp_finish(hal, hal_at)
    up_rows = hal[above].astype(F32)[PB:]
    down_rows = hal[below].astype(F32)[0:PB]
    hal_g[m] = jnp.concatenate([up_rows, down_rows], axis=0).astype(BF)
    halg_at = mp_start(hal_g)
    mp_finish(hal_g, halg_at)
    for p in range(4):
        i, j = p // 2, p % 2
        mask = jnp.concatenate([halo_mask(i, j, -1), halo_mask(i, j, PA)], axis=0)
        u = hidden(hal_g[p][:, :D], mask)
        ux[p, sz.top - PB : sz.top, :] = u[0:PB]
        ux[p, sz.top + KEYS : sz.top + KEYS + PB, :] = u[PB:]

    _, be = place(iota((sz.ext, 1), 0) + (PB - 8), PA + 3)

    def shifted(src, left, right):
        for i in range(2):
            left[i] = jnp.where(be == 0, 0.0, pltpu.roll(src[2 * i + 1], 1, 0))
            right[i] = jnp.where(be == PB - 1, 0.0, pltpu.roll(src[2 * i], sz.ext - 1, 0))

    def source(refs, i, j, di, dj, start):
        base, left, right = refs
        i2, up = (i + di) % 2, (i + di) // 2
        j2, across = (j + dj) % 2, (j + dj) // 2
        at = pl.ds(pl.multiple_of(start + PB * up, 8), PB)
        if across < 0:
            return left[i2, at, :]
        if across > 0:
            return right[i2, at, :]
        return base[2 * i2 + j2, at, :]

    TAPS = [(di, dj) for di in (-1, 0, 1) for dj in (-1, 0, 1)]
    shifted(ux, ul, ur)
    g_r[...] = jnp.zeros_like(g_r)
    du_r[...] = jnp.zeros_like(du_r)

    def activation(i, j, start):
        p = 2 * i + j
        z = vec(bd_ref) + sum(
            wd_ref[t : t + 1, :] * source((ux, ul, ur), i, j, di, dj, start)
            for t, (di, dj) in enumerate(TAPS)
        )
        phi = 0.5 * (1.0 + lax.erf(z * 0.7071067811865476))
        dens = jnp.exp(-0.5 * z * z) * 0.3989422804014327
        dz = dgx[p, pl.ds(pl.multiple_of(start, 8), PB), :] * (phi + z * dens)
        dzx[p, pl.ds(pl.multiple_of(start, 8), PB), :] = dz
        return z * phi, dz

    def fold(value):
        return jnp.sum(value.reshape(PB // 8, 8, C), axis=0)

    sums = [jnp.zeros((8, C), F32) for _ in range(10)]
    for i in range(2):
        for j in range(2):
            p = 2 * i + j
            activation(i, j, sz.top - PB if i == 1 else sz.top + KEYS)

            def forward_step(a, acc, i=i, j=j, p=p):
                start = sz.top + PB * a
                act, dz = activation(i, j, start)
                g_r[p, pl.ds(pl.multiple_of(PB * a, 8), PB), :] = act
                new = [
                    acc[t] + fold(dz * source((ux, ul, ur), i, j, di, dj, start))
                    for t, (di, dj) in enumerate(TAPS)
                ]
                return tuple(new) + (acc[9] + fold(dz),)

            sums = lax.fori_loop(0, PA, forward_step, tuple(sums))
    for t in range(10):
        ve_s[t : t + 1, :C] = rowsum(sums[t])
    shifted(dzx, dzl, dzr)
    for i in range(2):
        for j in range(2):
            p = 2 * i + j

            def backward_step(a, carry, i=i, j=j, p=p):
                start = sz.top + PB * a
                du_r[p, pl.ds(pl.multiple_of(PB * a, 8), PB), :] = sum(
                    wd_ref[t : t + 1, :] * source((dzx, dzl, dzr), i, j, -di, -dj, start)
                    for t, (di, dj) in enumerate(TAPS)
                )
                return carry

            lax.fori_loop(0, PA, backward_step, 0)
    dus = []
    for p in range(4):
        du = du_r[p].astype(BF).astype(F32) * token_mask(p // 2, p % 2)
        dus.append(du.astype(BF))
        dn2_s[p, :, :D] = nt(dus[p], w1_ref[...]).astype(BF)
    ve_s[10:11, :C] = sum(rowsum(v.astype(F32)) for v in dus)
    dn2_at = mp_scatter(lambda h: dn2_s.at[h], lambda k: dn2_r.at[k - 1])

    dub = jnp.concatenate(dus, axis=0)
    gb = g_r[...].reshape(T, C).astype(BF)
    e_s[0:D, :C] = tn(n2_r[...], dub).astype(BF)
    e_s[D : D + C, :D] = tn(gb, dfm[...]).astype(BF)

    for k in (1, 2, 3):
        arrived(dn2_r.at[k - 1], dn2_at + k)
    dn2 = dn2_s[m][:, :D].astype(F32) + sum(dn2_r[k][:, :D].astype(F32) for k in range(3))
    xhat2, rstd2 = spread(plane_rows(h1_r, PL * m))
    dfp = plane_rows(dfm, PL * m).astype(F32)
    dh1 = dfp + norm_back(dn2, vec(ln2g_ref), xhat2, rstd2)
    dh1_r[...] = dh1
    dab = dh1.astype(BF)
    docat = nt(dab, wo_cat).astype(BF)
    for h in range(4):
        dos[h] = docat[:, LANES * h : LANES * (h + 1)]
    do_at = mp_scatter(lambda h: dos.at[h], lambda k: do_all.at[m])
    do_all[m] = dos[m]
    dabg[m, :, :D] = dab
    dab_at = mp_start(dabg)
    ve_s[11:12, :D] = rowsum(dfp)
    ve_s[12:13, :D] = rowsum(dh1)
    ve_s[13:14, :D] = rowsum(dn2 * xhat2)
    ve_s[14:15, :D] = rowsum(dn2)
    ve_s[15:16, :] = jnp.zeros((1, sz.wide), F32)

    rt, ct = iota((D, 4 * LANES), 0), iota((D, 4 * LANES), 1)
    place_out = hot(((ct & (LANES - 1)) < FS) & (rt == FS * (ct >> 7) + (ct & (LANES - 1))))
    ff = nn(gb, nn(w2_ref[...], place_out).astype(BF)).astype(BF)
    for h in range(4):
        ff_s[h] = ff[:, LANES * h : LANES * (h + 1)]

    for k in (1, 2, 3):
        arrived(do_all.at[mpx(k)], do_at + k)
    ff_at = mp_scatter(lambda h: ff_s.at[h], lambda k: ff_r.at[k - 1])
    do2 = do_all[...].reshape(T, LANES).astype(F32)
    lane = iota((T, LANES), 1)
    o_own = og[m].astype(F32)
    o_mix = jnp.where(lane < HF, o_own, sum(og[h].astype(F32) for h in range(4)))
    prod = (do2 * o_mix).T
    dot_t = do2.T
    inv, f5 = row_r[0:1, :], row_r[1:2, :]
    da_t = jnp.concatenate([half, dot_t[0:HF] * inv], axis=0).astype(BF)
    db_t = jnp.concatenate([half, dot_t[HF:] * f5], axis=0).astype(BF)
    drow = rowsum(prod[0:HF]) * inv
    drow5 = rowsum(prod[HF:]) * f5
    dqt[...] = jnp.zeros_like(dqt)
    dqt5[...] = jnp.zeros_like(dqt5)

    def key_block(j):
        kv = kva[j, 0:PL, :]
        e = ebuf[j]
        ds = (e.astype(F32) * (nn(kv, da_t) - drow)).astype(BF)
        dks[j, 0:PL, :] = (nt(ds, qa_r[...]) + nt(e, da_t)).astype(BF)
        dqt[...] += tn(kv, ds)
        kv = kva[j, PL:, :]
        e = e5buf[j]
        ds = (e.astype(F32) * (nn(kv, db_t) - drow5)).astype(BF)
        dks[j, PL:, :] = (nt(ds, qb_r[...]) + nt(e, db_t)).astype(BF)
        dqt5[...] += tn(kv, ds)

    dk_at = take(8)

    def send_step(k, carry):
        j = lax.rem(d + k, sz.n_dp)
        key_block(j)
        copy(dks.at[j], dkr.at[k - 1], dk_at + k, (j, m)).start()
        return carry

    lax.fori_loop(1, sz.n_dp, send_step, 0)
    key_block(d)

    dq2 = (jnp.concatenate([dqt[0:HF], dqt5[0:HF]], axis=0) * HF ** (-0.5)).T.astype(BF)
    for h in range(4):
        dqs[h] = dq2[PL * h : PL * (h + 1)]
    dq_at = mp_scatter(lambda h: dqs.at[h], lambda k: dq_all.at[m])
    dq_all[m] = dqs[m]
    l_s[0:D, 0:LANES] = tn(n1_r[...], dq2).astype(BF)
    vl_s[...] = jnp.zeros_like(vl_s)
    vl_s[5:6, 0:LANES] = rowsum(dq2.astype(F32))
    mp_finish(dabg, dab_at)
    e_s[D + C :, :D] = tn(og[m], dabg[...].reshape(T, sz.wide)[:, :D]).astype(BF)
    e_at = dp_scatter(
        lambda j: e_s.at[pl.ds(pl.multiple_of(sz.echunk * j, 16), sz.echunk)],
        lambda k: e_r.at[k - 1],
    )
    ve_at = dp_scatter(lambda j: ve_s, lambda k: ve_r.at[d])
    ve_r[d] = ve_s[...]

    for k in (1, 2, 3):
        arrived(ff_r.at[k - 1], ff_at + k)
    sel = hot((c2 < FS) & (r2 == FS * m + c2))
    b2 = vec(b2_ref)
    b2q = sum(jnp.where(m == h, 1.0, 0.0) * b2[:, FS * h : FS * (h + 1)] for h in range(4))
    b2q = jnp.concatenate([b2q, jnp.zeros((1, LANES - FS), F32)], axis=1)
    for p in range(4):
        at = slice(PL * p, PL * (p + 1))
        h1 = h1_r[at, :]
        hi = h1.astype(BF)
        h1q = nn(hi, sel) + nn((h1 - hi.astype(F32)).astype(BF), sel)
        ffq = ff_s[m, at, :].astype(F32) + sum(ff_r[k, at, :].astype(F32) for k in range(3))
        blk_ref[at, :] = h1q + token_mask(p // 2, p % 2) * (ffq + b2q)

    for k in range(1, sz.n_dp):
        arrived(dkr.at[k - 1], dk_at + k)
    dkv = dks[d].astype(F32) + sum(dkr[k].astype(F32) for k in range(sz.n_dp - 1))
    dkvb = dkv.astype(BF)
    dkvg[m] = dkvb
    dkv_at = mp_start(dkvg)
    l_s[0:D, LANES : 2 * LANES] = tn(xr_r[...], dkvb[0:PL]).astype(BF)
    part = xr_r[pl.ds(pl.multiple_of(sz.step * m, 16), sz.quarter), :]
    l_s[0:D, 2 * LANES :] = tn(part, dkvb[PL:]).astype(BF)
    bvg = jnp.concatenate(
        [rowsum(dkvb[0:PL].astype(F32))[:, HF:], rowsum(dkvb[PL:].astype(F32))[:, HF:]], axis=1
    )
    vl_s[6:7, 0:LANES] = bvg
    rk, ck = iota((D, 5 * LANES), 0), iota((D, 5 * LANES), 1)
    lane5 = ck & (LANES - 1)
    head5 = ck >> 7
    w_all = (
        nn(wk, hot((lane5 < HF) & (rk == HF * head5 + lane5)))
        + nn(wv, hot((lane5 >= HF) & (rk == HF * head5 + lane5 - HF)))
    ).astype(BF)
    lane4 = ct & (LANES - 1)
    head4 = ct >> 7
    wq_cat = nn(
        wq, hot(rt == jnp.where(lane4 < HF, HF * head4 + lane4, last + lane4 - HF))
    ).astype(BF)
    mp_finish(dkvg, dkv_at)
    tail = jnp.concatenate(
        [dkvg[h, PL : PL + sz.step, :] for h in range(3)] + [dkvg[3, PL:, :]], axis=0
    )
    dkv_all = jnp.concatenate([dkvg[h, 0:PL, :] for h in range(4)] + [tail], axis=1)
    dxr = nt(dkv_all, w_all)
    xhr = xhr_r[...]
    vl_s[2:3, :D] = rowsum(dxr * xhr)
    vl_s[3:4, :D] = rowsum(dxr)
    drb = norm_back(dxr, vec(lnrg_ref), xhr, rsr_r[:, 0:1]).astype(BF)
    vl_s[4:5, :D] = rowsum(drb.astype(F32))
    l_s[D:, :D] = tn(plane_rows(n1_r, PL * m), drb).astype(BF)
    l_s[D:, D:] = jnp.zeros((D, sz.wide - D), BF)
    l_at = dp_scatter(
        lambda j: l_s.at[pl.ds(pl.multiple_of(sz.lchunk * j, 16), sz.lchunk)],
        lambda k: l_r.at[k - 1],
    )

    for k in (1, 2, 3):
        arrived(dq_all.at[mpx(k)], dq_at + k)
    dq_cat = jnp.concatenate([dq_all[h] for h in range(4)], axis=1)
    wr_m = wr_ref[pl.ds(pl.multiple_of(D * m, 16), D), :]
    dn1 = nt(dq_cat, wq_cat) + nt(drb, wr_m)
    xhat1, rstd1 = spread(plane_rows(xm_r, PL * m).astype(F32))
    vl_s[0:1, :D] = rowsum(dn1 * xhat1)
    vl_s[1:2, :D] = rowsum(dn1)
    vl_at = dp_scatter(lambda j: vl_s, lambda k: vl_r.at[d])
    vl_r[d] = vl_s[...]
    masks = [token_mask(p // 2, p % 2) for p in range(4)]
    mask_m = sum(jnp.where(m == p, 1.0, 0.0) * masks[p] for p in range(4))
    dxm = norm_back(dn1, vec(ln1g_ref), xhat1, rstd1)
    gp = (mask_m * (dh1_r[...] + dxm)).astype(BF)
    gpf = nn(gp, place_out).astype(BF)
    for h in range(4):
        gps[h] = gpf[:, LANES * h : LANES * (h + 1)]
    gp_at = mp_scatter(lambda h: gps.at[h], lambda k: gp_ref.at[m])
    gp_ref[m] = gps[m]

    for k in range(1, sz.n_dp):
        arrived(e_r.at[k - 1], e_at + k)
    mine = e_s[pl.ds(pl.multiple_of(sz.echunk * d, 16), sz.echunk), :].astype(F32)
    eg_ref[d] = (mine + sum(e_r[k].astype(F32) for k in range(sz.n_dp - 1))).astype(BF)
    eg_at = dp_start(eg_ref)
    for k in range(1, sz.n_dp):
        arrived(ve_r.at[dpx(k)], ve_at + k)
    veg_ref[m] = sum(ve_r[k] for k in range(sz.n_dp))
    veg_at = mp_start(veg_ref)

    for k in range(1, sz.n_dp):
        arrived(l_r.at[k - 1], l_at + k)
    mine = l_s[pl.ds(pl.multiple_of(sz.lchunk * d, 16), sz.lchunk), :].astype(F32)
    lg_ref[m, d] = (mine + sum(l_r[k].astype(F32) for k in range(sz.n_dp - 1))).astype(BF)
    own = lg_ref.at[m]
    lg_at = dp_start(own)
    over = take(3 * sz.n_dp)

    def across(k):
        j = dpx(k)
        send(lg_ref.at[m, j], lg_ref.at[m, j], over + 3 * k, (d, mpx(1)))
        send(lg_ref.at[m, j], lg_ref.at[m, j], over + 3 * k + 1, (d, mpx(2)))

    across(0)
    for k in range(1, sz.n_dp):
        arrived(vl_r.at[dpx(k)], vl_at + k)
    vlg_ref[m] = sum(vl_r[k] for k in range(sz.n_dp))
    vlg_at = mp_start(vlg_ref)
    dp_finish(own, lg_at, across)
    dp_finish(eg_ref, eg_at)
    first = sz.erows - 2 * HF
    for k in range(2 * HF // 16):
        row = first + 16 * k
        wog_ref[m, 16 * k : 16 * (k + 1), :] = eg_ref[
            row // sz.echunk, row % sz.echunk : row % sz.echunk + 16, :
        ]
    wog_at = mp_start(wog_ref)
    mp_finish(veg_ref, veg_at)
    mp_finish(vlg_ref, vlg_at)
    order = [0, 2, 4, 6, 1, 3, 5, 7]
    for k in order:
        j = dpx(k)
        arrived(lg_ref.at[mpx(2), j], over + 3 * k + 1)
        send(lg_ref.at[mpx(2), j], lg_ref.at[mpx(2), j], over + 3 * k + 2, (d, mpx(1)))
    mp_finish(wog_ref, wog_at)
    for k in order:
        arrived(lg_ref.at[mpx(1), dpx(k)], over + 3 * k)
        arrived(lg_ref.at[mpx(3), dpx(k)], over + 3 * k + 2)
    for k in (1, 2, 3):
        arrived(gp_ref.at[mpx(k)], gp_at + k)
    for c in pending:
        c.wait_send()
    for k in range(1, sz.n_dp):
        copy(dks.at[0], dkr.at[0], dk_at + k, (d, m)).wait_send()


def unpack_body(
    sz, blk_ref, gp_ref, eg_ref, wog_ref, lg_ref, veg_ref, vlg_ref,
    out_ref, gpix_ref, ln1g_ref, ln1b_ref, gwq_ref, gbq_ref, gwk_ref, gwv_ref, gbv_ref, gwr_ref, gbr_ref,
    lnrg_ref, lnrb_ref, gwo_ref, gbo_ref, ln2g_ref, ln2b_ref, gw1_ref, gb1_ref, gwd_ref, gbd_ref,
    gw2_ref, gb2_ref, out32,
):
    D, HF, PB, PA, PL = sz.width, HEAD_FEATURES, sz.pb, sz.pa, sz.plane
    C, FS = sz.hidden, sz.share
    m = lax.axis_index("mp")
    for i in range(2):
        for j in range(2):
            p = 2 * i + j
            for a in range(PA):
                at = pl.ds((2 * a + i) * sz.cols + j, PB, stride=2)
                out32[at, :] = blk_ref[PL * p + PB * a : PL * p + PB * (a + 1), 0:FS]
                gpix_ref[at, :] = gp_ref[p].astype(F32)[PB * a : PB * (a + 1), 0:FS]
    out_ref[...] = out32[...].astype(BF)

    lg = [lg_ref[h].reshape(sz.lrows, sz.wide) for h in range(4)]

    def heads(first, tail):
        parts = [lg[h][0:D, first : first + HF].astype(F32) for h in range(4)]
        parts.append(sum(lg[h][0:D, tail : tail + HF].astype(F32) for h in range(4)))
        return jnp.concatenate(parts, axis=1)

    gwq_ref[...] = heads(0, HF)
    gwk_ref[...] = heads(LANES, 2 * LANES)
    gwv_ref[...] = heads(LANES + HF, 2 * LANES + HF)
    for h in range(4):
        gwr_ref[D * h : D * (h + 1), :] = lg[h][D:, :D].astype(F32)
    for h in range(4):
        gwo_ref[HF * h : HF * (h + 1), :] = wog_ref[h][0:HF, :D].astype(F32)
    gwo_ref[HF * 4 :, :] = sum(wog_ref[h][HF:, :D].astype(F32) for h in range(4))
    eg = eg_ref[...].reshape(sz.erows, sz.wide)
    gw1_ref[...] = eg[0:D, :C].astype(F32)
    gw2_ref[...] = eg[D : D + C, :D].astype(F32)

    def row(value):
        return value.reshape(value.shape[1])

    ve = veg_ref[m]
    gwd_ref[...] = ve[0:9, :C]
    gbd_ref[...] = row(ve[9:10, :C])
    gb1_ref[...] = row(ve[10:11, :C])
    vs = sum(veg_ref[h] for h in range(4))
    gb2_ref[...] = row(vs[11:12, :D])
    gbo_ref[...] = row(vs[12:13, :D])
    ln2g_ref[...] = row(vs[13:14, :D])
    ln2b_ref[...] = row(vs[14:15, :D])
    vl = sum(vlg_ref[h] for h in range(4))
    ln1g_ref[...] = row(vl[0:1, :D])
    ln1b_ref[...] = row(vl[1:2, :D])
    lnrg_ref[...] = row(vlg_ref[0][2:3, :D])
    lnrb_ref[...] = row(vlg_ref[0][3:4, :D])
    gbr_ref[...] = row(vlg_ref[0][4:5, :D])

    def head_row(r):
        parts = [vlg_ref[h][r : r + 1, 0:HF] for h in range(4)] + [vl[r : r + 1, HF : 2 * HF]]
        return row(jnp.concatenate(parts, axis=1))

    gbq_ref[...] = head_row(5)
    gbv_ref[...] = head_row(6)


def on_device_fused(*args):
    pixels_in, cotangent, pixel_mask, tile_slot = args[:4]
    w_fc1 = args[19]
    sz = Sizes(
        lax.axis_size("dp"), lax.axis_size("mp"), pixels_in.shape[0], cotangent.shape[1], w_fc1.shape[1]
    )
    D, C, PL, T, W, LN = sz.width, sz.hidden, sz.plane, sz.all, sz.wide, LANES
    vm = pl.BlockSpec(memory_space=pltpu.VMEM)
    sm = pl.BlockSpec(memory_space=pltpu.SMEM)
    S = jax.ShapeDtypeStruct
    mids = [
        S((T, LN), F32), S((4, PL, LN), BF), S((sz.n_dp, sz.echunk, W), BF), S((4, 2 * HEAD_FEATURES, W), BF),
        S((4, sz.n_dp, sz.lchunk, W), BF), S((4, 16, W), F32), S((4, 8, W), F32),
    ]
    v = pltpu.VMEM
    scratch = dict(
        x32=v((sz.tokens, sz.share), F32), c32a=v((sz.tokens, LN), F32), c32b=v((sz.tokens, LN), F32),
        c32c=v((sz.tokens, D - 2 * LN), F32), xg=v((4, T, LN), BF), dfm=v((T, D), BF), dyh_s=v((48, W), BF),
        dyh=v((sz.n_dp, 48, W), BF), dyh_g=v((4, 48, W), BF), xm_r=v((T, D), BF), n1_r=v((T, D), BF),
        xhr_r=v((PL, D), F32), rsr_r=v((PL, LN), F32), xr_r=v((PL, D), BF), kva=v((sz.n_dp, sz.kvrows, LN), BF),
        qa_r=v((LN, T), BF), qb_r=v((LN, T), BF), sbuf=v((sz.n_dp, PL, T), F32), ebuf=v((sz.n_dp, PL, T), BF),
        e5buf=v((sz.n_dp, sz.quarter, T), BF), lse_r=v((4, 8, T), F32), og=v((4, T, LN), BF), row_r=v((8, T), F32),
        h1_r=v((T, D), F32), n2_r=v((T, D), BF), hal_s=v((2 * sz.pb, W), BF), hal=v((sz.n_dp, 2 * sz.pb, W), BF),
        hal_g=v((4, 2 * sz.pb, W), BF), ux=v((4, sz.ext, C), F32), ul=v((2, sz.ext, C), F32),
        ur=v((2, sz.ext, C), F32), dgx=v((4, sz.ext, C), F32), dzx=v((4, sz.ext, C), F32),
        dzl=v((2, sz.ext, C), F32), dzr=v((2, sz.ext, C), F32), g_r=v((4, PL, C), F32), du_r=v((4, PL, C), F32),
        dn2_s=v((4, PL, W), BF), dn2_r=v((3, PL, W), BF), dh1_r=v((PL, D), F32), dos=v((4, PL, LN), BF),
        do_all=v((4, PL, LN), BF), dabg=v((4, PL, W), BF), ff_s=v((4, T, LN), BF), ff_r=v((3, T, LN), BF),
        dks=v((sz.n_dp, sz.kvrows, LN), BF), dkr=v((sz.n_dp - 1, sz.kvrows, LN), BF), dkvg=v((4, sz.kvrows, LN), BF),
        dqs=v((4, PL, LN), BF), dq_all=v((4, PL, LN), BF), dqt=v((LN, T), F32), dqt5=v((LN, T), F32),
        e_s=v((sz.erows, W), BF), e_r=v((sz.n_dp - 1, sz.echunk, W), BF), l_s=v((sz.lrows, W), BF),
        l_r=v((sz.n_dp - 1, sz.lchunk, W), BF), ve_s=v((16, W), F32), ve_r=v((sz.n_dp, 16, W), F32),
        vl_s=v((8, W), F32), vl_r=v((sz.n_dp, 8, W), F32), gps=v((4, PL, LN), BF),
        ssem=pltpu.SemaphoreType.DMA((176,)), rsem=pltpu.SemaphoreType.DMA((176,)),
    )
    mid = pl.pallas_call(
        functools.partial(fused_body, sz),
        out_shape=mids,
        in_specs=[sm, sm] + [vm] * 23,
        out_specs=[vm] * len(mids),
        scratch_shapes=list(scratch.values()),
        compiler_params=pltpu.CompilerParams(
            collective_id=0, has_side_effects=True, vmem_limit_bytes=60 * 2**20
        ),
        name="fused_block",
    )(pixel_mask, tile_slot, pixels_in, cotangent, *args[4:])
    outs = [
        S((sz.tokens, sz.share), BF), S((sz.tokens, sz.share), F32), S((D,), F32), S((D,), F32), S((D, D), F32),
        S((D,), F32), S((D, D), F32), S((D, D), F32), S((D,), F32), S((4 * D, D), F32), S((D,), F32), S((D,), F32),
        S((D,), F32), S((D, D), F32), S((D,), F32), S((D,), F32), S((D,), F32), S((D, C), F32), S((C,), F32),
        S((9, C), F32), S((C,), F32), S((C, D), F32), S((D,), F32),
    ]
    return tuple(
        pl.pallas_call(
            functools.partial(unpack_body, sz),
            out_shape=outs,
            in_specs=[vm] * len(mids),
            out_specs=[vm] * len(outs),
            scratch_shapes=[pltpu.VMEM((sz.tokens, sz.share), F32)],
            compiler_params=pltpu.CompilerParams(vmem_limit_bytes=40 * 2**20),
            name="unpack",
        )(*mid)
    )


def choose(*args):
    tokens, width = args[1].shape
    whole_rows = tokens == FRAME * (FRAME // TILE_ROWS)
    shape = (lax.axis_size("dp"), lax.axis_size("mp"))
    if whole_rows and shape == (TILE_ROWS, 4) and TILE_ROWS == 8 and HEADS == 5 and width == 320 == args[19].shape[1]:
        return on_device_fused(*args)
    return on_device(*args)


def solution(mesh):
    return jax.shard_map(
        choose,
        mesh=mesh,
        in_specs=(
            P("dp", "mp"),
            P("dp", None),
            P("dp"),
            P(),
            P(),
            P(),
            P(),
            P(),
            P(),
            P(),
            P(),
            P(),
            P(),
            P(),
            P(),
            P(),
            P(),
            P(),
            P(),
            P(None, "mp"),
            P("mp"),
            P(None, "mp"),
            P("mp"),
            P("mp", None),
            P(),
        ),
        out_specs=(
            P("dp", "mp"),
            P("dp", "mp"),
            P(),
            P(),
            P(),
            P(),
            P(),
            P(),
            P(),
            P(),
            P(),
            P(),
            P(),
            P(),
            P(),
            P(),
            P(),
            P(None, "mp"),
            P("mp"),
            P(None, "mp"),
            P("mp"),
            P("mp", None),
            P(),
        ),
        check_vma=False,
    )
```

```python
import functools

import jax
import jax.numpy as jnp
from jax import lax
from jax.experimental import pallas as pl
from jax.experimental.pallas import tpu as pltpu
from jax.sharding import PartitionSpec as P

HEADS = 5
HEAD_FEATURES = 64
FRAME = 80
TILE_ROWS = 8


EPS = 1e-05
NEG = -1e30


def layer_norm(value, gain, shift):
    mean = jnp.mean(value, axis=-1, keepdims=True)
    centred = value - mean
    spread = jnp.mean(centred * centred, axis=-1, keepdims=True)
    return centred * lax.rsqrt(spread + EPS) * gain + shift


def depth_gelu(padded, kernel, shift):
    rows = padded.shape[0] - 2
    cols = padded.shape[1] - 2
    total = jnp.zeros((rows, cols, padded.shape[2]), jnp.float32) + shift
    for row_off in range(3):
        for col_off in range(3):
            total = (
                total
                + kernel[3 * row_off + col_off]
                * padded[row_off : row_off + rows, col_off : col_off + cols]
            )
    return jax.nn.gelu(total, approximate=False)


def mat(left, right):
    return jnp.dot(left, right, preferred_element_type=jnp.float32)


def pick(weights, table):
    return jnp.einsum(
        "j,jab->ab", weights.astype(table.dtype), table, preferred_element_type=jnp.float32
    )


def head_columns(weight_matrix, select_where):
    wide_layout = weight_matrix.astype(jnp.float32).reshape(
        weight_matrix.shape[0], HEADS, HEAD_FEATURES
    )
    return (
        jnp.einsum("uzx,nz->unx", wide_layout, select_where)
        .reshape(weight_matrix.shape[0], -1)
        .astype(jnp.bfloat16)
    )


def head_rows(weight_matrix, select_where):
    wide_layout = weight_matrix.astype(jnp.float32).reshape(
        HEADS, HEAD_FEATURES, weight_matrix.shape[1]
    )
    return (
        jnp.einsum("hed,sh->sed", wide_layout, select_where)
        .reshape(-1, weight_matrix.shape[1])
        .astype(jnp.bfloat16)
    )


def head_vector(vector_entries, select_where):
    return jnp.einsum(
        "he,sh->se", vector_entries.reshape(HEADS, HEAD_FEATURES), select_where
    ).reshape(-1)


def spread_columns(gradient_value, select_where):
    return jnp.einsum(
        "tvm,vq->tqm",
        gradient_value.reshape(gradient_value.shape[0], -1, HEAD_FEATURES),
        select_where,
    ).reshape(gradient_value.shape[0], -1)


def spread_rows(gradient_value, select_where):
    return jnp.einsum(
        "sed,sh->hed",
        gradient_value.reshape(-1, HEAD_FEATURES, gradient_value.shape[1]),
        select_where,
    ).reshape(-1, gradient_value.shape[1])


def spread_vector(gradient_value, select_where):
    return jnp.einsum("se,sh->he", gradient_value.reshape(-1, HEAD_FEATURES), select_where).reshape(
        -1
    )


def on_device(
    pixels_in,
    cotangent,
    pixel_mask,
    tile_slot,
    ln1_gain,
    ln1_bias,
    w_query,
    b_query,
    w_key,
    w_value,
    b_value,
    w_reduce,
    b_reduce,
    lnr_gain,
    lnr_bias,
    w_out,
    b_out,
    ln2_gain,
    ln2_bias,
    w_fc1,
    b_fc1,
    w_depth,
    b_depth,
    w_fc2,
    b_fc2,
):
    n_dp = lax.axis_size("dp")
    n_mp = lax.axis_size("mp")
    device = lax.axis_index("dp")
    part = lax.axis_index("mp")
    rows = FRAME // TILE_ROWS
    tokens = pixels_in.shape[0]
    cols = tokens // rows
    tiles_col = FRAME // cols
    per_frame = TILE_ROWS * tiles_col
    width = ln1_gain.shape[0]
    share = width // n_mp
    slots = -(-HEADS // n_mp)
    scale = HEAD_FEATURES ** (-0.5)
    maskf = pixel_mask.astype(jnp.float32)[:, None]
    head_ids = part + n_mp * jnp.arange(slots)
    select_where = (head_ids[:, None] == jnp.arange(HEADS)[None, :]).astype(jnp.float32)
    crops = tile_slot[:, 0]
    tiles = tile_slot[:, 1]
    is_me = jnp.arange(n_dp) == device
    own_crop = jnp.sum(jnp.where(is_me, crops, 0))
    own_tile = jnp.sum(jnp.where(is_me, tiles, 0))
    own_row = own_tile // tiles_col
    own_col = own_tile % tiles_col
    tile_row = tiles // tiles_col
    tile_col = tiles % tiles_col

    def beside(drow, dcol):
        hit = (crops == own_crop) & (tile_row == own_row + drow) & (tile_col == own_col + dcol)
        return hit.astype(jnp.float32)

    member = (crops[None, :] == own_crop) & (tiles[None, :] == jnp.arange(per_frame)[:, None])
    crop_devices = jnp.sum(jnp.where(member, jnp.arange(n_dp)[None, :], 0), axis=1)
    whole = lax.all_gather(pixels_in, "mp", axis=1, tiled=True)
    xm = whole.astype(jnp.float32) * maskf
    n1, first_norm_backward = jax.vjp(layer_norm, xm, ln1_gain, ln1_bias)
    n1b = n1.astype(jnp.bfloat16)
    wq = head_columns(w_query, select_where)
    wk = head_columns(w_key, select_where)
    wv = head_columns(w_value, select_where)
    wo = head_rows(w_out, select_where)
    qb = (mat(n1b, wq) + head_vector(b_query, select_where)).astype(jnp.bfloat16)
    patches = (
        n1b.reshape(rows // 2, 2, cols // 2, 2, width)
        .transpose(0, 2, 1, 3, 4)
        .reshape(-1, 4 * width)
    )
    reduced = mat(patches, w_reduce) + b_reduce
    xr, lnr_back = jax.vjp(layer_norm, reduced, lnr_gain, lnr_bias)
    xrb = xr.astype(jnp.bfloat16)
    kb = mat(xrb, wk).astype(jnp.bfloat16)
    vb = (mat(xrb, wv) + head_vector(b_value, select_where)).astype(jnp.bfloat16)
    kmask = (
        pixel_mask.reshape(rows // 2, 2, cols // 2, 2)[:, 0, :, 0].reshape(-1).astype(jnp.bfloat16)
    )
    keys_all, values_all, kmask_all = (
        lax.all_gather(kb, "dp", axis=0, tiled=True),
        lax.all_gather(vb, "dp", axis=0, tiled=True),
        lax.all_gather(kmask, "dp", axis=0, tiled=True),
    )
    per_key = kb.shape[0]
    keys_crop = keys_all.reshape(n_dp, per_key, -1)[crop_devices]
    values_crop = values_all.reshape(n_dp, per_key, -1)[crop_devices]
    usable_crop = kmask_all.reshape(n_dp, per_key)[crop_devices].astype(jnp.float32) > 0.5
    n_blocks = 4
    key_blocks = keys_crop.reshape(n_blocks, -1, slots, HEAD_FEATURES)
    value_blocks = values_crop.reshape(n_blocks, -1, slots, HEAD_FEATURES)
    usable_blocks = usable_crop.reshape(n_blocks, -1)
    queries = qb.reshape(tokens, slots, HEAD_FEATURES)

    def block_scores(key_block, usable_block):
        raw = (
            jnp.einsum("qsd,ksd->sqk", queries, key_block, preferred_element_type=jnp.float32)
            * scale
        )
        return jnp.where(usable_block[None, None, :], raw, NEG)

    def top_step(carry, blocks):
        top, total = carry
        key_block, usable_block = blocks
        scores = block_scores(key_block, usable_block)
        new_top = jnp.maximum(top, jnp.max(scores, axis=-1))
        total = total * jnp.exp(top - new_top) + jnp.sum(
            jnp.exp(scores - new_top[..., None]), axis=-1
        )
        return ((new_top, total), None)

    start = (jnp.full((slots, tokens), NEG, jnp.float32), jnp.zeros((slots, tokens), jnp.float32))
    (top, total), _ = lax.scan(top_step, start, (key_blocks, usable_blocks))
    lse = top + jnp.log(total)

    def out_step(acc, blocks):
        key_block, value_block, usable_block = blocks
        prob = jnp.exp(block_scores(key_block, usable_block) - lse[..., None])
        acc = acc + jnp.einsum(
            "sqk,ksd->qsd",
            prob.astype(jnp.bfloat16),
            value_block,
            preferred_element_type=jnp.float32,
        )
        return (acc, None)

    empty = jnp.zeros((tokens, slots, HEAD_FEATURES), jnp.float32)
    acc, _ = lax.scan(out_step, empty, (key_blocks, value_blocks, usable_blocks))
    ob = acc.reshape(tokens, -1).astype(jnp.bfloat16)
    branch = lax.psum(mat(ob, wo).astype(jnp.bfloat16), "mp").astype(jnp.float32) + b_out
    h1 = xm + branch * maskf
    n2, ln2_back = jax.vjp(layer_norm, h1, ln2_gain, ln2_bias)
    n2b = n2.astype(jnp.bfloat16)
    ub = ((mat(n2b, w_fc1) + b_fc1) * maskf).astype(jnp.bfloat16)
    channels = ub.shape[1]
    tile_u = ub.reshape(rows, cols, channels)
    lines, sides = (
        lax.all_gather(jnp.stack([tile_u[0], tile_u[-1]]), "dp", axis=0, tiled=True),
        lax.all_gather(jnp.stack([tile_u[:, 0], tile_u[:, -1]]), "dp", axis=0, tiled=True),
    )
    lines = lines.reshape(n_dp, 2, cols, channels)
    sides = sides.reshape(n_dp, 2, rows, channels)
    top_lines = lines[:, 0]
    bottom_lines = lines[:, 1]
    left_sides = sides[:, 0]
    right_sides = sides[:, 1]
    upper = jnp.concatenate(
        [
            pick(beside(-1, -1), bottom_lines[:, -1:]),
            pick(beside(-1, 0), bottom_lines),
            pick(beside(-1, 1), bottom_lines[:, :1]),
        ],
        axis=0,
    )
    lower = jnp.concatenate(
        [
            pick(beside(1, -1), top_lines[:, -1:]),
            pick(beside(1, 0), top_lines),
            pick(beside(1, 1), top_lines[:, :1]),
        ],
        axis=0,
    )
    middle = jnp.concatenate(
        [
            pick(beside(0, -1), right_sides)[:, None],
            tile_u.astype(jnp.float32),
            pick(beside(0, 1), left_sides)[:, None],
        ],
        axis=1,
    )
    padded = jnp.concatenate([upper[None], middle, lower[None]], axis=0)
    act, depth_back = jax.vjp(depth_gelu, padded, w_depth, b_depth)
    gb = act.reshape(tokens, channels).astype(jnp.bfloat16)
    ffn_mine = lax.psum_scatter(
        mat(gb, w_fc2).astype(jnp.bfloat16), "mp", scatter_dimension=1, tiled=True
    ).astype(jnp.float32)
    h1_mine = lax.dynamic_slice_in_dim(h1, part * share, share, 1)
    bias_mine = lax.dynamic_slice_in_dim(b_fc2, part * share, share, 0)
    block_result = (h1_mine + (ffn_mine + bias_mine) * maskf).astype(jnp.bfloat16)
    dy = cotangent.astype(jnp.float32)
    dff = dy * maskf
    grad_b_fc2 = jnp.sum(dff, axis=0)
    dfb = dff.astype(jnp.bfloat16)
    grad_w_fc2 = mat(gb.T, dfb)
    dgr = mat(dfb, w_fc2.T).astype(jnp.bfloat16).astype(jnp.float32).reshape(rows, cols, channels)
    dpad, grad_w_depth, grad_b_depth = depth_back(dgr)
    grad_lines, grad_sides = (
        lax.all_gather(
            jnp.stack([dpad[0], dpad[-1]]).astype(jnp.bfloat16), "dp", axis=0, tiled=True
        ).astype(jnp.float32),
        lax.all_gather(
            jnp.stack([dpad[1:-1, 0], dpad[1:-1, -1]]).astype(jnp.bfloat16),
            "dp",
            axis=0,
            tiled=True,
        ).astype(jnp.float32),
    )
    grad_lines = grad_lines.reshape(n_dp, 2, cols + 2, channels)
    grad_sides = grad_sides.reshape(n_dp, 2, rows, channels)
    top_grads = grad_lines[:, 0]
    bottom_grads = grad_lines[:, 1]
    dtile = dpad[1:-1, 1:-1]
    dtile = dtile.at[0].add(pick(beside(-1, 0), bottom_grads[:, 1:-1]))
    dtile = dtile.at[0, 0].add(pick(beside(-1, -1), bottom_grads[:, -1:])[0])
    dtile = dtile.at[0, -1].add(pick(beside(-1, 1), bottom_grads[:, :1])[0])
    dtile = dtile.at[-1].add(pick(beside(1, 0), top_grads[:, 1:-1]))
    dtile = dtile.at[-1, 0].add(pick(beside(1, -1), top_grads[:, -1:])[0])
    dtile = dtile.at[-1, -1].add(pick(beside(1, 1), top_grads[:, :1])[0])
    dtile = dtile.at[:, 0].add(pick(beside(0, -1), grad_sides[:, 1]))
    dtile = dtile.at[:, -1].add(pick(beside(0, 1), grad_sides[:, 0]))
    dub = (dtile.reshape(tokens, channels).astype(jnp.bfloat16).astype(jnp.float32) * maskf).astype(
        jnp.bfloat16
    )
    grad_b_fc1 = jnp.sum(dub.astype(jnp.float32), axis=0)
    grad_w_fc1 = mat(n2b.T, dub)
    dn2_part = mat(dub, w_fc1.T)
    zero_vector = jnp.zeros((width,), jnp.float32)
    dn2 = lax.psum(dn2_part.astype(jnp.bfloat16), "mp").astype(jnp.float32)
    dh1_norm, shared_gain, shared_bias = ln2_back(dn2)
    dh1 = dy + dh1_norm
    split_gain = zero_vector
    split_bias = zero_vector
    dattn = dh1 * maskf
    grad_b_out = jnp.sum(dattn, axis=0)
    dab = dattn.astype(jnp.bfloat16)
    grad_wo = mat(ob.T, dab)
    dob = mat(dab, wo.T).astype(jnp.bfloat16)
    dout = dob.reshape(tokens, slots, HEAD_FEATURES)
    drow = jnp.sum(dout.astype(jnp.float32) * acc, axis=-1).T

    def back_step(dq_acc, blocks):
        key_block, value_block, usable_block = blocks
        prob = jnp.exp(block_scores(key_block, usable_block) - lse[..., None])
        dv_block = jnp.einsum(
            "sqk,qsd->ksd", prob.astype(jnp.bfloat16), dout, preferred_element_type=jnp.float32
        )
        dprob = jnp.einsum("qsd,ksd->sqk", dout, value_block, preferred_element_type=jnp.float32)
        dscore = (prob * (dprob - drow[..., None])).astype(jnp.bfloat16)
        dq_acc = dq_acc + jnp.einsum(
            "sqk,ksd->qsd", dscore, key_block, preferred_element_type=jnp.float32
        )
        dk_block = (
            jnp.einsum("sqk,qsd->ksd", dscore, queries, preferred_element_type=jnp.float32) * scale
        )
        return (dq_acc, (dk_block, dv_block))

    dq_acc, (dk_blocks, dv_blocks) = lax.scan(
        back_step, empty, (key_blocks, value_blocks, usable_blocks)
    )
    zero_keys = jnp.zeros((n_dp, per_key, slots * HEAD_FEATURES), jnp.float32)
    dk_full = (
        zero_keys.at[crop_devices]
        .set(dk_blocks.reshape(per_frame, per_key, -1))
        .reshape(n_dp * per_key, -1)
    )
    dv_full = (
        zero_keys.at[crop_devices]
        .set(dv_blocks.reshape(per_frame, per_key, -1))
        .reshape(n_dp * per_key, -1)
    )
    dk_mine, dv_mine = (
        lax.psum_scatter(dk_full, "dp", scatter_dimension=0, tiled=True),
        lax.psum_scatter(dv_full, "dp", scatter_dimension=0, tiled=True),
    )
    dkb = dk_mine.astype(jnp.bfloat16)
    dvb = dv_mine.astype(jnp.bfloat16)
    dqb = (dq_acc * scale).reshape(tokens, -1).astype(jnp.bfloat16)
    grad_wq = mat(n1b.T, dqb)
    grad_bq = jnp.sum(dqb.astype(jnp.float32), axis=0)
    grad_wk = mat(xrb.T, dkb)
    grad_wv = mat(xrb.T, dvb)
    grad_bv = jnp.sum(dvb.astype(jnp.float32), axis=0)
    dxr, dn1_query = (
        lax.psum((mat(dkb, wk.T) + mat(dvb, wv.T)).astype(jnp.bfloat16), "mp").astype(jnp.float32),
        lax.psum(mat(dqb, wq.T).astype(jnp.bfloat16), "mp").astype(jnp.float32),
    )
    dreduced, grad_lnr_gain, grad_lnr_bias = lnr_back(dxr)
    drb = dreduced.astype(jnp.bfloat16)
    grad_w_reduce = mat(patches.T, drb)
    grad_b_reduce = jnp.sum(drb.astype(jnp.float32), axis=0)
    dpatch = (
        mat(drb, w_reduce.T)
        .reshape(rows // 2, cols // 2, 2, 2, width)
        .transpose(0, 2, 1, 3, 4)
        .reshape(tokens, width)
    )
    dxm, grad_ln1_gain, grad_ln1_bias = first_norm_backward(dn1_query + dpatch)
    grad_whole = (dxm + dh1) * maskf
    grad_input = lax.dynamic_slice_in_dim(grad_whole, part * share, share, 1)
    (
        grad_w_reduce,
        grad_b_reduce,
        grad_lnr_gain,
        grad_lnr_bias,
        grad_ln1_gain,
        grad_ln1_bias,
        shared_gain,
        shared_bias,
        grad_b_out,
        grad_b_fc2,
        grad_w_fc1,
        grad_b_fc1,
        grad_w_depth,
        grad_b_depth,
        grad_w_fc2,
    ) = lax.psum(
        (
            grad_w_reduce,
            grad_b_reduce,
            grad_lnr_gain,
            grad_lnr_bias,
            grad_ln1_gain,
            grad_ln1_bias,
            shared_gain,
            shared_bias,
            grad_b_out,
            grad_b_fc2,
            grad_w_fc1,
            grad_b_fc1,
            grad_w_depth,
            grad_b_depth,
            grad_w_fc2,
        ),
        "dp",
    )
    (
        grad_w_query,
        grad_b_query,
        grad_w_key,
        grad_w_value,
        grad_b_value,
        output_weight_gradient,
        split_gain,
        split_bias,
    ) = lax.psum(
        (
            spread_columns(grad_wq, select_where),
            spread_vector(grad_bq, select_where),
            spread_columns(grad_wk, select_where),
            spread_columns(grad_wv, select_where),
            spread_vector(grad_bv, select_where),
            spread_rows(grad_wo, select_where),
            split_gain,
            split_bias,
        ),
        ("dp", "mp"),
    )
    grad_ln2_gain = shared_gain + split_gain
    grad_ln2_bias = shared_bias + split_bias
    return (
        block_result,
        grad_input,
        grad_ln1_gain,
        grad_ln1_bias,
        grad_w_query,
        grad_b_query,
        grad_w_key,
        grad_w_value,
        grad_b_value,
        grad_w_reduce,
        grad_b_reduce,
        grad_lnr_gain,
        grad_lnr_bias,
        output_weight_gradient,
        grad_b_out,
        grad_ln2_gain,
        grad_ln2_bias,
        grad_w_fc1,
        grad_b_fc1,
        grad_w_depth,
        grad_b_depth,
        grad_w_fc2,
        grad_b_fc2,
    )


BF = jnp.bfloat16
F32 = jnp.float32
LANES = 128
SIDE_SMALL = 64
VMEM_MB = 56


def nn(a, b):
    return lax.dot_general(a, b, (((1,), (0,)), ((), ())), preferred_element_type=F32)


def nt(a, b):
    return lax.dot_general(a, b, (((1,), (1,)), ((), ())), preferred_element_type=F32)


def tn(a, b):
    return lax.dot_general(a, b, (((0,), (0,)), ((), ())), preferred_element_type=F32)


def iota(shape, axis):
    return lax.broadcasted_iota(jnp.int32, shape, axis)


def hot(cond):
    return jnp.where(cond, 1.0, 0.0).astype(BF)


def spread(value):
    mean = jnp.sum(value, axis=-1, keepdims=True) * (1.0 / value.shape[-1])
    centred = value - mean
    var = jnp.sum(centred * centred, axis=-1, keepdims=True) * (1.0 / value.shape[-1])
    rstd = lax.rsqrt(var + EPS)
    return centred * rstd, rstd


def norm_back(dn, gain, xhat, rstd):
    e = dn * gain
    scale = 1.0 / dn.shape[-1]
    mean_e = jnp.sum(e, axis=-1, keepdims=True) * scale
    mean_ex = jnp.sum(e * xhat, axis=-1, keepdims=True) * scale
    return rstd * (e - mean_e - xhat * mean_ex)


def rowsum(value):
    return jnp.sum(value, axis=0, keepdims=True)


class Sizes:
    def __init__(self, n_dp, n_mp, tokens, width, hidden):
        self.n_dp, self.n_mp = n_dp, n_mp
        self.tokens, self.width, self.hidden = tokens, width, hidden
        self.share = width // n_mp
        self.rows = FRAME // TILE_ROWS
        self.cols = tokens // self.rows
        self.pa, self.pb = self.rows // 2, self.cols // 2
        self.keys = self.pa * self.pb
        self.plane = -(-self.keys // 16) * 16
        self.all = 4 * self.plane
        self.step = self.plane // 16 // n_mp * 16
        self.quarter = self.plane - (n_mp - 1) * self.step
        self.wide = -(-width // LANES) * LANES
        self.kvrows = self.plane + self.quarter
        self.top = 8 + self.pb
        self.ext = self.top + self.keys + self.pb
        self.edge = 4 * 2 * self.pb
        self.inner = 4 * (self.keys - 2 * self.pb)
        self.edge_q = -(-self.edge // LANES) * LANES
        self.inner_q = -(-self.inner // LANES) * LANES
        self.queries = self.edge_q + self.inner_q
        self.echunk = (width + hidden) // n_dp
        self.lrows = width + HEAD_FEATURES
        self.lchunk = self.lrows // n_dp


class Load:
    def __init__(self, src, dst, sem):
        self.dst, self.shape, self.waiting = dst, dst.shape, True
        self.copy = pltpu.make_async_copy(src, dst, sem)
        self.copy.start()

    def ready(self):
        if self.waiting:
            self.waiting = False
            self.copy.wait()
        return self.dst

    def __getitem__(self, at):
        return self.ready()[at]


def fused_body(
    sz, names,
    mask_ref, slot_ref, *refs,
):
    ins, refs = refs[:23], refs[23:]
    outs, refs = refs[:7], refs[7:]
    blk_ref, gp_ref, eg_ref, lg1_ref, lg2_ref, veg_ref, vlg_ref = outs
    s = dict(zip(names, refs))
    D, HF, PB, PA, KEYS, PL, T = sz.width, HEAD_FEATURES, sz.pb, sz.pa, sz.keys, sz.plane, sz.all
    C, FS, W = sz.hidden, sz.share, sz.wide
    d = lax.axis_index("dp")
    m = lax.axis_index("mp")
    last = sz.n_mp * HF
    ssem, rsem = s["ssem"], s["rsem"]

    def mpx(k):
        if k == 0:
            return m
        if k == 1:
            return m + 1 - 2 * lax.rem(m, 2)
        if k == 2:
            return lax.rem(m + 2, 4)
        return 3 - m

    def dpx(k):
        z, x = d // 2, lax.rem(d, 2)
        if k & 1:
            x = 1 - x
        kz = k >> 1
        if kz == 1:
            z = z + 1 - 2 * lax.rem(z, 2)
        elif kz == 2:
            z = lax.rem(z + 2, 4)
        elif kz == 3:
            z = 3 - z
        return 2 * z + x

    counter = [0]
    pending = []

    def take(n):
        first = counter[0]
        counter[0] += n
        return first

    def copy(src, dst, sem, dev):
        return pltpu.make_async_remote_copy(
            src_ref=src, dst_ref=dst, send_sem=ssem.at[sem], recv_sem=rsem.at[sem],
            device_id=dev, device_id_type=pl.DeviceIdType.MESH,
        )

    def send(src, dst, sem, dev):
        c = copy(src, dst, sem, dev)
        c.start()
        pending.append(c)

    def arrived(ref, sem):
        copy(ref, ref, sem, (d, m)).wait_recv()

    opened = []

    def handle(finish):
        state = [False]

        def once(*a):
            if not state[0]:
                state[0] = True
                return finish(*a)

        opened.append(once)
        return once

    def mp_start(buf):
        base = take(3)
        send(buf.at[m], buf.at[m], base, (d, mpx(1)))
        send(buf.at[m], buf.at[m], base + 1, (d, mpx(2)))

        def middle():
            arrived(buf.at[mpx(2)], base + 1)
            send(buf.at[mpx(2)], buf.at[mpx(2)], base + 2, (d, mpx(1)))

        mid = handle(middle)

        def finish():
            mid()
            arrived(buf.at[mpx(1)], base)
            arrived(buf.at[mpx(3)], base + 2)

        return handle(finish), mid

    def dp_start(buf):
        base = take(7)
        for kz in (3, 2, 1):
            send(buf.at[d], buf.at[d], base + kz, (dpx(2 * kz), m))
        send(buf.at[d], buf.at[d], base, (dpx(1), m))

        def finish(each=lambda k: None):
            for kz in (1, 2, 3):
                arrived(buf.at[dpx(2 * kz)], base + kz)
                send(buf.at[dpx(2 * kz)], buf.at[dpx(2 * kz)], base + 3 + kz, (dpx(1), m))
                each(2 * kz)
            arrived(buf.at[dpx(1)], base)
            each(1)
            for kz in (1, 2, 3):
                arrived(buf.at[dpx(2 * kz + 1)], base + 3 + kz)
                each(2 * kz + 1)

        return handle(finish)

    def mp_scatter(block, dst, landed):
        base = take(4)
        for k in (2, 3, 1):
            send(block(mpx(k)), dst(k), base + k, (d, mpx(k)))

        def finish():
            for k in (1, 2, 3):
                arrived(landed(k), base + k)

        return handle(finish)

    def dp_scatter(block, dst, landed):
        base = take(8)
        for k in (6, 7, 4, 5, 2, 3, 1):
            send(block(dpx(k)), dst(k), base + k, (dpx(k), m))

        def finish():
            for k in range(1, sz.n_dp):
                arrived(landed(k), base + k)

        return handle(finish)

    def mp_sum(block, out, near, far):
        base = take(3)
        out[0] = block(mpx(1)).astype(BF)
        send(out.at[0], near.at[0], base, (d, mpx(1)))
        out[1] = block(mpx(3)).astype(BF)
        send(out.at[1], near.at[1], base + 1, (d, mpx(1)))

        def middle():
            value = block(mpx(2))
            arrived(near.at[1], base + 1)
            out[2] = (value + near[1].astype(F32)).astype(BF)
            send(out.at[2], far, base + 2, (d, mpx(2)))

        mid = handle(middle)

        def finish():
            mid()
            value = block(m)
            arrived(near.at[0], base)
            value = value + near[0].astype(F32)
            arrived(far, base + 2)
            return value + far[...].astype(F32)

        return mid, handle(finish)

    def dp_sum(chunk, near, out, far):
        base = take(8)
        for kz in (2, 3, 1, 0):
            send(chunk(dpx(2 * kz + 1)), near.at[kz], base + kz, (dpx(1), m))

        def middle():
            for kz in (2, 3, 1):
                value = chunk(dpx(2 * kz))[...].astype(F32)
                arrived(near.at[kz], base + kz)
                out[kz] = (value + near[kz].astype(F32)).astype(BF)
                send(out.at[kz], far.at[kz], base + 4 + kz, (dpx(2 * kz), m))

        mid = handle(middle)

        def finish():
            mid()
            value = chunk(d)[...].astype(F32)
            arrived(near.at[0], base)
            value = value + near[0].astype(F32)
            for kz in (1, 2, 3):
                arrived(far.at[kz], base + 4 + kz)
                value = value + far[kz].astype(F32)
            return value

        return mid, handle(finish)

    def dp_total(src, near, parts):
        base = take(4)
        z = d // 2
        send(src, near, base, (dpx(1), m))

        def middle():
            arrived(near, base)
            parts[z] = src[...] + near[...]
            for kz in (2, 3, 1):
                send(parts.at[z], parts.at[z], base + kz, (dpx(2 * kz), m))

        mid = handle(middle)

        def finish():
            mid()
            for kz in (1, 2, 3):
                arrived(parts.at[dpx(2 * kz) // 2], base + kz)
            return (parts[0] + parts[1]) + (parts[2] + parts[3])

        return mid, handle(finish)

    peers = [(d, mpx(k)) for k in (1, 2, 3)] + [(dpx(k), m) for k in range(1, 8)]
    bar = pltpu.get_barrier_semaphore()
    for dev in peers:
        pl.semaphore_signal(bar, inc=1, device_id=dev, device_id_type=pl.DeviceIdType.MESH)

    order = (0, 1, 2, 3, 8, 7, 9, 10, 11, 12, 4, 5, 6, 21, 22, 13, 14, 15, 16, 17, 18, 19, 20)
    loads = [None] * 23
    for i in order:
        dst = s["xt"].at[m] if i == 0 else s["in%d" % i]
        loads[i] = Load(ins[i], dst, s["isem"].at[i])
    (
        pix_ref, cot_ref, ln1g_ref, ln1b_ref, wq_ref, bq_ref, wk_ref, wv_ref, bv_ref, wr_ref, br_ref,
        lnrg_ref, lnrb_ref, wo_ref, bo_ref, ln2g_ref, ln2b_ref, w1_ref, b1_ref, wd_ref, bd_ref, w2_ref, b2_ref,
    ) = loads

    side = jnp.where(mask_ref[sz.cols - 1] > 0, FRAME, SIDE_SMALL)
    tile = slot_ref[1, d]
    tiles = [slot_ref[1, k] for k in range(sz.n_dp)]
    above = sum(jnp.where(tiles[k] == tile - 1, k, 0) for k in range(sz.n_dp))
    below = sum(jnp.where(tiles[k] == tile + 1, k, 0) for k in range(sz.n_dp))

    def place(p, count):
        a = sum(jnp.where(p >= PB * k, 1, 0) for k in range(1, count))
        return a, p - PB * a

    def token_mask(i, j):
        p = iota((PL, 1), 0)
        a, b = place(p, PA)
        inside = (p < KEYS) & (sz.rows * tile + 2 * a + i < side) & (2 * b + j < side)
        return jnp.where(inside, 1.0, 0.0)

    def row_mask(i, j, a):
        b = iota((PB, 1), 0)
        row = sz.rows * tile + 2 * a + i
        inside = (row >= 0) & (row < side) & (2 * b + j < side)
        return jnp.where(inside, 1.0, 0.0)

    def key_bias(p, tile_at):
        a, b = place(p, PA)
        usable = (p < KEYS) & (sz.rows * tile_at + 2 * a < side) & (2 * b < side)
        return jnp.where(usable, 0.0, NEG)

    def vec(ref):
        return ref[...].reshape(1, ref.shape[0])

    def own_part(row, size):
        return sum(
            jnp.where(m == h, 1.0, 0.0) * row[:, size * h : size * (h + 1)] for h in range(sz.n_mp)
        )

    def plane_rows(ref, start):
        return ref[pl.ds(pl.multiple_of(start, 16), PL), :]

    def plane(p):
        return slice(PL * p, PL * (p + 1))

    lanes3 = (s["t0"], s["t1"], s["t2"])

    def to_planes(rows_of):
        for n, ref in enumerate(lanes3):
            ref[...] = rows_of(LANES * n, min(D, LANES * (n + 1))).astype(F32).T
        for i in range(2):
            for j in range(2):
                parts = []
                for ref in lanes3:
                    rows = [
                        ref[pl.ds((2 * a + i) * sz.cols + j, PB, stride=2), :] for a in range(PA)
                    ] + [jnp.zeros((PL - KEYS, ref.shape[1]), F32)]
                    parts.append(jnp.concatenate(rows, axis=0))
                yield i, j, jnp.concatenate(parts, axis=1)

    def to_queries(planes):
        n = planes[0].shape[1]
        edge = [v for p in planes for v in (p[0:PB], p[KEYS - PB : KEYS])]
        inner = [p[PB : KEYS - PB] for p in planes]
        return jnp.concatenate(
            edge + [jnp.zeros((sz.edge_q - sz.edge, n), F32)]
            + inner + [jnp.zeros((sz.inner_q - sz.inner, n), F32)],
            axis=0,
        )

    def from_queries(edge, inner, p):
        n = KEYS - 2 * PB
        return jnp.concatenate(
            [
                edge[2 * PB * p : 2 * PB * p + PB], inner[n * p : n * (p + 1)],
                edge[2 * PB * p + PB : 2 * PB * (p + 1)], jnp.zeros((PL - KEYS, edge.shape[1]), F32),
            ],
            axis=0,
        )

    xt, dfm = s["xt"], s["dfm"]
    pl.semaphore_wait(bar, len(peers))
    pix_ref.ready()
    x_at, x_mid = mp_start(xt)

    for i, j, value in to_planes(lambda lo, hi: cot_ref[lo:hi, :]):
        dfm[plane(2 * i + j), :] = (value * token_mask(i, j)).astype(BF)
    dyh, dyh_g = s["dyh"], s["dyh_g"]
    dyh[d, :, :D] = dfm[pl.ds(pl.multiple_of(PL * m + (KEYS - PB) * (m // 2), 16), 48), :]
    dyh[d, :, D:] = jnp.zeros((48, W - D), BF)
    dy_at = dp_start(dyh)
    x_mid()

    r2, c2 = iota((D, LANES), 0), iota((D, LANES), 1)
    own_lo = hot((c2 < HF) & (r2 == HF * m + c2))
    own_hi = hot((c2 >= HF) & (r2 == HF * m + c2 - HF))
    last_lo = hot((c2 < HF) & (r2 == last + c2))
    last_hi = hot((c2 >= HF) & (r2 == last + c2 - HF))
    wq, wk, wv = wq_ref[...], wk_ref[...], wv_ref[...]
    wq2 = nn(wq, own_lo + last_hi).astype(BF)
    wkv = (nn(wk, own_lo) + nn(wv, own_hi)).astype(BF)
    wkv5 = (nn(wk, last_lo) + nn(wv, last_hi)).astype(BF)
    bq, bv = vec(bq_ref), vec(bv_ref)
    bq2 = jnp.concatenate([own_part(bq, HF), bq[:, last:]], axis=1)
    nil = jnp.zeros((1, HF), F32)
    bkv = jnp.concatenate([nil, own_part(bv, HF)], axis=1)
    bkv5 = jnp.concatenate([nil, bv[:, last:]], axis=1)
    wr_t = s["wr_t"]
    wr_t[...] = wr_ref[...].T

    xm_r, n1_r = s["xm_r"], s["n1_r"]
    x_at()
    x_all = xt[...].reshape(D, sz.tokens)
    for i, j, value in to_planes(lambda lo, hi: x_all[lo:hi, :]):
        xm = value * token_mask(i, j)
        xm_r[plane(2 * i + j), :] = xm.astype(BF)
        xhat, _ = spread(xm)
        n1_r[plane(2 * i + j), :] = (xhat * vec(ln1g_ref) + vec(ln1b_ref)).astype(BF)

    kva, xr_r = s["kva"], s["xr_r"]
    red = sum(nn(n1_r[plane(p), :], wr_t[D * p : D * (p + 1), :]) for p in range(4)) + vec(br_ref)
    xhr, rsr = spread(red)
    s["xhr_r"][...] = xhr
    s["rsr_r"][...] = jnp.broadcast_to(rsr, (PL, LANES))
    xr_r[...] = (xhr * vec(lnrg_ref) + vec(lnrb_ref)).astype(BF)
    kva[d, 0:PL, :] = (nn(xr_r[...], wkv) + bkv).astype(BF)
    quarter_rows = pl.ds(pl.multiple_of(sz.step * m, 16), sz.quarter)
    kva[d, PL:, :] = (nn(xr_r[quarter_rows, :], wkv5) + bkv5).astype(BF)
    kv_at = dp_start(kva)

    qa_r, qb_r = s["qa_r"], s["qb_r"]
    Q = sz.queries
    q2 = (nn(n1_r[...], wq2) + bq2).astype(BF).astype(F32) * HF ** (-0.5)
    q2t = to_queries([q2[plane(p)] for p in range(4)]).T
    half = jnp.zeros((HF, Q), F32)
    qa_r[...] = jnp.concatenate([q2t[0:HF], half], axis=0).astype(BF)
    qb_r[...] = jnp.concatenate([q2t[HF:], half], axis=0).astype(BF)

    dy_at()
    dyh_g[m] = dyh[jnp.where(m >= 2, above, below)]
    dyg_at, dyg_mid = mp_start(dyh_g)

    dgx, dzx = s["dgx"], s["dzx"]
    w2 = w2_ref[...]
    dgx[...] = jnp.zeros_like(dgx)
    dzx[...] = jnp.zeros_like(dzx)
    for p in range(4):
        dgx[p, sz.top : sz.top + PL, :] = nt(dfm[plane(p), :], w2).astype(BF).astype(F32)
    wo = wo_ref[...]
    wo_cat = jnp.concatenate(
        [b for h in range(4) for b in (wo[HF * h : HF * (h + 1)], wo[last:])], axis=0
    )
    limit5 = jnp.where(m == sz.n_mp - 1, KEYS - sz.step * m, sz.step)
    pk = iota((sz.quarter, 1), 0)
    bias5 = jnp.concatenate(
        [
            jnp.where(pk < limit5, key_bias(pk + sz.step * m, tiles[k]), NEG)
            for k in range(sz.n_dp)
        ],
        axis=0,
    )
    dyg_mid()
    kv_at()

    e5buf, ebuf, sbuf, row_r, ot_r = s["e5buf"], s["ebuf"], s["sbuf"], s["row_r"], s["ot_r"]
    kv5 = kva[:, PL:, :].reshape(sz.n_dp * sz.quarter, LANES)
    chunks = ((0, sz.edge_q, s["lse_a"], s["og_a"]), (sz.edge_q, sz.queries, s["lse_b"], s["og_b"]))
    fives = []
    for lo, hi, lse_r, _ in chunks:
        s5 = nn(kv5, qb_r[:, lo:hi]) + bias5
        m5 = jnp.max(s5, axis=0, keepdims=True)
        e5 = jnp.exp(s5 - m5).astype(BF)
        l5 = rowsum(e5.astype(F32))
        e5buf[:, :, lo:hi] = e5.reshape(sz.n_dp, sz.quarter, hi - lo)
        lse_r[m] = jnp.broadcast_to(m5 + jnp.log(l5), (8, hi - lo))
        at = mp_scatter(
            lambda h, r=lse_r: r.at[m], lambda k, r=lse_r: r.at[m], lambda k, r=lse_r: r.at[mpx(k)]
        )
        fives.append((m5, tn(kv5, e5), at))

    pk = iota((PL, 1), 0)
    ogs = []
    for (lo, hi, lse_r, og), (m5, o5t, lse_at) in zip(chunks, fives):

        def score_step(j, top, lo=lo, hi=hi):
            v = nn(kva[j, 0:PL, :], qa_r[:, lo:hi]) + key_bias(pk, slot_ref[1, j])
            sbuf[j, :, lo:hi] = v
            return jnp.maximum(top, jnp.max(v, axis=0, keepdims=True))

        top = lax.fori_loop(0, sz.n_dp, score_step, jnp.full((1, hi - lo), NEG, F32))

        def exp_step(j, total, lo=lo, hi=hi, top=top):
            e = jnp.exp(sbuf[j, :, lo:hi] - top).astype(BF)
            ebuf[j, :, lo:hi] = e
            return total + rowsum(e.astype(F32))

        total = lax.fori_loop(0, sz.n_dp, exp_step, jnp.zeros((1, hi - lo), F32))
        ot = tn(
            kva[:, 0:PL, :].reshape(sz.n_dp * PL, LANES),
            ebuf[:, :, lo:hi].reshape(sz.n_dp * PL, hi - lo),
        )
        inv = 1.0 / total
        lse_at()
        lses = [lse_r[h][0:1] for h in range(4)]
        lmax = jnp.maximum(jnp.maximum(lses[0], lses[1]), jnp.maximum(lses[2], lses[3]))
        lse5 = lmax + jnp.log(sum(jnp.exp(v - lmax) for v in lses))
        f5 = jnp.exp(m5 - lse5)
        row_r[0:1, lo:hi] = inv
        row_r[1:2, lo:hi] = f5
        o2t = jnp.concatenate([ot[HF:] * inv, o5t[HF:] * f5], axis=0)
        ot_r[:, lo:hi] = o2t
        og[m] = o2t.T[0 : og.shape[1]].astype(BF)
        ogs.append(mp_start(og))

    og_a, og_b = s["og_a"], s["og_b"]
    hal, hal_g, h1_r, n2_r = s["hal"], s["hal_g"], s["h1_r"], s["n2_r"]

    def second_norm(h1):
        xhat, _ = spread(h1)
        return (xhat * vec(ln2g_ref) + vec(ln2b_ref)).astype(BF)

    ogs[0][0]()
    border = pl.ds(pl.multiple_of(2 * PB * m, 16), 2 * PB)
    oc = jnp.concatenate([og_a[h, border, :] for h in range(4)], axis=1)
    xmine = plane_rows(xm_r, PL * m).astype(F32)
    xmine = jnp.concatenate([xmine[0:PB], xmine[KEYS - PB : KEYS]], axis=0)
    im, jm = m // 2, lax.rem(m, 2)
    emask = jnp.concatenate([row_mask(im, jm, 0), row_mask(im, jm, PA - 1)], axis=0)
    hal[d, :, :D] = second_norm(xmine + emask * (nn(oc, wo_cat) + vec(bo_ref)))
    hal[d, :, D:] = jnp.zeros((2 * PB, W - D), BF)
    hal_at = dp_start(hal)

    dyg_at()
    for p in range(4):
        i, j = p // 2, p % 2
        start = sz.top - PB if i == 1 else sz.top + KEYS
        rows = dyh_g[p][:, :D].astype(F32)[0:PB] * row_mask(i, j, -1 if i == 1 else PA)
        dgx[p, start : start + PB, :] = nt(rows.astype(BF), w2).astype(BF).astype(F32)
    for k in range(sz.n_dp):
        e5buf[k] = (e5buf[k].astype(F32) * row_r[1:2, :]).astype(BF)

    ogs[1][0]()
    mixed = []
    for og in (og_a, og_b):
        oc = jnp.concatenate([og[h] for h in range(4)], axis=1)
        mixed.append(nn(oc, wo_cat) + vec(bo_ref))
    w1, b1 = w1_ref[...], vec(b1_ref)

    def hidden(rows, mask):
        return ((nn(rows, w1) + b1) * mask).astype(BF).astype(F32)

    ux, ul, ur, dzl, dzr = s["ux"], s["ul"], s["ur"], s["dzl"], s["dzr"]
    for p in range(4):
        mask = token_mask(p // 2, p % 2)
        h1 = xm_r[plane(p), :].astype(F32) + mask * from_queries(mixed[0], mixed[1], p)
        h1_r[plane(p), :] = h1
        n2_r[plane(p), :] = second_norm(h1)
        ux[p, 0 : sz.top, :] = jnp.zeros((sz.top, C), F32)
        ux[p, sz.top : sz.top + PL, :] = hidden(n2_r[plane(p), :], mask)
    ogp = s["ogp"]
    for p in range(4):
        ogp[plane(p), :] = from_queries(og_a[m].astype(F32), og_b[m].astype(F32), p).astype(BF)
    w2p = s["w2p"]
    rt, ct = iota((D, 4 * LANES), 0), iota((D, 4 * LANES), 1)
    lane4, head4 = ct & (LANES - 1), ct >> 7
    place_out = hot((lane4 < FS) & (rt == FS * head4 + lane4))
    w2_wide = nn(w2, place_out).astype(BF)
    for h in range(4):
        w2p[h] = w2_wide[:, LANES * h : LANES * (h + 1)]
    hal_at()
    up_rows = hal[above].astype(F32)[PB:]
    down_rows = hal[below].astype(F32)[0:PB]
    hal_g[m] = jnp.concatenate([up_rows, down_rows], axis=0).astype(BF)
    halg_at, _ = mp_start(hal_g)
    g_r, du_r = s["g_r"], s["du_r"]
    g_r[...] = jnp.zeros_like(g_r)
    du_r[...] = jnp.zeros_like(du_r)
    halg_at()
    for p in range(4):
        i, j = p // 2, p % 2
        mask = jnp.concatenate([row_mask(i, j, -1), row_mask(i, j, PA)], axis=0)
        u = hidden(hal_g[p][:, :D], mask)
        ux[p, sz.top - PB : sz.top, :] = u[0:PB]
        ux[p, sz.top + KEYS : sz.top + KEYS + PB, :] = u[PB:]

    _, be = place(iota((sz.ext, 1), 0) + (PB - 8), PA + 3)
    wd_ref, bd_row = wd_ref.ready(), vec(bd_ref)

    def shifted(src, left, right):
        for i in range(2):
            left[i] = jnp.where(be == 0, 0.0, pltpu.roll(src[2 * i + 1], 1, 0))
            right[i] = jnp.where(be == PB - 1, 0.0, pltpu.roll(src[2 * i], sz.ext - 1, 0))

    def source(refs, i, j, di, dj, start):
        base, left, right = refs
        i2, up = (i + di) % 2, (i + di) // 2
        j2, across = (j + dj) % 2, (j + dj) // 2
        at = pl.ds(pl.multiple_of(start + PB * up, 8), PB)
        if across < 0:
            return left[i2, at, :]
        if across > 0:
            return right[i2, at, :]
        return base[2 * i2 + j2, at, :]

    TAPS = [(di, dj) for di in (-1, 0, 1) for dj in (-1, 0, 1)]
    shifted(ux, ul, ur)

    def activation(i, j, start):
        p = 2 * i + j
        z = bd_row + sum(
            wd_ref[t : t + 1, :] * source((ux, ul, ur), i, j, di, dj, start)
            for t, (di, dj) in enumerate(TAPS)
        )
        phi = 0.5 * (1.0 + lax.erf(z * 0.7071067811865476))
        dens = jnp.exp(-0.5 * z * z) * 0.3989422804014327
        dz = dgx[p, pl.ds(pl.multiple_of(start, 8), PB), :] * (phi + z * dens)
        dzx[p, pl.ds(pl.multiple_of(start, 8), PB), :] = dz
        return z * phi, dz

    def fold(value):
        return jnp.sum(value.reshape(PB // 8, 8, C), axis=0)

    ve_s, vl_s = s["ve_s"], s["vl_s"]
    sums = [jnp.zeros((8, C), F32) for _ in range(10)]
    for i in range(2):
        for j in range(2):
            p = 2 * i + j
            activation(i, j, sz.top - PB if i == 1 else sz.top + KEYS)

            def forward_step(a, acc, i=i, j=j, p=p):
                start = sz.top + PB * a
                act, dz = activation(i, j, start)
                g_r[p, pl.ds(pl.multiple_of(PB * a, 8), PB), :] = act
                new = [
                    acc[t] + fold(dz * source((ux, ul, ur), i, j, di, dj, start))
                    for t, (di, dj) in enumerate(TAPS)
                ]
                return tuple(new) + (acc[9] + fold(dz),)

            sums = lax.fori_loop(0, PA, forward_step, tuple(sums))
    for t in range(10):
        ve_s[t : t + 1, :C] = rowsum(sums[t])
    shifted(dzx, dzl, dzr)
    dub = s["dub"]
    for i in range(2):
        for j in range(2):
            p = 2 * i + j

            def backward_step(a, carry, i=i, j=j, p=p):
                start = sz.top + PB * a
                du_r[p, pl.ds(pl.multiple_of(PB * a, 8), PB), :] = sum(
                    wd_ref[t : t + 1, :] * source((dzx, dzl, dzr), i, j, -di, -dj, start)
                    for t, (di, dj) in enumerate(TAPS)
                )
                return carry

            lax.fori_loop(0, PA, backward_step, 0)
            dub[p] = (du_r[p].astype(BF).astype(F32) * token_mask(i, j)).astype(BF)
    dn2_mid, dn2_at = mp_sum(lambda h: nt(dub[h], w1), s["dn2_s"], s["dn2_n"], s["dn2_f"])
    dn2_mid()

    e_s = s["e_s"]
    gb = g_r[...].reshape(T, C).astype(BF)
    du_all = dub[...].reshape(T, C)
    e_s[0:D, :C] = tn(n2_r[...], du_all).astype(BF)
    e_s[D:, :D] = tn(gb, dfm[...]).astype(BF)
    e_at = dp_scatter(
        lambda j: e_s.at[pl.ds(pl.multiple_of(sz.echunk * j, 16), sz.echunk)],
        lambda k: s["e_r"].at[k - 1],
        lambda k: s["e_r"].at[k - 1],
    )
    ve_s[10:11, :C] = rowsum(du_all.astype(F32))

    xhat2, rstd2 = spread(plane_rows(h1_r, PL * m))
    dfp = plane_rows(dfm, PL * m).astype(F32)
    ve_s[11:12, :D] = rowsum(dfp)
    dn2 = dn2_at()
    dh1 = dfp + norm_back(dn2, vec(ln2g_ref), xhat2, rstd2)
    s["dh1_r"][...] = dh1
    dab = dh1.astype(BF)
    docat = nt(dab, wo_cat).astype(BF)
    dos, do_all, dabg = s["dos"], s["do_all"], s["dabg"]
    for h in range(4):
        dos[h] = docat[:, LANES * h : LANES * (h + 1)]
    do_at = mp_scatter(lambda h: dos.at[h], lambda k: do_all.at[m], lambda k: do_all.at[mpx(k)])
    do_all[m] = dos[m]
    dabg[m, :, :D] = dab
    dab_at, dab_mid = mp_start(dabg)
    ve_s[12:13, :D] = rowsum(dh1)
    ve_s[13:14, :D] = rowsum(dn2 * xhat2)
    ve_s[14:15, :D] = rowsum(dn2)
    ve_s[15:16, :] = jnp.zeros((1, W), F32)
    ve_mid, ve_at = dp_total(ve_s, s["ve_n"], s["ve_p"])

    ff_mid, ff_at = mp_sum(lambda h: nn(gb, w2p[h]), s["ff_s"], s["ff_n"], s["ff_f"])

    do_at()
    dr_r = s["dr_r"]
    dot_t = to_queries([do_all[p].astype(F32) for p in range(4)]).T
    dr_r[m] = jnp.broadcast_to(rowsum(dot_t[HF:] * ot_r[HF:, :]), (8, Q))
    dr_at = mp_scatter(lambda h: dr_r.at[m], lambda k: dr_r.at[m], lambda k: dr_r.at[mpx(k)])
    da_own = (dot_t[0:HF] * row_r[0:1, :]).astype(BF)
    drow = rowsum(da_own.astype(F32) * ot_r[0:HF, :])
    da_t = jnp.concatenate([half.astype(BF), da_own], axis=0)
    db_t = jnp.concatenate([half, dot_t[HF:]], axis=0).astype(BF)
    dqt, dqt5 = s["dqt"], s["dqt5"]
    dqt[...] = jnp.zeros_like(dqt)
    dqt5[...] = jnp.zeros_like(dqt5)
    ff_mid()
    dr_at()
    drow5 = sum(dr_r[h][0:1] for h in range(4))

    def key_block(j):
        kv = kva[j, 0:PL, :]
        e = ebuf[j]
        ds = (e.astype(F32) * (nn(kv, da_t) - drow)).astype(BF)
        own = nt(ds, qa_r[...]) + nt(e, da_t)
        dqt[...] += tn(kv, ds)
        kv = kva[j, PL:, :]
        e = e5buf[j]
        ds = (e.astype(F32) * (nn(kv, db_t) - drow5)).astype(BF)
        dqt5[...] += tn(kv, ds)
        return jnp.concatenate([own, nt(ds, qb_r[...]) + nt(e, db_t)], axis=0)

    dk_x, dk_n, dk_o, dk_f = s["dk_x"], s["dk_n"], s["dk_o"], s["dk_f"]
    dk_at = take(8)
    for kz in (2, 3, 1, 0):
        dk_x[kz] = key_block(dpx(2 * kz + 1)).astype(BF)
        send(dk_x.at[kz], dk_n.at[kz], dk_at + kz, (dpx(1), m))
    for kz in (2, 3, 1):
        value = key_block(dpx(2 * kz))
        arrived(dk_n.at[kz], dk_at + kz)
        dk_o[kz] = (value + dk_n[kz].astype(F32)).astype(BF)
        send(dk_o.at[kz], dk_f.at[kz], dk_at + 4 + kz, (dpx(2 * kz), m))
    dkv = key_block(d)

    def dk_finish():
        arrived(dk_n.at[0], dk_at)
        total = dkv + dk_n[0].astype(F32)
        for kz in (1, 2, 3):
            arrived(dk_f.at[kz], dk_at + 4 + kz)
            total = total + dk_f[kz].astype(F32)
        return total

    dk_fin = handle(dk_finish)

    dq2 = (jnp.concatenate([dqt[0:HF], dqt5[0:HF]], axis=0) * HF ** (-0.5)).T
    dqs, dq_all = s["dqs"], s["dq_all"]
    for h in range(4):
        dqs[h] = from_queries(dq2[: sz.edge_q], dq2[sz.edge_q :], h).astype(BF)
    dq_at = mp_scatter(lambda h: dqs.at[h], lambda k: dq_all.at[m], lambda k: dq_all.at[mpx(k)])
    dq_all[m] = dqs[m]
    ve_mid()
    l1_s, l2_s = s["l1_s"], s["l2_s"]
    dqp = dqs[...].reshape(T, LANES)
    l1_s[0:D, 0:LANES] = tn(n1_r[...], dqp).astype(BF)
    vl_s[...] = jnp.zeros_like(vl_s)
    vl_s[5:6, 0:LANES] = rowsum(dqp.astype(F32))
    dab_at()
    gwo = tn(ogp[...], dabg[...].reshape(T, W)[:, :D]).astype(BF)
    l1_s[D:, :D] = gwo[0:HF]
    l2_s[D:, :D] = gwo[HF:]

    ff = ff_at()
    sel = hot((c2 < FS) & (r2 == FS * m + c2))
    b2q = jnp.concatenate(
        [own_part(vec(b2_ref), FS), jnp.zeros((1, LANES - FS), F32)], axis=1
    )
    for p in range(4):
        h1 = h1_r[plane(p), :]
        hi = h1.astype(BF)
        h1q = nn(hi, sel) + nn((h1 - hi.astype(F32)).astype(BF), sel)
        blk_ref[plane(p), :] = h1q + token_mask(p // 2, p % 2) * (ff[plane(p)] + b2q)

    e_at()
    mine = e_s[pl.ds(pl.multiple_of(sz.echunk * d, 16), sz.echunk), :].astype(F32)
    eg_ref[d] = (mine + sum(s["e_r"][k].astype(F32) for k in range(sz.n_dp - 1))).astype(BF)

    dkvb = dk_fin().astype(BF)
    dkvg = s["dkvg"]
    dkvg[m] = dkvb
    dkv_at, dkv_mid = mp_start(dkvg)
    l1_s[0:D, LANES : 2 * LANES] = tn(xr_r[...], dkvb[0:PL]).astype(BF)
    l1_s[0:D, 2 * LANES :] = tn(xr_r[quarter_rows, :], dkvb[PL:]).astype(BF)

    def lchunk(ref):
        return lambda j: ref.at[pl.ds(pl.multiple_of(sz.lchunk * j, 16), sz.lchunk)]

    l1_mid, l1_at = dp_sum(lchunk(l1_s), s["l1_n"], s["l1_o"], s["l1_f"])
    vl_s[6:7, 0:LANES] = jnp.concatenate(
        [rowsum(dkvb[0:PL].astype(F32))[:, HF:], rowsum(dkvb[PL:].astype(F32))[:, HF:]], axis=1
    )
    rk, ck = iota((D, 5 * LANES), 0), iota((D, 5 * LANES), 1)
    lane5, head5 = ck & (LANES - 1), ck >> 7
    w_all = (
        nn(wk, hot((lane5 < HF) & (rk == HF * head5 + lane5)))
        + nn(wv, hot((lane5 >= HF) & (rk == HF * head5 + lane5 - HF)))
    ).astype(BF)
    wq_cat = nn(
        wq, hot(rt == jnp.where(lane4 < HF, HF * head4 + lane4, last + lane4 - HF))
    ).astype(BF)
    dq_at()
    dq_cat = jnp.concatenate([dq_all[h] for h in range(4)], axis=1)
    dn1 = nt(dq_cat, wq_cat)
    xhat1, rstd1 = spread(plane_rows(xm_r, PL * m).astype(F32))
    dkv_at()
    rest = jnp.concatenate(
        [dkvg[h, PL : PL + sz.step, :] for h in range(3)] + [dkvg[3, PL:, :]], axis=0
    )
    dkv_all = jnp.concatenate([dkvg[h, 0:PL, :] for h in range(4)] + [rest], axis=1)
    dxr = nt(dkv_all, w_all)
    xhr = s["xhr_r"][...]
    drb = norm_back(dxr, vec(lnrg_ref), xhr, s["rsr_r"][:, 0:1]).astype(BF)
    l2_s[0:D, :D] = tn(drb, plane_rows(n1_r, PL * m)).astype(BF)
    l1_mid()
    l2_mid, l2_at = dp_sum(lchunk(l2_s), s["l2_n"], s["l2_o"], s["l2_f"])
    vl_s[2:3, :D] = rowsum(dxr * xhr)
    vl_s[3:4, :D] = rowsum(dxr)
    vl_s[4:5, :D] = rowsum(drb.astype(F32))

    wr_m = wr_t[pl.ds(pl.multiple_of(D * m, 16), D), :]
    dn1 = dn1 + nt(drb, wr_m)
    vl_s[0:1, :D] = rowsum(dn1 * xhat1)
    vl_s[1:2, :D] = rowsum(dn1)
    vl_mid, vl_at = dp_total(vl_s, s["vl_n"], s["vl_p"])
    dxm = norm_back(dn1, vec(ln1g_ref), xhat1, rstd1)
    gp = (token_mask(im, jm) * (s["dh1_r"][...] + dxm)).astype(BF)
    gpf = nn(gp, place_out).astype(BF)
    gps = s["gps"]
    for h in range(4):
        gps[h] = gpf[:, LANES * h : LANES * (h + 1)]
    gp_at = mp_scatter(lambda h: gps.at[h], lambda k: gp_ref.at[m], lambda k: gp_ref.at[mpx(k)])
    gp_ref[m] = gps[m]

    def gather(buf):
        own = buf.at[m]
        near = dp_start(own)
        base = take(3 * sz.n_dp)

        def across(k):
            j = dpx(k)
            send(buf.at[m, j], buf.at[m, j], base + 3 * k, (d, mpx(1)))
            send(buf.at[m, j], buf.at[m, j], base + 3 * k + 1, (d, mpx(2)))

        across(0)
        seq = (0, 2, 4, 6, 1, 3, 5, 7)

        def middle():
            for k in seq:
                j = dpx(k)
                arrived(buf.at[mpx(2), j], base + 3 * k + 1)
                send(buf.at[mpx(2), j], buf.at[mpx(2), j], base + 3 * k + 2, (d, mpx(1)))

        mid = handle(middle)

        def finish():
            near(across)
            mid()
            for k in seq:
                arrived(buf.at[mpx(1), dpx(k)], base + 3 * k)
                arrived(buf.at[mpx(3), dpx(k)], base + 3 * k + 2)

        return lambda: near(across), handle(finish)

    lg1_ref[m, d] = l1_at().astype(BF)
    lg1_near, lg1_at = gather(lg1_ref)
    l2_mid()
    vl_mid()
    eg_at = dp_start(eg_ref)
    veg_ref[m] = ve_at()
    veg_at, _ = mp_start(veg_ref)
    lg1_near()
    lg2_ref[m, d] = l2_at().astype(BF)
    lg2_near, lg2_at = gather(lg2_ref)
    vlg_ref[m] = vl_at()
    vlg_at, _ = mp_start(vlg_ref)
    lg2_near()
    eg_at()
    gp_at()
    veg_at()
    lg1_at()
    vlg_at()
    lg2_at()
    for c in pending:
        c.wait_send()


def unpack_body(
    sz, blk_ref, gp_ref, eg_ref, lg1_ref, lg2_ref, veg_ref, vlg_ref,
    out_ref, gpix_ref, ln1g_ref, ln1b_ref, gwq_ref, gbq_ref, gwk_ref, gwv_ref, gbv_ref, gwr_ref, gbr_ref,
    lnrg_ref, lnrb_ref, gwo_ref, gbo_ref, ln2g_ref, ln2b_ref, gw1_ref, gb1_ref, gwd_ref, gbd_ref,
    gw2_ref, gb2_ref, out32, gp32,
):
    D, HF, PB, PA, PL = sz.width, HEAD_FEATURES, sz.pb, sz.pa, sz.plane
    C, FS = sz.hidden, sz.share
    m = lax.axis_index("mp")
    for i in range(2):
        for j in range(2):
            p = 2 * i + j
            for a in range(PA):
                at = pl.ds((2 * a + i) * sz.cols + j, PB, stride=2)
                out32[at, :] = blk_ref[PL * p + PB * a : PL * p + PB * (a + 1), 0:FS]
                gp32[at, :] = gp_ref[p].astype(F32)[PB * a : PB * (a + 1), 0:FS]
    out_ref[...] = out32[...].T.astype(BF)
    gpix_ref[...] = gp32[...].T

    lg1 = [lg1_ref[h].reshape(sz.lrows, sz.wide) for h in range(4)]
    lg2 = [lg2_ref[h].reshape(sz.lrows, sz.wide) for h in range(4)]

    def heads(first, tail):
        parts = [lg1[h][0:D, first : first + HF].astype(F32) for h in range(4)]
        parts.append(sum(lg1[h][0:D, tail : tail + HF].astype(F32) for h in range(4)))
        return jnp.concatenate(parts, axis=1)

    gwq_ref[...] = heads(0, HF)
    gwk_ref[...] = heads(LANES, 2 * LANES)
    gwv_ref[...] = heads(LANES + HF, 2 * LANES + HF)
    gwr_ref[...] = jnp.concatenate([lg2[h][0:D, :D].astype(F32) for h in range(4)], axis=1)
    for h in range(4):
        gwo_ref[HF * h : HF * (h + 1), :] = lg1[h][D:, :D].astype(F32)
    gwo_ref[HF * 4 :, :] = sum(lg2[h][D:, :D].astype(F32) for h in range(4))
    eg = eg_ref[...].reshape(D + C, sz.wide)
    gw1_ref[...] = eg[0:D, :C].astype(F32)
    gw2_ref[...] = eg[D:, :D].astype(F32)

    def row(value):
        return value.reshape(value.shape[1])

    ve = veg_ref[m]
    gwd_ref[...] = ve[0:9, :C]
    gbd_ref[...] = row(ve[9:10, :C])
    gb1_ref[...] = row(ve[10:11, :C])
    vs = sum(veg_ref[h] for h in range(4))
    gb2_ref[...] = row(vs[11:12, :D])
    gbo_ref[...] = row(vs[12:13, :D])
    ln2g_ref[...] = row(vs[13:14, :D])
    ln2b_ref[...] = row(vs[14:15, :D])
    vl = sum(vlg_ref[h] for h in range(4))
    ln1g_ref[...] = row(vl[0:1, :D])
    ln1b_ref[...] = row(vl[1:2, :D])
    lnrg_ref[...] = row(vlg_ref[0][2:3, :D])
    lnrb_ref[...] = row(vlg_ref[0][3:4, :D])
    gbr_ref[...] = row(vlg_ref[0][4:5, :D])

    def head_row(r):
        parts = [vlg_ref[h][r : r + 1, 0:HF] for h in range(4)] + [vl[r : r + 1, HF : 2 * HF]]
        return row(jnp.concatenate(parts, axis=1))

    gbq_ref[...] = head_row(5)
    gbv_ref[...] = head_row(6)


def on_device_fused(*args):
    pixels_in, cotangent, pixel_mask, tile_slot = args[:4]
    w_fc1 = args[19]
    sz = Sizes(
        lax.axis_size("dp"), lax.axis_size("mp"), pixels_in.shape[0], cotangent.shape[1], w_fc1.shape[1]
    )
    D, C, PL, T, W, LN, HF = sz.width, sz.hidden, sz.plane, sz.all, sz.wide, LANES, HEAD_FEATURES
    Q, N, PB = sz.queries, sz.n_dp, sz.pb
    sm = pl.BlockSpec(memory_space=pltpu.SMEM)
    vm = pl.BlockSpec(memory_space=pltpu.VMEM)
    hbm = pl.BlockSpec(memory_space=pl.ANY)
    S = jax.ShapeDtypeStruct
    ins = [pixels_in.T, cotangent.T, *args[4:11], args[11].T, *args[12:]]
    mids = [
        S((T, LN), F32), S((4, PL, LN), BF), S((N, sz.echunk, W), BF), S((4, N, sz.lchunk, W), BF),
        S((4, N, sz.lchunk, W), BF), S((4, 16, W), F32), S((4, 8, W), F32),
    ]
    shapes = {
        BF: dict(
            xt=(4, sz.share, sz.tokens), dfm=(T, D), dyh=(N, 48, W), dyh_g=(4, 48, W), xm_r=(T, D), n1_r=(T, D),
            xr_r=(PL, D), kva=(N, sz.kvrows, LN), qa_r=(LN, Q), qb_r=(LN, Q), ebuf=(N, PL, Q),
            e5buf=(N, sz.quarter, Q), og_a=(4, sz.edge, LN), og_b=(4, sz.inner, LN), n2_r=(T, D),
            hal=(N, 2 * PB, W), hal_g=(4, 2 * PB, W), dub=(4, PL, C), dn2_s=(3, PL, D), dn2_n=(2, PL, D),
            dn2_f=(PL, D), dos=(4, PL, LN), do_all=(4, PL, LN), dabg=(4, PL, W), ff_s=(3, T, LN), ff_n=(2, T, LN),
            ff_f=(T, LN), dk_x=(4, sz.kvrows, LN), dk_n=(4, sz.kvrows, LN), dk_o=(4, sz.kvrows, LN),
            dk_f=(4, sz.kvrows, LN), dkvg=(4, sz.kvrows, LN), dqs=(4, PL, LN), dq_all=(4, PL, LN),
            e_s=(D + C, W), e_r=(N - 1, sz.echunk, W), l1_s=(sz.lrows, W), l1_n=(4, sz.lchunk, W),
            l1_o=(4, sz.lchunk, W), l1_f=(4, sz.lchunk, W), l2_s=(sz.lrows, W), l2_n=(4, sz.lchunk, W),
            l2_o=(4, sz.lchunk, W), l2_f=(4, sz.lchunk, W), gps=(4, PL, LN), wr_t=(4 * D, D), ogp=(T, LN),
            w2p=(4, C, LN),
        ),
        F32: dict(
            t0=(sz.tokens, LN), t1=(sz.tokens, LN), t2=(sz.tokens, D - 2 * LN), xhr_r=(PL, D), rsr_r=(PL, LN),
            sbuf=(N, PL, Q), lse_a=(4, 8, sz.edge_q), lse_b=(4, 8, sz.inner_q), row_r=(8, Q), ot_r=(LN, Q),
            h1_r=(T, D), ux=(4, sz.ext, C), ul=(2, sz.ext, C), ur=(2, sz.ext, C), dgx=(4, sz.ext, C),
            dzx=(4, sz.ext, C), dzl=(2, sz.ext, C), dzr=(2, sz.ext, C), g_r=(4, PL, C), du_r=(4, PL, C),
            dh1_r=(PL, D), dr_r=(4, 8, Q), dqt=(LN, Q), dqt5=(LN, Q), ve_s=(16, W), ve_n=(16, W),
            ve_p=(4, 16, W), vl_s=(8, W), vl_n=(8, W), vl_p=(4, 8, W),
        ),
    }
    scratch = {k: pltpu.VMEM(v, t) for t, group in shapes.items() for k, v in group.items()}
    for i in range(1, len(ins)):
        scratch["in%d" % i] = pltpu.VMEM(ins[i].shape, ins[i].dtype)
    scratch["ssem"] = pltpu.SemaphoreType.DMA((200,))
    scratch["rsem"] = pltpu.SemaphoreType.DMA((200,))
    scratch["isem"] = pltpu.SemaphoreType.DMA((len(ins),))
    mid = pl.pallas_call(
        functools.partial(fused_body, sz, tuple(scratch)),
        out_shape=mids,
        in_specs=[sm, sm] + [hbm] * len(ins),
        out_specs=[vm] * len(mids),
        scratch_shapes=list(scratch.values()),
        compiler_params=pltpu.CompilerParams(
            collective_id=0, has_side_effects=True, vmem_limit_bytes=VMEM_MB * 2**20
        ),
        name="fused_block",
    )(pixel_mask, tile_slot.T, *ins)
    outs = [
        S((sz.share, sz.tokens), BF), S((sz.share, sz.tokens), F32), S((D,), F32), S((D,), F32), S((D, D), F32),
        S((D,), F32), S((D, D), F32), S((D, D), F32), S((D,), F32), S((D, 4 * D), F32), S((D,), F32), S((D,), F32),
        S((D,), F32), S((D, D), F32), S((D,), F32), S((D,), F32), S((D,), F32), S((D, C), F32), S((C,), F32),
        S((9, C), F32), S((C,), F32), S((C, D), F32), S((D,), F32),
    ]
    res = list(
        pl.pallas_call(
            functools.partial(unpack_body, sz),
            out_shape=outs,
            in_specs=[vm] * len(mids),
            out_specs=[vm] * len(outs),
            scratch_shapes=[pltpu.VMEM((sz.tokens, sz.share), F32)] * 2,
            compiler_params=pltpu.CompilerParams(vmem_limit_bytes=24 * 2**20),
            name="unpack",
        )(*mid)
    )
    for k in (0, 1, 9):
        res[k] = res[k].T
    return tuple(res)


def choose(*args):
    tokens, width = args[1].shape
    whole_rows = tokens == FRAME * (FRAME // TILE_ROWS)
    shape = (lax.axis_size("dp"), lax.axis_size("mp"))
    if whole_rows and shape == (TILE_ROWS, 4) and TILE_ROWS == 8 and HEADS == 5 and width == 320 == args[19].shape[1]:
        return on_device_fused(*args)
    return on_device(*args)


def solution(mesh):
    return jax.shard_map(
        choose,
        mesh=mesh,
        in_specs=(
            P("dp", "mp"),
            P("dp", None),
            P("dp"),
            P(),
            P(),
            P(),
            P(),
            P(),
            P(),
            P(),
            P(),
            P(),
            P(),
            P(),
            P(),
            P(),
            P(),
            P(),
            P(),
            P(None, "mp"),
            P("mp"),
            P(None, "mp"),
            P("mp"),
            P("mp", None),
            P(),
        ),
        out_specs=(
            P("dp", "mp"),
            P("dp", "mp"),
            P(),
            P(),
            P(),
            P(),
            P(),
            P(),
            P(),
            P(),
            P(),
            P(),
            P(),
            P(),
            P(),
            P(),
            P(),
            P(None, "mp"),
            P("mp"),
            P(None, "mp"),
            P("mp"),
            P("mp", None),
            P(),
        ),
        check_vma=False,
    )
```

```python
import functools

import jax
import jax.numpy as jnp
from jax import lax
from jax.experimental import pallas as pl
from jax.experimental.pallas import tpu as pltpu
from jax.sharding import PartitionSpec as P

HEADS = 5
HEAD_FEATURES = 64
FRAME = 80
TILE_ROWS = 8


EPS = 1e-05
NEG = -1e30


def layer_norm(value, gain, shift):
    mean = jnp.mean(value, axis=-1, keepdims=True)
    centred = value - mean
    spread = jnp.mean(centred * centred, axis=-1, keepdims=True)
    return centred * lax.rsqrt(spread + EPS) * gain + shift


def depth_gelu(padded, kernel, shift):
    rows = padded.shape[0] - 2
    cols = padded.shape[1] - 2
    total = jnp.zeros((rows, cols, padded.shape[2]), jnp.float32) + shift
    for row_off in range(3):
        for col_off in range(3):
            total = (
                total
                + kernel[3 * row_off + col_off]
                * padded[row_off : row_off + rows, col_off : col_off + cols]
            )
    return jax.nn.gelu(total, approximate=False)


def mat(left, right):
    return jnp.dot(left, right, preferred_element_type=jnp.float32)


def pick(weights, table):
    return jnp.einsum(
        "j,jab->ab", weights.astype(table.dtype), table, preferred_element_type=jnp.float32
    )


def head_columns(weight_matrix, select_where):
    wide_layout = weight_matrix.astype(jnp.float32).reshape(
        weight_matrix.shape[0], HEADS, HEAD_FEATURES
    )
    return (
        jnp.einsum("uzx,nz->unx", wide_layout, select_where)
        .reshape(weight_matrix.shape[0], -1)
        .astype(jnp.bfloat16)
    )


def head_rows(weight_matrix, select_where):
    wide_layout = weight_matrix.astype(jnp.float32).reshape(
        HEADS, HEAD_FEATURES, weight_matrix.shape[1]
    )
    return (
        jnp.einsum("hed,sh->sed", wide_layout, select_where)
        .reshape(-1, weight_matrix.shape[1])
        .astype(jnp.bfloat16)
    )


def head_vector(vector_entries, select_where):
    return jnp.einsum(
        "he,sh->se", vector_entries.reshape(HEADS, HEAD_FEATURES), select_where
    ).reshape(-1)


def spread_columns(gradient_value, select_where):
    return jnp.einsum(
        "tvm,vq->tqm",
        gradient_value.reshape(gradient_value.shape[0], -1, HEAD_FEATURES),
        select_where,
    ).reshape(gradient_value.shape[0], -1)


def spread_rows(gradient_value, select_where):
    return jnp.einsum(
        "sed,sh->hed",
        gradient_value.reshape(-1, HEAD_FEATURES, gradient_value.shape[1]),
        select_where,
    ).reshape(-1, gradient_value.shape[1])


def spread_vector(gradient_value, select_where):
    return jnp.einsum("se,sh->he", gradient_value.reshape(-1, HEAD_FEATURES), select_where).reshape(
        -1
    )


def on_device(
    pixels_in,
    cotangent,
    pixel_mask,
    tile_slot,
    ln1_gain,
    ln1_bias,
    w_query,
    b_query,
    w_key,
    w_value,
    b_value,
    w_reduce,
    b_reduce,
    lnr_gain,
    lnr_bias,
    w_out,
    b_out,
    ln2_gain,
    ln2_bias,
    w_fc1,
    b_fc1,
    w_depth,
    b_depth,
    w_fc2,
    b_fc2,
):
    n_dp = lax.axis_size("dp")
    n_mp = lax.axis_size("mp")
    device = lax.axis_index("dp")
    part = lax.axis_index("mp")
    rows = FRAME // TILE_ROWS
    tokens = pixels_in.shape[0]
    cols = tokens // rows
    tiles_col = FRAME // cols
    per_frame = TILE_ROWS * tiles_col
    width = ln1_gain.shape[0]
    share = width // n_mp
    slots = -(-HEADS // n_mp)
    scale = HEAD_FEATURES ** (-0.5)
    maskf = pixel_mask.astype(jnp.float32)[:, None]
    head_ids = part + n_mp * jnp.arange(slots)
    select_where = (head_ids[:, None] == jnp.arange(HEADS)[None, :]).astype(jnp.float32)
    crops = tile_slot[:, 0]
    tiles = tile_slot[:, 1]
    is_me = jnp.arange(n_dp) == device
    own_crop = jnp.sum(jnp.where(is_me, crops, 0))
    own_tile = jnp.sum(jnp.where(is_me, tiles, 0))
    own_row = own_tile // tiles_col
    own_col = own_tile % tiles_col
    tile_row = tiles // tiles_col
    tile_col = tiles % tiles_col

    def beside(drow, dcol):
        hit = (crops == own_crop) & (tile_row == own_row + drow) & (tile_col == own_col + dcol)
        return hit.astype(jnp.float32)

    member = (crops[None, :] == own_crop) & (tiles[None, :] == jnp.arange(per_frame)[:, None])
    crop_devices = jnp.sum(jnp.where(member, jnp.arange(n_dp)[None, :], 0), axis=1)
    whole = lax.all_gather(pixels_in, "mp", axis=1, tiled=True)
    xm = whole.astype(jnp.float32) * maskf
    n1, first_norm_backward = jax.vjp(layer_norm, xm, ln1_gain, ln1_bias)
    n1b = n1.astype(jnp.bfloat16)
    wq = head_columns(w_query, select_where)
    wk = head_columns(w_key, select_where)
    wv = head_columns(w_value, select_where)
    wo = head_rows(w_out, select_where)
    qb = (mat(n1b, wq) + head_vector(b_query, select_where)).astype(jnp.bfloat16)
    patches = (
        n1b.reshape(rows // 2, 2, cols // 2, 2, width)
        .transpose(0, 2, 1, 3, 4)
        .reshape(-1, 4 * width)
    )
    reduced = mat(patches, w_reduce) + b_reduce
    xr, lnr_back = jax.vjp(layer_norm, reduced, lnr_gain, lnr_bias)
    xrb = xr.astype(jnp.bfloat16)
    kb = mat(xrb, wk).astype(jnp.bfloat16)
    vb = (mat(xrb, wv) + head_vector(b_value, select_where)).astype(jnp.bfloat16)
    kmask = (
        pixel_mask.reshape(rows // 2, 2, cols // 2, 2)[:, 0, :, 0].reshape(-1).astype(jnp.bfloat16)
    )
    keys_all, values_all, kmask_all = (
        lax.all_gather(kb, "dp", axis=0, tiled=True),
        lax.all_gather(vb, "dp", axis=0, tiled=True),
        lax.all_gather(kmask, "dp", axis=0, tiled=True),
    )
    per_key = kb.shape[0]
    keys_crop = keys_all.reshape(n_dp, per_key, -1)[crop_devices]
    values_crop = values_all.reshape(n_dp, per_key, -1)[crop_devices]
    usable_crop = kmask_all.reshape(n_dp, per_key)[crop_devices].astype(jnp.float32) > 0.5
    n_blocks = 4
    key_blocks = keys_crop.reshape(n_blocks, -1, slots, HEAD_FEATURES)
    value_blocks = values_crop.reshape(n_blocks, -1, slots, HEAD_FEATURES)
    usable_blocks = usable_crop.reshape(n_blocks, -1)
    queries = qb.reshape(tokens, slots, HEAD_FEATURES)

    def block_scores(key_block, usable_block):
        raw = (
            jnp.einsum("qsd,ksd->sqk", queries, key_block, preferred_element_type=jnp.float32)
            * scale
        )
        return jnp.where(usable_block[None, None, :], raw, NEG)

    def top_step(carry, blocks):
        top, total = carry
        key_block, usable_block = blocks
        scores = block_scores(key_block, usable_block)
        new_top = jnp.maximum(top, jnp.max(scores, axis=-1))
        total = total * jnp.exp(top - new_top) + jnp.sum(
            jnp.exp(scores - new_top[..., None]), axis=-1
        )
        return ((new_top, total), None)

    start = (jnp.full((slots, tokens), NEG, jnp.float32), jnp.zeros((slots, tokens), jnp.float32))
    (top, total), _ = lax.scan(top_step, start, (key_blocks, usable_blocks))
    lse = top + jnp.log(total)

    def out_step(acc, blocks):
        key_block, value_block, usable_block = blocks
        prob = jnp.exp(block_scores(key_block, usable_block) - lse[..., None])
        acc = acc + jnp.einsum(
            "sqk,ksd->qsd",
            prob.astype(jnp.bfloat16),
            value_block,
            preferred_element_type=jnp.float32,
        )
        return (acc, None)

    empty = jnp.zeros((tokens, slots, HEAD_FEATURES), jnp.float32)
    acc, _ = lax.scan(out_step, empty, (key_blocks, value_blocks, usable_blocks))
    ob = acc.reshape(tokens, -1).astype(jnp.bfloat16)
    branch = lax.psum(mat(ob, wo).astype(jnp.bfloat16), "mp").astype(jnp.float32) + b_out
    h1 = xm + branch * maskf
    n2, ln2_back = jax.vjp(layer_norm, h1, ln2_gain, ln2_bias)
    n2b = n2.astype(jnp.bfloat16)
    ub = ((mat(n2b, w_fc1) + b_fc1) * maskf).astype(jnp.bfloat16)
    channels = ub.shape[1]
    tile_u = ub.reshape(rows, cols, channels)
    lines, sides = (
        lax.all_gather(jnp.stack([tile_u[0], tile_u[-1]]), "dp", axis=0, tiled=True),
        lax.all_gather(jnp.stack([tile_u[:, 0], tile_u[:, -1]]), "dp", axis=0, tiled=True),
    )
    lines = lines.reshape(n_dp, 2, cols, channels)
    sides = sides.reshape(n_dp, 2, rows, channels)
    top_lines = lines[:, 0]
    bottom_lines = lines[:, 1]
    left_sides = sides[:, 0]
    right_sides = sides[:, 1]
    upper = jnp.concatenate(
        [
            pick(beside(-1, -1), bottom_lines[:, -1:]),
            pick(beside(-1, 0), bottom_lines),
            pick(beside(-1, 1), bottom_lines[:, :1]),
        ],
        axis=0,
    )
    lower = jnp.concatenate(
        [
            pick(beside(1, -1), top_lines[:, -1:]),
            pick(beside(1, 0), top_lines),
            pick(beside(1, 1), top_lines[:, :1]),
        ],
        axis=0,
    )
    middle = jnp.concatenate(
        [
            pick(beside(0, -1), right_sides)[:, None],
            tile_u.astype(jnp.float32),
            pick(beside(0, 1), left_sides)[:, None],
        ],
        axis=1,
    )
    padded = jnp.concatenate([upper[None], middle, lower[None]], axis=0)
    act, depth_back = jax.vjp(depth_gelu, padded, w_depth, b_depth)
    gb = act.reshape(tokens, channels).astype(jnp.bfloat16)
    ffn_mine = lax.psum_scatter(
        mat(gb, w_fc2).astype(jnp.bfloat16), "mp", scatter_dimension=1, tiled=True
    ).astype(jnp.float32)
    h1_mine = lax.dynamic_slice_in_dim(h1, part * share, share, 1)
    bias_mine = lax.dynamic_slice_in_dim(b_fc2, part * share, share, 0)
    block_result = (h1_mine + (ffn_mine + bias_mine) * maskf).astype(jnp.bfloat16)
    dy = cotangent.astype(jnp.float32)
    dff = dy * maskf
    grad_b_fc2 = jnp.sum(dff, axis=0)
    dfb = dff.astype(jnp.bfloat16)
    grad_w_fc2 = mat(gb.T, dfb)
    dgr = mat(dfb, w_fc2.T).astype(jnp.bfloat16).astype(jnp.float32).reshape(rows, cols, channels)
    dpad, grad_w_depth, grad_b_depth = depth_back(dgr)
    grad_lines, grad_sides = (
        lax.all_gather(
            jnp.stack([dpad[0], dpad[-1]]).astype(jnp.bfloat16), "dp", axis=0, tiled=True
        ).astype(jnp.float32),
        lax.all_gather(
            jnp.stack([dpad[1:-1, 0], dpad[1:-1, -1]]).astype(jnp.bfloat16),
            "dp",
            axis=0,
            tiled=True,
        ).astype(jnp.float32),
    )
    grad_lines = grad_lines.reshape(n_dp, 2, cols + 2, channels)
    grad_sides = grad_sides.reshape(n_dp, 2, rows, channels)
    top_grads = grad_lines[:, 0]
    bottom_grads = grad_lines[:, 1]
    dtile = dpad[1:-1, 1:-1]
    dtile = dtile.at[0].add(pick(beside(-1, 0), bottom_grads[:, 1:-1]))
    dtile = dtile.at[0, 0].add(pick(beside(-1, -1), bottom_grads[:, -1:])[0])
    dtile = dtile.at[0, -1].add(pick(beside(-1, 1), bottom_grads[:, :1])[0])
    dtile = dtile.at[-1].add(pick(beside(1, 0), top_grads[:, 1:-1]))
    dtile = dtile.at[-1, 0].add(pick(beside(1, -1), top_grads[:, -1:])[0])
    dtile = dtile.at[-1, -1].add(pick(beside(1, 1), top_grads[:, :1])[0])
    dtile = dtile.at[:, 0].add(pick(beside(0, -1), grad_sides[:, 1]))
    dtile = dtile.at[:, -1].add(pick(beside(0, 1), grad_sides[:, 0]))
    dub = (dtile.reshape(tokens, channels).astype(jnp.bfloat16).astype(jnp.float32) * maskf).astype(
        jnp.bfloat16
    )
    grad_b_fc1 = jnp.sum(dub.astype(jnp.float32), axis=0)
    grad_w_fc1 = mat(n2b.T, dub)
    dn2_part = mat(dub, w_fc1.T)
    zero_vector = jnp.zeros((width,), jnp.float32)
    dn2 = lax.psum(dn2_part.astype(jnp.bfloat16), "mp").astype(jnp.float32)
    dh1_norm, shared_gain, shared_bias = ln2_back(dn2)
    dh1 = dy + dh1_norm
    split_gain = zero_vector
    split_bias = zero_vector
    dattn = dh1 * maskf
    grad_b_out = jnp.sum(dattn, axis=0)
    dab = dattn.astype(jnp.bfloat16)
    grad_wo = mat(ob.T, dab)
    dob = mat(dab, wo.T).astype(jnp.bfloat16)
    dout = dob.reshape(tokens, slots, HEAD_FEATURES)
    drow = jnp.sum(dout.astype(jnp.float32) * acc, axis=-1).T

    def back_step(dq_acc, blocks):
        key_block, value_block, usable_block = blocks
        prob = jnp.exp(block_scores(key_block, usable_block) - lse[..., None])
        dv_block = jnp.einsum(
            "sqk,qsd->ksd", prob.astype(jnp.bfloat16), dout, preferred_element_type=jnp.float32
        )
        dprob = jnp.einsum("qsd,ksd->sqk", dout, value_block, preferred_element_type=jnp.float32)
        dscore = (prob * (dprob - drow[..., None])).astype(jnp.bfloat16)
        dq_acc = dq_acc + jnp.einsum(
            "sqk,ksd->qsd", dscore, key_block, preferred_element_type=jnp.float32
        )
        dk_block = (
            jnp.einsum("sqk,qsd->ksd", dscore, queries, preferred_element_type=jnp.float32) * scale
        )
        return (dq_acc, (dk_block, dv_block))

    dq_acc, (dk_blocks, dv_blocks) = lax.scan(
        back_step, empty, (key_blocks, value_blocks, usable_blocks)
    )
    zero_keys = jnp.zeros((n_dp, per_key, slots * HEAD_FEATURES), jnp.float32)
    dk_full = (
        zero_keys.at[crop_devices]
        .set(dk_blocks.reshape(per_frame, per_key, -1))
        .reshape(n_dp * per_key, -1)
    )
    dv_full = (
        zero_keys.at[crop_devices]
        .set(dv_blocks.reshape(per_frame, per_key, -1))
        .reshape(n_dp * per_key, -1)
    )
    dk_mine, dv_mine = (
        lax.psum_scatter(dk_full, "dp", scatter_dimension=0, tiled=True),
        lax.psum_scatter(dv_full, "dp", scatter_dimension=0, tiled=True),
    )
    dkb = dk_mine.astype(jnp.bfloat16)
    dvb = dv_mine.astype(jnp.bfloat16)
    dqb = (dq_acc * scale).reshape(tokens, -1).astype(jnp.bfloat16)
    grad_wq = mat(n1b.T, dqb)
    grad_bq = jnp.sum(dqb.astype(jnp.float32), axis=0)
    grad_wk = mat(xrb.T, dkb)
    grad_wv = mat(xrb.T, dvb)
    grad_bv = jnp.sum(dvb.astype(jnp.float32), axis=0)
    dxr, dn1_query = (
        lax.psum((mat(dkb, wk.T) + mat(dvb, wv.T)).astype(jnp.bfloat16), "mp").astype(jnp.float32),
        lax.psum(mat(dqb, wq.T).astype(jnp.bfloat16), "mp").astype(jnp.float32),
    )
    dreduced, grad_lnr_gain, grad_lnr_bias = lnr_back(dxr)
    drb = dreduced.astype(jnp.bfloat16)
    grad_w_reduce = mat(patches.T, drb)
    grad_b_reduce = jnp.sum(drb.astype(jnp.float32), axis=0)
    dpatch = (
        mat(drb, w_reduce.T)
        .reshape(rows // 2, cols // 2, 2, 2, width)
        .transpose(0, 2, 1, 3, 4)
        .reshape(tokens, width)
    )
    dxm, grad_ln1_gain, grad_ln1_bias = first_norm_backward(dn1_query + dpatch)
    grad_whole = (dxm + dh1) * maskf
    grad_input = lax.dynamic_slice_in_dim(grad_whole, part * share, share, 1)
    (
        grad_w_reduce,
        grad_b_reduce,
        grad_lnr_gain,
        grad_lnr_bias,
        grad_ln1_gain,
        grad_ln1_bias,
        shared_gain,
        shared_bias,
        grad_b_out,
        grad_b_fc2,
        grad_w_fc1,
        grad_b_fc1,
        grad_w_depth,
        grad_b_depth,
        grad_w_fc2,
    ) = lax.psum(
        (
            grad_w_reduce,
            grad_b_reduce,
            grad_lnr_gain,
            grad_lnr_bias,
            grad_ln1_gain,
            grad_ln1_bias,
            shared_gain,
            shared_bias,
            grad_b_out,
            grad_b_fc2,
            grad_w_fc1,
            grad_b_fc1,
            grad_w_depth,
            grad_b_depth,
            grad_w_fc2,
        ),
        "dp",
    )
    (
        grad_w_query,
        grad_b_query,
        grad_w_key,
        grad_w_value,
        grad_b_value,
        output_weight_gradient,
        split_gain,
        split_bias,
    ) = lax.psum(
        (
            spread_columns(grad_wq, select_where),
            spread_vector(grad_bq, select_where),
            spread_columns(grad_wk, select_where),
            spread_columns(grad_wv, select_where),
            spread_vector(grad_bv, select_where),
            spread_rows(grad_wo, select_where),
            split_gain,
            split_bias,
        ),
        ("dp", "mp"),
    )
    grad_ln2_gain = shared_gain + split_gain
    grad_ln2_bias = shared_bias + split_bias
    return (
        block_result,
        grad_input,
        grad_ln1_gain,
        grad_ln1_bias,
        grad_w_query,
        grad_b_query,
        grad_w_key,
        grad_w_value,
        grad_b_value,
        grad_w_reduce,
        grad_b_reduce,
        grad_lnr_gain,
        grad_lnr_bias,
        output_weight_gradient,
        grad_b_out,
        grad_ln2_gain,
        grad_ln2_bias,
        grad_w_fc1,
        grad_b_fc1,
        grad_w_depth,
        grad_b_depth,
        grad_w_fc2,
        grad_b_fc2,
    )


BF = jnp.bfloat16
F32 = jnp.float32
LANES = 128
SIDE_SMALL = 64
VMEM_MB = 56


def nn(a, b):
    return lax.dot_general(a, b, (((1,), (0,)), ((), ())), preferred_element_type=F32)


def nt(a, b):
    return lax.dot_general(a, b, (((1,), (1,)), ((), ())), preferred_element_type=F32)


def tn(a, b):
    return lax.dot_general(a, b, (((0,), (0,)), ((), ())), preferred_element_type=F32)


def iota(shape, axis):
    return lax.broadcasted_iota(jnp.int32, shape, axis)


def hot(cond):
    return jnp.where(cond, 1.0, 0.0).astype(BF)


def spread(value):
    mean = jnp.sum(value, axis=-1, keepdims=True) * (1.0 / value.shape[-1])
    centred = value - mean
    var = jnp.sum(centred * centred, axis=-1, keepdims=True) * (1.0 / value.shape[-1])
    rstd = lax.rsqrt(var + EPS)
    return centred * rstd, rstd


def norm_back(dn, gain, xhat, rstd):
    e = dn * gain
    scale = 1.0 / dn.shape[-1]
    mean_e = jnp.sum(e, axis=-1, keepdims=True) * scale
    mean_ex = jnp.sum(e * xhat, axis=-1, keepdims=True) * scale
    return rstd * (e - mean_e - xhat * mean_ex)


def rowsum(value):
    return jnp.sum(value, axis=0, keepdims=True)


class Sizes:
    def __init__(self, n_dp, n_mp, tokens, width, hidden):
        self.n_dp, self.n_mp = n_dp, n_mp
        self.tokens, self.width, self.hidden = tokens, width, hidden
        self.share = width // n_mp
        self.rows = FRAME // TILE_ROWS
        self.cols = tokens // self.rows
        self.pa, self.pb = self.rows // 2, self.cols // 2
        self.keys = self.pa * self.pb
        self.plane = -(-self.keys // 16) * 16
        self.all = 4 * self.plane
        self.step = self.plane // 16 // n_mp * 16
        self.quarter = self.plane - (n_mp - 1) * self.step
        self.wide = -(-width // LANES) * LANES
        self.kvrows = self.plane + self.quarter
        self.top = 8 + self.pb
        self.ext = self.top + self.keys + self.pb
        self.edge = 4 * 2 * self.pb
        self.inner = 4 * (self.keys - 2 * self.pb)
        self.edge_q = -(-self.edge // LANES) * LANES
        self.inner_q = -(-self.inner // LANES) * LANES
        self.queries = self.edge_q + self.inner_q
        self.echunk = (width + hidden) // n_dp
        self.half = width - 2 * LANES
        self.wrows = 2 * width + width // 2
        self.l2rows = -(-(self.wrows + self.share) // (16 * n_dp)) * 16 * n_dp
        self.orows = HEAD_FEATURES + HEAD_FEATURES // n_mp
        self.l1rows = -(-(2 * width + 2 * self.orows + self.orows // 2) // (16 * n_dp)) * 16 * n_dp


class Load:
    def __init__(self, src, dst, sem):
        self.dst, self.shape, self.waiting = dst, dst.shape, True
        self.copy = pltpu.make_async_copy(src, dst, sem)
        self.copy.start()

    def ready(self):
        if self.waiting:
            self.waiting = False
            self.copy.wait()
        return self.dst

    def __getitem__(self, at):
        return self.ready()[at]


def fused_body(
    sz, names,
    mask_ref, slot_ref, *refs,
):
    ins, refs = refs[:23], refs[23:]
    outs, refs = refs[:7], refs[7:]
    s = dict(zip(names, refs))
    blk_ref, gp_ref, eg_ref, lg1_ref, lg2_ref, veg_ref, vlg_ref = (s["out%d" % i] for i in range(7))
    stores = []

    def store(i):
        c = pltpu.make_async_copy(s["out%d" % i], outs[i], s["osem"].at[i])
        c.start()
        stores.append(c)

    D, HF, PB, PA, KEYS, PL, T = sz.width, HEAD_FEATURES, sz.pb, sz.pa, sz.keys, sz.plane, sz.all
    C, FS, W = sz.hidden, sz.share, sz.wide
    d = lax.axis_index("dp")
    m = lax.axis_index("mp")
    last = sz.n_mp * HF
    ssem, rsem = s["ssem"], s["rsem"]

    def mpx(k):
        if k == 0:
            return m
        if k == 1:
            return m + 1 - 2 * lax.rem(m, 2)
        if k == 2:
            return lax.rem(m + 2, 4)
        return 3 - m

    def dpx(k):
        z, x = d // 2, lax.rem(d, 2)
        if k & 1:
            x = 1 - x
        kz = k >> 1
        if kz == 1:
            z = z + 1 - 2 * lax.rem(z, 2)
        elif kz == 2:
            z = lax.rem(z + 2, 4)
        elif kz == 3:
            z = 3 - z
        return 2 * z + x

    counter = [0]
    pending = []

    def take(n):
        first = counter[0]
        counter[0] += n
        return first

    def copy(src, dst, sem, dev):
        return pltpu.make_async_remote_copy(
            src_ref=src, dst_ref=dst, send_sem=ssem.at[sem], recv_sem=rsem.at[sem],
            device_id=dev, device_id_type=pl.DeviceIdType.MESH,
        )

    def send(src, dst, sem, dev):
        c = copy(src, dst, sem, dev)
        c.start()
        pending.append(c)

    def arrived(ref, sem):
        copy(ref, ref, sem, (d, m)).wait_recv()

    opened = []

    def handle(finish):
        state = [False]

        def once(*a):
            if not state[0]:
                state[0] = True
                return finish(*a)

        opened.append(once)
        return once

    def mp_start(buf):
        base = take(3)
        send(buf.at[m], buf.at[m], base, (d, mpx(1)))
        send(buf.at[m], buf.at[m], base + 1, (d, mpx(2)))

        def middle():
            arrived(buf.at[mpx(2)], base + 1)
            send(buf.at[mpx(2)], buf.at[mpx(2)], base + 2, (d, mpx(1)))

        mid = handle(middle)

        def finish():
            mid()
            arrived(buf.at[mpx(1)], base)
            arrived(buf.at[mpx(3)], base + 2)

        return handle(finish), mid

    def dp_start(buf, each=lambda k: None):
        base = take(7)
        for kz in (3, 2, 1):
            send(buf.at[d], buf.at[d], base + kz, (dpx(2 * kz), m))
        send(buf.at[d], buf.at[d], base, (dpx(1), m))

        def along(kz):
            arrived(buf.at[dpx(2 * kz)], base + kz)
            send(buf.at[dpx(2 * kz)], buf.at[dpx(2 * kz)], base + 3 + kz, (dpx(1), m))
            each(2 * kz)

        def across(kz):
            arrived(buf.at[dpx(2 * kz + 1)], base + 3 + kz if kz else base)
            each(2 * kz + 1)

        steps = [handle(lambda kz=kz: along(kz)) for kz in (1, 2, 3)] + [handle(lambda: across(0))]

        def mid():
            for step in steps:
                step()

        def finish():
            mid()
            for kz in (1, 2, 3):
                across(kz)

        return handle(finish), mid, steps

    def mp_scatter(block, dst, landed):
        base = take(4)
        for k in (2, 3, 1):
            send(block(mpx(k)), dst(k), base + k, (d, mpx(k)))

        def finish():
            for k in (1, 2, 3):
                arrived(landed(k), base + k)

        return handle(finish)

    def dp_scatter(block, dst, landed):
        base = take(8)
        for k in (6, 7, 4, 5, 2, 3, 1):
            send(block(dpx(k)), dst(k), base + k, (dpx(k), m))

        def finish():
            for k in range(1, sz.n_dp):
                arrived(landed(k), base + k)

        return handle(finish)

    def mp_sum(block, out, near, far):
        base = take(3)
        out[0] = block(mpx(1)).astype(BF)
        send(out.at[0], near.at[0], base, (d, mpx(1)))
        out[1] = block(mpx(3)).astype(BF)
        send(out.at[1], near.at[1], base + 1, (d, mpx(1)))

        def middle():
            value = block(mpx(2))
            arrived(near.at[1], base + 1)
            out[2] = (value + near[1].astype(F32)).astype(BF)
            send(out.at[2], far, base + 2, (d, mpx(2)))

        mid = handle(middle)

        def finish():
            mid()
            value = block(m)
            arrived(near.at[0], base)
            value = value + near[0].astype(F32)
            arrived(far, base + 2)
            return value + far[...].astype(F32)

        return mid, handle(finish)

    def dp_sum(chunk, near, out, far):
        base = take(8)
        for kz in (2, 3, 1, 0):
            send(chunk(dpx(2 * kz + 1)), near.at[kz], base + kz, (dpx(1), m))

        def middle():
            for kz in (2, 3, 1):
                value = chunk(dpx(2 * kz))[...].astype(F32)
                arrived(near.at[kz], base + kz)
                out[kz] = (value + near[kz].astype(F32)).astype(BF)
                send(out.at[kz], far.at[kz], base + 4 + kz, (dpx(2 * kz), m))

        mid = handle(middle)

        def finish():
            mid()
            value = chunk(d)[...].astype(F32)
            arrived(near.at[0], base)
            value = value + near[0].astype(F32)
            for kz in (1, 2, 3):
                arrived(far.at[kz], base + 4 + kz)
                value = value + far[kz].astype(F32)
            return value

        return mid, handle(finish)

    def dp_total(src, near, parts):
        base = take(4)
        z = d // 2
        send(src, near, base, (dpx(1), m))

        def middle():
            arrived(near, base)
            parts[z] = src[...] + near[...]
            for kz in (2, 3, 1):
                send(parts.at[z], parts.at[z], base + kz, (dpx(2 * kz), m))

        mid = handle(middle)

        def finish():
            mid()
            for kz in (1, 2, 3):
                arrived(parts.at[dpx(2 * kz) // 2], base + kz)
            return (parts[0] + parts[1]) + (parts[2] + parts[3])

        return mid, handle(finish)

    peers = [(d, mpx(k)) for k in (1, 2, 3)] + [(dpx(k), m) for k in range(1, 8)]
    bar = pltpu.get_barrier_semaphore()
    for dev in peers:
        pl.semaphore_signal(bar, inc=1, device_id=dev, device_id_type=pl.DeviceIdType.MESH)

    order = (0, 1, 2, 3, 8, 7, 9, 10, 11, 12, 4, 5, 6, 21, 22, 13, 14, 15, 16, 17, 18, 19, 20)
    loads = [None] * 23
    for i in order:
        dst = s["xt"].at[m] if i == 0 else s["in%d" % i]
        loads[i] = Load(ins[i], dst, s["isem"].at[i])
    (
        pix_ref, cot_ref, ln1g_ref, ln1b_ref, wq_ref, bq_ref, wk_ref, wv_ref, bv_ref, wr_ref, br_ref,
        lnrg_ref, lnrb_ref, wo_ref, bo_ref, ln2g_ref, ln2b_ref, w1_ref, b1_ref, wd_ref, bd_ref, w2_ref, b2_ref,
    ) = loads

    side = jnp.where(mask_ref[sz.cols - 1] > 0, FRAME, SIDE_SMALL)
    tile = slot_ref[1, d]
    tiles = [slot_ref[1, k] for k in range(sz.n_dp)]
    above = sum(jnp.where(tiles[k] == tile - 1, k, 0) for k in range(sz.n_dp))
    below = sum(jnp.where(tiles[k] == tile + 1, k, 0) for k in range(sz.n_dp))

    def place(p, count):
        a = sum(jnp.where(p >= PB * k, 1, 0) for k in range(1, count))
        return a, p - PB * a

    def token_mask(i, j):
        p = iota((PL, 1), 0)
        a, b = place(p, PA)
        inside = (p < KEYS) & (sz.rows * tile + 2 * a + i < side) & (2 * b + j < side)
        return jnp.where(inside, 1.0, 0.0)

    def row_mask(i, j, a):
        b = iota((PB, 1), 0)
        row = sz.rows * tile + 2 * a + i
        inside = (row >= 0) & (row < side) & (2 * b + j < side)
        return jnp.where(inside, 1.0, 0.0)

    def key_bias(p, tile_at):
        a, b = place(p, PA)
        usable = (p < KEYS) & (sz.rows * tile_at + 2 * a < side) & (2 * b < side)
        return jnp.where(usable, 0.0, NEG)

    def vec(ref):
        return ref[...].reshape(1, ref.shape[0])

    def own_part(row, size):
        return sum(
            jnp.where(m == h, 1.0, 0.0) * row[:, size * h : size * (h + 1)] for h in range(sz.n_mp)
        )

    def plane_rows(ref, start):
        return ref[pl.ds(pl.multiple_of(start, 16), PL), :]

    def plane(p):
        return slice(PL * p, PL * (p + 1))

    lanes3 = (s["t0"], s["t1"], s["t2"])

    def to_planes(rows_of):
        for n, ref in enumerate(lanes3):
            ref[...] = rows_of(LANES * n, min(D, LANES * (n + 1))).astype(F32).T
        for i in range(2):
            for j in range(2):
                parts = []
                for ref in lanes3:
                    rows = [
                        ref[pl.ds((2 * a + i) * sz.cols + j, PB, stride=2), :] for a in range(PA)
                    ] + [jnp.zeros((PL - KEYS, ref.shape[1]), F32)]
                    parts.append(jnp.concatenate(rows, axis=0))
                yield i, j, jnp.concatenate(parts, axis=1)

    def to_queries(planes):
        n = planes[0].shape[1]
        edge = [v for p in planes for v in (p[0:PB], p[KEYS - PB : KEYS])]
        inner = [p[PB : KEYS - PB] for p in planes]
        return jnp.concatenate(
            edge + [jnp.zeros((sz.edge_q - sz.edge, n), F32)]
            + inner + [jnp.zeros((sz.inner_q - sz.inner, n), F32)],
            axis=0,
        )

    def from_queries(edge, inner, p):
        n = KEYS - 2 * PB
        return jnp.concatenate(
            [
                edge[2 * PB * p : 2 * PB * p + PB], inner[n * p : n * (p + 1)],
                edge[2 * PB * p + PB : 2 * PB * (p + 1)], jnp.zeros((PL - KEYS, edge.shape[1]), F32),
            ],
            axis=0,
        )

    xt, dfm = s["xt"], s["dfm"]
    pl.semaphore_wait(bar, len(peers))
    pix_ref.ready()
    x_at, x_mid = mp_start(xt)

    for i, j, value in to_planes(lambda lo, hi: cot_ref[lo:hi, :]):
        dfm[plane(2 * i + j), :] = (value * token_mask(i, j)).astype(BF)
    dyh, dyh_g = s["dyh"], s["dyh_g"]
    dyh[d, :, :D] = dfm[pl.ds(pl.multiple_of(PL * m + (KEYS - PB) * (m // 2), 16), 48), :]
    dyh[d, :, D:] = jnp.zeros((48, W - D), BF)
    dy_at, _, _ = dp_start(dyh)
    x_mid()

    r2, c2 = iota((D, LANES), 0), iota((D, LANES), 1)
    own_lo = hot((c2 < HF) & (r2 == HF * m + c2))
    own_hi = hot((c2 >= HF) & (r2 == HF * m + c2 - HF))
    last_lo = hot((c2 < HF) & (r2 == last + c2))
    last_hi = hot((c2 >= HF) & (r2 == last + c2 - HF))
    wq, wk, wv = wq_ref[...], wk_ref[...], wv_ref[...]
    wq2 = nn(wq, own_lo + last_hi).astype(BF)
    wkv = (nn(wk, own_lo) + nn(wv, own_hi)).astype(BF)
    wkv5 = (nn(wk, last_lo) + nn(wv, last_hi)).astype(BF)
    bq, bv = vec(bq_ref), vec(bv_ref)
    bq2 = jnp.concatenate([own_part(bq, HF), bq[:, last:]], axis=1)
    nil = jnp.zeros((1, HF), F32)
    bkv = jnp.concatenate([nil, own_part(bv, HF)], axis=1)
    bkv5 = jnp.concatenate([nil, bv[:, last:]], axis=1)
    rt, ct = iota((D, 4 * LANES), 0), iota((D, 4 * LANES), 1)
    lane4, head4 = ct & (LANES - 1), ct >> 7
    place_out = hot((lane4 < FS) & (rt == FS * head4 + lane4))
    rk, ck = iota((D, 5 * LANES), 0), iota((D, 5 * LANES), 1)
    lane5, head5 = ck & (LANES - 1), ck >> 7
    w_all, wq_cat, w2_t, wo_cat = s["w_all"], s["wq_cat"], s["w2_t"], s["wo_cat"]
    w_all[...] = (
        nn(wk, hot((lane5 < HF) & (rk == HF * head5 + lane5)))
        + nn(wv, hot((lane5 >= HF) & (rk == HF * head5 + lane5 - HF)))
    ).astype(BF)
    wq_cat[...] = nn(
        wq, hot(rt == jnp.where(lane4 < HF, HF * head4 + lane4, last + lane4 - HF))
    ).astype(BF)
    w2 = w2_ref[...]
    w2_t[...] = w2.T
    wo = wo_ref[...]
    wo_cat[...] = jnp.concatenate(
        [b for h in range(4) for b in (wo[HF * h : HF * (h + 1)], wo[last:])], axis=0
    )
    wr_t = s["wr_t"]
    wr_t[...] = wr_ref[...].T

    xm_r, n1_r = s["xm_r"], s["n1_r"]
    x_at()
    x_all = xt[...].reshape(D, sz.tokens)
    for i, j, value in to_planes(lambda lo, hi: x_all[lo:hi, :]):
        xm = value * token_mask(i, j)
        xm_r[plane(2 * i + j), :] = xm.astype(BF)
        xhat, _ = spread(xm)
        n1_r[plane(2 * i + j), :] = (xhat * vec(ln1g_ref) + vec(ln1b_ref)).astype(BF)

    kva, xr_r = s["kva"], s["xr_r"]
    red = sum(nn(n1_r[plane(p), :], wr_t[D * p : D * (p + 1), :]) for p in range(4)) + vec(br_ref)
    xhr, rsr = spread(red)
    s["xhr_r"][...] = xhr
    s["rsr_r"][...] = jnp.broadcast_to(rsr, (PL, LANES))
    xr_r[...] = (xhr * vec(lnrg_ref) + vec(lnrb_ref)).astype(BF)
    kva[d, 0:PL, :] = (nn(xr_r[...], wkv) + bkv).astype(BF)
    quarter_rows = pl.ds(pl.multiple_of(sz.step * m, 16), sz.quarter)
    kva[d, PL:, :] = (nn(xr_r[quarter_rows, :], wkv5) + bkv5).astype(BF)
    kv_at, _, _ = dp_start(kva)

    qa_r, qb_r = s["qa_r"], s["qb_r"]
    Q = sz.queries
    q2 = (nn(n1_r[...], wq2) + bq2).astype(BF).astype(F32) * HF ** (-0.5)
    q2t = to_queries([q2[plane(p)] for p in range(4)]).T
    half = jnp.zeros((HF, Q), F32)
    qa_r[...] = jnp.concatenate([q2t[0:HF], half], axis=0).astype(BF)
    qb_r[...] = jnp.concatenate([q2t[HF:], half], axis=0).astype(BF)

    dy_at()
    dyh_g[m] = dyh[jnp.where(m >= 2, above, below)]
    dyg_at, dyg_mid = mp_start(dyh_g)

    dgx, dzx = s["dgx"], s["dzx"]
    for p in range(4):
        dgx[p, sz.top : sz.top + PL, :] = nt(dfm[plane(p), :], w2).astype(BF).astype(F32)
    limit5 = jnp.where(m == sz.n_mp - 1, KEYS - sz.step * m, sz.step)
    pk = iota((sz.quarter, 1), 0)
    bias5 = jnp.concatenate(
        [
            jnp.where(pk < limit5, key_bias(pk + sz.step * m, tiles[k]), NEG)
            for k in range(sz.n_dp)
        ],
        axis=0,
    )
    dyg_mid()
    kv_at()

    e5buf, ebuf, sbuf, row_r, ot_r = s["e5buf"], s["ebuf"], s["sbuf"], s["row_r"], s["ot_r"]
    kv5 = kva[:, PL:, :].reshape(sz.n_dp * sz.quarter, LANES)
    chunks = ((0, sz.edge_q, s["lse_a"], s["og_a"]), (sz.edge_q, sz.queries, s["lse_b"], s["og_b"]))
    fives = []
    for lo, hi, lse_r, _ in chunks:
        s5 = nn(kv5, qb_r[:, lo:hi]) + bias5
        m5 = jnp.max(s5, axis=0, keepdims=True)
        e5 = jnp.exp(s5 - m5).astype(BF)
        l5 = rowsum(e5.astype(F32))
        e5buf[:, :, lo:hi] = e5.reshape(sz.n_dp, sz.quarter, hi - lo)
        lse_r[m] = jnp.broadcast_to(m5 + jnp.log(l5), (8, hi - lo))
        at = mp_scatter(
            lambda h, r=lse_r: r.at[m], lambda k, r=lse_r: r.at[m], lambda k, r=lse_r: r.at[mpx(k)]
        )
        fives.append((m5, tn(kv5, e5), at))

    pk = iota((PL, 1), 0)
    ogs = []
    for (lo, hi, lse_r, og), (m5, o5t, lse_at) in zip(chunks, fives):

        def score_step(j, top, lo=lo, hi=hi):
            v = nn(kva[j, 0:PL, :], qa_r[:, lo:hi]) + key_bias(pk, slot_ref[1, j])
            sbuf[j, :, lo:hi] = v
            return jnp.maximum(top, jnp.max(v, axis=0, keepdims=True))

        top = lax.fori_loop(0, sz.n_dp, score_step, jnp.full((1, hi - lo), NEG, F32))
        if ogs:
            ogs[0][1]()

        def exp_step(j, total, lo=lo, hi=hi, top=top):
            e = jnp.exp(sbuf[j, :, lo:hi] - top).astype(BF)
            ebuf[j, :, lo:hi] = e
            return total + rowsum(e.astype(F32))

        total = lax.fori_loop(0, sz.n_dp, exp_step, jnp.zeros((1, hi - lo), F32))
        ot = tn(
            kva[:, 0:PL, :].reshape(sz.n_dp * PL, LANES),
            ebuf[:, :, lo:hi].reshape(sz.n_dp * PL, hi - lo),
        )
        inv = 1.0 / total
        lse_at()
        lses = [lse_r[h][0:1] for h in range(4)]
        lmax = jnp.maximum(jnp.maximum(lses[0], lses[1]), jnp.maximum(lses[2], lses[3]))
        lse5 = lmax + jnp.log(sum(jnp.exp(v - lmax) for v in lses))
        f5 = jnp.exp(m5 - lse5)
        row_r[0:1, lo:hi] = inv
        row_r[1:2, lo:hi] = f5
        o2t = jnp.concatenate([ot[HF:] * inv, o5t[HF:] * f5], axis=0)
        ot_r[:, lo:hi] = o2t
        og[m] = o2t.T[0 : og.shape[1]].astype(BF)
        ogs.append(mp_start(og))

    og_a, og_b = s["og_a"], s["og_b"]
    hal, hal_g, h1_r, n2_r = s["hal"], s["hal_g"], s["h1_r"], s["n2_r"]

    def second_norm(h1):
        xhat, _ = spread(h1)
        return (xhat * vec(ln2g_ref) + vec(ln2b_ref)).astype(BF)

    ogs[0][0]()
    border = pl.ds(pl.multiple_of(2 * PB * m, 16), 2 * PB)
    oc = jnp.concatenate([og_a[h, border, :] for h in range(4)], axis=1)
    xmine = plane_rows(xm_r, PL * m).astype(F32)
    xmine = jnp.concatenate([xmine[0:PB], xmine[KEYS - PB : KEYS]], axis=0)
    im, jm = m // 2, lax.rem(m, 2)
    emask = jnp.concatenate([row_mask(im, jm, 0), row_mask(im, jm, PA - 1)], axis=0)
    hal[d, :, :D] = second_norm(xmine + emask * (nn(oc, wo_cat[...]) + vec(bo_ref)))
    hal[d, :, D:] = jnp.zeros((2 * PB, W - D), BF)
    hal_at, hal_mid, hal_steps = dp_start(hal)
    ogs[1][1]()

    dyg_at()
    for p in range(4):
        i, j = p // 2, p % 2
        start = sz.top - PB if i == 1 else sz.top + KEYS
        rows = dyh_g[p][:, :D].astype(F32)[0:PB] * row_mask(i, j, -1 if i == 1 else PA)
        dgx[p, start : start + PB, :] = nt(rows.astype(BF), w2).astype(BF).astype(F32)
    ogs[1][0]()
    mixed = []
    for og in (og_a, og_b):
        oc = jnp.concatenate([og[h] for h in range(4)], axis=1)
        mixed.append(nn(oc, wo_cat[...]) + vec(bo_ref))
    w1, b1 = w1_ref[...], vec(b1_ref)

    def hidden(rows, mask):
        return ((nn(rows, w1) + b1) * mask).astype(BF).astype(F32)

    ux, ul, ur, dzl, dzr = s["ux"], s["ul"], s["ur"], s["dzl"], s["dzr"]
    b40 = iota((PB, 1), 0)

    def shift(src, left, right, i, start):
        at = slice(start, start + PB)
        left[i, at, :] = jnp.where(b40 == 0, 0.0, pltpu.roll(src[2 * i + 1, at, :], 1, 0))
        right[i, at, :] = jnp.where(b40 == PB - 1, 0.0, pltpu.roll(src[2 * i, at, :], PB - 1, 0))

    for p in range(4):
        mask = token_mask(p // 2, p % 2)
        h1 = xm_r[plane(p), :].astype(F32) + mask * from_queries(mixed[0], mixed[1], p)
        h1_r[plane(p), :] = h1
        n2_r[plane(p), :] = second_norm(h1)
        ux[p, sz.top : sz.top + PL, :] = hidden(n2_r[plane(p), :], mask)
    for i in range(2):
        for a in range(PA):
            shift(ux, ul, ur, i, sz.top + PB * a)
    hal_steps[0]()

    wd_ref, bd_row = wd_ref.ready(), vec(bd_ref)
    g_r, du_r = s["g_r"], s["du_r"]
    for p in range(4):
        g_r[p, KEYS:PL, :] = jnp.zeros((PL - KEYS, C), F32)
        du_r[p, KEYS:PL, :] = jnp.zeros((PL - KEYS, C), F32)

    def source(refs, i, j, di, dj, start):
        base, left, right = refs
        i2, up = (i + di) % 2, (i + di) // 2
        j2, across = (j + dj) % 2, (j + dj) // 2
        at = pl.ds(pl.multiple_of(start + PB * up, 8), PB)
        if across < 0:
            return left[i2, at, :]
        if across > 0:
            return right[i2, at, :]
        return base[2 * i2 + j2, at, :]

    TAPS = [(di, dj) for di in (-1, 0, 1) for dj in (-1, 0, 1)]

    def activation(i, j, start):
        p = 2 * i + j
        z = bd_row + sum(
            wd_ref[t : t + 1, :] * source((ux, ul, ur), i, j, di, dj, start)
            for t, (di, dj) in enumerate(TAPS)
        )
        phi = 0.5 * (1.0 + lax.erf(z * 0.7071067811865476))
        dens = jnp.exp(-0.5 * z * z) * 0.3989422804014327
        dz = dgx[p, pl.ds(pl.multiple_of(start, 8), PB), :] * (phi + z * dens)
        dzx[p, pl.ds(pl.multiple_of(start, 8), PB), :] = dz
        return z * phi, dz

    def fold(value):
        return jnp.sum(value.reshape(PB // 8, 8, C), axis=0)

    def forward_step(i, j):
        p = 2 * i + j

        def step(a, acc):
            start = sz.top + PB * a
            act, dz = activation(i, j, start)
            g_r[p, pl.ds(pl.multiple_of(PB * a, 8), PB), :] = act
            new = [
                acc[t] + fold(dz * source((ux, ul, ur), i, j, di, dj, start))
                for t, (di, dj) in enumerate(TAPS)
            ]
            return tuple(new) + (acc[9] + fold(dz),)

        return step

    sums = tuple(jnp.zeros((8, C), F32) for _ in range(10))
    for i in range(2):
        for j in range(2):
            sums = lax.fori_loop(1 - i, PA - i, forward_step(i, j), sums)
        hal_steps[1 + i]()
    hal_at()
    up_rows = hal[above].astype(F32)[PB:]
    down_rows = hal[below].astype(F32)[0:PB]
    hal_g[m] = jnp.concatenate([up_rows, down_rows], axis=0).astype(BF)
    halg_at, _ = mp_start(hal_g)
    for k in range(sz.n_dp):
        e5buf[k] = (e5buf[k].astype(F32) * row_r[1:2, :]).astype(BF)
    ogp = s["ogp"]
    lane = iota((T, LANES), 1)
    fifth = [sum(og[h].astype(F32) for h in range(4)) for og in (og_a, og_b)]
    owns = [og[m].astype(F32) for og in (og_a, og_b)]
    for p in range(4):
        ogp[plane(p), :] = jnp.where(
            lane[plane(p)] < HF, from_queries(*owns, p), from_queries(*fifth, p)
        ).astype(BF)
    halg_at()
    for p in range(4):
        i, j = p // 2, p % 2
        mask = jnp.concatenate([row_mask(i, j, -1), row_mask(i, j, PA)], axis=0)
        u = hidden(hal_g[p][:, :D], mask)
        ux[p, sz.top - PB : sz.top, :] = u[0:PB]
        ux[p, sz.top + KEYS : sz.top + KEYS + PB, :] = u[PB:]
    for i in range(2):
        shift(ux, ul, ur, i, sz.top - PB)
        shift(ux, ul, ur, i, sz.top + KEYS)
    for i in range(2):
        for j in range(2):
            activation(i, j, sz.top - PB if i == 1 else sz.top + KEYS)
            sums = forward_step(i, j)((PA - 1) * i, sums)
    e_s, ve_s, vl_s = s["e_s"], s["ve_s"], s["vl_s"]
    for i in range(2):
        for a in range(PA + 1):
            shift(dzx, dzl, dzr, i, sz.top + PB * (a - i))
    dub = s["dub"]
    for i in range(2):
        for j in range(2):
            p = 2 * i + j

            def backward_step(a, carry, i=i, j=j, p=p):
                start = sz.top + PB * a
                du_r[p, pl.ds(pl.multiple_of(PB * a, 8), PB), :] = sum(
                    wd_ref[t : t + 1, :] * source((dzx, dzl, dzr), i, j, -di, -dj, start)
                    for t, (di, dj) in enumerate(TAPS)
                )
                return carry

            lax.fori_loop(0, PA, backward_step, 0)
            dub[p] = (du_r[p].astype(BF).astype(F32) * token_mask(i, j)).astype(BF)
    dn2_mid, dn2_at = mp_sum(lambda h: nt(dub[h], w1), s["dn2_s"], s["dn2_n"], s["dn2_f"])
    dn2_mid()

    gb = g_r[...].reshape(T, C).astype(BF)
    du_all = dub[...].reshape(T, C)
    e_s[0:D, :C] = tn(n2_r[...], du_all).astype(BF)
    e_s[D:, :D] = tn(gb, dfm[...]).astype(BF)

    def rows_of(ref, n):
        return lambda j: ref.at[pl.ds(pl.multiple_of(n * j, 16), n)]

    e_mid, e_at = dp_sum(rows_of(e_s, sz.echunk), s["e_n"], s["e_o"], s["e_f"])
    for t in range(10):
        ve_s[t : t + 1, :C] = rowsum(sums[t])
    ve_s[10:11, :C] = rowsum(du_all.astype(F32))

    xhat2, rstd2 = spread(plane_rows(h1_r, PL * m))
    dfp = plane_rows(dfm, PL * m).astype(F32)
    ve_s[11:12, :D] = rowsum(dfp)
    dn2 = dn2_at()
    dh1 = dfp + norm_back(dn2, vec(ln2g_ref), xhat2, rstd2)
    dab = dh1.astype(BF)
    docat = nt(dab, wo_cat[...]).astype(BF)
    dos, do_all, dabg = s["dos"], s["do_all"], s["dabg"]
    for h in range(4):
        dos[h] = docat[:, LANES * h : LANES * (h + 1)]
    do_at = mp_scatter(lambda h: dos.at[h], lambda k: do_all.at[m], lambda k: do_all.at[mpx(k)])
    do_all[m] = dos[m]
    s["dh1_r"][...] = dh1
    dabg[m, :, :D] = dab
    ve_s[12:13, :D] = rowsum(dh1)
    ve_s[13:14, :D] = rowsum(dn2 * xhat2)
    ve_s[14:15, :D] = rowsum(dn2)
    ve_s[15:16, :] = jnp.zeros((1, W), F32)
    ve_mid, ve_at = dp_total(ve_s, s["ve_n"], s["ve_p"])
    e_mid()

    def ff_block(h):
        return nt(w2_t[pl.ds(pl.multiple_of(FS * h, 16), FS), :], gb)

    ff_mid, ff_at = mp_sum(ff_block, s["ff_s"], s["ff_n"], s["ff_f"])

    do_at()
    dr_r = s["dr_r"]
    dot_t = to_queries([do_all[p].astype(F32) for p in range(4)]).T
    dr_r[m] = jnp.broadcast_to(rowsum(dot_t[HF:] * ot_r[HF:, :]), (8, Q))
    dr_at = mp_scatter(lambda h: dr_r.at[m], lambda k: dr_r.at[m], lambda k: dr_r.at[mpx(k)])
    dab_at, dab_mid = mp_start(dabg)
    da_own = (dot_t[0:HF] * row_r[0:1, :]).astype(BF)
    drow = rowsum(da_own.astype(F32) * ot_r[0:HF, :])
    da_t = jnp.concatenate([half.astype(BF), da_own], axis=0)
    db_t = jnp.concatenate([half, dot_t[HF:]], axis=0).astype(BF)
    dqt, dqt5 = s["dqt"], s["dqt5"]
    dqt[...] = jnp.zeros_like(dqt)
    dqt5[...] = jnp.zeros_like(dqt5)
    five_row = []

    def own_keys(j):
        kv, e = kva[j, 0:PL, :], ebuf[j]
        ds = (e.astype(F32) * (nn(kv, da_t) - drow)).astype(BF)
        dqt[...] += tn(kv, ds)
        return nt(ds, qa_r[...]) + nt(e, da_t)

    def last_keys(j):
        kv, e = kva[j, PL:, :], e5buf[j]
        ds = (e.astype(F32) * (nn(kv, db_t) - five_row[0])).astype(BF)
        dqt5[...] += tn(kv, ds)
        return nt(ds, qb_r[...]) + nt(e, db_t)

    dk_x, dk_n, dk_o, dk_f = s["dk_x"], s["dk_n"], s["dk_o"], s["dk_f"]
    dk_at = take(8)

    def dk_across(kz, own):
        dk_x[kz] = jnp.concatenate([own, last_keys(dpx(2 * kz + 1))], axis=0).astype(BF)
        send(dk_x.at[kz], dk_n.at[kz], dk_at + kz, (dpx(1), m))

    def dk_along(kz):
        j = dpx(2 * kz)
        value = jnp.concatenate([own_keys(j), last_keys(j)], axis=0)
        arrived(dk_n.at[kz], dk_at + kz)
        dk_o[kz] = (value + dk_n[kz].astype(F32)).astype(BF)
        send(dk_o.at[kz], dk_f.at[kz], dk_at + 4 + kz, (dpx(2 * kz), m))

    own2 = own_keys(dpx(5))
    own3 = own_keys(dpx(7))
    dr_at()
    five_row.append(sum(dr_r[h][0:1] for h in range(4)))
    dk_across(2, own2)
    dk_across(3, own3)
    ve_mid()
    dk_across(1, own_keys(dpx(3)))
    dab_mid()
    dk_across(0, own_keys(dpx(1)))
    dk_along(2)
    dk_along(3)
    ff_mid()
    dk_along(1)
    dkv = jnp.concatenate([own_keys(d), last_keys(d)], axis=0)

    def dk_finish():
        arrived(dk_n.at[0], dk_at)
        total = dkv + dk_n[0].astype(F32)
        for kz in (1, 2, 3):
            arrived(dk_f.at[kz], dk_at + 4 + kz)
            total = total + dk_f[kz].astype(F32)
        return total

    dk_fin = handle(dk_finish)

    dq2 = (jnp.concatenate([dqt[0:HF], dqt5[0:HF]], axis=0) * HF ** (-0.5)).T
    dqs, dq_all = s["dqs"], s["dq_all"]
    for h in range(4):
        dqs[h] = from_queries(dq2[: sz.edge_q], dq2[sz.edge_q :], h).astype(BF)
    dq_at = mp_scatter(lambda h: dqs.at[h], lambda k: dq_all.at[m], lambda k: dq_all.at[mpx(k)])
    dq_all[m] = dqs[m]
    eg_ref[d] = e_at().astype(BF)
    eg_at, eg_mid, _ = dp_start(eg_ref)
    l1_s, l2_s = s["l1_s"], s["l2_s"]
    dqp = dqs[...].reshape(T, LANES)
    l1_s[0:D, :] = tn(n1_r[...], dqp).astype(BF)
    vl_s[...] = jnp.zeros_like(vl_s)
    vl_s[5:6, 0:LANES] = rowsum(dqp.astype(F32))

    def packed(value):
        n = value.shape[0] // 2
        parts = [value[:, 0:LANES], value[:, LANES : 2 * LANES]]
        parts.append(jnp.concatenate([value[0:n, 2 * LANES :], value[n:, 2 * LANES :]], axis=1))
        return jnp.concatenate(parts, axis=0)

    def fill(ref, first, value):
        rest = jnp.zeros((ref.shape[0] - first - value.shape[0], LANES), F32)
        ref[first:, :] = jnp.concatenate([value, rest], axis=0).astype(BF)

    def own_rows(value, n):
        return sum(jnp.where(m == h, 1.0, 0.0) * value[n * h : n * (h + 1)] for h in range(4))

    dab_at()
    gwo = tn(ogp[...], dabg[...].reshape(T, W)[:, :D])
    fill(l1_s, 2 * D, packed(jnp.concatenate([gwo[0:HF], own_rows(gwo[HF:], HF // 4)], axis=0)))

    dkvb = dk_fin().astype(BF)
    dkvg = s["dkvg"]
    dkvg[m] = dkvb
    dkv_at, dkv_mid = mp_start(dkvg)
    l1_s[D : 2 * D, :] = tn(xr_r[...], dkvb[0:PL]).astype(BF)
    l1_mid, l1_at = dp_sum(rows_of(l1_s, sz.l1rows // sz.n_dp), s["l1_n"], s["l1_o"], s["l1_f"])
    vl_s[6:7, 0:LANES] = jnp.concatenate(
        [rowsum(dkvb[0:PL].astype(F32))[:, HF:], rowsum(dkvb[PL:].astype(F32))[:, HF:]], axis=1
    )
    dq_at()
    dq_cat = jnp.concatenate([dq_all[h] for h in range(4)], axis=1)
    dn1 = nt(dq_cat, wq_cat[...])
    xhat1, rstd1 = spread(plane_rows(xm_r, PL * m).astype(F32))
    dkv_mid()
    dkv_at()
    rest = jnp.concatenate(
        [dkvg[h, PL : PL + sz.step, :] for h in range(3)] + [dkvg[3, PL:, :]], axis=0
    )
    dkv_all = jnp.concatenate([dkvg[h, 0:PL, :] for h in range(4)] + [rest], axis=1)
    dxr = nt(dkv_all, w_all[...])
    xhr = s["xhr_r"][...]
    drb = norm_back(dxr, vec(lnrg_ref), xhr, s["rsr_r"][:, 0:1]).astype(BF)
    l2_s[0 : sz.wrows, :] = packed(tn(drb, plane_rows(n1_r, PL * m))).astype(BF)
    fill(l2_s, sz.wrows, own_rows(tn(xr_r[...], rest), FS))
    l2_mid, l2_at = dp_sum(rows_of(l2_s, sz.l2rows // sz.n_dp), s["l2_n"], s["l2_o"], s["l2_f"])
    l1_mid()
    vl_s[2:3, :D] = rowsum(dxr * xhr)
    vl_s[3:4, :D] = rowsum(dxr)
    vl_s[4:5, :D] = rowsum(drb.astype(F32))

    wr_m = wr_t[pl.ds(pl.multiple_of(D * m, 16), D), :]
    dn1 = dn1 + nt(drb, wr_m)
    vl_s[0:1, :D] = rowsum(dn1 * xhat1)
    vl_s[1:2, :D] = rowsum(dn1)
    vl_mid, vl_at = dp_total(vl_s, s["vl_n"], s["vl_p"])
    dxm = norm_back(dn1, vec(ln1g_ref), xhat1, rstd1)
    gp = (token_mask(im, jm) * (s["dh1_r"][...] + dxm)).astype(BF)
    gpf = nn(gp, place_out).astype(BF)
    gps = s["gps"]
    for h in range(4):
        gps[h] = gpf[:, LANES * h : LANES * (h + 1)]
    gp_at = mp_scatter(lambda h: gps.at[h], lambda k: gp_ref.at[m], lambda k: gp_ref.at[mpx(k)])
    gp_ref[m] = gps[m]
    eg_mid()

    ff = ff_at().T
    ff = jnp.concatenate([ff, jnp.zeros((T, LANES - FS), F32)], axis=1)
    sel = hot((c2 < FS) & (r2 == FS * m + c2))
    b2q = jnp.concatenate(
        [own_part(vec(b2_ref), FS), jnp.zeros((1, LANES - FS), F32)], axis=1
    )
    for p in range(4):
        h1 = h1_r[plane(p), :]
        hi = h1.astype(BF)
        h1q = nn(hi, sel) + nn((h1 - hi.astype(F32)).astype(BF), sel)
        blk_ref[plane(p), :] = h1q + token_mask(p // 2, p % 2) * (ff[plane(p)] + b2q)
    store(0)
    veg_ref[m] = ve_at()
    veg_at, _ = mp_start(veg_ref)

    def gather(buf):
        base = take(3 * sz.n_dp)

        def onward(k):
            j = dpx(k)
            send(buf.at[m, j], buf.at[m, j], base + 3 * k, (d, mpx(1)))
            send(buf.at[m, j], buf.at[m, j], base + 3 * k + 1, (d, mpx(2)))

        near, mid, steps = dp_start(buf.at[m], onward)
        onward(0)
        seq = (0, 2, 4, 6, 1, 3, 5, 7)

        def relay(k):
            j = dpx(k)
            arrived(buf.at[mpx(2), j], base + 3 * k + 1)
            send(buf.at[mpx(2), j], buf.at[mpx(2), j], base + 3 * k + 2, (d, mpx(1)))

        relays = [handle(lambda k=k: relay(k)) for k in seq]

        def finish():
            near()
            for r in relays:
                r()
            for k in seq:
                arrived(buf.at[mpx(1), dpx(k)], base + 3 * k)
                arrived(buf.at[mpx(3), dpx(k)], base + 3 * k + 2)

        return near, mid, relays, handle(finish)

    lg1_ref[m, d] = l1_at().astype(BF)
    near1, mid1, relays1, lg1_at = gather(lg1_ref)
    l2_mid()
    vl_mid()
    mid1()
    lg2_ref[m, d] = l2_at().astype(BF)
    near2, mid2, relays2, lg2_at = gather(lg2_ref)
    near1()
    vlg_ref[m] = vl_at()
    vlg_at, _ = mp_start(vlg_ref)
    for r in relays1[:4]:
        r()
    mid2()
    for r in relays1[4:]:
        r()
    near2()
    for r in relays2:
        r()
    eg_at()
    store(2)
    gp_at()
    store(1)
    veg_at()
    store(5)
    lg1_at()
    store(3)
    vlg_at()
    store(6)
    lg2_at()
    store(4)
    for c in pending:
        c.wait_send()
    for c in stores:
        c.wait()


def unpack_body(sz, *refs):
    srcs, refs = refs[:7], refs[7:]
    (
        out_ref, gpix_ref, ln1g_ref, ln1b_ref, gwq_ref, gbq_ref, gwk_ref, gwv_ref, gbv_ref, gwr_ref, gbr_ref,
        lnrg_ref, lnrb_ref, gwo_ref, gbo_ref, ln2g_ref, ln2b_ref, gw1_ref, gb1_ref, gwd_ref, gbd_ref,
        gw2_ref, gb2_ref,
    ), refs = refs[:23], refs[23:]
    out32, gp32, sem = refs[7:]
    order = (5, 6, 0, 1, 2, 3, 4)
    loads = [None] * 7
    for i in order:
        loads[i] = Load(srcs[i], refs[i], sem.at[i])
    blk_ref, gp_ref, eg_ref, lg1_ref, lg2_ref, veg_ref, vlg_ref = loads
    D, HF, PB, PA, PL = sz.width, HEAD_FEATURES, sz.pb, sz.pa, sz.plane
    C, FS = sz.hidden, sz.share
    m = lax.axis_index("mp")

    def row(value):
        return value.reshape(value.shape[1])

    ve = veg_ref[m]
    gwd_ref[...] = ve[0:9, :C]
    gbd_ref[...] = row(ve[9:10, :C])
    gb1_ref[...] = row(ve[10:11, :C])
    vs = sum(veg_ref[h] for h in range(4))
    gb2_ref[...] = row(vs[11:12, :D])
    gbo_ref[...] = row(vs[12:13, :D])
    ln2g_ref[...] = row(vs[13:14, :D])
    ln2b_ref[...] = row(vs[14:15, :D])
    vl = sum(vlg_ref[h] for h in range(4))
    ln1g_ref[...] = row(vl[0:1, :D])
    ln1b_ref[...] = row(vl[1:2, :D])
    lnrg_ref[...] = row(vlg_ref[0][2:3, :D])
    lnrb_ref[...] = row(vlg_ref[0][3:4, :D])
    gbr_ref[...] = row(vlg_ref[0][4:5, :D])

    def head_row(r):
        parts = [vlg_ref[h][r : r + 1, 0:HF] for h in range(4)] + [vl[r : r + 1, HF : 2 * HF]]
        return row(jnp.concatenate(parts, axis=1))

    gbq_ref[...] = head_row(5)
    gbv_ref[...] = head_row(6)
    for i in range(2):
        for j in range(2):
            p = 2 * i + j
            for a in range(PA):
                at = pl.ds((2 * a + i) * sz.cols + j, PB, stride=2)
                out32[at, :] = blk_ref[PL * p + PB * a : PL * p + PB * (a + 1), 0:FS]
                gp32[at, :] = gp_ref[p].astype(F32)[PB * a : PB * (a + 1), 0:FS]
    out_ref[...] = out32[...].T.astype(BF)
    gpix_ref[...] = gp32[...].T
    eg = eg_ref[...].reshape(D + C, sz.wide)
    gw1_ref[...] = eg[0:D, :C].astype(F32)
    gw2_ref[...] = eg[D:, :D].astype(F32)

    def unpacked(value):
        n = value.shape[0] * 2 // 5
        tail = value[2 * n :]
        tail = jnp.concatenate([tail[:, 0:HF], tail[:, HF:]], axis=0)
        return jnp.concatenate([value[0:n], value[n : 2 * n], tail], axis=1)

    lg1 = [lg1_ref[h].reshape(sz.l1rows, LANES).astype(F32) for h in range(4)]
    lg2 = [lg2_ref[h].reshape(sz.l2rows, LANES).astype(F32) for h in range(4)]
    tail = jnp.concatenate([lg2[h][sz.wrows : sz.wrows + FS] for h in range(4)], axis=0)
    fifth = sum(lg1[h][0:D, HF:] for h in range(4))
    gwq_ref[...] = jnp.concatenate([lg1[h][0:D, 0:HF] for h in range(4)] + [fifth], axis=1)
    gwk_ref[...] = jnp.concatenate([lg1[h][D : 2 * D, 0:HF] for h in range(4)] + [tail[:, 0:HF]], axis=1)
    gwv_ref[...] = jnp.concatenate([lg1[h][D : 2 * D, HF:] for h in range(4)] + [tail[:, HF:]], axis=1)
    gwr_ref[...] = jnp.concatenate([unpacked(lg2[h][0 : sz.wrows]) for h in range(4)], axis=1)
    n = HF // 4
    for h in range(4):
        wo = unpacked(lg1[h][2 * D : 2 * D + 5 * sz.orows // 2])
        gwo_ref[HF * h : HF * (h + 1), :] = wo[0:HF]
        gwo_ref[4 * HF + n * h : 4 * HF + n * (h + 1), :] = wo[HF:]


def on_device_fused(*args):
    pixels_in, cotangent, pixel_mask, tile_slot = args[:4]
    w_fc1 = args[19]
    sz = Sizes(
        lax.axis_size("dp"), lax.axis_size("mp"), pixels_in.shape[0], cotangent.shape[1], w_fc1.shape[1]
    )
    D, C, PL, T, W, LN, HF = sz.width, sz.hidden, sz.plane, sz.all, sz.wide, LANES, HEAD_FEATURES
    Q, N, PB = sz.queries, sz.n_dp, sz.pb
    sm = pl.BlockSpec(memory_space=pltpu.SMEM)
    vm = pl.BlockSpec(memory_space=pltpu.VMEM)
    hbm = pl.BlockSpec(memory_space=pltpu.HBM)
    S = jax.ShapeDtypeStruct
    ins = [pixels_in.T, cotangent.T, *args[4:11], args[11].T, *args[12:]]
    mids = [
        S((T, LN), F32), S((4, PL, LN), BF), S((N, sz.echunk, W), BF), S((4, N, sz.l1rows // N, LN), BF),
        S((4, N, sz.l2rows // N, LN), BF), S((4, 16, W), F32), S((4, 8, W), F32),
    ]
    chunks = dict(e=(sz.echunk, W), l1=(sz.l1rows // N, LN), l2=(sz.l2rows // N, LN))
    shapes = {
        BF: dict(
            xt=(4, sz.share, sz.tokens), dfm=(T, D), dyh=(N, 48, W), dyh_g=(4, 48, W), xm_r=(T, D), n1_r=(T, D),
            xr_r=(PL, D), kva=(N, sz.kvrows, LN), qa_r=(LN, Q), qb_r=(LN, Q), ebuf=(N, PL, Q),
            e5buf=(N, sz.quarter, Q), og_a=(4, sz.edge, LN), og_b=(4, sz.inner, LN), n2_r=(T, D),
            hal=(N, 2 * PB, W), hal_g=(4, 2 * PB, W), dub=(4, PL, C), dn2_s=(3, PL, D), dn2_n=(2, PL, D),
            dn2_f=(PL, D), dos=(4, PL, LN), do_all=(4, PL, LN), dabg=(4, PL, W), ff_s=(3, sz.share, T), ff_n=(2, sz.share, T),
            ff_f=(sz.share, T), dk_x=(4, sz.kvrows, LN), dk_n=(4, sz.kvrows, LN), dk_o=(4, sz.kvrows, LN),
            dk_f=(4, sz.kvrows, LN), dkvg=(4, sz.kvrows, LN), dqs=(4, PL, LN), dq_all=(4, PL, LN),
            e_s=(D + C, W), gps=(4, PL, LN), wr_t=(4 * D, D), ogp=(T, LN),
            w2_t=(D, C), w_all=(D, 5 * LN), wq_cat=(D, 4 * LN), wo_cat=(4 * LN, D), l1_s=(sz.l1rows, LN),
            l2_s=(sz.l2rows, LN),
            **{n + "_" + k: (4, *v) for k in "nof" for n, v in chunks.items()},
        ),
        F32: dict(
            t0=(sz.tokens, LN), t1=(sz.tokens, LN), t2=(sz.tokens, D - 2 * LN), xhr_r=(PL, D), rsr_r=(PL, LN),
            sbuf=(N, PL, Q), lse_a=(4, 8, sz.edge_q), lse_b=(4, 8, sz.inner_q), row_r=(8, Q), ot_r=(LN, Q),
            h1_r=(T, D), ux=(4, sz.ext, C), ul=(2, sz.ext, C), ur=(2, sz.ext, C), dgx=(4, sz.ext, C),
            dzx=(4, sz.ext, C), dzl=(2, sz.ext, C), dzr=(2, sz.ext, C), g_r=(4, PL, C), du_r=(4, PL, C),
            dh1_r=(PL, D), dr_r=(4, 8, Q), dqt=(LN, Q), dqt5=(LN, Q), ve_s=(16, W), ve_n=(16, W),
            ve_p=(4, 16, W), vl_s=(8, W), vl_n=(8, W), vl_p=(4, 8, W),
        ),
    }
    scratch = {k: pltpu.VMEM(v, t) for t, group in shapes.items() for k, v in group.items()}
    for i in range(1, len(ins)):
        scratch["in%d" % i] = pltpu.VMEM(ins[i].shape, ins[i].dtype)
    scratch["ssem"] = pltpu.SemaphoreType.DMA((200,))
    scratch["rsem"] = pltpu.SemaphoreType.DMA((200,))
    for i, v in enumerate(mids):
        scratch["out%d" % i] = pltpu.VMEM(v.shape, v.dtype)
    scratch["osem"] = pltpu.SemaphoreType.DMA((len(mids),))
    scratch["isem"] = pltpu.SemaphoreType.DMA((len(ins),))
    mid = pl.pallas_call(
        functools.partial(fused_body, sz, tuple(scratch)),
        out_shape=mids,
        in_specs=[sm, sm] + [hbm] * len(ins),
        out_specs=[hbm] * len(mids),
        scratch_shapes=list(scratch.values()),
        compiler_params=pltpu.CompilerParams(
            collective_id=0, has_side_effects=True, vmem_limit_bytes=VMEM_MB * 2**20
        ),
        name="fused_block",
    )(pixel_mask, tile_slot.T, *ins)
    outs = [
        S((sz.share, sz.tokens), BF), S((sz.share, sz.tokens), F32), S((D,), F32), S((D,), F32), S((D, D), F32),
        S((D,), F32), S((D, D), F32), S((D, D), F32), S((D,), F32), S((D, 4 * D), F32), S((D,), F32), S((D,), F32),
        S((D,), F32), S((D, D), F32), S((D,), F32), S((D,), F32), S((D,), F32), S((D, C), F32), S((C,), F32),
        S((9, C), F32), S((C,), F32), S((C, D), F32), S((D,), F32),
    ]
    res = list(
        pl.pallas_call(
            functools.partial(unpack_body, sz),
            out_shape=outs,
            in_specs=[hbm] * len(mids),
            out_specs=[vm] * len(outs),
            scratch_shapes=[pltpu.VMEM(v.shape, v.dtype) for v in mids]
            + [pltpu.VMEM((sz.tokens, sz.share), F32)] * 2
            + [pltpu.SemaphoreType.DMA((len(mids),))],
            compiler_params=pltpu.CompilerParams(vmem_limit_bytes=60 * 2**20),
            name="unpack",
        )(*mid)
    )
    for k in (0, 1, 9):
        res[k] = res[k].T
    return tuple(res)


def choose(*args):
    tokens, width = args[1].shape
    whole_rows = tokens == FRAME * (FRAME // TILE_ROWS)
    shape = (lax.axis_size("dp"), lax.axis_size("mp"))
    if whole_rows and shape == (TILE_ROWS, 4) and TILE_ROWS == 8 and HEADS == 5 and width == 320 == args[19].shape[1]:
        return on_device_fused(*args)
    return on_device(*args)


def solution(mesh):
    return jax.shard_map(
        choose,
        mesh=mesh,
        in_specs=(
            P("dp", "mp"),
            P("dp", None),
            P("dp"),
            P(),
            P(),
            P(),
            P(),
            P(),
            P(),
            P(),
            P(),
            P(),
            P(),
            P(),
            P(),
            P(),
            P(),
            P(),
            P(),
            P(None, "mp"),
            P("mp"),
            P(None, "mp"),
            P("mp"),
            P("mp", None),
            P(),
        ),
        out_specs=(
            P("dp", "mp"),
            P("dp", "mp"),
            P(),
            P(),
            P(),
            P(),
            P(),
            P(),
            P(),
            P(),
            P(),
            P(),
            P(),
            P(),
            P(),
            P(),
            P(),
            P(None, "mp"),
            P("mp"),
            P(None, "mp"),
            P("mp"),
            P("mp", None),
            P(),
        ),
        check_vma=False,
    )
```

```python
import functools

import jax
import jax.numpy as jnp
from jax import lax
from jax.experimental import pallas as pl
from jax.experimental.pallas import tpu as pltpu
from jax.sharding import PartitionSpec as P

HEADS = 5
HEAD_FEATURES = 64
FRAME = 80
TILE_ROWS = 8


EPS = 1e-05
NEG = -1e30


def layer_norm(value, gain, shift):
    mean = jnp.mean(value, axis=-1, keepdims=True)
    centred = value - mean
    spread = jnp.mean(centred * centred, axis=-1, keepdims=True)
    return centred * lax.rsqrt(spread + EPS) * gain + shift


def depth_gelu(padded, kernel, shift):
    rows = padded.shape[0] - 2
    cols = padded.shape[1] - 2
    total = jnp.zeros((rows, cols, padded.shape[2]), jnp.float32) + shift
    for row_off in range(3):
        for col_off in range(3):
            total = (
                total
                + kernel[3 * row_off + col_off]
                * padded[row_off : row_off + rows, col_off : col_off + cols]
            )
    return jax.nn.gelu(total, approximate=False)


def mat(left, right):
    return jnp.dot(left, right, preferred_element_type=jnp.float32)


def pick(weights, table):
    return jnp.einsum(
        "j,jab->ab", weights.astype(table.dtype), table, preferred_element_type=jnp.float32
    )


def head_columns(weight_matrix, select_where):
    wide_layout = weight_matrix.astype(jnp.float32).reshape(
        weight_matrix.shape[0], HEADS, HEAD_FEATURES
    )
    return (
        jnp.einsum("uzx,nz->unx", wide_layout, select_where)
        .reshape(weight_matrix.shape[0], -1)
        .astype(jnp.bfloat16)
    )


def head_rows(weight_matrix, select_where):
    wide_layout = weight_matrix.astype(jnp.float32).reshape(
        HEADS, HEAD_FEATURES, weight_matrix.shape[1]
    )
    return (
        jnp.einsum("hed,sh->sed", wide_layout, select_where)
        .reshape(-1, weight_matrix.shape[1])
        .astype(jnp.bfloat16)
    )


def head_vector(vector_entries, select_where):
    return jnp.einsum(
        "he,sh->se", vector_entries.reshape(HEADS, HEAD_FEATURES), select_where
    ).reshape(-1)


def spread_columns(gradient_value, select_where):
    return jnp.einsum(
        "tvm,vq->tqm",
        gradient_value.reshape(gradient_value.shape[0], -1, HEAD_FEATURES),
        select_where,
    ).reshape(gradient_value.shape[0], -1)


def spread_rows(gradient_value, select_where):
    return jnp.einsum(
        "sed,sh->hed",
        gradient_value.reshape(-1, HEAD_FEATURES, gradient_value.shape[1]),
        select_where,
    ).reshape(-1, gradient_value.shape[1])


def spread_vector(gradient_value, select_where):
    return jnp.einsum("se,sh->he", gradient_value.reshape(-1, HEAD_FEATURES), select_where).reshape(
        -1
    )


def on_device(
    pixels_in,
    cotangent,
    pixel_mask,
    tile_slot,
    ln1_gain,
    ln1_bias,
    w_query,
    b_query,
    w_key,
    w_value,
    b_value,
    w_reduce,
    b_reduce,
    lnr_gain,
    lnr_bias,
    w_out,
    b_out,
    ln2_gain,
    ln2_bias,
    w_fc1,
    b_fc1,
    w_depth,
    b_depth,
    w_fc2,
    b_fc2,
):
    n_dp = lax.axis_size("dp")
    n_mp = lax.axis_size("mp")
    device = lax.axis_index("dp")
    part = lax.axis_index("mp")
    rows = FRAME // TILE_ROWS
    tokens = pixels_in.shape[0]
    cols = tokens // rows
    tiles_col = FRAME // cols
    per_frame = TILE_ROWS * tiles_col
    width = ln1_gain.shape[0]
    share = width // n_mp
    slots = -(-HEADS // n_mp)
    scale = HEAD_FEATURES ** (-0.5)
    maskf = pixel_mask.astype(jnp.float32)[:, None]
    head_ids = part + n_mp * jnp.arange(slots)
    select_where = (head_ids[:, None] == jnp.arange(HEADS)[None, :]).astype(jnp.float32)
    crops = tile_slot[:, 0]
    tiles = tile_slot[:, 1]
    is_me = jnp.arange(n_dp) == device
    own_crop = jnp.sum(jnp.where(is_me, crops, 0))
    own_tile = jnp.sum(jnp.where(is_me, tiles, 0))
    own_row = own_tile // tiles_col
    own_col = own_tile % tiles_col
    tile_row = tiles // tiles_col
    tile_col = tiles % tiles_col

    def beside(drow, dcol):
        hit = (crops == own_crop) & (tile_row == own_row + drow) & (tile_col == own_col + dcol)
        return hit.astype(jnp.float32)

    member = (crops[None, :] == own_crop) & (tiles[None, :] == jnp.arange(per_frame)[:, None])
    crop_devices = jnp.sum(jnp.where(member, jnp.arange(n_dp)[None, :], 0), axis=1)
    whole = lax.all_gather(pixels_in, "mp", axis=1, tiled=True)
    xm = whole.astype(jnp.float32) * maskf
    n1, first_norm_backward = jax.vjp(layer_norm, xm, ln1_gain, ln1_bias)
    n1b = n1.astype(jnp.bfloat16)
    wq = head_columns(w_query, select_where)
    wk = head_columns(w_key, select_where)
    wv = head_columns(w_value, select_where)
    wo = head_rows(w_out, select_where)
    qb = (mat(n1b, wq) + head_vector(b_query, select_where)).astype(jnp.bfloat16)
    patches = (
        n1b.reshape(rows // 2, 2, cols // 2, 2, width)
        .transpose(0, 2, 1, 3, 4)
        .reshape(-1, 4 * width)
    )
    reduced = mat(patches, w_reduce) + b_reduce
    xr, lnr_back = jax.vjp(layer_norm, reduced, lnr_gain, lnr_bias)
    xrb = xr.astype(jnp.bfloat16)
    kb = mat(xrb, wk).astype(jnp.bfloat16)
    vb = (mat(xrb, wv) + head_vector(b_value, select_where)).astype(jnp.bfloat16)
    kmask = (
        pixel_mask.reshape(rows // 2, 2, cols // 2, 2)[:, 0, :, 0].reshape(-1).astype(jnp.bfloat16)
    )
    keys_all, values_all, kmask_all = (
        lax.all_gather(kb, "dp", axis=0, tiled=True),
        lax.all_gather(vb, "dp", axis=0, tiled=True),
        lax.all_gather(kmask, "dp", axis=0, tiled=True),
    )
    per_key = kb.shape[0]
    keys_crop = keys_all.reshape(n_dp, per_key, -1)[crop_devices]
    values_crop = values_all.reshape(n_dp, per_key, -1)[crop_devices]
    usable_crop = kmask_all.reshape(n_dp, per_key)[crop_devices].astype(jnp.float32) > 0.5
    n_blocks = 4
    key_blocks = keys_crop.reshape(n_blocks, -1, slots, HEAD_FEATURES)
    value_blocks = values_crop.reshape(n_blocks, -1, slots, HEAD_FEATURES)
    usable_blocks = usable_crop.reshape(n_blocks, -1)
    queries = qb.reshape(tokens, slots, HEAD_FEATURES)

    def block_scores(key_block, usable_block):
        raw = (
            jnp.einsum("qsd,ksd->sqk", queries, key_block, preferred_element_type=jnp.float32)
            * scale
        )
        return jnp.where(usable_block[None, None, :], raw, NEG)

    def top_step(carry, blocks):
        top, total = carry
        key_block, usable_block = blocks
        scores = block_scores(key_block, usable_block)
        new_top = jnp.maximum(top, jnp.max(scores, axis=-1))
        total = total * jnp.exp(top - new_top) + jnp.sum(
            jnp.exp(scores - new_top[..., None]), axis=-1
        )
        return ((new_top, total), None)

    start = (jnp.full((slots, tokens), NEG, jnp.float32), jnp.zeros((slots, tokens), jnp.float32))
    (top, total), _ = lax.scan(top_step, start, (key_blocks, usable_blocks))
    lse = top + jnp.log(total)

    def out_step(acc, blocks):
        key_block, value_block, usable_block = blocks
        prob = jnp.exp(block_scores(key_block, usable_block) - lse[..., None])
        acc = acc + jnp.einsum(
            "sqk,ksd->qsd",
            prob.astype(jnp.bfloat16),
            value_block,
            preferred_element_type=jnp.float32,
        )
        return (acc, None)

    empty = jnp.zeros((tokens, slots, HEAD_FEATURES), jnp.float32)
    acc, _ = lax.scan(out_step, empty, (key_blocks, value_blocks, usable_blocks))
    ob = acc.reshape(tokens, -1).astype(jnp.bfloat16)
    branch = lax.psum(mat(ob, wo).astype(jnp.bfloat16), "mp").astype(jnp.float32) + b_out
    h1 = xm + branch * maskf
    n2, ln2_back = jax.vjp(layer_norm, h1, ln2_gain, ln2_bias)
    n2b = n2.astype(jnp.bfloat16)
    ub = ((mat(n2b, w_fc1) + b_fc1) * maskf).astype(jnp.bfloat16)
    channels = ub.shape[1]
    tile_u = ub.reshape(rows, cols, channels)
    lines, sides = (
        lax.all_gather(jnp.stack([tile_u[0], tile_u[-1]]), "dp", axis=0, tiled=True),
        lax.all_gather(jnp.stack([tile_u[:, 0], tile_u[:, -1]]), "dp", axis=0, tiled=True),
    )
    lines = lines.reshape(n_dp, 2, cols, channels)
    sides = sides.reshape(n_dp, 2, rows, channels)
    top_lines = lines[:, 0]
    bottom_lines = lines[:, 1]
    left_sides = sides[:, 0]
    right_sides = sides[:, 1]
    upper = jnp.concatenate(
        [
            pick(beside(-1, -1), bottom_lines[:, -1:]),
            pick(beside(-1, 0), bottom_lines),
            pick(beside(-1, 1), bottom_lines[:, :1]),
        ],
        axis=0,
    )
    lower = jnp.concatenate(
        [
            pick(beside(1, -1), top_lines[:, -1:]),
            pick(beside(1, 0), top_lines),
            pick(beside(1, 1), top_lines[:, :1]),
        ],
        axis=0,
    )
    middle = jnp.concatenate(
        [
            pick(beside(0, -1), right_sides)[:, None],
            tile_u.astype(jnp.float32),
            pick(beside(0, 1), left_sides)[:, None],
        ],
        axis=1,
    )
    padded = jnp.concatenate([upper[None], middle, lower[None]], axis=0)
    act, depth_back = jax.vjp(depth_gelu, padded, w_depth, b_depth)
    gb = act.reshape(tokens, channels).astype(jnp.bfloat16)
    ffn_mine = lax.psum_scatter(
        mat(gb, w_fc2).astype(jnp.bfloat16), "mp", scatter_dimension=1, tiled=True
    ).astype(jnp.float32)
    h1_mine = lax.dynamic_slice_in_dim(h1, part * share, share, 1)
    bias_mine = lax.dynamic_slice_in_dim(b_fc2, part * share, share, 0)
    block_result = (h1_mine + (ffn_mine + bias_mine) * maskf).astype(jnp.bfloat16)
    dy = cotangent.astype(jnp.float32)
    dff = dy * maskf
    grad_b_fc2 = jnp.sum(dff, axis=0)
    dfb = dff.astype(jnp.bfloat16)
    grad_w_fc2 = mat(gb.T, dfb)
    dgr = mat(dfb, w_fc2.T).astype(jnp.bfloat16).astype(jnp.float32).reshape(rows, cols, channels)
    dpad, grad_w_depth, grad_b_depth = depth_back(dgr)
    grad_lines, grad_sides = (
        lax.all_gather(
            jnp.stack([dpad[0], dpad[-1]]).astype(jnp.bfloat16), "dp", axis=0, tiled=True
        ).astype(jnp.float32),
        lax.all_gather(
            jnp.stack([dpad[1:-1, 0], dpad[1:-1, -1]]).astype(jnp.bfloat16),
            "dp",
            axis=0,
            tiled=True,
        ).astype(jnp.float32),
    )
    grad_lines = grad_lines.reshape(n_dp, 2, cols + 2, channels)
    grad_sides = grad_sides.reshape(n_dp, 2, rows, channels)
    top_grads = grad_lines[:, 0]
    bottom_grads = grad_lines[:, 1]
    dtile = dpad[1:-1, 1:-1]
    dtile = dtile.at[0].add(pick(beside(-1, 0), bottom_grads[:, 1:-1]))
    dtile = dtile.at[0, 0].add(pick(beside(-1, -1), bottom_grads[:, -1:])[0])
    dtile = dtile.at[0, -1].add(pick(beside(-1, 1), bottom_grads[:, :1])[0])
    dtile = dtile.at[-1].add(pick(beside(1, 0), top_grads[:, 1:-1]))
    dtile = dtile.at[-1, 0].add(pick(beside(1, -1), top_grads[:, -1:])[0])
    dtile = dtile.at[-1, -1].add(pick(beside(1, 1), top_grads[:, :1])[0])
    dtile = dtile.at[:, 0].add(pick(beside(0, -1), grad_sides[:, 1]))
    dtile = dtile.at[:, -1].add(pick(beside(0, 1), grad_sides[:, 0]))
    dub = (dtile.reshape(tokens, channels).astype(jnp.bfloat16).astype(jnp.float32) * maskf).astype(
        jnp.bfloat16
    )
    grad_b_fc1 = jnp.sum(dub.astype(jnp.float32), axis=0)
    grad_w_fc1 = mat(n2b.T, dub)
    dn2_part = mat(dub, w_fc1.T)
    zero_vector = jnp.zeros((width,), jnp.float32)
    dn2 = lax.psum(dn2_part.astype(jnp.bfloat16), "mp").astype(jnp.float32)
    dh1_norm, shared_gain, shared_bias = ln2_back(dn2)
    dh1 = dy + dh1_norm
    split_gain = zero_vector
    split_bias = zero_vector
    dattn = dh1 * maskf
    grad_b_out = jnp.sum(dattn, axis=0)
    dab = dattn.astype(jnp.bfloat16)
    grad_wo = mat(ob.T, dab)
    dob = mat(dab, wo.T).astype(jnp.bfloat16)
    dout = dob.reshape(tokens, slots, HEAD_FEATURES)
    drow = jnp.sum(dout.astype(jnp.float32) * acc, axis=-1).T

    def back_step(dq_acc, blocks):
        key_block, value_block, usable_block = blocks
        prob = jnp.exp(block_scores(key_block, usable_block) - lse[..., None])
        dv_block = jnp.einsum(
            "sqk,qsd->ksd", prob.astype(jnp.bfloat16), dout, preferred_element_type=jnp.float32
        )
        dprob = jnp.einsum("qsd,ksd->sqk", dout, value_block, preferred_element_type=jnp.float32)
        dscore = (prob * (dprob - drow[..., None])).astype(jnp.bfloat16)
        dq_acc = dq_acc + jnp.einsum(
            "sqk,ksd->qsd", dscore, key_block, preferred_element_type=jnp.float32
        )
        dk_block = (
            jnp.einsum("sqk,qsd->ksd", dscore, queries, preferred_element_type=jnp.float32) * scale
        )
        return (dq_acc, (dk_block, dv_block))

    dq_acc, (dk_blocks, dv_blocks) = lax.scan(
        back_step, empty, (key_blocks, value_blocks, usable_blocks)
    )
    zero_keys = jnp.zeros((n_dp, per_key, slots * HEAD_FEATURES), jnp.float32)
    dk_full = (
        zero_keys.at[crop_devices]
        .set(dk_blocks.reshape(per_frame, per_key, -1))
        .reshape(n_dp * per_key, -1)
    )
    dv_full = (
        zero_keys.at[crop_devices]
        .set(dv_blocks.reshape(per_frame, per_key, -1))
        .reshape(n_dp * per_key, -1)
    )
    dk_mine, dv_mine = (
        lax.psum_scatter(dk_full, "dp", scatter_dimension=0, tiled=True),
        lax.psum_scatter(dv_full, "dp", scatter_dimension=0, tiled=True),
    )
    dkb = dk_mine.astype(jnp.bfloat16)
    dvb = dv_mine.astype(jnp.bfloat16)
    dqb = (dq_acc * scale).reshape(tokens, -1).astype(jnp.bfloat16)
    grad_wq = mat(n1b.T, dqb)
    grad_bq = jnp.sum(dqb.astype(jnp.float32), axis=0)
    grad_wk = mat(xrb.T, dkb)
    grad_wv = mat(xrb.T, dvb)
    grad_bv = jnp.sum(dvb.astype(jnp.float32), axis=0)
    dxr, dn1_query = (
        lax.psum((mat(dkb, wk.T) + mat(dvb, wv.T)).astype(jnp.bfloat16), "mp").astype(jnp.float32),
        lax.psum(mat(dqb, wq.T).astype(jnp.bfloat16), "mp").astype(jnp.float32),
    )
    dreduced, grad_lnr_gain, grad_lnr_bias = lnr_back(dxr)
    drb = dreduced.astype(jnp.bfloat16)
    grad_w_reduce = mat(patches.T, drb)
    grad_b_reduce = jnp.sum(drb.astype(jnp.float32), axis=0)
    dpatch = (
        mat(drb, w_reduce.T)
        .reshape(rows // 2, cols // 2, 2, 2, width)
        .transpose(0, 2, 1, 3, 4)
        .reshape(tokens, width)
    )
    dxm, grad_ln1_gain, grad_ln1_bias = first_norm_backward(dn1_query + dpatch)
    grad_whole = (dxm + dh1) * maskf
    grad_input = lax.dynamic_slice_in_dim(grad_whole, part * share, share, 1)
    (
        grad_w_reduce,
        grad_b_reduce,
        grad_lnr_gain,
        grad_lnr_bias,
        grad_ln1_gain,
        grad_ln1_bias,
        shared_gain,
        shared_bias,
        grad_b_out,
        grad_b_fc2,
        grad_w_fc1,
        grad_b_fc1,
        grad_w_depth,
        grad_b_depth,
        grad_w_fc2,
    ) = lax.psum(
        (
            grad_w_reduce,
            grad_b_reduce,
            grad_lnr_gain,
            grad_lnr_bias,
            grad_ln1_gain,
            grad_ln1_bias,
            shared_gain,
            shared_bias,
            grad_b_out,
            grad_b_fc2,
            grad_w_fc1,
            grad_b_fc1,
            grad_w_depth,
            grad_b_depth,
            grad_w_fc2,
        ),
        "dp",
    )
    (
        grad_w_query,
        grad_b_query,
        grad_w_key,
        grad_w_value,
        grad_b_value,
        output_weight_gradient,
        split_gain,
        split_bias,
    ) = lax.psum(
        (
            spread_columns(grad_wq, select_where),
            spread_vector(grad_bq, select_where),
            spread_columns(grad_wk, select_where),
            spread_columns(grad_wv, select_where),
            spread_vector(grad_bv, select_where),
            spread_rows(grad_wo, select_where),
            split_gain,
            split_bias,
        ),
        ("dp", "mp"),
    )
    grad_ln2_gain = shared_gain + split_gain
    grad_ln2_bias = shared_bias + split_bias
    return (
        block_result,
        grad_input,
        grad_ln1_gain,
        grad_ln1_bias,
        grad_w_query,
        grad_b_query,
        grad_w_key,
        grad_w_value,
        grad_b_value,
        grad_w_reduce,
        grad_b_reduce,
        grad_lnr_gain,
        grad_lnr_bias,
        output_weight_gradient,
        grad_b_out,
        grad_ln2_gain,
        grad_ln2_bias,
        grad_w_fc1,
        grad_b_fc1,
        grad_w_depth,
        grad_b_depth,
        grad_w_fc2,
        grad_b_fc2,
    )


BF = jnp.bfloat16
F32 = jnp.float32
LANES = 128
SIDE_SMALL = 64
VMEM_MB = 56


def nn(a, b):
    return lax.dot_general(a, b, (((1,), (0,)), ((), ())), preferred_element_type=F32)


def nt(a, b):
    return lax.dot_general(a, b, (((1,), (1,)), ((), ())), preferred_element_type=F32)


def tn(a, b):
    return lax.dot_general(a, b, (((0,), (0,)), ((), ())), preferred_element_type=F32)


def iota(shape, axis):
    return lax.broadcasted_iota(jnp.int32, shape, axis)


def hot(cond):
    return jnp.where(cond, 1.0, 0.0).astype(BF)


def spread(value):
    mean = jnp.sum(value, axis=-1, keepdims=True) * (1.0 / value.shape[-1])
    centred = value - mean
    var = jnp.sum(centred * centred, axis=-1, keepdims=True) * (1.0 / value.shape[-1])
    rstd = lax.rsqrt(var + EPS)
    return centred * rstd, rstd


def norm_back(dn, gain, xhat, rstd):
    e = dn * gain
    scale = 1.0 / dn.shape[-1]
    mean_e = jnp.sum(e, axis=-1, keepdims=True) * scale
    mean_ex = jnp.sum(e * xhat, axis=-1, keepdims=True) * scale
    return rstd * (e - mean_e - xhat * mean_ex)


def rowsum(value):
    return jnp.sum(value, axis=0, keepdims=True)


class Sizes:
    def __init__(self, n_dp, n_mp, tokens, width, hidden):
        self.n_dp, self.n_mp = n_dp, n_mp
        self.tokens, self.width, self.hidden = tokens, width, hidden
        self.share = width // n_mp
        self.rows = FRAME // TILE_ROWS
        self.cols = tokens // self.rows
        self.pa, self.pb = self.rows // 2, self.cols // 2
        self.keys = self.pa * self.pb
        self.plane = -(-self.keys // 16) * 16
        self.all = 4 * self.plane
        self.step = self.plane // 16 // n_mp * 16
        self.quarter = self.plane - (n_mp - 1) * self.step
        self.wide = -(-width // LANES) * LANES
        self.kvrows = self.plane + self.quarter
        self.top = 8 + self.pb
        self.ext = self.top + self.keys + self.pb
        self.edge = 4 * 2 * self.pb
        self.edge_q = -(-self.edge // LANES) * LANES
        self.queries = -(-4 * self.keys // LANES) * LANES
        self.echunk = (width + hidden) // n_dp
        self.half = width - 2 * LANES
        self.wrows = 2 * width + width // 2
        self.l2rows = -(-(self.wrows + self.share) // (16 * n_dp)) * 16 * n_dp
        self.orows = HEAD_FEATURES + HEAD_FEATURES // n_mp
        self.l1rows = -(-(2 * width + 2 * self.orows + self.orows // 2) // (16 * n_dp)) * 16 * n_dp


class Load:
    def __init__(self, src, dst, sem):
        self.dst, self.shape, self.waiting = dst, dst.shape, True
        self.copy = pltpu.make_async_copy(src, dst, sem)
        self.copy.start()

    def ready(self):
        if self.waiting:
            self.waiting = False
            self.copy.wait()
        return self.dst

    def __getitem__(self, at):
        return self.ready()[at]


def fused_body(
    sz, names,
    mask_ref, slot_ref, *refs,
):
    ins, refs = refs[:23], refs[23:]
    outs, refs = refs[:7], refs[7:]
    s = dict(zip(names, refs))
    blk_ref, gp_ref, eg_ref, lg1_ref, lg2_ref, veg_ref, vlg_ref = (s["out%d" % i] for i in range(7))
    stores = []

    def store(i):
        c = pltpu.make_async_copy(s["out%d" % i], outs[i], s["osem"].at[i])
        c.start()
        stores.append(c)

    D, HF, PB, PA, KEYS, PL, T = sz.width, HEAD_FEATURES, sz.pb, sz.pa, sz.keys, sz.plane, sz.all
    C, FS, W = sz.hidden, sz.share, sz.wide
    d = lax.axis_index("dp")
    m = lax.axis_index("mp")
    last = sz.n_mp * HF
    ssem, rsem = s["ssem"], s["rsem"]

    def mpx(k):
        if k == 0:
            return m
        if k == 1:
            return m + 1 - 2 * lax.rem(m, 2)
        if k == 2:
            return lax.rem(m + 2, 4)
        return 3 - m

    def dpx(k):
        z, x = d // 2, lax.rem(d, 2)
        if k & 1:
            x = 1 - x
        kz = k >> 1
        if kz == 1:
            z = z + 1 - 2 * lax.rem(z, 2)
        elif kz == 2:
            z = lax.rem(z + 2, 4)
        elif kz == 3:
            z = 3 - z
        return 2 * z + x

    counter = [0]
    pending = []

    def take(n):
        first = counter[0]
        counter[0] += n
        return first

    def copy(src, dst, sem, dev):
        return pltpu.make_async_remote_copy(
            src_ref=src, dst_ref=dst, send_sem=ssem.at[sem], recv_sem=rsem.at[sem],
            device_id=dev, device_id_type=pl.DeviceIdType.MESH,
        )

    def send(src, dst, sem, dev):
        c = copy(src, dst, sem, dev)
        c.start()
        pending.append(c)

    def arrived(ref, sem):
        copy(ref, ref, sem, (d, m)).wait_recv()

    opened = []

    def handle(finish):
        state = [False]

        def once(*a):
            if not state[0]:
                state[0] = True
                return finish(*a)

        opened.append(once)
        return once

    def mp_start(buf):
        base = take(3)
        send(buf.at[m], buf.at[m], base, (d, mpx(1)))
        send(buf.at[m], buf.at[m], base + 1, (d, mpx(2)))

        def middle():
            arrived(buf.at[mpx(2)], base + 1)
            send(buf.at[mpx(2)], buf.at[mpx(2)], base + 2, (d, mpx(1)))

        mid = handle(middle)

        def finish():
            mid()
            arrived(buf.at[mpx(1)], base)
            arrived(buf.at[mpx(3)], base + 2)

        return handle(finish), mid

    def dp_start(buf, each=lambda k: None):
        base = take(7)
        for kz in (3, 2, 1):
            send(buf.at[d], buf.at[d], base + kz, (dpx(2 * kz), m))
        send(buf.at[d], buf.at[d], base, (dpx(1), m))

        def along(kz):
            arrived(buf.at[dpx(2 * kz)], base + kz)
            send(buf.at[dpx(2 * kz)], buf.at[dpx(2 * kz)], base + 3 + kz, (dpx(1), m))
            each(2 * kz)

        def across(kz):
            arrived(buf.at[dpx(2 * kz + 1)], base + 3 + kz if kz else base)
            each(2 * kz + 1)

        steps = [handle(lambda kz=kz: along(kz)) for kz in (1, 2, 3)]
        steps += [handle(lambda kz=kz: across(kz)) for kz in range(4)]

        def mid():
            for step in steps[:4]:
                step()

        def finish():
            for step in steps:
                step()

        return handle(finish), mid, steps

    def dp_pick(buf, chosen, out, came):
        base = take(4)
        z = d // 2
        for kz in (3, 2, 1):
            send(buf.at[z], buf.at[z], base + kz, (dpx(2 * kz), m))

        def middle():
            for kz in (1, 2, 3):
                arrived(buf.at[dpx(2 * kz) // 2], base + kz)
            out[...] = chosen(*beside(dpx(1)))
            send(out, came, base, (dpx(1), m))

        mid = handle(middle)

        def finish():
            mid()
            arrived(came, base)

        return handle(finish), mid

    def mp_scatter(block, dst, landed):
        base = take(4)
        for k in (2, 3, 1):
            send(block(mpx(k)), dst(k), base + k, (d, mpx(k)))

        def finish():
            for k in (1, 2, 3):
                arrived(landed(k), base + k)

        return handle(finish)

    def dp_scatter(block, dst, landed):
        base = take(8)
        for k in (6, 7, 4, 5, 2, 3, 1):
            send(block(dpx(k)), dst(k), base + k, (dpx(k), m))

        def finish():
            for k in range(1, sz.n_dp):
                arrived(landed(k), base + k)

        return handle(finish)

    def mp_sum(block, out, near, far):
        base = take(3)
        out[0] = block(mpx(1)).astype(BF)
        send(out.at[0], near.at[0], base, (d, mpx(1)))
        out[1] = block(mpx(3)).astype(BF)
        send(out.at[1], near.at[1], base + 1, (d, mpx(1)))

        def middle():
            value = block(mpx(2))
            arrived(near.at[1], base + 1)
            out[2] = (value + near[1].astype(F32)).astype(BF)
            send(out.at[2], far, base + 2, (d, mpx(2)))

        mid = handle(middle)

        def finish():
            mid()
            value = block(m)
            arrived(near.at[0], base)
            value = value + near[0].astype(F32)
            arrived(far, base + 2)
            return value + far[...].astype(F32)

        return mid, handle(finish)

    def dp_sum(chunk, near, out, far):
        base = take(8)
        for kz in (2, 3, 1, 0):
            send(chunk(dpx(2 * kz + 1)), near.at[kz], base + kz, (dpx(1), m))

        def middle():
            for kz in (2, 3, 1):
                value = chunk(dpx(2 * kz))[...].astype(F32)
                arrived(near.at[kz], base + kz)
                out[kz] = (value + near[kz].astype(F32)).astype(BF)
                send(out.at[kz], far.at[kz], base + 4 + kz, (dpx(2 * kz), m))

        mid = handle(middle)

        def finish():
            mid()
            value = chunk(d)[...].astype(F32)
            arrived(near.at[0], base)
            value = value + near[0].astype(F32)
            for kz in (1, 2, 3):
                arrived(far.at[kz], base + 4 + kz)
                value = value + far[kz].astype(F32)
            return value

        return mid, handle(finish)

    def dp_total(src, near, parts):
        base = take(4)
        z = d // 2
        send(src, near, base, (dpx(1), m))

        def middle():
            arrived(near, base)
            parts[z] = src[...] + near[...]
            for kz in (2, 3, 1):
                send(parts.at[z], parts.at[z], base + kz, (dpx(2 * kz), m))

        mid = handle(middle)

        def finish():
            mid()
            for kz in (1, 2, 3):
                arrived(parts.at[dpx(2 * kz) // 2], base + kz)
            return (parts[0] + parts[1]) + (parts[2] + parts[3])

        return mid, handle(finish)

    peers = [(d, mpx(k)) for k in (1, 2, 3)] + [(dpx(k), m) for k in range(1, 8)]
    bar = pltpu.get_barrier_semaphore()
    for dev in peers:
        pl.semaphore_signal(bar, inc=1, device_id=dev, device_id_type=pl.DeviceIdType.MESH)

    order = (0, 1, 2, 3, 8, 7, 9, 10, 11, 12, 4, 5, 6, 21, 22, 13, 14, 15, 16, 17, 18, 19, 20)
    loads = [None] * 23
    for i in order:
        dst = s["xt"].at[m] if i == 0 else s["in%d" % i]
        loads[i] = Load(ins[i], dst, s["isem"].at[i])
    (
        pix_ref, cot_ref, ln1g_ref, ln1b_ref, wq_ref, bq_ref, wk_ref, wv_ref, bv_ref, wr_ref, br_ref,
        lnrg_ref, lnrb_ref, wo_ref, bo_ref, ln2g_ref, ln2b_ref, w1_ref, b1_ref, wd_ref, bd_ref, w2_ref, b2_ref,
    ) = loads

    side = jnp.where(mask_ref[sz.cols - 1] > 0, FRAME, SIDE_SMALL)
    tile = slot_ref[1, d]
    tiles = [slot_ref[1, k] for k in range(sz.n_dp)]

    def beside(at):
        t = slot_ref[1, at]
        up = sum(jnp.where(tiles[k] == t - 1, k, 0) for k in range(sz.n_dp))
        down = sum(jnp.where(tiles[k] == t + 1, k, 0) for k in range(sz.n_dp))
        return up, down

    above, below = beside(d)

    def same_x(j):
        return lax.rem(j, 2) == lax.rem(d, 2)

    def place(p, count):
        a = sum(jnp.where(p >= PB * k, 1, 0) for k in range(1, count))
        return a, p - PB * a

    def token_mask(i, j):
        p = iota((PL, 1), 0)
        a, b = place(p, PA)
        inside = (p < KEYS) & (sz.rows * tile + 2 * a + i < side) & (2 * b + j < side)
        return jnp.where(inside, 1.0, 0.0)

    def row_mask(i, j, a):
        b = iota((PB, 1), 0)
        row = sz.rows * tile + 2 * a + i
        inside = (row >= 0) & (row < side) & (2 * b + j < side)
        return jnp.where(inside, 1.0, 0.0)

    def key_bias(p, tile_at):
        a, b = place(p, PA)
        usable = (p < KEYS) & (sz.rows * tile_at + 2 * a < side) & (2 * b < side)
        return jnp.where(usable, 0.0, NEG)

    def vec(ref):
        return ref[...].reshape(1, ref.shape[0])

    def own_part(row, size):
        return sum(
            jnp.where(m == h, 1.0, 0.0) * row[:, size * h : size * (h + 1)] for h in range(sz.n_mp)
        )

    def plane_rows(ref, start):
        return ref[pl.ds(pl.multiple_of(start, 16), PL), :]

    def plane(p):
        return slice(PL * p, PL * (p + 1))

    lanes3 = (s["t0"], s["t1"], s["t2"])

    def to_planes(rows_of):
        for n, ref in enumerate(lanes3):
            ref[...] = rows_of(LANES * n, min(D, LANES * (n + 1))).astype(F32).T
        for i in range(2):
            for j in range(2):
                parts = []
                for ref in lanes3:
                    rows = [
                        ref[pl.ds((2 * a + i) * sz.cols + j, PB, stride=2), :] for a in range(PA)
                    ] + [jnp.zeros((PL - KEYS, ref.shape[1]), F32)]
                    parts.append(jnp.concatenate(rows, axis=0))
                yield i, j, jnp.concatenate(parts, axis=1)

    def from_queries(rows, p):
        n = rows.shape[1]
        return jnp.concatenate([rows[KEYS * p : KEYS * (p + 1)], jnp.zeros((PL - KEYS, n), F32)], axis=0)

    def to_queries(planes):
        n = planes[0].shape[1]
        rows = [v[0:KEYS] for v in planes]
        return jnp.concatenate(rows + [jnp.zeros((sz.queries - 4 * KEYS, n), F32)], axis=0)

    xt, dfm = s["xt"], s["dfm"]
    pl.semaphore_wait(bar, len(peers))
    pix_ref.ready()
    x_at, x_mid = mp_start(xt)

    edge, edge_g, EP = s["edge"], s["edge_g"], 4 * PB
    lane_pad = jnp.zeros((FS, sz.edge_q - 2 * EP), BF)
    edge[d // 2] = jnp.concatenate([xt[m, :, 0:EP], xt[m, :, sz.tokens - EP :], lane_pad], axis=1)

    def edge_chosen(up, down):
        return jnp.concatenate([edge[up // 2][:, EP : 2 * EP], edge[down // 2][:, 0:EP], lane_pad], axis=1)

    edge_at, edge_mid = dp_pick(edge, edge_chosen, s["edge_s"], s["edge_x"])

    for i, j, value in to_planes(lambda lo, hi: cot_ref[lo:hi, :]):
        dfm[plane(2 * i + j), :] = (value * token_mask(i, j)).astype(BF)
    dyh, dyh_g = s["dyh"], s["dyh_g"]
    dyh[d // 2, :, :D] = dfm[pl.ds(pl.multiple_of(PL * m + (KEYS - PB) * (m // 2), 16), 48), :]
    dyh[d // 2, :, D:] = jnp.zeros((48, W - D), BF)
    x_mid()

    r2, c2 = iota((D, LANES), 0), iota((D, LANES), 1)
    own_lo = hot((c2 < HF) & (r2 == HF * m + c2))
    own_hi = hot((c2 >= HF) & (r2 == HF * m + c2 - HF))
    last_lo = hot((c2 < HF) & (r2 == last + c2))
    last_hi = hot((c2 >= HF) & (r2 == last + c2 - HF))
    wq, wk, wv = wq_ref[...], wk_ref[...], wv_ref[...]
    wq2 = nn(wq, own_lo + last_hi).astype(BF)
    wkv = (nn(wk, own_lo) + nn(wv, own_hi)).astype(BF)
    wkv5 = (nn(wk, last_lo) + nn(wv, last_hi)).astype(BF)
    bq, bv = vec(bq_ref), vec(bv_ref)
    bq2 = jnp.concatenate([own_part(bq, HF), bq[:, last:]], axis=1)
    nil = jnp.zeros((1, HF), F32)
    bkv = jnp.concatenate([nil, own_part(bv, HF)], axis=1)
    bkv5 = jnp.concatenate([nil, bv[:, last:]], axis=1)
    w2 = w2_ref[...]
    wr_t = s["wr_t"]
    wr_t[...] = wr_ref[...].T

    xm_r, n1_r = s["xm_r"], s["n1_r"]
    x_at()
    x_all = xt[...].reshape(D, sz.tokens)
    for i, j, value in to_planes(lambda lo, hi: x_all[lo:hi, :]):
        xm = value * token_mask(i, j)
        xm_r[plane(2 * i + j), :] = xm.astype(BF)
        xhat, _ = spread(xm)
        n1_r[plane(2 * i + j), :] = (xhat * vec(ln1g_ref) + vec(ln1b_ref)).astype(BF)

    kva, xr_r = s["kva"], s["xr_r"]
    red = sum(nn(n1_r[plane(p), :], wr_t[D * p : D * (p + 1), :]) for p in range(4)) + vec(br_ref)
    xhr, rsr = spread(red)
    s["xhr_r"][...] = xhr
    s["rsr_r"][...] = jnp.broadcast_to(rsr, (PL, LANES))
    xr_r[...] = (xhr * vec(lnrg_ref) + vec(lnrb_ref)).astype(BF)
    kva[d, 0:PL, :] = (nn(xr_r[...], wkv) + bkv).astype(BF)
    quarter_rows = pl.ds(pl.multiple_of(sz.step * m, 16), sz.quarter)
    kva[d, PL:, :] = (nn(xr_r[quarter_rows, :], wkv5) + bkv5).astype(BF)
    _, _, kv_steps = dp_start(kva)

    def dy_chosen(up, down):
        return dyh[jnp.where(m >= 2, up, down) // 2]

    dy_at, dy_mid = dp_pick(dyh, dy_chosen, s["dyh_s"], s["dyh_x"])

    qa_r, qb_r, qc_r, qd_r = s["qa_r"], s["qb_r"], s["qc_r"], s["qd_r"]
    Q = sz.queries

    def feature_major(q_rows, own_r, last_r):
        q2t = q_rows.T
        nil = jnp.zeros((HF, q2t.shape[1]), F32)
        own_r[...] = jnp.concatenate([q2t[0:HF], nil], axis=0).astype(BF)
        last_r[...] = jnp.concatenate([q2t[HF:], nil], axis=0).astype(BF)

    def query(rows):
        return (nn(rows, wq2) + bq2).astype(BF).astype(F32) * HF ** (-0.5)

    q2 = query(n1_r[...])
    feature_major(to_queries([q2[plane(p)] for p in range(4)]), qa_r, qb_r)
    half = jnp.zeros((HF, Q), F32)

    e5buf, ebuf, ot_r = s["e5buf"], s["ebuf"], s["ot_r"]
    limit5 = jnp.where(m == sz.n_mp - 1, KEYS - sz.step * m, sz.step)
    pk, pk5 = iota((PL, 1), 0), iota((sz.quarter, 1), 0)

    def attend(kv, q_r, bias, ebuf, o_r):
        v = nn(kv, q_r[...]) + bias
        top = jnp.max(v, axis=0, keepdims=True)
        e = jnp.exp(v - top).astype(BF)
        if ebuf is not None:
            ebuf[...] = e
        o_r[...] = tn(kv, e)[HF:]
        return top, rowsum(e.astype(F32))

    def biases(j):
        return (
            key_bias(pk, slot_ref[1, j]),
            jnp.where(pk5 < limit5, key_bias(pk5 + sz.step * m, slot_ref[1, j]), NEG),
        )

    own, five, own_h, five_h = ([None] * sz.n_dp for _ in range(4))

    def block(k):
        j = dpx(k)
        bias, bias5 = biases(j)
        own[k] = attend(kva[j, 0:PL, :], qa_r, bias, ebuf.at[j], s["o_own"].at[k])
        five[k] = attend(kva[j, PL:, :], qb_r, bias5, e5buf.at[j], s["o_five"].at[k])

    def block_h(k):
        j = dpx(k)
        bias, bias5 = biases(j)
        own_h[k] = attend(kva[j, 0:PL, :], qc_r, bias, None, s["oh_own"].at[k])
        five_h[k] = attend(kva[j, PL:, :], qd_r, bias5, None, s["oh_five"].at[k])

    block(0)
    rt, ct = iota((D, 4 * LANES), 0), iota((D, 4 * LANES), 1)
    lane4, head4 = ct & (LANES - 1), ct >> 7
    place_out = hot((lane4 < FS) & (rt == FS * head4 + lane4))
    rk, ck = iota((D, 5 * LANES), 0), iota((D, 5 * LANES), 1)
    lane5, head5 = ck & (LANES - 1), ck >> 7
    w_all, wq_cat, w2_t, wo_cat = s["w_all"], s["wq_cat"], s["w2_t"], s["wo_cat"]
    w_all[...] = (
        nn(wk, hot((lane5 < HF) & (rk == HF * head5 + lane5)))
        + nn(wv, hot((lane5 >= HF) & (rk == HF * head5 + lane5 - HF)))
    ).astype(BF)
    wq_cat[...] = nn(
        wq, hot(rt == jnp.where(lane4 < HF, HF * head4 + lane4, last + lane4 - HF))
    ).astype(BF)
    w2_t[...] = w2.T
    wo = wo_ref[...]
    wo_cat[...] = jnp.concatenate(
        [b for h in range(4) for b in (wo[HF * h : HF * (h + 1)], wo[last:])], axis=0
    )
    dgx, dzx = s["dgx"], s["dzx"]
    for p in range(4):
        dgx[p, sz.top : sz.top + PL, :] = nt(dfm[plane(p), :], w2).astype(BF).astype(F32)
    edge_at()
    up = jnp.where(
        same_x(above), edge[above // 2][:, EP : 2 * EP].astype(F32), s["edge_x"][:, 0:EP].astype(F32)
    )
    down = jnp.where(
        same_x(below), edge[below // 2][:, 0:EP].astype(F32), s["edge_x"][:, EP : 2 * EP].astype(F32)
    )
    edge_g[m] = jnp.concatenate([up, down, lane_pad.astype(F32)], axis=1).astype(BF)
    edgeg_at, edgeg_mid = mp_start(edge_g)
    kv_steps[3]()
    block(1)
    edgeg_mid()
    kv_steps[0]()
    block(2)
    edgeg_at()

    xh_r = s["xh_r"]
    e_all = edge_g[...].reshape(D, sz.edge_q)
    for n, ref in enumerate(lanes3):
        ref[0 : sz.edge_q, :] = e_all[LANES * n : min(D, LANES * (n + 1))].astype(F32).T
    rows = []
    for i in range(2):
        for j in range(2):
            for a, first in ((-1, 0), (PA, EP)):
                at = pl.ds(first + sz.cols * i + j, PB, stride=2)
                value = jnp.concatenate([ref[at, :] for ref in lanes3], axis=1)
                rows.append(value * row_mask(i, j, a))
    xh = jnp.concatenate(rows, axis=0)
    xh_r[...] = xh.astype(BF)
    xhat, _ = spread(xh)
    q2 = query((xhat * vec(ln1g_ref) + vec(ln1b_ref)).astype(BF))
    q2 = jnp.concatenate([q2, jnp.zeros((sz.edge_q - sz.edge, LANES), F32)], axis=0)
    feature_major(q2, qc_r, qd_r)
    kv_steps[1]()
    block(4)
    kv_steps[2]()
    block(6)
    for k in (0, 1, 2, 4, 6):
        block_h(k)
    dy_mid()
    for k, step in ((3, 4), (5, 5), (7, 6)):
        kv_steps[step]()
        block(k)
        block_h(k)

    def joined(parts, o_r):
        top = functools.reduce(jnp.maximum, [t for t, _ in parts])
        scale = [jnp.exp(t - top) for t, _ in parts]
        total = sum(f * n for f, (_, n) in zip(scale, parts))
        inv = 1.0 / total
        scale = [f * inv for f in scale]
        return top + jnp.log(total), scale, sum(f * o_r[k] for k, f in enumerate(scale))

    lse_r, LR = s["lse_r"], (Q + sz.edge_q) // LANES
    lse5, scale5, o5_t = joined(five, s["o_five"])
    lse5h, _, o5h_t = joined(five_h, s["oh_five"])
    flat = [lse5[:, LANES * n : LANES * (n + 1)] for n in range(Q // LANES)]
    flat += [lse5h[:, LANES * n : LANES * (n + 1)] for n in range(sz.edge_q // LANES)]
    lse_r[m] = jnp.concatenate(flat + [jnp.zeros((16 - LR, LANES), F32)], axis=0)
    lse_at = mp_scatter(lambda h: lse_r.at[m], lambda k: lse_r.at[m], lambda k: lse_r.at[mpx(k)])
    _, scale, o_t = joined(own, s["o_own"])
    o2 = jnp.concatenate([o_t, o5_t], axis=0).T.astype(BF)
    chunks = ((s["og_a"], s["ow_a"]), (s["og_b"], s["ow_b"]), (s["og_c"], s["ow_c"]))
    ogs = []
    for n in range(2):
        og = chunks[n][0]
        og[m] = o2[2 * KEYS * n : 2 * KEYS * (n + 1)]
        ogs.append(mp_start(og))
    _, _, oh_t = joined(own_h, s["oh_own"])
    s["og_c"][m] = jnp.concatenate([oh_t, o5h_t], axis=0).T[0 : sz.edge].astype(BF)
    ogs.append(mp_start(s["og_c"]))

    lse_at()
    lse4 = [
        jnp.concatenate([lse_r[h][n : n + 1] for n in range(LR)], axis=1) for h in range(4)
    ]
    top = functools.reduce(jnp.maximum, lse4)
    whole = top + jnp.log(sum(jnp.exp(v - top) for v in lse4))
    share_all = jnp.exp(jnp.concatenate(lse4 + [jnp.zeros((4, Q + sz.edge_q), F32)], axis=0) - whole).T
    share = jnp.exp(lse5 - whole[:, 0:Q])

    def weighed(n, first):
        og, ow = chunks[n]
        rows = og.shape[1]
        lane = iota((rows, LANES), 1)
        ogs[n][0]()
        for h in range(4):
            part = share_all[first : first + rows, h : h + 1]
            ow[h] = (og[h].astype(F32) * jnp.where(lane < HF, 1.0, part)).astype(BF)
        oc = jnp.concatenate([ow[h] for h in range(4)], axis=1)
        return nn(oc, wo_cat[...]) + vec(bo_ref)

    h1_r, n2_r = s["h1_r"], s["n2_r"]

    def second_norm(h1):
        xhat, _ = spread(h1)
        return (xhat * vec(ln2g_ref) + vec(ln2b_ref)).astype(BF)

    w1, b1 = w1_ref[...], vec(b1_ref)

    def hidden(rows, mask):
        return ((nn(rows, w1) + b1) * mask).astype(BF).astype(F32)

    ux, ul, ur, dzl, dzr = s["ux"], s["ul"], s["ur"], s["dzl"], s["dzr"]
    b40 = iota((PB, 1), 0)

    def shift(src, left, right, i, start):
        at = slice(start, start + PB)
        left[i, at, :] = jnp.where(b40 == 0, 0.0, pltpu.roll(src[2 * i + 1, at, :], 1, 0))
        right[i, at, :] = jnp.where(b40 == PB - 1, 0.0, pltpu.roll(src[2 * i, at, :], PB - 1, 0))

    for n in range(2):
        mixed = weighed(n, 2 * KEYS * n)
        ogs[n + 1][1]()
        for p in (2 * n, 2 * n + 1):
            mask = token_mask(n, p % 2)
            h1 = xm_r[plane(p), :].astype(F32) + mask * from_queries(mixed, p % 2)
            h1_r[plane(p), :] = h1
            n2_r[plane(p), :] = second_norm(h1)
            ux[p, sz.top : sz.top + PL, :] = hidden(n2_r[plane(p), :], mask)
        for a in range(PA):
            shift(ux, ul, ur, n, sz.top + PB * a)

    wd_ref, bd_row = wd_ref.ready(), vec(bd_ref)
    g_r, du_r = s["g_r"], s["du_r"]
    for p in range(4):
        g_r[p, KEYS:PL, :] = jnp.zeros((PL - KEYS, C), F32)
        du_r[p, KEYS:PL, :] = jnp.zeros((PL - KEYS, C), F32)

    def source(refs, i, j, di, dj, start):
        base, left, right = refs
        i2, up = (i + di) % 2, (i + di) // 2
        j2, across = (j + dj) % 2, (j + dj) // 2
        at = pl.ds(pl.multiple_of(start + PB * up, 8), PB)
        if across < 0:
            return left[i2, at, :]
        if across > 0:
            return right[i2, at, :]
        return base[2 * i2 + j2, at, :]

    TAPS = [(di, dj) for di in (-1, 0, 1) for dj in (-1, 0, 1)]

    def activation(i, j, start):
        p = 2 * i + j
        z = bd_row + sum(
            wd_ref[t : t + 1, :] * source((ux, ul, ur), i, j, di, dj, start)
            for t, (di, dj) in enumerate(TAPS)
        )
        phi = 0.5 * (1.0 + lax.erf(z * 0.7071067811865476))
        dens = jnp.exp(-0.5 * z * z) * 0.3989422804014327
        dz = dgx[p, pl.ds(pl.multiple_of(start, 8), PB), :] * (phi + z * dens)
        dzx[p, pl.ds(pl.multiple_of(start, 8), PB), :] = dz
        return z * phi, dz

    def fold(value):
        return jnp.sum(value.reshape(PB // 8, 8, C), axis=0)

    def forward_step(i, j):
        p = 2 * i + j

        def step(a, acc):
            start = sz.top + PB * a
            act, dz = activation(i, j, start)
            g_r[p, pl.ds(pl.multiple_of(PB * a, 8), PB), :] = act
            new = [
                acc[t] + fold(dz * source((ux, ul, ur), i, j, di, dj, start))
                for t, (di, dj) in enumerate(TAPS)
            ]
            return tuple(new) + (acc[9] + fold(dz),)

        return step

    dy_at()
    beside_j = jnp.where(m >= 2, above, below)
    dyh_g[m] = jnp.where(
        same_x(beside_j), dyh[beside_j // 2].astype(F32), s["dyh_x"][...].astype(F32)
    ).astype(BF)
    dyg_at, dyg_mid = mp_start(dyh_g)

    sums = tuple(jnp.zeros((8, C), F32) for _ in range(10))
    for i in range(2):
        for j in range(2):
            sums = lax.fori_loop(1 - i, PA - i, forward_step(i, j), sums)
    dyg_mid()
    ot_r[...] = jnp.concatenate([o_t, o5_t * share], axis=0)
    mixed = weighed(2, Q)
    dyg_at()
    for p in range(4):
        i, j = p // 2, p % 2
        start = sz.top - PB if i == 1 else sz.top + KEYS
        rows = dyh_g[p][:, :D].astype(F32)[0:PB] * row_mask(i, j, -1 if i == 1 else PA)
        dgx[p, start : start + PB, :] = nt(rows.astype(BF), w2).astype(BF).astype(F32)
    xh = xh_r[...].astype(F32)
    for p in range(4):
        i, j = p // 2, p % 2
        mask = jnp.concatenate([row_mask(i, j, -1), row_mask(i, j, PA)], axis=0)
        at = slice(2 * PB * p, 2 * PB * (p + 1))
        u = hidden(second_norm(xh[at] + mask * mixed[at]), mask)
        ux[p, sz.top - PB : sz.top, :] = u[0:PB]
        ux[p, sz.top + KEYS : sz.top + KEYS + PB, :] = u[PB:]
    for i in range(2):
        shift(ux, ul, ur, i, sz.top - PB)
        shift(ux, ul, ur, i, sz.top + KEYS)
    for i in range(2):
        for j in range(2):
            activation(i, j, sz.top - PB if i == 1 else sz.top + KEYS)
            sums = forward_step(i, j)((PA - 1) * i, sums)
    e_s, ve_s, vl_s = s["e_s"], s["ve_s"], s["vl_s"]
    for i in range(2):
        for a in range(PA + 1):
            shift(dzx, dzl, dzr, i, sz.top + PB * (a - i))
    dub = s["dub"]
    for i in range(2):
        for j in range(2):
            p = 2 * i + j

            def backward_step(a, carry, i=i, j=j, p=p):
                start = sz.top + PB * a
                du_r[p, pl.ds(pl.multiple_of(PB * a, 8), PB), :] = sum(
                    wd_ref[t : t + 1, :] * source((dzx, dzl, dzr), i, j, -di, -dj, start)
                    for t, (di, dj) in enumerate(TAPS)
                )
                return carry

            lax.fori_loop(0, PA, backward_step, 0)
            dub[p] = (du_r[p].astype(BF).astype(F32) * token_mask(i, j)).astype(BF)
    dn2_mid, dn2_at = mp_sum(lambda h: nt(dub[h], w1), s["dn2_s"], s["dn2_n"], s["dn2_f"])
    dn2_mid()

    gb = g_r[...].reshape(T, C).astype(BF)
    du_all = dub[...].reshape(T, C)
    e_s[0:D, :C] = tn(n2_r[...], du_all).astype(BF)
    e_s[D:, :D] = tn(gb, dfm[...]).astype(BF)

    def rows_of(ref, n):
        return lambda j: ref.at[pl.ds(pl.multiple_of(n * j, 16), n)]

    e_mid, e_at = dp_sum(rows_of(e_s, sz.echunk), s["e_n"], s["e_o"], s["e_f"])
    for t in range(10):
        ve_s[t : t + 1, :C] = rowsum(sums[t])
    ve_s[10:11, :C] = rowsum(du_all.astype(F32))

    for k in range(sz.n_dp):
        j = dpx(k)
        ebuf[j] = (ebuf[j].astype(F32) * scale[k]).astype(BF)
        e5buf[j] = (e5buf[j].astype(F32) * (scale5[k] * share)).astype(BF)
    ogp = s["ogp"]
    lane = iota((PL, LANES), 1)
    for n, (og, ow) in enumerate(chunks[:2]):
        mine, fifth = og[m].astype(F32), sum(ow[h].astype(F32) for h in range(4))
        for q in range(2):
            ogp[plane(2 * n + q), :] = jnp.where(
                lane < HF, from_queries(mine, q), from_queries(fifth, q)
            ).astype(BF)

    xhat2, rstd2 = spread(plane_rows(h1_r, PL * m))
    dfp = plane_rows(dfm, PL * m).astype(F32)
    ve_s[11:12, :D] = rowsum(dfp)
    dn2 = dn2_at()
    dh1 = dfp + norm_back(dn2, vec(ln2g_ref), xhat2, rstd2)
    dab = dh1.astype(BF)
    docat = nt(dab, wo_cat[...]).astype(BF)
    dos, do_all, dabg = s["dos"], s["do_all"], s["dabg"]
    for h in range(4):
        dos[h] = docat[:, LANES * h : LANES * (h + 1)]
    do_at = mp_scatter(lambda h: dos.at[h], lambda k: do_all.at[m], lambda k: do_all.at[mpx(k)])
    do_all[m] = dos[m]
    s["dh1_r"][...] = dh1
    dabg[m, :, :D] = dab
    ve_s[12:13, :D] = rowsum(dh1)
    ve_s[13:14, :D] = rowsum(dn2 * xhat2)
    ve_s[14:15, :D] = rowsum(dn2)
    ve_s[15:16, :] = jnp.zeros((1, W), F32)
    ve_mid, ve_at = dp_total(ve_s, s["ve_n"], s["ve_p"])
    e_mid()

    def ff_block(h):
        return nt(w2_t[pl.ds(pl.multiple_of(FS * h, 16), FS), :], gb)

    ff_mid, ff_at = mp_sum(ff_block, s["ff_s"], s["ff_n"], s["ff_f"])

    do_at()
    dr_r = s["dr_r"]
    dot_t = to_queries([do_all[p].astype(F32) for p in range(4)]).T
    dr_r[m] = jnp.broadcast_to(rowsum(dot_t[HF:] * ot_r[HF:, :]), (8, Q))
    dr_at = mp_scatter(lambda h: dr_r.at[m], lambda k: dr_r.at[m], lambda k: dr_r.at[mpx(k)])
    dab_at, dab_mid = mp_start(dabg)
    drow = rowsum(dot_t[0:HF] * ot_r[0:HF, :])
    da_t = jnp.concatenate([half, dot_t[0:HF]], axis=0).astype(BF)
    db_t = jnp.concatenate([half, dot_t[HF:]], axis=0).astype(BF)
    dqt, dqt5 = s["dqt"], s["dqt5"]
    dqt[...] = jnp.zeros_like(dqt)
    dqt5[...] = jnp.zeros_like(dqt5)
    five_row = []

    def own_keys(j):
        kv, e = kva[j, 0:PL, :], ebuf[j]
        ds = (e.astype(F32) * (nn(kv, da_t) - drow)).astype(BF)
        dqt[...] += tn(kv, ds)
        return nt(ds, qa_r[...]) + nt(e, da_t)

    def last_keys(j):
        kv, e = kva[j, PL:, :], e5buf[j]
        ds = (e.astype(F32) * (nn(kv, db_t) - five_row[0])).astype(BF)
        dqt5[...] += tn(kv, ds)
        return nt(ds, qb_r[...]) + nt(e, db_t)

    dk_x, dk_n, dk_o, dk_f = s["dk_x"], s["dk_n"], s["dk_o"], s["dk_f"]
    dk_at = take(8)

    def dk_across(kz, own):
        dk_x[kz] = jnp.concatenate([own, last_keys(dpx(2 * kz + 1))], axis=0).astype(BF)
        send(dk_x.at[kz], dk_n.at[kz], dk_at + kz, (dpx(1), m))

    def dk_along(kz):
        j = dpx(2 * kz)
        value = jnp.concatenate([own_keys(j), last_keys(j)], axis=0)
        arrived(dk_n.at[kz], dk_at + kz)
        dk_o[kz] = (value + dk_n[kz].astype(F32)).astype(BF)
        send(dk_o.at[kz], dk_f.at[kz], dk_at + 4 + kz, (dpx(2 * kz), m))

    own2 = own_keys(dpx(5))
    own3 = own_keys(dpx(7))
    dr_at()
    five_row.append(sum(dr_r[h][0:1] for h in range(4)))
    dk_across(2, own2)
    dk_across(3, own3)
    ve_mid()
    dk_across(1, own_keys(dpx(3)))
    dab_mid()
    dk_across(0, own_keys(dpx(1)))
    dk_along(2)
    dk_along(3)
    ff_mid()
    dk_along(1)
    dkv = jnp.concatenate([own_keys(d), last_keys(d)], axis=0)

    def dk_finish():
        arrived(dk_n.at[0], dk_at)
        total = dkv + dk_n[0].astype(F32)
        for kz in (1, 2, 3):
            arrived(dk_f.at[kz], dk_at + 4 + kz)
            total = total + dk_f[kz].astype(F32)
        return total

    dk_fin = handle(dk_finish)

    dq2 = (jnp.concatenate([dqt[0:HF], dqt5[0:HF]], axis=0) * HF ** (-0.5)).T
    dqs, dq_all = s["dqs"], s["dq_all"]
    for h in range(4):
        dqs[h] = from_queries(dq2, h).astype(BF)
    dq_at = mp_scatter(lambda h: dqs.at[h], lambda k: dq_all.at[m], lambda k: dq_all.at[mpx(k)])
    dq_all[m] = dqs[m]
    eg_ref[d] = e_at().astype(BF)
    eg_at, eg_mid, _ = dp_start(eg_ref)
    l1_s, l2_s = s["l1_s"], s["l2_s"]
    dqp = dqs[...].reshape(T, LANES)
    l1_s[0:D, :] = tn(n1_r[...], dqp).astype(BF)
    vl_s[...] = jnp.zeros_like(vl_s)
    vl_s[5:6, 0:LANES] = rowsum(dqp.astype(F32))

    def packed(value):
        n = value.shape[0] // 2
        parts = [value[:, 0:LANES], value[:, LANES : 2 * LANES]]
        parts.append(jnp.concatenate([value[0:n, 2 * LANES :], value[n:, 2 * LANES :]], axis=1))
        return jnp.concatenate(parts, axis=0)

    def fill(ref, first, value):
        rest = jnp.zeros((ref.shape[0] - first - value.shape[0], LANES), F32)
        ref[first:, :] = jnp.concatenate([value, rest], axis=0).astype(BF)

    def own_rows(value, n):
        return sum(jnp.where(m == h, 1.0, 0.0) * value[n * h : n * (h + 1)] for h in range(4))

    dab_at()
    gwo = tn(ogp[...], dabg[...].reshape(T, W)[:, :D])
    fill(l1_s, 2 * D, packed(jnp.concatenate([gwo[0:HF], own_rows(gwo[HF:], HF // 4)], axis=0)))

    dkvb = dk_fin().astype(BF)
    dkvg = s["dkvg"]
    dkvg[m] = dkvb
    dkv_at, dkv_mid = mp_start(dkvg)
    l1_s[D : 2 * D, :] = tn(xr_r[...], dkvb[0:PL]).astype(BF)
    l1_mid, l1_at = dp_sum(rows_of(l1_s, sz.l1rows // sz.n_dp), s["l1_n"], s["l1_o"], s["l1_f"])
    vl_s[6:7, 0:LANES] = jnp.concatenate(
        [rowsum(dkvb[0:PL].astype(F32))[:, HF:], rowsum(dkvb[PL:].astype(F32))[:, HF:]], axis=1
    )
    dq_at()
    dq_cat = jnp.concatenate([dq_all[h] for h in range(4)], axis=1)
    dn1 = nt(dq_cat, wq_cat[...])
    xhat1, rstd1 = spread(plane_rows(xm_r, PL * m).astype(F32))
    dkv_mid()
    dkv_at()
    rest = jnp.concatenate(
        [dkvg[h, PL : PL + sz.step, :] for h in range(3)] + [dkvg[3, PL:, :]], axis=0
    )
    dkv_all = jnp.concatenate([dkvg[h, 0:PL, :] for h in range(4)] + [rest], axis=1)
    dxr = nt(dkv_all, w_all[...])
    xhr = s["xhr_r"][...]
    drb = norm_back(dxr, vec(lnrg_ref), xhr, s["rsr_r"][:, 0:1]).astype(BF)
    l2_s[0 : sz.wrows, :] = packed(tn(drb, plane_rows(n1_r, PL * m))).astype(BF)
    fill(l2_s, sz.wrows, own_rows(tn(xr_r[...], rest), FS))
    l2_mid, l2_at = dp_sum(rows_of(l2_s, sz.l2rows // sz.n_dp), s["l2_n"], s["l2_o"], s["l2_f"])
    l1_mid()
    vl_s[2:3, :D] = rowsum(dxr * xhr)
    vl_s[3:4, :D] = rowsum(dxr)
    vl_s[4:5, :D] = rowsum(drb.astype(F32))

    wr_m = wr_t[pl.ds(pl.multiple_of(D * m, 16), D), :]
    dn1 = dn1 + nt(drb, wr_m)
    vl_s[0:1, :D] = rowsum(dn1 * xhat1)
    vl_s[1:2, :D] = rowsum(dn1)
    vl_mid, vl_at = dp_total(vl_s, s["vl_n"], s["vl_p"])
    dxm = norm_back(dn1, vec(ln1g_ref), xhat1, rstd1)
    gp = (token_mask(m // 2, lax.rem(m, 2)) * (s["dh1_r"][...] + dxm)).astype(BF)
    gpf = nn(gp, place_out).astype(BF)
    gps = s["gps"]
    for h in range(4):
        gps[h] = gpf[:, LANES * h : LANES * (h + 1)]
    gp_at = mp_scatter(lambda h: gps.at[h], lambda k: gp_ref.at[m], lambda k: gp_ref.at[mpx(k)])
    gp_ref[m] = gps[m]
    eg_mid()

    ff = ff_at().T
    ff = jnp.concatenate([ff, jnp.zeros((T, LANES - FS), F32)], axis=1)
    sel = hot((c2 < FS) & (r2 == FS * m + c2))
    b2q = jnp.concatenate(
        [own_part(vec(b2_ref), FS), jnp.zeros((1, LANES - FS), F32)], axis=1
    )
    for p in range(4):
        h1 = h1_r[plane(p), :]
        hi = h1.astype(BF)
        h1q = nn(hi, sel) + nn((h1 - hi.astype(F32)).astype(BF), sel)
        blk_ref[plane(p), :] = h1q + token_mask(p // 2, p % 2) * (ff[plane(p)] + b2q)
    store(0)
    veg_ref[m] = ve_at()
    veg_at, _ = mp_start(veg_ref)

    def gather(buf):
        base = take(3 * sz.n_dp)

        def onward(k):
            j = dpx(k)
            send(buf.at[m, j], buf.at[m, j], base + 3 * k, (d, mpx(1)))
            send(buf.at[m, j], buf.at[m, j], base + 3 * k + 1, (d, mpx(2)))

        near, mid, steps = dp_start(buf.at[m], onward)
        onward(0)
        seq = (0, 2, 4, 6, 1, 3, 5, 7)

        def relay(k):
            j = dpx(k)
            arrived(buf.at[mpx(2), j], base + 3 * k + 1)
            send(buf.at[mpx(2), j], buf.at[mpx(2), j], base + 3 * k + 2, (d, mpx(1)))

        relays = [handle(lambda k=k: relay(k)) for k in seq]

        def finish():
            near()
            for r in relays:
                r()
            for k in seq:
                arrived(buf.at[mpx(1), dpx(k)], base + 3 * k)
                arrived(buf.at[mpx(3), dpx(k)], base + 3 * k + 2)

        return near, mid, relays, handle(finish)

    lg1_ref[m, d] = l1_at().astype(BF)
    near1, mid1, relays1, lg1_at = gather(lg1_ref)
    l2_mid()
    vl_mid()
    mid1()
    lg2_ref[m, d] = l2_at().astype(BF)
    near2, mid2, relays2, lg2_at = gather(lg2_ref)
    near1()
    vlg_ref[m] = vl_at()
    vlg_at, _ = mp_start(vlg_ref)
    for r in relays1[:4]:
        r()
    mid2()
    for r in relays1[4:]:
        r()
    near2()
    for r in relays2:
        r()
    eg_at()
    store(2)
    gp_at()
    store(1)
    veg_at()
    store(5)
    lg1_at()
    store(3)
    vlg_at()
    store(6)
    lg2_at()
    store(4)
    for c in pending:
        c.wait_send()
    for c in stores:
        c.wait()


def unpack_body(sz, *refs):
    srcs, refs = refs[:7], refs[7:]
    (
        out_ref, gpix_ref, ln1g_ref, ln1b_ref, gwq_ref, gbq_ref, gwk_ref, gwv_ref, gbv_ref, gwr_ref, gbr_ref,
        lnrg_ref, lnrb_ref, gwo_ref, gbo_ref, ln2g_ref, ln2b_ref, gw1_ref, gb1_ref, gwd_ref, gbd_ref,
        gw2_ref, gb2_ref,
    ), refs = refs[:23], refs[23:]
    out32, gp32, sem = refs[7:]
    order = (5, 6, 0, 1, 2, 3, 4)
    loads = [None] * 7
    for i in order:
        loads[i] = Load(srcs[i], refs[i], sem.at[i])
    blk_ref, gp_ref, eg_ref, lg1_ref, lg2_ref, veg_ref, vlg_ref = loads
    D, HF, PB, PA, PL = sz.width, HEAD_FEATURES, sz.pb, sz.pa, sz.plane
    C, FS = sz.hidden, sz.share
    m = lax.axis_index("mp")

    def row(value):
        return value.reshape(value.shape[1])

    ve = veg_ref[m]
    gwd_ref[...] = ve[0:9, :C]
    gbd_ref[...] = row(ve[9:10, :C])
    gb1_ref[...] = row(ve[10:11, :C])
    vs = sum(veg_ref[h] for h in range(4))
    gb2_ref[...] = row(vs[11:12, :D])
    gbo_ref[...] = row(vs[12:13, :D])
    ln2g_ref[...] = row(vs[13:14, :D])
    ln2b_ref[...] = row(vs[14:15, :D])
    vl = sum(vlg_ref[h] for h in range(4))
    ln1g_ref[...] = row(vl[0:1, :D])
    ln1b_ref[...] = row(vl[1:2, :D])
    lnrg_ref[...] = row(vlg_ref[0][2:3, :D])
    lnrb_ref[...] = row(vlg_ref[0][3:4, :D])
    gbr_ref[...] = row(vlg_ref[0][4:5, :D])

    def head_row(r):
        parts = [vlg_ref[h][r : r + 1, 0:HF] for h in range(4)] + [vl[r : r + 1, HF : 2 * HF]]
        return row(jnp.concatenate(parts, axis=1))

    gbq_ref[...] = head_row(5)
    gbv_ref[...] = head_row(6)
    for i in range(2):
        for j in range(2):
            p = 2 * i + j
            for a in range(PA):
                at = pl.ds((2 * a + i) * sz.cols + j, PB, stride=2)
                out32[at, :] = blk_ref[PL * p + PB * a : PL * p + PB * (a + 1), 0:FS]
                gp32[at, :] = gp_ref[p].astype(F32)[PB * a : PB * (a + 1), 0:FS]
    out_ref[...] = out32[...].T.astype(BF)
    gpix_ref[...] = gp32[...].T
    eg = eg_ref[...].reshape(D + C, sz.wide)
    gw1_ref[...] = eg[0:D, :C].astype(F32)
    gw2_ref[...] = eg[D:, :D].astype(F32)

    def unpacked(value):
        n = value.shape[0] * 2 // 5
        tail = value[2 * n :]
        tail = jnp.concatenate([tail[:, 0:HF], tail[:, HF:]], axis=0)
        return jnp.concatenate([value[0:n], value[n : 2 * n], tail], axis=1)

    lg1 = [lg1_ref[h].reshape(sz.l1rows, LANES).astype(F32) for h in range(4)]
    lg2 = [lg2_ref[h].reshape(sz.l2rows, LANES).astype(F32) for h in range(4)]
    tail = jnp.concatenate([lg2[h][sz.wrows : sz.wrows + FS] for h in range(4)], axis=0)
    fifth = sum(lg1[h][0:D, HF:] for h in range(4))
    gwq_ref[...] = jnp.concatenate([lg1[h][0:D, 0:HF] for h in range(4)] + [fifth], axis=1)
    gwk_ref[...] = jnp.concatenate([lg1[h][D : 2 * D, 0:HF] for h in range(4)] + [tail[:, 0:HF]], axis=1)
    gwv_ref[...] = jnp.concatenate([lg1[h][D : 2 * D, HF:] for h in range(4)] + [tail[:, HF:]], axis=1)
    gwr_ref[...] = jnp.concatenate([unpacked(lg2[h][0 : sz.wrows]) for h in range(4)], axis=1)
    n = HF // 4
    for h in range(4):
        wo = unpacked(lg1[h][2 * D : 2 * D + 5 * sz.orows // 2])
        gwo_ref[HF * h : HF * (h + 1), :] = wo[0:HF]
        gwo_ref[4 * HF + n * h : 4 * HF + n * (h + 1), :] = wo[HF:]


def on_device_fused(*args):
    pixels_in, cotangent, pixel_mask, tile_slot = args[:4]
    w_fc1 = args[19]
    sz = Sizes(
        lax.axis_size("dp"), lax.axis_size("mp"), pixels_in.shape[0], cotangent.shape[1], w_fc1.shape[1]
    )
    D, C, PL, T, W, LN, HF = sz.width, sz.hidden, sz.plane, sz.all, sz.wide, LANES, HEAD_FEATURES
    Q, N, PB = sz.queries, sz.n_dp, sz.pb
    sm = pl.BlockSpec(memory_space=pltpu.SMEM)
    vm = pl.BlockSpec(memory_space=pltpu.VMEM)
    hbm = pl.BlockSpec(memory_space=pltpu.HBM)
    S = jax.ShapeDtypeStruct
    ins = [pixels_in.T, cotangent.T, *args[4:11], args[11].T, *args[12:]]
    mids = [
        S((T, LN), F32), S((4, PL, LN), BF), S((N, sz.echunk, W), BF), S((4, N, sz.l1rows // N, LN), BF),
        S((4, N, sz.l2rows // N, LN), BF), S((4, 16, W), F32), S((4, 8, W), F32),
    ]
    chunks = dict(e=(sz.echunk, W), l1=(sz.l1rows // N, LN), l2=(sz.l2rows // N, LN))
    shapes = {
        BF: dict(
            xt=(4, sz.share, sz.tokens), dfm=(T, D), dyh=(4, 48, W), dyh_s=(48, W), dyh_x=(48, W), dyh_g=(4, 48, W),
            edge=(4, sz.share, sz.edge_q), edge_s=(sz.share, sz.edge_q), edge_x=(sz.share, sz.edge_q),
            edge_g=(4, sz.share, sz.edge_q), xh_r=(sz.edge, D), qc_r=(LN, sz.edge_q), qd_r=(LN, sz.edge_q), xm_r=(T, D), n1_r=(T, D),
            xr_r=(PL, D), kva=(N, sz.kvrows, LN), qa_r=(LN, Q), qb_r=(LN, Q), ebuf=(N, PL, Q),
            e5buf=(N, sz.quarter, Q), og_a=(4, 2 * sz.keys, LN), og_b=(4, 2 * sz.keys, LN), og_c=(4, sz.edge, LN),
            ow_a=(4, 2 * sz.keys, LN), ow_b=(4, 2 * sz.keys, LN), ow_c=(4, sz.edge, LN), n2_r=(T, D),
            dub=(4, PL, C), dn2_s=(3, PL, D), dn2_n=(2, PL, D),
            dn2_f=(PL, D), dos=(4, PL, LN), do_all=(4, PL, LN), dabg=(4, PL, W), ff_s=(3, sz.share, T), ff_n=(2, sz.share, T),
            ff_f=(sz.share, T), dk_x=(4, sz.kvrows, LN), dk_n=(4, sz.kvrows, LN), dk_o=(4, sz.kvrows, LN),
            dk_f=(4, sz.kvrows, LN), dkvg=(4, sz.kvrows, LN), dqs=(4, PL, LN), dq_all=(4, PL, LN),
            e_s=(D + C, W), gps=(4, PL, LN), wr_t=(4 * D, D), ogp=(T, LN),
            w2_t=(D, C), w_all=(D, 5 * LN), wq_cat=(D, 4 * LN), wo_cat=(4 * LN, D), l1_s=(sz.l1rows, LN),
            l2_s=(sz.l2rows, LN),
            **{n + "_" + k: (4, *v) for k in "nof" for n, v in chunks.items()},
        ),
        F32: dict(
            t0=(sz.tokens, LN), t1=(sz.tokens, LN), t2=(sz.tokens, D - 2 * LN), xhr_r=(PL, D), rsr_r=(PL, LN),
            o_own=(N, HF, Q), o_five=(N, HF, Q), oh_own=(N, HF, sz.edge_q), oh_five=(N, HF, sz.edge_q),
            lse_r=(4, 16, LN), ot_r=(LN, Q),
            h1_r=(T, D), ux=(4, sz.ext, C), ul=(2, sz.ext, C), ur=(2, sz.ext, C), dgx=(4, sz.ext, C),
            dzx=(4, sz.ext, C), dzl=(2, sz.ext, C), dzr=(2, sz.ext, C), g_r=(4, PL, C), du_r=(4, PL, C),
            dh1_r=(PL, D), dr_r=(4, 8, Q), dqt=(LN, Q), dqt5=(LN, Q), ve_s=(16, W), ve_n=(16, W),
            ve_p=(4, 16, W), vl_s=(8, W), vl_n=(8, W), vl_p=(4, 8, W),
        ),
    }
    scratch = {k: pltpu.VMEM(v, t) for t, group in shapes.items() for k, v in group.items()}
    for i in range(1, len(ins)):
        scratch["in%d" % i] = pltpu.VMEM(ins[i].shape, ins[i].dtype)
    scratch["ssem"] = pltpu.SemaphoreType.DMA((200,))
    scratch["rsem"] = pltpu.SemaphoreType.DMA((200,))
    for i, v in enumerate(mids):
        scratch["out%d" % i] = pltpu.VMEM(v.shape, v.dtype)
    scratch["osem"] = pltpu.SemaphoreType.DMA((len(mids),))
    scratch["isem"] = pltpu.SemaphoreType.DMA((len(ins),))
    mid = pl.pallas_call(
        functools.partial(fused_body, sz, tuple(scratch)),
        out_shape=mids,
        in_specs=[sm, sm] + [hbm] * len(ins),
        out_specs=[hbm] * len(mids),
        scratch_shapes=list(scratch.values()),
        compiler_params=pltpu.CompilerParams(
            collective_id=0, has_side_effects=True, vmem_limit_bytes=VMEM_MB * 2**20
        ),
        name="fused_block",
    )(pixel_mask, tile_slot.T, *ins)
    outs = [
        S((sz.share, sz.tokens), BF), S((sz.share, sz.tokens), F32), S((D,), F32), S((D,), F32), S((D, D), F32),
        S((D,), F32), S((D, D), F32), S((D, D), F32), S((D,), F32), S((D, 4 * D), F32), S((D,), F32), S((D,), F32),
        S((D,), F32), S((D, D), F32), S((D,), F32), S((D,), F32), S((D,), F32), S((D, C), F32), S((C,), F32),
        S((9, C), F32), S((C,), F32), S((C, D), F32), S((D,), F32),
    ]
    res = list(
        pl.pallas_call(
            functools.partial(unpack_body, sz),
            out_shape=outs,
            in_specs=[hbm] * len(mids),
            out_specs=[vm] * len(outs),
            scratch_shapes=[pltpu.VMEM(v.shape, v.dtype) for v in mids]
            + [pltpu.VMEM((sz.tokens, sz.share), F32)] * 2
            + [pltpu.SemaphoreType.DMA((len(mids),))],
            compiler_params=pltpu.CompilerParams(vmem_limit_bytes=60 * 2**20),
            name="unpack",
        )(*mid)
    )
    for k in (0, 1, 9):
        res[k] = res[k].T
    return tuple(res)


def choose(*args):
    tokens, width = args[1].shape
    whole_rows = tokens == FRAME * (FRAME // TILE_ROWS)
    shape = (lax.axis_size("dp"), lax.axis_size("mp"))
    if whole_rows and shape == (TILE_ROWS, 4) and TILE_ROWS == 8 and HEADS == 5 and width == 320 == args[19].shape[1]:
        return on_device_fused(*args)
    return on_device(*args)


def solution(mesh):
    return jax.shard_map(
        choose,
        mesh=mesh,
        in_specs=(
            P("dp", "mp"),
            P("dp", None),
            P("dp"),
            P(),
            P(),
            P(),
            P(),
            P(),
            P(),
            P(),
            P(),
            P(),
            P(),
            P(),
            P(),
            P(),
            P(),
            P(),
            P(),
            P(None, "mp"),
            P("mp"),
            P(None, "mp"),
            P("mp"),
            P("mp", None),
            P(),
        ),
        out_specs=(
            P("dp", "mp"),
            P("dp", "mp"),
            P(),
            P(),
            P(),
            P(),
            P(),
            P(),
            P(),
            P(),
            P(),
            P(),
            P(),
            P(),
            P(),
            P(),
            P(),
            P(None, "mp"),
            P("mp"),
            P(None, "mp"),
            P("mp"),
            P("mp", None),
            P(),
        ),
        check_vma=False,
    )
```

```python
import functools

import jax
import jax.numpy as jnp
from jax import lax
from jax.experimental import pallas as pl
from jax.experimental.pallas import tpu as pltpu
from jax.sharding import PartitionSpec as P

HEADS = 5
HEAD_FEATURES = 64
FRAME = 80
TILE_ROWS = 8


EPS = 1e-05
NEG = -1e30


def layer_norm(value, gain, shift):
    mean = jnp.mean(value, axis=-1, keepdims=True)
    centred = value - mean
    spread = jnp.mean(centred * centred, axis=-1, keepdims=True)
    return centred * lax.rsqrt(spread + EPS) * gain + shift


def depth_gelu(padded, kernel, shift):
    rows = padded.shape[0] - 2
    cols = padded.shape[1] - 2
    total = jnp.zeros((rows, cols, padded.shape[2]), jnp.float32) + shift
    for row_off in range(3):
        for col_off in range(3):
            total = (
                total
                + kernel[3 * row_off + col_off]
                * padded[row_off : row_off + rows, col_off : col_off + cols]
            )
    return jax.nn.gelu(total, approximate=False)


def mat(left, right):
    return jnp.dot(left, right, preferred_element_type=jnp.float32)


def pick(weights, table):
    return jnp.einsum(
        "j,jab->ab", weights.astype(table.dtype), table, preferred_element_type=jnp.float32
    )


def head_columns(weight_matrix, select_where):
    wide_layout = weight_matrix.astype(jnp.float32).reshape(
        weight_matrix.shape[0], HEADS, HEAD_FEATURES
    )
    return (
        jnp.einsum("uzx,nz->unx", wide_layout, select_where)
        .reshape(weight_matrix.shape[0], -1)
        .astype(jnp.bfloat16)
    )


def head_rows(weight_matrix, select_where):
    wide_layout = weight_matrix.astype(jnp.float32).reshape(
        HEADS, HEAD_FEATURES, weight_matrix.shape[1]
    )
    return (
        jnp.einsum("hed,sh->sed", wide_layout, select_where)
        .reshape(-1, weight_matrix.shape[1])
        .astype(jnp.bfloat16)
    )


def head_vector(vector_entries, select_where):
    return jnp.einsum(
        "he,sh->se", vector_entries.reshape(HEADS, HEAD_FEATURES), select_where
    ).reshape(-1)


def spread_columns(gradient_value, select_where):
    return jnp.einsum(
        "tvm,vq->tqm",
        gradient_value.reshape(gradient_value.shape[0], -1, HEAD_FEATURES),
        select_where,
    ).reshape(gradient_value.shape[0], -1)


def spread_rows(gradient_value, select_where):
    return jnp.einsum(
        "sed,sh->hed",
        gradient_value.reshape(-1, HEAD_FEATURES, gradient_value.shape[1]),
        select_where,
    ).reshape(-1, gradient_value.shape[1])


def spread_vector(gradient_value, select_where):
    return jnp.einsum("se,sh->he", gradient_value.reshape(-1, HEAD_FEATURES), select_where).reshape(
        -1
    )


def on_device(
    pixels_in,
    cotangent,
    pixel_mask,
    tile_slot,
    ln1_gain,
    ln1_bias,
    w_query,
    b_query,
    w_key,
    w_value,
    b_value,
    w_reduce,
    b_reduce,
    lnr_gain,
    lnr_bias,
    w_out,
    b_out,
    ln2_gain,
    ln2_bias,
    w_fc1,
    b_fc1,
    w_depth,
    b_depth,
    w_fc2,
    b_fc2,
):
    n_dp = lax.axis_size("dp")
    n_mp = lax.axis_size("mp")
    device = lax.axis_index("dp")
    part = lax.axis_index("mp")
    rows = FRAME // TILE_ROWS
    tokens = pixels_in.shape[0]
    cols = tokens // rows
    tiles_col = FRAME // cols
    per_frame = TILE_ROWS * tiles_col
    width = ln1_gain.shape[0]
    share = width // n_mp
    slots = -(-HEADS // n_mp)
    scale = HEAD_FEATURES ** (-0.5)
    maskf = pixel_mask.astype(jnp.float32)[:, None]
    head_ids = part + n_mp * jnp.arange(slots)
    select_where = (head_ids[:, None] == jnp.arange(HEADS)[None, :]).astype(jnp.float32)
    crops = tile_slot[:, 0]
    tiles = tile_slot[:, 1]
    is_me = jnp.arange(n_dp) == device
    own_crop = jnp.sum(jnp.where(is_me, crops, 0))
    own_tile = jnp.sum(jnp.where(is_me, tiles, 0))
    own_row = own_tile // tiles_col
    own_col = own_tile % tiles_col
    tile_row = tiles // tiles_col
    tile_col = tiles % tiles_col

    def beside(drow, dcol):
        hit = (crops == own_crop) & (tile_row == own_row + drow) & (tile_col == own_col + dcol)
        return hit.astype(jnp.float32)

    member = (crops[None, :] == own_crop) & (tiles[None, :] == jnp.arange(per_frame)[:, None])
    crop_devices = jnp.sum(jnp.where(member, jnp.arange(n_dp)[None, :], 0), axis=1)
    whole = lax.all_gather(pixels_in, "mp", axis=1, tiled=True)
    xm = whole.astype(jnp.float32) * maskf
    n1, first_norm_backward = jax.vjp(layer_norm, xm, ln1_gain, ln1_bias)
    n1b = n1.astype(jnp.bfloat16)
    wq = head_columns(w_query, select_where)
    wk = head_columns(w_key, select_where)
    wv = head_columns(w_value, select_where)
    wo = head_rows(w_out, select_where)
    qb = (mat(n1b, wq) + head_vector(b_query, select_where)).astype(jnp.bfloat16)
    patches = (
        n1b.reshape(rows // 2, 2, cols // 2, 2, width)
        .transpose(0, 2, 1, 3, 4)
        .reshape(-1, 4 * width)
    )
    reduced = mat(patches, w_reduce) + b_reduce
    xr, lnr_back = jax.vjp(layer_norm, reduced, lnr_gain, lnr_bias)
    xrb = xr.astype(jnp.bfloat16)
    kb = mat(xrb, wk).astype(jnp.bfloat16)
    vb = (mat(xrb, wv) + head_vector(b_value, select_where)).astype(jnp.bfloat16)
    kmask = (
        pixel_mask.reshape(rows // 2, 2, cols // 2, 2)[:, 0, :, 0].reshape(-1).astype(jnp.bfloat16)
    )
    keys_all, values_all, kmask_all = (
        lax.all_gather(kb, "dp", axis=0, tiled=True),
        lax.all_gather(vb, "dp", axis=0, tiled=True),
        lax.all_gather(kmask, "dp", axis=0, tiled=True),
    )
    per_key = kb.shape[0]
    keys_crop = keys_all.reshape(n_dp, per_key, -1)[crop_devices]
    values_crop = values_all.reshape(n_dp, per_key, -1)[crop_devices]
    usable_crop = kmask_all.reshape(n_dp, per_key)[crop_devices].astype(jnp.float32) > 0.5
    n_blocks = 4
    key_blocks = keys_crop.reshape(n_blocks, -1, slots, HEAD_FEATURES)
    value_blocks = values_crop.reshape(n_blocks, -1, slots, HEAD_FEATURES)
    usable_blocks = usable_crop.reshape(n_blocks, -1)
    queries = qb.reshape(tokens, slots, HEAD_FEATURES)

    def block_scores(key_block, usable_block):
        raw = (
            jnp.einsum("qsd,ksd->sqk", queries, key_block, preferred_element_type=jnp.float32)
            * scale
        )
        return jnp.where(usable_block[None, None, :], raw, NEG)

    def top_step(carry, blocks):
        top, total = carry
        key_block, usable_block = blocks
        scores = block_scores(key_block, usable_block)
        new_top = jnp.maximum(top, jnp.max(scores, axis=-1))
        total = total * jnp.exp(top - new_top) + jnp.sum(
            jnp.exp(scores - new_top[..., None]), axis=-1
        )
        return ((new_top, total), None)

    start = (jnp.full((slots, tokens), NEG, jnp.float32), jnp.zeros((slots, tokens), jnp.float32))
    (top, total), _ = lax.scan(top_step, start, (key_blocks, usable_blocks))
    lse = top + jnp.log(total)

    def out_step(acc, blocks):
        key_block, value_block, usable_block = blocks
        prob = jnp.exp(block_scores(key_block, usable_block) - lse[..., None])
        acc = acc + jnp.einsum(
            "sqk,ksd->qsd",
            prob.astype(jnp.bfloat16),
            value_block,
            preferred_element_type=jnp.float32,
        )
        return (acc, None)

    empty = jnp.zeros((tokens, slots, HEAD_FEATURES), jnp.float32)
    acc, _ = lax.scan(out_step, empty, (key_blocks, value_blocks, usable_blocks))
    ob = acc.reshape(tokens, -1).astype(jnp.bfloat16)
    branch = lax.psum(mat(ob, wo).astype(jnp.bfloat16), "mp").astype(jnp.float32) + b_out
    h1 = xm + branch * maskf
    n2, ln2_back = jax.vjp(layer_norm, h1, ln2_gain, ln2_bias)
    n2b = n2.astype(jnp.bfloat16)
    ub = ((mat(n2b, w_fc1) + b_fc1) * maskf).astype(jnp.bfloat16)
    channels = ub.shape[1]
    tile_u = ub.reshape(rows, cols, channels)
    lines, sides = (
        lax.all_gather(jnp.stack([tile_u[0], tile_u[-1]]), "dp", axis=0, tiled=True),
        lax.all_gather(jnp.stack([tile_u[:, 0], tile_u[:, -1]]), "dp", axis=0, tiled=True),
    )
    lines = lines.reshape(n_dp, 2, cols, channels)
    sides = sides.reshape(n_dp, 2, rows, channels)
    top_lines = lines[:, 0]
    bottom_lines = lines[:, 1]
    left_sides = sides[:, 0]
    right_sides = sides[:, 1]
    upper = jnp.concatenate(
        [
            pick(beside(-1, -1), bottom_lines[:, -1:]),
            pick(beside(-1, 0), bottom_lines),
            pick(beside(-1, 1), bottom_lines[:, :1]),
        ],
        axis=0,
    )
    lower = jnp.concatenate(
        [
            pick(beside(1, -1), top_lines[:, -1:]),
            pick(beside(1, 0), top_lines),
            pick(beside(1, 1), top_lines[:, :1]),
        ],
        axis=0,
    )
    middle = jnp.concatenate(
        [
            pick(beside(0, -1), right_sides)[:, None],
            tile_u.astype(jnp.float32),
            pick(beside(0, 1), left_sides)[:, None],
        ],
        axis=1,
    )
    padded = jnp.concatenate([upper[None], middle, lower[None]], axis=0)
    act, depth_back = jax.vjp(depth_gelu, padded, w_depth, b_depth)
    gb = act.reshape(tokens, channels).astype(jnp.bfloat16)
    ffn_mine = lax.psum_scatter(
        mat(gb, w_fc2).astype(jnp.bfloat16), "mp", scatter_dimension=1, tiled=True
    ).astype(jnp.float32)
    h1_mine = lax.dynamic_slice_in_dim(h1, part * share, share, 1)
    bias_mine = lax.dynamic_slice_in_dim(b_fc2, part * share, share, 0)
    block_result = (h1_mine + (ffn_mine + bias_mine) * maskf).astype(jnp.bfloat16)
    dy = cotangent.astype(jnp.float32)
    dff = dy * maskf
    grad_b_fc2 = jnp.sum(dff, axis=0)
    dfb = dff.astype(jnp.bfloat16)
    grad_w_fc2 = mat(gb.T, dfb)
    dgr = mat(dfb, w_fc2.T).astype(jnp.bfloat16).astype(jnp.float32).reshape(rows, cols, channels)
    dpad, grad_w_depth, grad_b_depth = depth_back(dgr)
    grad_lines, grad_sides = (
        lax.all_gather(
            jnp.stack([dpad[0], dpad[-1]]).astype(jnp.bfloat16), "dp", axis=0, tiled=True
        ).astype(jnp.float32),
        lax.all_gather(
            jnp.stack([dpad[1:-1, 0], dpad[1:-1, -1]]).astype(jnp.bfloat16),
            "dp",
            axis=0,
            tiled=True,
        ).astype(jnp.float32),
    )
    grad_lines = grad_lines.reshape(n_dp, 2, cols + 2, channels)
    grad_sides = grad_sides.reshape(n_dp, 2, rows, channels)
    top_grads = grad_lines[:, 0]
    bottom_grads = grad_lines[:, 1]
    dtile = dpad[1:-1, 1:-1]
    dtile = dtile.at[0].add(pick(beside(-1, 0), bottom_grads[:, 1:-1]))
    dtile = dtile.at[0, 0].add(pick(beside(-1, -1), bottom_grads[:, -1:])[0])
    dtile = dtile.at[0, -1].add(pick(beside(-1, 1), bottom_grads[:, :1])[0])
    dtile = dtile.at[-1].add(pick(beside(1, 0), top_grads[:, 1:-1]))
    dtile = dtile.at[-1, 0].add(pick(beside(1, -1), top_grads[:, -1:])[0])
    dtile = dtile.at[-1, -1].add(pick(beside(1, 1), top_grads[:, :1])[0])
    dtile = dtile.at[:, 0].add(pick(beside(0, -1), grad_sides[:, 1]))
    dtile = dtile.at[:, -1].add(pick(beside(0, 1), grad_sides[:, 0]))
    dub = (dtile.reshape(tokens, channels).astype(jnp.bfloat16).astype(jnp.float32) * maskf).astype(
        jnp.bfloat16
    )
    grad_b_fc1 = jnp.sum(dub.astype(jnp.float32), axis=0)
    grad_w_fc1 = mat(n2b.T, dub)
    dn2_part = mat(dub, w_fc1.T)
    zero_vector = jnp.zeros((width,), jnp.float32)
    dn2 = lax.psum(dn2_part.astype(jnp.bfloat16), "mp").astype(jnp.float32)
    dh1_norm, shared_gain, shared_bias = ln2_back(dn2)
    dh1 = dy + dh1_norm
    split_gain = zero_vector
    split_bias = zero_vector
    dattn = dh1 * maskf
    grad_b_out = jnp.sum(dattn, axis=0)
    dab = dattn.astype(jnp.bfloat16)
    grad_wo = mat(ob.T, dab)
    dob = mat(dab, wo.T).astype(jnp.bfloat16)
    dout = dob.reshape(tokens, slots, HEAD_FEATURES)
    drow = jnp.sum(dout.astype(jnp.float32) * acc, axis=-1).T

    def back_step(dq_acc, blocks):
        key_block, value_block, usable_block = blocks
        prob = jnp.exp(block_scores(key_block, usable_block) - lse[..., None])
        dv_block = jnp.einsum(
            "sqk,qsd->ksd", prob.astype(jnp.bfloat16), dout, preferred_element_type=jnp.float32
        )
        dprob = jnp.einsum("qsd,ksd->sqk", dout, value_block, preferred_element_type=jnp.float32)
        dscore = (prob * (dprob - drow[..., None])).astype(jnp.bfloat16)
        dq_acc = dq_acc + jnp.einsum(
            "sqk,ksd->qsd", dscore, key_block, preferred_element_type=jnp.float32
        )
        dk_block = (
            jnp.einsum("sqk,qsd->ksd", dscore, queries, preferred_element_type=jnp.float32) * scale
        )
        return (dq_acc, (dk_block, dv_block))

    dq_acc, (dk_blocks, dv_blocks) = lax.scan(
        back_step, empty, (key_blocks, value_blocks, usable_blocks)
    )
    zero_keys = jnp.zeros((n_dp, per_key, slots * HEAD_FEATURES), jnp.float32)
    dk_full = (
        zero_keys.at[crop_devices]
        .set(dk_blocks.reshape(per_frame, per_key, -1))
        .reshape(n_dp * per_key, -1)
    )
    dv_full = (
        zero_keys.at[crop_devices]
        .set(dv_blocks.reshape(per_frame, per_key, -1))
        .reshape(n_dp * per_key, -1)
    )
    dk_mine, dv_mine = (
        lax.psum_scatter(dk_full, "dp", scatter_dimension=0, tiled=True),
        lax.psum_scatter(dv_full, "dp", scatter_dimension=0, tiled=True),
    )
    dkb = dk_mine.astype(jnp.bfloat16)
    dvb = dv_mine.astype(jnp.bfloat16)
    dqb = (dq_acc * scale).reshape(tokens, -1).astype(jnp.bfloat16)
    grad_wq = mat(n1b.T, dqb)
    grad_bq = jnp.sum(dqb.astype(jnp.float32), axis=0)
    grad_wk = mat(xrb.T, dkb)
    grad_wv = mat(xrb.T, dvb)
    grad_bv = jnp.sum(dvb.astype(jnp.float32), axis=0)
    dxr, dn1_query = (
        lax.psum((mat(dkb, wk.T) + mat(dvb, wv.T)).astype(jnp.bfloat16), "mp").astype(jnp.float32),
        lax.psum(mat(dqb, wq.T).astype(jnp.bfloat16), "mp").astype(jnp.float32),
    )
    dreduced, grad_lnr_gain, grad_lnr_bias = lnr_back(dxr)
    drb = dreduced.astype(jnp.bfloat16)
    grad_w_reduce = mat(patches.T, drb)
    grad_b_reduce = jnp.sum(drb.astype(jnp.float32), axis=0)
    dpatch = (
        mat(drb, w_reduce.T)
        .reshape(rows // 2, cols // 2, 2, 2, width)
        .transpose(0, 2, 1, 3, 4)
        .reshape(tokens, width)
    )
    dxm, grad_ln1_gain, grad_ln1_bias = first_norm_backward(dn1_query + dpatch)
    grad_whole = (dxm + dh1) * maskf
    grad_input = lax.dynamic_slice_in_dim(grad_whole, part * share, share, 1)
    (
        grad_w_reduce,
        grad_b_reduce,
        grad_lnr_gain,
        grad_lnr_bias,
        grad_ln1_gain,
        grad_ln1_bias,
        shared_gain,
        shared_bias,
        grad_b_out,
        grad_b_fc2,
        grad_w_fc1,
        grad_b_fc1,
        grad_w_depth,
        grad_b_depth,
        grad_w_fc2,
    ) = lax.psum(
        (
            grad_w_reduce,
            grad_b_reduce,
            grad_lnr_gain,
            grad_lnr_bias,
            grad_ln1_gain,
            grad_ln1_bias,
            shared_gain,
            shared_bias,
            grad_b_out,
            grad_b_fc2,
            grad_w_fc1,
            grad_b_fc1,
            grad_w_depth,
            grad_b_depth,
            grad_w_fc2,
        ),
        "dp",
    )
    (
        grad_w_query,
        grad_b_query,
        grad_w_key,
        grad_w_value,
        grad_b_value,
        output_weight_gradient,
        split_gain,
        split_bias,
    ) = lax.psum(
        (
            spread_columns(grad_wq, select_where),
            spread_vector(grad_bq, select_where),
            spread_columns(grad_wk, select_where),
            spread_columns(grad_wv, select_where),
            spread_vector(grad_bv, select_where),
            spread_rows(grad_wo, select_where),
            split_gain,
            split_bias,
        ),
        ("dp", "mp"),
    )
    grad_ln2_gain = shared_gain + split_gain
    grad_ln2_bias = shared_bias + split_bias
    return (
        block_result,
        grad_input,
        grad_ln1_gain,
        grad_ln1_bias,
        grad_w_query,
        grad_b_query,
        grad_w_key,
        grad_w_value,
        grad_b_value,
        grad_w_reduce,
        grad_b_reduce,
        grad_lnr_gain,
        grad_lnr_bias,
        output_weight_gradient,
        grad_b_out,
        grad_ln2_gain,
        grad_ln2_bias,
        grad_w_fc1,
        grad_b_fc1,
        grad_w_depth,
        grad_b_depth,
        grad_w_fc2,
        grad_b_fc2,
    )


BF = jnp.bfloat16
F32 = jnp.float32
LANES = 128
SIDE_SMALL = 64
VMEM_MB = 52


def nn(a, b):
    return lax.dot_general(a, b, (((1,), (0,)), ((), ())), preferred_element_type=F32)


def nt(a, b):
    return lax.dot_general(a, b, (((1,), (1,)), ((), ())), preferred_element_type=F32)


def tn(a, b):
    return lax.dot_general(a, b, (((0,), (0,)), ((), ())), preferred_element_type=F32)


def iota(shape, axis):
    return lax.broadcasted_iota(jnp.int32, shape, axis)


def hot(cond):
    return jnp.where(cond, 1.0, 0.0).astype(BF)


def spread(value):
    mean = jnp.sum(value, axis=-1, keepdims=True) * (1.0 / value.shape[-1])
    centred = value - mean
    var = jnp.sum(centred * centred, axis=-1, keepdims=True) * (1.0 / value.shape[-1])
    rstd = lax.rsqrt(var + EPS)
    return centred * rstd, rstd


def norm_back(dn, gain, xhat, rstd):
    e = dn * gain
    scale = 1.0 / dn.shape[-1]
    mean_e = jnp.sum(e, axis=-1, keepdims=True) * scale
    mean_ex = jnp.sum(e * xhat, axis=-1, keepdims=True) * scale
    return rstd * (e - mean_e - xhat * mean_ex)


def rowsum(value):
    return jnp.sum(value, axis=0, keepdims=True)


class Sizes:
    def __init__(self, n_dp, n_mp, tokens, width, hidden):
        self.n_dp, self.n_mp = n_dp, n_mp
        self.tokens, self.width, self.hidden = tokens, width, hidden
        self.share = width // n_mp
        self.rows = FRAME // TILE_ROWS
        self.cols = tokens // self.rows
        self.pa, self.pb = self.rows // 2, self.cols // 2
        self.keys = self.pa * self.pb
        self.plane = -(-self.keys // 16) * 16
        self.all = 4 * self.plane
        self.step = self.plane // 16 // n_mp * 16
        self.quarter = self.plane - (n_mp - 1) * self.step
        self.wide = -(-width // LANES) * LANES
        self.kvrows = self.plane + self.quarter
        self.top = 8 + self.pb
        self.ext = self.top + self.keys + self.pb
        self.edge = 4 * 2 * self.pb
        self.edge_q = -(-self.edge // LANES) * LANES
        self.queries = -(-4 * self.keys // LANES) * LANES
        self.echunk = (width + hidden) // n_dp
        self.prows = -(-(2 * self.plane + self.plane // 2) // 16) * 16
        self.wrows = 2 * width + width // 2
        self.l2rows = -(-(self.wrows + self.share) // (16 * n_dp)) * 16 * n_dp
        self.orows = HEAD_FEATURES + HEAD_FEATURES // n_mp
        self.l1rows = -(-(2 * width + 2 * self.orows + self.orows // 2) // (16 * n_dp)) * 16 * n_dp


class Load:
    def __init__(self, src, dst, sem):
        self.dst, self.shape, self.waiting = dst, dst.shape, True
        self.copy = pltpu.make_async_copy(src, dst, sem)
        self.copy.start()

    def ready(self):
        if self.waiting:
            self.waiting = False
            self.copy.wait()
        return self.dst

    def __getitem__(self, at):
        return self.ready()[at]


def fused_body(
    sz, names,
    mask_ref, slot_ref, *refs,
):
    ins, refs = refs[:23], refs[23:]
    outs, refs = refs[:7], refs[7:]
    s = dict(zip(names, refs))
    blk_ref, gp_ref, eg_ref, lg1_ref, lg2_ref, veg_ref, vlg_ref = outs
    D, HF, PB, PA, KEYS, PL, T = sz.width, HEAD_FEATURES, sz.pb, sz.pa, sz.keys, sz.plane, sz.all
    C, FS, W = sz.hidden, sz.share, sz.wide
    d = lax.axis_index("dp")
    m = lax.axis_index("mp")
    last = sz.n_mp * HF
    ssem, rsem = s["ssem"], s["rsem"]

    def mpx(k):
        if k == 0:
            return m
        if k == 1:
            return m + 1 - 2 * lax.rem(m, 2)
        if k == 2:
            return lax.rem(m + 2, 4)
        return 3 - m

    def dpx(k):
        z, x = d // 2, lax.rem(d, 2)
        if k & 1:
            x = 1 - x
        kz = k >> 1
        if kz == 1:
            z = z + 1 - 2 * lax.rem(z, 2)
        elif kz == 2:
            z = lax.rem(z + 2, 4)
        elif kz == 3:
            z = 3 - z
        return 2 * z + x

    counter = [0]
    pending = []

    def take(n):
        first = counter[0]
        counter[0] += n
        return first

    def copy(src, dst, sem, dev):
        return pltpu.make_async_remote_copy(
            src_ref=src, dst_ref=dst, send_sem=ssem.at[sem], recv_sem=rsem.at[sem],
            device_id=dev, device_id_type=pl.DeviceIdType.MESH,
        )

    def send(src, dst, sem, dev):
        c = copy(src, dst, sem, dev)
        c.start()
        pending.append(c)

    def drain(keep=0):
        while len(pending) > keep:
            pending.pop(0).wait_send()

    def arrived(ref, sem):
        copy(ref, ref, sem, (d, m)).wait_recv()

    opened = []

    def handle(finish):
        state = [False]

        def once(*a):
            if not state[0]:
                state[0] = True
                return finish(*a)

        opened.append(once)
        return once

    def mp_start(buf):
        base = take(3)
        send(buf.at[m], buf.at[m], base, (d, mpx(1)))
        send(buf.at[m], buf.at[m], base + 1, (d, mpx(2)))

        def middle():
            arrived(buf.at[mpx(2)], base + 1)
            send(buf.at[mpx(2)], buf.at[mpx(2)], base + 2, (d, mpx(1)))

        mid = handle(middle)

        def finish():
            mid()
            arrived(buf.at[mpx(1)], base)
            arrived(buf.at[mpx(3)], base + 2)

        return handle(finish), mid

    def dp_start(buf, each=lambda k: None):
        base = take(7)
        for kz in (3, 2, 1):
            send(buf.at[d], buf.at[d], base + kz, (dpx(2 * kz), m))
        send(buf.at[d], buf.at[d], base, (dpx(1), m))

        def along(kz):
            arrived(buf.at[dpx(2 * kz)], base + kz)
            send(buf.at[dpx(2 * kz)], buf.at[dpx(2 * kz)], base + 3 + kz, (dpx(1), m))
            each(2 * kz)

        def across(kz):
            arrived(buf.at[dpx(2 * kz + 1)], base + 3 + kz if kz else base)
            each(2 * kz + 1)

        steps = [handle(lambda kz=kz: along(kz)) for kz in (1, 2, 3)]
        steps += [handle(lambda kz=kz: across(kz)) for kz in range(4)]

        def mid():
            for step in steps[:4]:
                step()

        def finish():
            for step in steps:
                step()

        return handle(finish), mid, steps

    def dp_pick(buf, chosen, out, came):
        base = take(4)
        z = d // 2
        for kz in (3, 2, 1):
            send(buf.at[z], buf.at[z], base + kz, (dpx(2 * kz), m))

        def middle():
            for kz in (1, 2, 3):
                arrived(buf.at[dpx(2 * kz) // 2], base + kz)
            out[...] = chosen(*beside(dpx(1)))
            send(out, came, base, (dpx(1), m))

        mid = handle(middle)

        def finish():
            mid()
            arrived(came, base)

        return handle(finish), mid

    def mp_scatter(block, dst, landed):
        base = take(4)
        for k in (2, 3, 1):
            send(block(mpx(k)), dst(k), base + k, (d, mpx(k)))

        def finish():
            for k in (1, 2, 3):
                arrived(landed(k), base + k)

        return handle(finish)

    def dp_scatter(block, dst, landed):
        base = take(8)
        for k in (6, 7, 4, 5, 2, 3, 1):
            send(block(dpx(k)), dst(k), base + k, (dpx(k), m))

        def finish():
            for k in range(1, sz.n_dp):
                arrived(landed(k), base + k)

        return handle(finish)

    def mp_sum(block, out, near, far):
        base = take(3)
        out[0] = block(mpx(1)).astype(BF)
        send(out.at[0], near.at[0], base, (d, mpx(1)))
        out[1] = block(mpx(3)).astype(BF)
        send(out.at[1], near.at[1], base + 1, (d, mpx(1)))

        def middle():
            value = block(mpx(2))
            arrived(near.at[1], base + 1)
            out[2] = (value + near[1].astype(F32)).astype(BF)
            send(out.at[2], far, base + 2, (d, mpx(2)))

        mid = handle(middle)

        def finish():
            mid()
            value = block(m)
            arrived(near.at[0], base)
            value = value + near[0].astype(F32)
            arrived(far, base + 2)
            return value + far[...].astype(F32)

        return mid, handle(finish)

    def dp_sum(chunk, near, out, far):
        base = take(8)
        for kz in (2, 3, 1, 0):
            send(chunk(dpx(2 * kz + 1)), near.at[kz], base + kz, (dpx(1), m))

        def middle():
            for kz in (2, 3, 1):
                value = chunk(dpx(2 * kz))[...].astype(F32)
                arrived(near.at[kz], base + kz)
                out[kz] = (value + near[kz].astype(F32)).astype(BF)
                send(out.at[kz], far.at[kz], base + 4 + kz, (dpx(2 * kz), m))

        mid = handle(middle)

        def finish():
            mid()
            value = chunk(d)[...].astype(F32)
            arrived(near.at[0], base)
            value = value + near[0].astype(F32)
            for kz in (1, 2, 3):
                arrived(far.at[kz], base + 4 + kz)
                value = value + far[kz].astype(F32)
            return value

        return mid, handle(finish)

    def dp_total(src, near, parts):
        base = take(4)
        z = d // 2
        send(src, near, base, (dpx(1), m))

        def middle():
            arrived(near, base)
            parts[z] = src[...] + near[...]
            for kz in (2, 3, 1):
                send(parts.at[z], parts.at[z], base + kz, (dpx(2 * kz), m))

        mid = handle(middle)

        def finish():
            mid()
            for kz in (1, 2, 3):
                arrived(parts.at[dpx(2 * kz) // 2], base + kz)
            return (parts[0] + parts[1]) + (parts[2] + parts[3])

        return mid, handle(finish)

    peers = [(d, mpx(k)) for k in (1, 2, 3)] + [(dpx(k), m) for k in range(1, 8)]
    bar = pltpu.get_barrier_semaphore()
    for dev in peers:
        pl.semaphore_signal(bar, inc=1, device_id=dev, device_id_type=pl.DeviceIdType.MESH)

    order = (0, 1, 2, 3, 8, 7, 9, 10, 11, 12, 4, 5, 6, 21, 22, 13, 14, 15, 16, 17, 18, 19, 20)
    loads = [None] * 23
    for i in order:
        dst = s["xt"].at[m] if i == 0 else s["in%d" % i]
        loads[i] = Load(ins[i], dst, s["isem"].at[i])
    (
        pix_ref, cot_ref, ln1g_ref, ln1b_ref, wq_ref, bq_ref, wk_ref, wv_ref, bv_ref, wr_ref, br_ref,
        lnrg_ref, lnrb_ref, wo_ref, bo_ref, ln2g_ref, ln2b_ref, w1_ref, b1_ref, wd_ref, bd_ref, w2_ref, b2_ref,
    ) = loads

    side = jnp.where(mask_ref[sz.cols - 1] > 0, FRAME, SIDE_SMALL)
    tile = slot_ref[1, d]
    tiles = [slot_ref[1, k] for k in range(sz.n_dp)]

    def beside(at):
        t = slot_ref[1, at]
        up = sum(jnp.where(tiles[k] == t - 1, k, 0) for k in range(sz.n_dp))
        down = sum(jnp.where(tiles[k] == t + 1, k, 0) for k in range(sz.n_dp))
        return up, down

    above, below = beside(d)

    def same_x(j):
        return lax.rem(j, 2) == lax.rem(d, 2)

    def place(p, count):
        a = sum(jnp.where(p >= PB * k, 1, 0) for k in range(1, count))
        return a, p - PB * a

    def token_mask(i, j):
        p = iota((PL, 1), 0)
        a, b = place(p, PA)
        inside = (p < KEYS) & (sz.rows * tile + 2 * a + i < side) & (2 * b + j < side)
        return jnp.where(inside, 1.0, 0.0)

    def row_mask(i, j, a):
        b = iota((PB, 1), 0)
        row = sz.rows * tile + 2 * a + i
        inside = (row >= 0) & (row < side) & (2 * b + j < side)
        return jnp.where(inside, 1.0, 0.0)

    def key_bias(p, tile_at):
        a, b = place(p, PA)
        usable = (p < KEYS) & (sz.rows * tile_at + 2 * a < side) & (2 * b < side)
        return jnp.where(usable, 0.0, NEG)

    def vec(ref):
        return ref[...].reshape(1, ref.shape[0])

    def own_part(row, size):
        return sum(
            jnp.where(m == h, 1.0, 0.0) * row[:, size * h : size * (h + 1)] for h in range(sz.n_mp)
        )

    def plane_rows(ref, start):
        return ref[pl.ds(pl.multiple_of(start, 16), PL), :]

    def plane(p):
        return slice(PL * p, PL * (p + 1))

    lanes3 = (s["t0"], s["t1"], s["t2"])

    def to_planes(rows_of):
        for n, ref in enumerate(lanes3):
            ref[...] = rows_of(LANES * n, min(D, LANES * (n + 1))).astype(F32).T
        for i in range(2):
            for j in range(2):
                parts = []
                for ref in lanes3:
                    rows = [
                        ref[pl.ds((2 * a + i) * sz.cols + j, PB, stride=2), :] for a in range(PA)
                    ] + [jnp.zeros((PL - KEYS, ref.shape[1]), F32)]
                    parts.append(jnp.concatenate(rows, axis=0))
                yield i, j, jnp.concatenate(parts, axis=1)

    def from_queries(rows, p):
        n = rows.shape[1]
        return jnp.concatenate([rows[KEYS * p : KEYS * (p + 1)], jnp.zeros((PL - KEYS, n), F32)], axis=0)

    def to_queries(planes):
        n = planes[0].shape[1]
        rows = [v[0:KEYS] for v in planes]
        return jnp.concatenate(rows + [jnp.zeros((sz.queries - 4 * KEYS, n), F32)], axis=0)

    xt, dfm = s["xt"], s["dfm"]
    pl.semaphore_wait(bar, len(peers))
    pix_ref.ready()
    x_at, x_mid = mp_start(xt)

    edge, edge_g, EP = s["edge"], s["edge_g"], 4 * PB
    lane_pad = jnp.zeros((FS, sz.edge_q - 2 * EP), BF)
    edge[d // 2] = jnp.concatenate([xt[m, :, 0:EP], xt[m, :, sz.tokens - EP :], lane_pad], axis=1)

    def edge_chosen(up, down):
        return jnp.concatenate([edge[up // 2][:, EP : 2 * EP], edge[down // 2][:, 0:EP], lane_pad], axis=1)

    edge_at, edge_mid = dp_pick(edge, edge_chosen, s["edge_s"], s["edge_x"])

    for i, j, value in to_planes(lambda lo, hi: cot_ref[lo:hi, :]):
        dfm[plane(2 * i + j), :] = (value * token_mask(i, j)).astype(BF)
    dyh, dyh_g = s["dyh"], s["dyh_g"]
    dyh[d // 2, :, :D] = dfm[pl.ds(pl.multiple_of(PL * m + (KEYS - PB) * (m // 2), 16), 48), :]
    dyh[d // 2, :, D:] = jnp.zeros((48, W - D), BF)
    x_mid()

    r2, c2 = iota((D, LANES), 0), iota((D, LANES), 1)
    own_lo = hot((c2 < HF) & (r2 == HF * m + c2))
    own_hi = hot((c2 >= HF) & (r2 == HF * m + c2 - HF))
    last_lo = hot((c2 < HF) & (r2 == last + c2))
    last_hi = hot((c2 >= HF) & (r2 == last + c2 - HF))
    wq, wk, wv = wq_ref[...], wk_ref[...], wv_ref[...]
    wq2 = nn(wq, own_lo + last_hi).astype(BF)
    wkv = (nn(wk, own_lo) + nn(wv, own_hi)).astype(BF)
    wkv5 = (nn(wk, last_lo) + nn(wv, last_hi)).astype(BF)
    bq, bv = vec(bq_ref), vec(bv_ref)
    bq2 = jnp.concatenate([own_part(bq, HF), bq[:, last:]], axis=1)
    nil = jnp.zeros((1, HF), F32)
    bkv = jnp.concatenate([nil, own_part(bv, HF)], axis=1)
    bkv5 = jnp.concatenate([nil, bv[:, last:]], axis=1)
    w2 = w2_ref[...]
    wo_cat = s["wo_cat"]
    wo = wo_ref[...]
    wo_cat[...] = jnp.concatenate(
        [b for h in range(4) for b in (wo[HF * h : HF * (h + 1)], wo[last:])], axis=0
    )
    wr_t = s["wr_t"]
    wr_t[...] = wr_ref[...].T

    xm_r, n1_r = s["xm_r"], s["n1_r"]
    x_at()
    x_all = xt[...].reshape(D, sz.tokens)
    for i, j, value in to_planes(lambda lo, hi: x_all[lo:hi, :]):
        xm = value * token_mask(i, j)
        xm_r[plane(2 * i + j), :] = xm.astype(BF)
        xhat, _ = spread(xm)
        n1_r[plane(2 * i + j), :] = (xhat * vec(ln1g_ref) + vec(ln1b_ref)).astype(BF)

    kva, xr_r = s["kva"], s["xr_r"]
    red = sum(nn(n1_r[plane(p), :], wr_t[D * p : D * (p + 1), :]) for p in range(4)) + vec(br_ref)
    xhr, rsr = spread(red)
    s["xhr_r"][...] = xhr
    s["rsr_r"][...] = jnp.broadcast_to(rsr, (PL, LANES))
    xr_r[...] = (xhr * vec(lnrg_ref) + vec(lnrb_ref)).astype(BF)
    kva[d, 0:PL, :] = (nn(xr_r[...], wkv) + bkv).astype(BF)
    quarter_rows = pl.ds(pl.multiple_of(sz.step * m, 16), sz.quarter)
    kva[d, PL:, :] = (nn(xr_r[quarter_rows, :], wkv5) + bkv5).astype(BF)
    _, _, kv_steps = dp_start(kva)
    edge_mid()

    def dy_chosen(up, down):
        return dyh[jnp.where(m >= 2, up, down) // 2]

    dy_at, dy_mid = dp_pick(dyh, dy_chosen, s["dyh_s"], s["dyh_x"])

    qa_r, qb_r, qc_r, qd_r = s["qa_r"], s["qb_r"], s["qc_r"], s["qd_r"]
    Q = sz.queries

    def feature_major(q_rows, own_r, last_r):
        q2t = q_rows.T
        nil = jnp.zeros((HF, q2t.shape[1]), F32)
        own_r[...] = jnp.concatenate([q2t[0:HF], nil], axis=0).astype(BF)
        last_r[...] = jnp.concatenate([q2t[HF:], nil], axis=0).astype(BF)

    def query(rows):
        return (nn(rows, wq2) + bq2).astype(BF).astype(F32) * HF ** (-0.5)

    q2 = query(n1_r[...])
    feature_major(to_queries([q2[plane(p)] for p in range(4)]), qa_r, qb_r)
    half = jnp.zeros((HF, Q), F32)

    e5buf, ebuf, ot_r = s["e5buf"], s["ebuf"], s["ot_r"]
    limit5 = jnp.where(m == sz.n_mp - 1, KEYS - sz.step * m, sz.step)
    pk, pk5 = iota((PL, 1), 0), iota((sz.quarter, 1), 0)

    def attend(ks, rows, q_r, bias_of, ebuf, o_r):
        js = [dpx(k) for k in ks]
        n = rows.stop - rows.start
        kv = jnp.concatenate([kva[j, rows, :] for j in js], axis=0)
        bias = jnp.concatenate([bias_of(j) for j in js], axis=0)
        v = nn(kv, q_r[...]) + bias
        top = jnp.max(v, axis=0, keepdims=True)
        e = jnp.exp(v - top).astype(BF)
        if ebuf is not None:
            for q, j in enumerate(js):
                ebuf[j] = e[n * q : n * (q + 1)]
        o_r[ks[0]] = tn(kv, e)[HF:]
        return ks, top, rowsum(e.astype(F32))

    def bias_own(j):
        return key_bias(pk, slot_ref[1, j])

    def bias_last(j):
        return jnp.where(pk5 < limit5, key_bias(pk5 + sz.step * m, slot_ref[1, j]), NEG)

    own, five, own_h, five_h = [], [], [], []
    ROWS, LAST = slice(0, PL), slice(PL, sz.kvrows)

    def block(*ks):
        own.append(attend(ks, ROWS, qa_r, bias_own, ebuf, s["o_own"]))
        five.append(attend(ks, LAST, qb_r, bias_last, e5buf, s["o_five"]))

    def block_h(*ks):
        own_h.append(attend(ks, ROWS, qc_r, bias_own, None, s["oh_own"]))
        five_h.append(attend(ks, LAST, qd_r, bias_last, None, s["oh_five"]))

    block(0)
    edge_at()
    up = jnp.where(
        same_x(above), edge[above // 2][:, EP : 2 * EP].astype(F32), s["edge_x"][:, 0:EP].astype(F32)
    )
    down = jnp.where(
        same_x(below), edge[below // 2][:, 0:EP].astype(F32), s["edge_x"][:, EP : 2 * EP].astype(F32)
    )
    edge_g[m] = jnp.concatenate([up, down, lane_pad.astype(F32)], axis=1).astype(BF)
    edgeg_at, edgeg_mid = mp_start(edge_g)
    kv_steps[3]()
    kv_steps[0]()
    edgeg_mid()
    block(1, 2)
    kv_steps[1]()
    kv_steps[2]()
    block(4, 6)
    edgeg_at()

    xh_r = s["xh_r"]
    e_all = edge_g[...].reshape(D, sz.edge_q)
    for n, ref in enumerate(lanes3):
        ref[0 : sz.edge_q, :] = e_all[LANES * n : min(D, LANES * (n + 1))].astype(F32).T
    rows = []
    for i in range(2):
        for j in range(2):
            for a, first in ((-1, 0), (PA, EP)):
                at = pl.ds(first + sz.cols * i + j, PB, stride=2)
                value = jnp.concatenate([ref[at, :] for ref in lanes3], axis=1)
                rows.append(value * row_mask(i, j, a))
    xh = jnp.concatenate(rows, axis=0)
    xh_r[...] = xh.astype(BF)
    xhat, _ = spread(xh)
    q2 = query((xhat * vec(ln1g_ref) + vec(ln1b_ref)).astype(BF))
    q2 = jnp.concatenate([q2, jnp.zeros((sz.edge_q - sz.edge, LANES), F32)], axis=0)
    feature_major(q2, qc_r, qd_r)
    block_h(0, 1, 2, 4, 6)
    kv_steps[4]()
    kv_steps[5]()
    block(3, 5)
    block_h(3, 5)
    kv_steps[6]()
    block(7)
    block_h(7)

    def joined(parts, o_r):
        top = functools.reduce(jnp.maximum, [t for _, t, _ in parts])
        scale = [jnp.exp(t - top) for _, t, _ in parts]
        total = sum(f * n for f, (_, _, n) in zip(scale, parts))
        inv = 1.0 / total
        scale = [f * inv for f in scale]
        out = sum(f * o_r[ks[0]] for f, (ks, _, _) in zip(scale, parts))
        return top + jnp.log(total), {k: f for f, (ks, _, _) in zip(scale, parts) for k in ks}, out

    lse_r, LR = s["lse_r"], (Q + sz.edge_q) // LANES
    lse5, scale5, o5_t = joined(five, s["o_five"])
    lse5h, _, o5h_t = joined(five_h, s["oh_five"])
    flat = [lse5[:, LANES * n : LANES * (n + 1)] for n in range(Q // LANES)]
    flat += [lse5h[:, LANES * n : LANES * (n + 1)] for n in range(sz.edge_q // LANES)]
    lse_r[m] = jnp.concatenate(flat + [jnp.zeros((16 - LR, LANES), F32)], axis=0)
    lse_at = mp_scatter(lambda h: lse_r.at[m], lambda k: lse_r.at[m], lambda k: lse_r.at[mpx(k)])
    _, scale, o_t = joined(own, s["o_own"])
    o2 = jnp.concatenate([o_t, o5_t], axis=0).T.astype(BF)
    chunks = ((s["og_a"], s["ow_a"]), (s["og_b"], s["ow_b"]), (s["og_c"], s["ow_c"]))
    ogs = []
    for n in range(2):
        og = chunks[n][0]
        og[m] = o2[2 * KEYS * n : 2 * KEYS * (n + 1)]
        ogs.append(mp_start(og))
    _, _, oh_t = joined(own_h, s["oh_own"])
    s["og_c"][m] = jnp.concatenate([oh_t, o5h_t], axis=0).T[0 : sz.edge].astype(BF)
    ogs.append(mp_start(s["og_c"]))
    drain(12)
    rt, ct = iota((D, 4 * LANES), 0), iota((D, 4 * LANES), 1)
    lane4, head4 = ct & (LANES - 1), ct >> 7
    place_out = hot((lane4 < FS) & (rt == FS * head4 + lane4))
    rk, ck = iota((D, 5 * LANES), 0), iota((D, 5 * LANES), 1)
    lane5, head5 = ck & (LANES - 1), ck >> 7
    w_all, wq_cat, w2_t = s["w_all"], s["wq_cat"], s["w2_t"]
    w_all[...] = (
        nn(wk, hot((lane5 < HF) & (rk == HF * head5 + lane5)))
        + nn(wv, hot((lane5 >= HF) & (rk == HF * head5 + lane5 - HF)))
    ).astype(BF)
    wq_cat[...] = nn(
        wq, hot(rt == jnp.where(lane4 < HF, HF * head4 + lane4, last + lane4 - HF))
    ).astype(BF)
    w2_t[...] = w2.T
    dgx, dzx = s["dgx"], s["dzx"]
    for p in range(4):
        dgx[p, sz.top : sz.top + PL, :] = nt(dfm[plane(p), :], w2).astype(BF).astype(F32)
    dy_mid()

    lse_at()
    lse4 = [
        jnp.concatenate([lse_r[h][n : n + 1] for n in range(LR)], axis=1) for h in range(4)
    ]
    top = functools.reduce(jnp.maximum, lse4)
    whole = top + jnp.log(sum(jnp.exp(v - top) for v in lse4))
    share_all = jnp.exp(jnp.concatenate(lse4 + [jnp.zeros((4, Q + sz.edge_q), F32)], axis=0) - whole).T
    share = jnp.exp(lse5 - whole[:, 0:Q])

    def weighed(n, first):
        og, ow = chunks[n]
        rows = og.shape[1]
        lane = iota((rows, LANES), 1)
        ogs[n][0]()
        for h in range(4):
            part = share_all[first : first + rows, h : h + 1]
            ow[h] = (og[h].astype(F32) * jnp.where(lane < HF, 1.0, part)).astype(BF)
        oc = jnp.concatenate([ow[h] for h in range(4)], axis=1)
        return nn(oc, wo_cat[...]) + vec(bo_ref)

    h1_r, n2_r = s["h1_r"], s["n2_r"]

    def second_norm(h1):
        xhat, _ = spread(h1)
        return (xhat * vec(ln2g_ref) + vec(ln2b_ref)).astype(BF)

    w1, b1 = w1_ref[...], vec(b1_ref)

    def hidden(rows, mask):
        return ((nn(rows, w1) + b1) * mask).astype(BF).astype(F32)

    ux, ul, ur, dzl, dzr = s["ux"], s["ul"], s["ur"], s["dzl"], s["dzr"]
    b40 = iota((PB, 1), 0)

    def shift(src, left, right, i, start):
        at = slice(start, start + PB)
        left[i, at, :] = jnp.where(b40 == 0, 0.0, pltpu.roll(src[2 * i + 1, at, :], 1, 0))
        right[i, at, :] = jnp.where(b40 == PB - 1, 0.0, pltpu.roll(src[2 * i, at, :], PB - 1, 0))

    for n in range(2):
        mixed = weighed(n, 2 * KEYS * n)
        ogs[n + 1][1]()
        for p in (2 * n, 2 * n + 1):
            mask = token_mask(n, p % 2)
            h1 = xm_r[plane(p), :].astype(F32) + mask * from_queries(mixed, p % 2)
            h1_r[plane(p), :] = h1
            n2_r[plane(p), :] = second_norm(h1)
            ux[p, sz.top : sz.top + PL, :] = hidden(n2_r[plane(p), :], mask)
        for a in range(PA):
            shift(ux, ul, ur, n, sz.top + PB * a)

    wd_ref, bd_row = wd_ref.ready(), vec(bd_ref)
    g_r, du_r = s["g_r"], s["du_r"]
    for p in range(4):
        g_r[p, KEYS:PL, :] = jnp.zeros((PL - KEYS, C), F32)
        du_r[p, KEYS:PL, :] = jnp.zeros((PL - KEYS, C), F32)

    def source(refs, i, j, di, dj, start):
        base, left, right = refs
        i2, up = (i + di) % 2, (i + di) // 2
        j2, across = (j + dj) % 2, (j + dj) // 2
        at = pl.ds(pl.multiple_of(start + PB * up, 8), PB)
        if across < 0:
            return left[i2, at, :]
        if across > 0:
            return right[i2, at, :]
        return base[2 * i2 + j2, at, :]

    TAPS = [(di, dj) for di in (-1, 0, 1) for dj in (-1, 0, 1)]

    def activation(i, j, start):
        p = 2 * i + j
        z = bd_row + sum(
            wd_ref[t : t + 1, :] * source((ux, ul, ur), i, j, di, dj, start)
            for t, (di, dj) in enumerate(TAPS)
        )
        phi = 0.5 * (1.0 + lax.erf(z * 0.7071067811865476))
        dens = jnp.exp(-0.5 * z * z) * 0.3989422804014327
        dz = dgx[p, pl.ds(pl.multiple_of(start, 8), PB), :] * (phi + z * dens)
        dzx[p, pl.ds(pl.multiple_of(start, 8), PB), :] = dz
        return z * phi, dz

    def fold(value):
        return jnp.sum(value.reshape(PB // 8, 8, C), axis=0)

    def forward_step(i, j):
        p = 2 * i + j

        def step(a, acc):
            start = sz.top + PB * a
            act, dz = activation(i, j, start)
            g_r[p, pl.ds(pl.multiple_of(PB * a, 8), PB), :] = act
            new = [
                acc[t] + fold(dz * source((ux, ul, ur), i, j, di, dj, start))
                for t, (di, dj) in enumerate(TAPS)
            ]
            return tuple(new) + (acc[9] + fold(dz),)

        return step

    dy_at()
    beside_j = jnp.where(m >= 2, above, below)
    dyh_g[m] = jnp.where(
        same_x(beside_j), dyh[beside_j // 2].astype(F32), s["dyh_x"][...].astype(F32)
    ).astype(BF)
    dyg_at, dyg_mid = mp_start(dyh_g)

    sums = tuple(jnp.zeros((8, C), F32) for _ in range(10))
    for i in range(2):
        for j in range(2):
            sums = lax.fori_loop(1 - i, PA - i, forward_step(i, j), sums)
    for i in range(2):
        for a in range(1, PA):
            shift(dzx, dzl, dzr, i, sz.top + PB * (a - i))

    def backward_step(i, j):
        p = 2 * i + j

        def step(a, carry):
            start = sz.top + PB * a
            du_r[p, pl.ds(pl.multiple_of(PB * a, 8), PB), :] = sum(
                wd_ref[t : t + 1, :] * source((dzx, dzl, dzr), i, j, -di, -dj, start)
                for t, (di, dj) in enumerate(TAPS)
            )
            return carry

        return step

    dyg_mid()
    for i in range(2):
        for j in range(2):
            lax.fori_loop(1, PA - 1, backward_step(i, j), 0)
    ot_r[...] = jnp.concatenate([o_t, o5_t * share], axis=0)
    mixed = weighed(2, Q)
    dyg_at()
    for p in range(4):
        i, j = p // 2, p % 2
        start = sz.top - PB if i == 1 else sz.top + KEYS
        rows = dyh_g[p][:, :D].astype(F32)[0:PB] * row_mask(i, j, -1 if i == 1 else PA)
        dgx[p, start : start + PB, :] = nt(rows.astype(BF), w2).astype(BF).astype(F32)
    xh = xh_r[...].astype(F32)
    for p in range(4):
        i, j = p // 2, p % 2
        mask = jnp.concatenate([row_mask(i, j, -1), row_mask(i, j, PA)], axis=0)
        at = slice(2 * PB * p, 2 * PB * (p + 1))
        u = hidden(second_norm(xh[at] + mask * mixed[at]), mask)
        ux[p, sz.top - PB : sz.top, :] = u[0:PB]
        ux[p, sz.top + KEYS : sz.top + KEYS + PB, :] = u[PB:]
    for i in range(2):
        shift(ux, ul, ur, i, sz.top - PB)
        shift(ux, ul, ur, i, sz.top + KEYS)
    for i in range(2):
        for j in range(2):
            activation(i, j, sz.top - PB if i == 1 else sz.top + KEYS)
            sums = forward_step(i, j)((PA - 1) * i, sums)
    e_s, ve_s, vl_s = s["e_s"], s["ve_s"], s["vl_s"]
    shift(dzx, dzl, dzr, 0, sz.top)
    shift(dzx, dzl, dzr, 0, sz.top + KEYS)
    shift(dzx, dzl, dzr, 1, sz.top - PB)
    shift(dzx, dzl, dzr, 1, sz.top + KEYS - PB)
    dub = s["dub"]
    for i in range(2):
        for j in range(2):
            p = 2 * i + j
            for a in (0, PA - 1):
                backward_step(i, j)(a, 0)
            dub[p] = (du_r[p].astype(BF).astype(F32) * token_mask(i, j)).astype(BF)
    def packed(value):
        n = value.shape[0] // 2
        parts = [value[:, 0:LANES], value[:, LANES : 2 * LANES]]
        parts.append(jnp.concatenate([value[0:n, 2 * LANES :], value[n:, 2 * LANES :]], axis=1))
        return jnp.concatenate(parts, axis=0)

    def unpacked(value, rows):
        n = rows // 2
        rest = value[2 * rows : 2 * rows + n]
        rest = jnp.concatenate([rest[:, 0:HF], rest[:, HF:]], axis=0)
        return jnp.concatenate([value[0:rows], value[rows : 2 * rows], rest], axis=1)

    def dn2_block(h):
        value = packed(nt(dub[h], w1))
        rest = jnp.zeros((sz.prows - value.shape[0], LANES), F32)
        return jnp.concatenate([value, rest], axis=0)

    dn2_mid, dn2_at = mp_sum(dn2_block, s["dn2_s"], s["dn2_n"], s["dn2_f"])
    dn2_mid()

    gb = g_r[...].reshape(T, C).astype(BF)
    du_all = dub[...].reshape(T, C)
    e_s[0:D, :C] = tn(n2_r[...], du_all).astype(BF)
    e_s[D:, :D] = tn(gb, dfm[...]).astype(BF)

    def rows_of(ref, n):
        return lambda j: ref.at[pl.ds(pl.multiple_of(n * j, 16), n)]

    e_mid, e_at = dp_sum(rows_of(e_s, sz.echunk), s["e_n"], s["e_o"], s["e_f"])
    for t in range(10):
        ve_s[t : t + 1, :C] = rowsum(sums[t])
    ve_s[10:11, :C] = rowsum(du_all.astype(F32))

    for k in range(sz.n_dp):
        j = dpx(k)
        ebuf[j] = (ebuf[j].astype(F32) * scale[k]).astype(BF)
        e5buf[j] = (e5buf[j].astype(F32) * (scale5[k] * share)).astype(BF)
    ogp = s["ogp"]
    lane = iota((PL, LANES), 1)
    for n, (og, ow) in enumerate(chunks[:2]):
        mine, fifth = og[m].astype(F32), sum(ow[h].astype(F32) for h in range(4))
        for q in range(2):
            ogp[plane(2 * n + q), :] = jnp.where(
                lane < HF, from_queries(mine, q), from_queries(fifth, q)
            ).astype(BF)

    drain(12)

    xhat2, rstd2 = spread(plane_rows(h1_r, PL * m))
    dfp = plane_rows(dfm, PL * m).astype(F32)
    ve_s[11:12, :D] = rowsum(dfp)
    dn2 = unpacked(dn2_at(), PL)
    dh1 = dfp + norm_back(dn2, vec(ln2g_ref), xhat2, rstd2)
    dab = dh1.astype(BF)
    docat = nt(dab, wo_cat[...]).astype(BF)
    dos, do_all, dabg = s["dos"], s["do_all"], s["dabg"]
    for h in range(4):
        dos[h] = docat[:, LANES * h : LANES * (h + 1)]
    do_at = mp_scatter(lambda h: dos.at[h], lambda k: do_all.at[m], lambda k: do_all.at[mpx(k)])
    do_all[m] = dos[m]
    s["dh1_r"][...] = dh1
    dabg[m, :, :D] = dab
    ve_s[12:13, :D] = rowsum(dh1)
    ve_s[13:14, :D] = rowsum(dn2 * xhat2)
    ve_s[14:15, :D] = rowsum(dn2)
    ve_s[15:16, :] = jnp.zeros((1, W), F32)
    ve_mid, ve_at = dp_total(ve_s, s["ve_n"], s["ve_p"])
    e_mid()
    ve_mid()

    def ff_block(h):
        return nt(w2_t[pl.ds(pl.multiple_of(FS * h, 16), FS), :], gb)

    ff_mid, ff_at = mp_sum(ff_block, s["ff_s"], s["ff_n"], s["ff_f"])

    drain(16)
    do_at()
    dr_r = s["dr_r"]
    dot_t = to_queries([do_all[p].astype(F32) for p in range(4)]).T
    dr_r[m] = jnp.broadcast_to(rowsum(dot_t[HF:] * ot_r[HF:, :]), (8, Q))
    dr_at = mp_scatter(lambda h: dr_r.at[m], lambda k: dr_r.at[m], lambda k: dr_r.at[mpx(k)])
    dab_at, dab_mid = mp_start(dabg)
    drow = rowsum(dot_t[0:HF] * ot_r[0:HF, :])
    da_t = jnp.concatenate([half, dot_t[0:HF]], axis=0).astype(BF)
    db_t = jnp.concatenate([half, dot_t[HF:]], axis=0).astype(BF)
    dqt, dqt5 = s["dqt"], s["dqt5"]
    dqt[...] = jnp.zeros_like(dqt)
    dqt5[...] = jnp.zeros_like(dqt5)
    five_row = []

    def key_grads(js, rows, ebuf, q_r, do_t, d_row, dq):
        n = rows.stop - rows.start
        kv = jnp.concatenate([kva[j, rows, :] for j in js], axis=0)
        e = jnp.concatenate([ebuf[j] for j in js], axis=0)
        ds = (e.astype(F32) * (nn(kv, do_t) - d_row)).astype(BF)
        value = nt(ds, q_r[...]) + nt(e, do_t)
        dq[...] += tn(kv, ds)
        return [value[n * q : n * (q + 1)] for q in range(len(js))]

    def own_keys(*ks):
        return key_grads([dpx(k) for k in ks], ROWS, ebuf, qa_r, da_t, drow, dqt)

    def last_keys(*ks):
        return key_grads([dpx(k) for k in ks], LAST, e5buf, qb_r, db_t, five_row[0], dqt5)

    dk_x, dk_n, dk_o, dk_f = s["dk_x"], s["dk_n"], s["dk_o"], s["dk_f"]
    dl_x, dl_n, dl_o, dl_f = s["dl_x"], s["dl_n"], s["dl_o"], s["dl_f"]
    dk_at = take(8)
    dl_at = take(4)
    for pair in ((2, 3), (1, 0)):
        for kz, value in zip(pair, own_keys(*(2 * kz + 1 for kz in pair))):
            dk_x[kz] = value.astype(BF)
            send(dk_x.at[kz], dk_n.at[kz], dk_at + kz, (dpx(1), m))
    dr_at()
    five_row.append(sum(dr_r[h][0:1] for h in range(4)))
    for kz, value in enumerate(last_keys(1, 3, 5, 7)):
        dl_x[kz] = value.astype(BF)
    send(dl_x, dl_n, dl_at, (dpx(1), m))
    dab_mid()

    def dk_along(kz, value):
        arrived(dk_n.at[kz], dk_at + kz)
        dk_o[kz] = (value + dk_n[kz].astype(F32)).astype(BF)
        send(dk_o.at[kz], dk_f.at[kz], dk_at + 4 + kz, (dpx(2 * kz), m))

    for kz, value in zip((2, 3), own_keys(4, 6)):
        dk_along(kz, value)
    ff_mid()
    value, dkv = own_keys(2, 0)
    dk_along(1, value)
    dkl, *values = last_keys(0, 2, 4, 6)
    arrived(dl_n, dl_at)
    for kz in (2, 3, 1):
        dl_o[kz] = (values[kz - 1] + dl_n[kz].astype(F32)).astype(BF)
        send(dl_o.at[kz], dl_f.at[kz], dl_at + kz, (dpx(2 * kz), m))

    def dk_finish():
        arrived(dk_n.at[0], dk_at)
        total, last = dkv + dk_n[0].astype(F32), dkl + dl_n[0].astype(F32)
        for kz in (1, 2, 3):
            arrived(dk_f.at[kz], dk_at + 4 + kz)
            total = total + dk_f[kz].astype(F32)
        for kz in (1, 2, 3):
            arrived(dl_f.at[kz], dl_at + kz)
            last = last + dl_f[kz].astype(F32)
        return jnp.concatenate([total, last], axis=0)

    dk_fin = handle(dk_finish)

    dq2 = (jnp.concatenate([dqt[0:HF], dqt5[0:HF]], axis=0) * HF ** (-0.5)).T
    dqs, dq_all = s["dqs"], s["dq_all"]
    for h in range(4):
        dqs[h] = from_queries(dq2, h).astype(BF)
    dq_at = mp_scatter(lambda h: dqs.at[h], lambda k: dq_all.at[m], lambda k: dq_all.at[mpx(k)])
    dq_all[m] = dqs[m]
    eg_ref[d] = e_at().astype(BF)
    eg_at, eg_mid, _ = dp_start(eg_ref)
    l1_s, l2_s = s["l1_s"], s["l2_s"]
    dqp = dqs[...].reshape(T, LANES)
    l1_s[0:D, :] = tn(n1_r[...], dqp).astype(BF)
    vl_s[...] = jnp.zeros_like(vl_s)
    vl_s[5:6, 0:LANES] = rowsum(dqp.astype(F32))

    def fill(ref, first, value):
        rest = jnp.zeros((ref.shape[0] - first - value.shape[0], LANES), F32)
        ref[first:, :] = jnp.concatenate([value, rest], axis=0).astype(BF)

    def own_rows(value, n):
        return sum(jnp.where(m == h, 1.0, 0.0) * value[n * h : n * (h + 1)] for h in range(4))

    dab_at()
    gwo = tn(ogp[...], dabg[...].reshape(T, W)[:, :D])
    fill(l1_s, 2 * D, packed(jnp.concatenate([gwo[0:HF], own_rows(gwo[HF:], HF // 4)], axis=0)))

    dkvb = dk_fin().astype(BF)
    dkvg = s["dkvg"]
    dkvg[m] = dkvb
    dkv_at, dkv_mid = mp_start(dkvg)
    l1_s[D : 2 * D, :] = tn(xr_r[...], dkvb[0:PL]).astype(BF)
    l1_mid, l1_at = dp_sum(rows_of(l1_s, sz.l1rows // sz.n_dp), s["l1_n"], s["l1_o"], s["l1_f"])
    vl_s[6:7, 0:LANES] = jnp.concatenate(
        [rowsum(dkvb[0:PL].astype(F32))[:, HF:], rowsum(dkvb[PL:].astype(F32))[:, HF:]], axis=1
    )
    dq_at()
    dq_cat = jnp.concatenate([dq_all[h] for h in range(4)], axis=1)
    dn1 = nt(dq_cat, wq_cat[...])
    xhat1, rstd1 = spread(plane_rows(xm_r, PL * m).astype(F32))
    drain(12)
    dkv_mid()
    dkv_at()
    l1_mid()
    rest = jnp.concatenate(
        [dkvg[h, PL : PL + sz.step, :] for h in range(3)] + [dkvg[3, PL:, :]], axis=0
    )
    dkv_all = jnp.concatenate([dkvg[h, 0:PL, :] for h in range(4)] + [rest], axis=1)
    dxr = nt(dkv_all, w_all[...])
    xhr = s["xhr_r"][...]
    drb = norm_back(dxr, vec(lnrg_ref), xhr, s["rsr_r"][:, 0:1]).astype(BF)
    l2_s[0 : sz.wrows, :] = packed(tn(drb, plane_rows(n1_r, PL * m))).astype(BF)
    fill(l2_s, sz.wrows, own_rows(tn(xr_r[...], rest), FS))
    l2_mid, l2_at = dp_sum(rows_of(l2_s, sz.l2rows // sz.n_dp), s["l2_n"], s["l2_o"], s["l2_f"])
    vl_s[2:3, :D] = rowsum(dxr * xhr)
    vl_s[3:4, :D] = rowsum(dxr)
    vl_s[4:5, :D] = rowsum(drb.astype(F32))

    wr_m = wr_t[pl.ds(pl.multiple_of(D * m, 16), D), :]
    dn1 = dn1 + nt(drb, wr_m)
    vl_s[0:1, :D] = rowsum(dn1 * xhat1)
    vl_s[1:2, :D] = rowsum(dn1)
    vl_mid, vl_at = dp_total(vl_s, s["vl_n"], s["vl_p"])
    dxm = norm_back(dn1, vec(ln1g_ref), xhat1, rstd1)
    gp = (token_mask(m // 2, lax.rem(m, 2)) * (s["dh1_r"][...] + dxm)).astype(BF)
    gpf = nn(gp, place_out).astype(BF)
    gps = s["gps"]
    for h in range(4):
        gps[h] = gpf[:, LANES * h : LANES * (h + 1)]
    gp_at = mp_scatter(lambda h: gps.at[h], lambda k: gp_ref.at[m], lambda k: gp_ref.at[mpx(k)])
    gp_ref[m] = gps[m]

    veg_ref[m] = ve_at()
    veg_at, _ = mp_start(veg_ref)

    def gather(buf):
        base = take(3 * sz.n_dp)

        def onward(k):
            j = dpx(k)
            send(buf.at[m, j], buf.at[m, j], base + 3 * k, (d, mpx(1)))
            send(buf.at[m, j], buf.at[m, j], base + 3 * k + 1, (d, mpx(2)))

        near, mid, steps = dp_start(buf.at[m], onward)
        onward(0)
        seq = (0, 2, 4, 6, 1, 3, 5, 7)

        def relay(k):
            j = dpx(k)
            arrived(buf.at[mpx(2), j], base + 3 * k + 1)
            send(buf.at[mpx(2), j], buf.at[mpx(2), j], base + 3 * k + 2, (d, mpx(1)))

        relays = [handle(lambda k=k: relay(k)) for k in seq]

        def finish():
            near()
            for r in relays:
                r()
            for k in seq:
                arrived(buf.at[mpx(1), dpx(k)], base + 3 * k)
                arrived(buf.at[mpx(3), dpx(k)], base + 3 * k + 2)

        return near, mid, relays, handle(finish)

    drain(12)
    lg1_ref[m, d] = l1_at().astype(BF)
    near1, mid1, relays1, lg1_at = gather(lg1_ref)
    l2_mid()
    vl_mid()
    eg_mid()
    ff = ff_at().T
    ff = jnp.concatenate([ff, jnp.zeros((T, LANES - FS), F32)], axis=1)
    sel = hot((c2 < FS) & (r2 == FS * m + c2))
    b2q = jnp.concatenate(
        [own_part(vec(b2_ref), FS), jnp.zeros((1, LANES - FS), F32)], axis=1
    )
    for p in range(4):
        h1 = h1_r[plane(p), :]
        hi = h1.astype(BF)
        h1q = nn(hi, sel) + nn((h1 - hi.astype(F32)).astype(BF), sel)
        blk_ref[plane(p), :] = h1q + token_mask(p // 2, p % 2) * (ff[plane(p)] + b2q)
    mid1()
    drain(24)
    lg2_ref[m, d] = l2_at().astype(BF)
    near2, mid2, relays2, lg2_at = gather(lg2_ref)
    near1()
    vlg_ref[m] = vl_at()
    vlg_at, _ = mp_start(vlg_ref)
    for r in relays1[:4]:
        r()
    drain(16)
    mid2()
    for r in relays1[4:]:
        r()
    drain(24)
    near2()
    drain(16)
    for r in relays2:
        r()
        drain(16)
    eg_at()
    gp_at()
    veg_at()
    lg1_at()
    vlg_at()
    lg2_at()
    drain()


def unpack_body(sz, *refs):
    srcs, refs = refs[:7], refs[7:]
    dsts, refs = refs[:23], refs[23:]
    (
        out_ref, gpix_ref, ln1g_ref, ln1b_ref, gwq_ref, gbq_ref, gwk_ref, gwv_ref, gbv_ref, gwr_ref, gbr_ref,
        lnrg_ref, lnrb_ref, gwo_ref, gbo_ref, ln2g_ref, ln2b_ref, gw1_ref, gb1_ref, gwd_ref, gbd_ref,
        gw2_ref, gb2_ref,
    ), outs, refs = refs[:23], refs[:23], refs[23:]
    out32, gp32, osem = refs
    stores = []

    def store(*which):
        for i in which:
            c = pltpu.make_async_copy(outs[i], dsts[i], osem.at[i])
            c.start()
            stores.append(c)

    blk_ref, gp_ref, eg_ref, lg1_ref, lg2_ref, veg_ref, vlg_ref = srcs
    D, HF, PB, PA, PL = sz.width, HEAD_FEATURES, sz.pb, sz.pa, sz.plane
    C, FS = sz.hidden, sz.share
    m = lax.axis_index("mp")

    def row(value):
        return value.reshape(value.shape[1])

    ve = veg_ref[m]
    gwd_ref[...] = ve[0:9, :C]
    gbd_ref[...] = row(ve[9:10, :C])
    gb1_ref[...] = row(ve[10:11, :C])
    vs = sum(veg_ref[h] for h in range(4))
    gb2_ref[...] = row(vs[11:12, :D])
    gbo_ref[...] = row(vs[12:13, :D])
    ln2g_ref[...] = row(vs[13:14, :D])
    ln2b_ref[...] = row(vs[14:15, :D])
    vl = sum(vlg_ref[h] for h in range(4))
    ln1g_ref[...] = row(vl[0:1, :D])
    ln1b_ref[...] = row(vl[1:2, :D])
    lnrg_ref[...] = row(vlg_ref[0][2:3, :D])
    lnrb_ref[...] = row(vlg_ref[0][3:4, :D])
    gbr_ref[...] = row(vlg_ref[0][4:5, :D])

    def head_row(r):
        parts = [vlg_ref[h][r : r + 1, 0:HF] for h in range(4)] + [vl[r : r + 1, HF : 2 * HF]]
        return row(jnp.concatenate(parts, axis=1))

    gbq_ref[...] = head_row(5)
    gbv_ref[...] = head_row(6)
    store(2, 3, 5, 8, 10, 11, 12, 14, 15, 16, 18, 19, 20, 22)
    for i in range(2):
        for j in range(2):
            p = 2 * i + j
            for a in range(PA):
                at = pl.ds((2 * a + i) * sz.cols + j, PB, stride=2)
                out32[at, :] = blk_ref[PL * p + PB * a : PL * p + PB * (a + 1), 0:FS]
                gp32[at, :] = gp_ref[p].astype(F32)[PB * a : PB * (a + 1), 0:FS]
    out_ref[...] = out32[...].T.astype(BF)
    gpix_ref[...] = gp32[...].T
    store(0, 1)
    eg = eg_ref[...].reshape(D + C, sz.wide)
    gw1_ref[...] = eg[0:D, :C].astype(F32)
    gw2_ref[...] = eg[D:, :D].astype(F32)
    store(17, 21)

    def unpacked(value):
        n = value.shape[0] * 2 // 5
        tail = value[2 * n :]
        tail = jnp.concatenate([tail[:, 0:HF], tail[:, HF:]], axis=0)
        return jnp.concatenate([value[0:n], value[n : 2 * n], tail], axis=1)

    lg1 = [lg1_ref[h].reshape(sz.l1rows, LANES).astype(F32) for h in range(4)]
    lg2 = [lg2_ref[h].reshape(sz.l2rows, LANES).astype(F32) for h in range(4)]
    tail = jnp.concatenate([lg2[h][sz.wrows : sz.wrows + FS] for h in range(4)], axis=0)
    fifth = sum(lg1[h][0:D, HF:] for h in range(4))
    gwq_ref[...] = jnp.concatenate([lg1[h][0:D, 0:HF] for h in range(4)] + [fifth], axis=1)
    gwk_ref[...] = jnp.concatenate([lg1[h][D : 2 * D, 0:HF] for h in range(4)] + [tail[:, 0:HF]], axis=1)
    gwv_ref[...] = jnp.concatenate([lg1[h][D : 2 * D, HF:] for h in range(4)] + [tail[:, HF:]], axis=1)
    store(4, 6, 7)
    gwr_ref[...] = jnp.concatenate([unpacked(lg2[h][0 : sz.wrows]) for h in range(4)], axis=1)
    store(9)
    n = HF // 4
    for h in range(4):
        wo = unpacked(lg1[h][2 * D : 2 * D + 5 * sz.orows // 2])
        gwo_ref[HF * h : HF * (h + 1), :] = wo[0:HF]
        gwo_ref[4 * HF + n * h : 4 * HF + n * (h + 1), :] = wo[HF:]
    store(13)
    for c in stores:
        c.wait()


def on_device_fused(*args):
    pixels_in, cotangent, pixel_mask, tile_slot = args[:4]
    w_fc1 = args[19]
    sz = Sizes(
        lax.axis_size("dp"), lax.axis_size("mp"), pixels_in.shape[0], cotangent.shape[1], w_fc1.shape[1]
    )
    D, C, PL, T, W, LN, HF = sz.width, sz.hidden, sz.plane, sz.all, sz.wide, LANES, HEAD_FEATURES
    Q, N, PB = sz.queries, sz.n_dp, sz.pb
    sm = pl.BlockSpec(memory_space=pltpu.SMEM)
    vm = pl.BlockSpec(memory_space=pltpu.VMEM)
    hbm = pl.BlockSpec(memory_space=pltpu.HBM)
    S = jax.ShapeDtypeStruct
    ins = [pixels_in.T, cotangent.T, *args[4:11], args[11].T, *args[12:]]
    mids = [
        S((T, LN), F32), S((4, PL, LN), BF), S((N, sz.echunk, W), BF), S((4, N, sz.l1rows // N, LN), BF),
        S((4, N, sz.l2rows // N, LN), BF), S((4, 16, W), F32), S((4, 8, W), F32),
    ]
    chunks = dict(e=(sz.echunk, W), l1=(sz.l1rows // N, LN), l2=(sz.l2rows // N, LN))
    shapes = {
        BF: dict(
            xt=(4, sz.share, sz.tokens), dfm=(T, D), dyh=(4, 48, W), dyh_s=(48, W), dyh_x=(48, W), dyh_g=(4, 48, W),
            edge=(4, sz.share, sz.edge_q), edge_s=(sz.share, sz.edge_q), edge_x=(sz.share, sz.edge_q),
            edge_g=(4, sz.share, sz.edge_q), xh_r=(sz.edge, D), qc_r=(LN, sz.edge_q), qd_r=(LN, sz.edge_q), xm_r=(T, D), n1_r=(T, D),
            xr_r=(PL, D), kva=(N, sz.kvrows, LN), qa_r=(LN, Q), qb_r=(LN, Q), ebuf=(N, PL, Q),
            e5buf=(N, sz.quarter, Q), og_a=(4, 2 * sz.keys, LN), og_b=(4, 2 * sz.keys, LN), og_c=(4, sz.edge, LN),
            ow_a=(4, 2 * sz.keys, LN), ow_b=(4, 2 * sz.keys, LN), ow_c=(4, sz.edge, LN), n2_r=(T, D),
            dub=(4, PL, C), dn2_s=(3, sz.prows, LN), dn2_n=(2, sz.prows, LN),
            dn2_f=(sz.prows, LN), dos=(4, PL, LN), do_all=(4, PL, LN), dabg=(4, PL, W), ff_s=(3, sz.share, T), ff_n=(2, sz.share, T),
            ff_f=(sz.share, T), **{"dk_" + k: (4, PL, LN) for k in "xnof"}, **{"dl_" + k: (4, sz.quarter, LN) for k in "xnof"}, dkvg=(4, sz.kvrows, LN), dqs=(4, PL, LN), dq_all=(4, PL, LN),
            e_s=(D + C, W), gps=(4, PL, LN), wr_t=(4 * D, D), ogp=(T, LN),
            w2_t=(D, C), w_all=(D, 5 * LN), wq_cat=(D, 4 * LN), wo_cat=(4 * LN, D), l1_s=(sz.l1rows, LN),
            l2_s=(sz.l2rows, LN),
            **{n + "_" + k: (4, *v) for k in "nof" for n, v in chunks.items()},
        ),
        F32: dict(
            t0=(sz.tokens, LN), t1=(sz.tokens, LN), t2=(sz.tokens, D - 2 * LN), xhr_r=(PL, D), rsr_r=(PL, LN),
            o_own=(N, HF, Q), o_five=(N, HF, Q), oh_own=(N, HF, sz.edge_q), oh_five=(N, HF, sz.edge_q),
            lse_r=(4, 16, LN), ot_r=(LN, Q),
            h1_r=(T, D), ux=(4, sz.ext, C), ul=(2, sz.ext, C), ur=(2, sz.ext, C), dgx=(4, sz.ext, C),
            dzx=(4, sz.ext, C), dzl=(2, sz.ext, C), dzr=(2, sz.ext, C), g_r=(4, PL, C), du_r=(4, PL, C),
            dh1_r=(PL, D), dr_r=(4, 8, Q), dqt=(LN, Q), dqt5=(LN, Q), ve_s=(16, W), ve_n=(16, W),
            ve_p=(4, 16, W), vl_s=(8, W), vl_n=(8, W), vl_p=(4, 8, W),
        ),
    }
    scratch = {k: pltpu.VMEM(v, t) for t, group in shapes.items() for k, v in group.items()}
    for i in range(1, len(ins)):
        scratch["in%d" % i] = pltpu.VMEM(ins[i].shape, ins[i].dtype)
    scratch["ssem"] = pltpu.SemaphoreType.DMA((200,))
    scratch["rsem"] = pltpu.SemaphoreType.DMA((200,))
    scratch["isem"] = pltpu.SemaphoreType.DMA((len(ins),))
    mid = pl.pallas_call(
        functools.partial(fused_body, sz, tuple(scratch)),
        out_shape=[pltpu.VMEM(v.shape, v.dtype) for v in mids],
        in_specs=[sm, sm] + [hbm] * len(ins),
        out_specs=[vm] * len(mids),
        scratch_shapes=list(scratch.values()),
        compiler_params=pltpu.CompilerParams(
            collective_id=0, has_side_effects=True, vmem_limit_bytes=VMEM_MB * 2**20
        ),
        name="fused_block",
    )(pixel_mask, tile_slot.T, *(pltpu.with_memory_space_constraint(v, pltpu.HBM) for v in ins))
    outs = [
        S((sz.share, sz.tokens), BF), S((sz.share, sz.tokens), F32), S((D,), F32), S((D,), F32), S((D, D), F32),
        S((D,), F32), S((D, D), F32), S((D, D), F32), S((D,), F32), S((D, 4 * D), F32), S((D,), F32), S((D,), F32),
        S((D,), F32), S((D, D), F32), S((D,), F32), S((D,), F32), S((D,), F32), S((D, C), F32), S((C,), F32),
        S((9, C), F32), S((C,), F32), S((C, D), F32), S((D,), F32),
    ]
    res = list(
        pl.pallas_call(
            functools.partial(unpack_body, sz),
            out_shape=outs,
            in_specs=[vm] * len(mids),
            out_specs=[hbm] * len(outs),
            scratch_shapes=[pltpu.VMEM(v.shape, v.dtype) for v in outs]
            + [pltpu.VMEM((sz.tokens, sz.share), F32)] * 2
            + [pltpu.SemaphoreType.DMA((len(outs),))],
            compiler_params=pltpu.CompilerParams(vmem_limit_bytes=40 * 2**20),
            name="unpack",
        )(*mid)
    )
    for k in (0, 1, 9):
        res[k] = res[k].T
    return tuple(res)


def choose(*args):
    tokens, width = args[1].shape
    whole_rows = tokens == FRAME * (FRAME // TILE_ROWS)
    shape = (lax.axis_size("dp"), lax.axis_size("mp"))
    if whole_rows and shape == (TILE_ROWS, 4) and TILE_ROWS == 8 and HEADS == 5 and width == 320 == args[19].shape[1]:
        return on_device_fused(*args)
    return on_device(*args)


def solution(mesh):
    return jax.shard_map(
        choose,
        mesh=mesh,
        in_specs=(
            P("dp", "mp"),
            P("dp", None),
            P("dp"),
            P(),
            P(),
            P(),
            P(),
            P(),
            P(),
            P(),
            P(),
            P(),
            P(),
            P(),
            P(),
            P(),
            P(),
            P(),
            P(),
            P(None, "mp"),
            P("mp"),
            P(None, "mp"),
            P("mp"),
            P("mp", None),
            P(),
        ),
        out_specs=(
            P("dp", "mp"),
            P("dp", "mp"),
            P(),
            P(),
            P(),
            P(),
            P(),
            P(),
            P(),
            P(),
            P(),
            P(),
            P(),
            P(),
            P(),
            P(),
            P(),
            P(None, "mp"),
            P("mp"),
            P(None, "mp"),
            P("mp"),
            P("mp", None),
            P(),
        ),
        check_vma=False,
    )
```

```python
import functools

import jax
import jax.numpy as jnp
from jax import lax
from jax.experimental import pallas as pl
from jax.experimental.pallas import tpu as pltpu
from jax.sharding import PartitionSpec as P

HEADS = 5
HEAD_FEATURES = 64
FRAME = 80
TILE_ROWS = 8


EPS = 1e-05
NEG = -1e30


def layer_norm(value, gain, shift):
    mean = jnp.mean(value, axis=-1, keepdims=True)
    centred = value - mean
    spread = jnp.mean(centred * centred, axis=-1, keepdims=True)
    return centred * lax.rsqrt(spread + EPS) * gain + shift


def depth_gelu(padded, kernel, shift):
    rows = padded.shape[0] - 2
    cols = padded.shape[1] - 2
    total = jnp.zeros((rows, cols, padded.shape[2]), jnp.float32) + shift
    for row_off in range(3):
        for col_off in range(3):
            total = (
                total
                + kernel[3 * row_off + col_off]
                * padded[row_off : row_off + rows, col_off : col_off + cols]
            )
    return jax.nn.gelu(total, approximate=False)


def mat(left, right):
    return jnp.dot(left, right, preferred_element_type=jnp.float32)


def pick(weights, table):
    return jnp.einsum(
        "j,jab->ab", weights.astype(table.dtype), table, preferred_element_type=jnp.float32
    )


def head_columns(weight_matrix, select_where):
    wide_layout = weight_matrix.astype(jnp.float32).reshape(
        weight_matrix.shape[0], HEADS, HEAD_FEATURES
    )
    return (
        jnp.einsum("uzx,nz->unx", wide_layout, select_where)
        .reshape(weight_matrix.shape[0], -1)
        .astype(jnp.bfloat16)
    )


def head_rows(weight_matrix, select_where):
    wide_layout = weight_matrix.astype(jnp.float32).reshape(
        HEADS, HEAD_FEATURES, weight_matrix.shape[1]
    )
    return (
        jnp.einsum("hed,sh->sed", wide_layout, select_where)
        .reshape(-1, weight_matrix.shape[1])
        .astype(jnp.bfloat16)
    )


def head_vector(vector_entries, select_where):
    return jnp.einsum(
        "he,sh->se", vector_entries.reshape(HEADS, HEAD_FEATURES), select_where
    ).reshape(-1)


def spread_columns(gradient_value, select_where):
    return jnp.einsum(
        "tvm,vq->tqm",
        gradient_value.reshape(gradient_value.shape[0], -1, HEAD_FEATURES),
        select_where,
    ).reshape(gradient_value.shape[0], -1)


def spread_rows(gradient_value, select_where):
    return jnp.einsum(
        "sed,sh->hed",
        gradient_value.reshape(-1, HEAD_FEATURES, gradient_value.shape[1]),
        select_where,
    ).reshape(-1, gradient_value.shape[1])


def spread_vector(gradient_value, select_where):
    return jnp.einsum("se,sh->he", gradient_value.reshape(-1, HEAD_FEATURES), select_where).reshape(
        -1
    )


def on_device(
    pixels_in,
    cotangent,
    pixel_mask,
    tile_slot,
    ln1_gain,
    ln1_bias,
    w_query,
    b_query,
    w_key,
    w_value,
    b_value,
    w_reduce,
    b_reduce,
    lnr_gain,
    lnr_bias,
    w_out,
    b_out,
    ln2_gain,
    ln2_bias,
    w_fc1,
    b_fc1,
    w_depth,
    b_depth,
    w_fc2,
    b_fc2,
):
    n_dp = lax.axis_size("dp")
    n_mp = lax.axis_size("mp")
    device = lax.axis_index("dp")
    part = lax.axis_index("mp")
    rows = FRAME // TILE_ROWS
    tokens = pixels_in.shape[0]
    cols = tokens // rows
    tiles_col = FRAME // cols
    per_frame = TILE_ROWS * tiles_col
    width = ln1_gain.shape[0]
    share = width // n_mp
    slots = -(-HEADS // n_mp)
    scale = HEAD_FEATURES ** (-0.5)
    maskf = pixel_mask.astype(jnp.float32)[:, None]
    head_ids = part + n_mp * jnp.arange(slots)
    select_where = (head_ids[:, None] == jnp.arange(HEADS)[None, :]).astype(jnp.float32)
    crops = tile_slot[:, 0]
    tiles = tile_slot[:, 1]
    is_me = jnp.arange(n_dp) == device
    own_crop = jnp.sum(jnp.where(is_me, crops, 0))
    own_tile = jnp.sum(jnp.where(is_me, tiles, 0))
    own_row = own_tile // tiles_col
    own_col = own_tile % tiles_col
    tile_row = tiles // tiles_col
    tile_col = tiles % tiles_col

    def beside(drow, dcol):
        hit = (crops == own_crop) & (tile_row == own_row + drow) & (tile_col == own_col + dcol)
        return hit.astype(jnp.float32)

    member = (crops[None, :] == own_crop) & (tiles[None, :] == jnp.arange(per_frame)[:, None])
    crop_devices = jnp.sum(jnp.where(member, jnp.arange(n_dp)[None, :], 0), axis=1)
    whole = lax.all_gather(pixels_in, "mp", axis=1, tiled=True)
    xm = whole.astype(jnp.float32) * maskf
    n1, first_norm_backward = jax.vjp(layer_norm, xm, ln1_gain, ln1_bias)
    n1b = n1.astype(jnp.bfloat16)
    wq = head_columns(w_query, select_where)
    wk = head_columns(w_key, select_where)
    wv = head_columns(w_value, select_where)
    wo = head_rows(w_out, select_where)
    qb = (mat(n1b, wq) + head_vector(b_query, select_where)).astype(jnp.bfloat16)
    patches = (
        n1b.reshape(rows // 2, 2, cols // 2, 2, width)
        .transpose(0, 2, 1, 3, 4)
        .reshape(-1, 4 * width)
    )
    reduced = mat(patches, w_reduce) + b_reduce
    xr, lnr_back = jax.vjp(layer_norm, reduced, lnr_gain, lnr_bias)
    xrb = xr.astype(jnp.bfloat16)
    kb = mat(xrb, wk).astype(jnp.bfloat16)
    vb = (mat(xrb, wv) + head_vector(b_value, select_where)).astype(jnp.bfloat16)
    kmask = (
        pixel_mask.reshape(rows // 2, 2, cols // 2, 2)[:, 0, :, 0].reshape(-1).astype(jnp.bfloat16)
    )
    keys_all, values_all, kmask_all = (
        lax.all_gather(kb, "dp", axis=0, tiled=True),
        lax.all_gather(vb, "dp", axis=0, tiled=True),
        lax.all_gather(kmask, "dp", axis=0, tiled=True),
    )
    per_key = kb.shape[0]
    keys_crop = keys_all.reshape(n_dp, per_key, -1)[crop_devices]
    values_crop = values_all.reshape(n_dp, per_key, -1)[crop_devices]
    usable_crop = kmask_all.reshape(n_dp, per_key)[crop_devices].astype(jnp.float32) > 0.5
    n_blocks = 4
    key_blocks = keys_crop.reshape(n_blocks, -1, slots, HEAD_FEATURES)
    value_blocks = values_crop.reshape(n_blocks, -1, slots, HEAD_FEATURES)
    usable_blocks = usable_crop.reshape(n_blocks, -1)
    queries = qb.reshape(tokens, slots, HEAD_FEATURES)

    def block_scores(key_block, usable_block):
        raw = (
            jnp.einsum("qsd,ksd->sqk", queries, key_block, preferred_element_type=jnp.float32)
            * scale
        )
        return jnp.where(usable_block[None, None, :], raw, NEG)

    def top_step(carry, blocks):
        top, total = carry
        key_block, usable_block = blocks
        scores = block_scores(key_block, usable_block)
        new_top = jnp.maximum(top, jnp.max(scores, axis=-1))
        total = total * jnp.exp(top - new_top) + jnp.sum(
            jnp.exp(scores - new_top[..., None]), axis=-1
        )
        return ((new_top, total), None)

    start = (jnp.full((slots, tokens), NEG, jnp.float32), jnp.zeros((slots, tokens), jnp.float32))
    (top, total), _ = lax.scan(top_step, start, (key_blocks, usable_blocks))
    lse = top + jnp.log(total)

    def out_step(acc, blocks):
        key_block, value_block, usable_block = blocks
        prob = jnp.exp(block_scores(key_block, usable_block) - lse[..., None])
        acc = acc + jnp.einsum(
            "sqk,ksd->qsd",
            prob.astype(jnp.bfloat16),
            value_block,
            preferred_element_type=jnp.float32,
        )
        return (acc, None)

    empty = jnp.zeros((tokens, slots, HEAD_FEATURES), jnp.float32)
    acc, _ = lax.scan(out_step, empty, (key_blocks, value_blocks, usable_blocks))
    ob = acc.reshape(tokens, -1).astype(jnp.bfloat16)
    branch = lax.psum(mat(ob, wo).astype(jnp.bfloat16), "mp").astype(jnp.float32) + b_out
    h1 = xm + branch * maskf
    n2, ln2_back = jax.vjp(layer_norm, h1, ln2_gain, ln2_bias)
    n2b = n2.astype(jnp.bfloat16)
    ub = ((mat(n2b, w_fc1) + b_fc1) * maskf).astype(jnp.bfloat16)
    channels = ub.shape[1]
    tile_u = ub.reshape(rows, cols, channels)
    lines, sides = (
        lax.all_gather(jnp.stack([tile_u[0], tile_u[-1]]), "dp", axis=0, tiled=True),
        lax.all_gather(jnp.stack([tile_u[:, 0], tile_u[:, -1]]), "dp", axis=0, tiled=True),
    )
    lines = lines.reshape(n_dp, 2, cols, channels)
    sides = sides.reshape(n_dp, 2, rows, channels)
    top_lines = lines[:, 0]
    bottom_lines = lines[:, 1]
    left_sides = sides[:, 0]
    right_sides = sides[:, 1]
    upper = jnp.concatenate(
        [
            pick(beside(-1, -1), bottom_lines[:, -1:]),
            pick(beside(-1, 0), bottom_lines),
            pick(beside(-1, 1), bottom_lines[:, :1]),
        ],
        axis=0,
    )
    lower = jnp.concatenate(
        [
            pick(beside(1, -1), top_lines[:, -1:]),
            pick(beside(1, 0), top_lines),
            pick(beside(1, 1), top_lines[:, :1]),
        ],
        axis=0,
    )
    middle = jnp.concatenate(
        [
            pick(beside(0, -1), right_sides)[:, None],
            tile_u.astype(jnp.float32),
            pick(beside(0, 1), left_sides)[:, None],
        ],
        axis=1,
    )
    padded = jnp.concatenate([upper[None], middle, lower[None]], axis=0)
    act, depth_back = jax.vjp(depth_gelu, padded, w_depth, b_depth)
    gb = act.reshape(tokens, channels).astype(jnp.bfloat16)
    ffn_mine = lax.psum_scatter(
        mat(gb, w_fc2).astype(jnp.bfloat16), "mp", scatter_dimension=1, tiled=True
    ).astype(jnp.float32)
    h1_mine = lax.dynamic_slice_in_dim(h1, part * share, share, 1)
    bias_mine = lax.dynamic_slice_in_dim(b_fc2, part * share, share, 0)
    block_result = (h1_mine + (ffn_mine + bias_mine) * maskf).astype(jnp.bfloat16)
    dy = cotangent.astype(jnp.float32)
    dff = dy * maskf
    grad_b_fc2 = jnp.sum(dff, axis=0)
    dfb = dff.astype(jnp.bfloat16)
    grad_w_fc2 = mat(gb.T, dfb)
    dgr = mat(dfb, w_fc2.T).astype(jnp.bfloat16).astype(jnp.float32).reshape(rows, cols, channels)
    dpad, grad_w_depth, grad_b_depth = depth_back(dgr)
    grad_lines, grad_sides = (
        lax.all_gather(
            jnp.stack([dpad[0], dpad[-1]]).astype(jnp.bfloat16), "dp", axis=0, tiled=True
        ).astype(jnp.float32),
        lax.all_gather(
            jnp.stack([dpad[1:-1, 0], dpad[1:-1, -1]]).astype(jnp.bfloat16),
            "dp",
            axis=0,
            tiled=True,
        ).astype(jnp.float32),
    )
    grad_lines = grad_lines.reshape(n_dp, 2, cols + 2, channels)
    grad_sides = grad_sides.reshape(n_dp, 2, rows, channels)
    top_grads = grad_lines[:, 0]
    bottom_grads = grad_lines[:, 1]
    dtile = dpad[1:-1, 1:-1]
    dtile = dtile.at[0].add(pick(beside(-1, 0), bottom_grads[:, 1:-1]))
    dtile = dtile.at[0, 0].add(pick(beside(-1, -1), bottom_grads[:, -1:])[0])
    dtile = dtile.at[0, -1].add(pick(beside(-1, 1), bottom_grads[:, :1])[0])
    dtile = dtile.at[-1].add(pick(beside(1, 0), top_grads[:, 1:-1]))
    dtile = dtile.at[-1, 0].add(pick(beside(1, -1), top_grads[:, -1:])[0])
    dtile = dtile.at[-1, -1].add(pick(beside(1, 1), top_grads[:, :1])[0])
    dtile = dtile.at[:, 0].add(pick(beside(0, -1), grad_sides[:, 1]))
    dtile = dtile.at[:, -1].add(pick(beside(0, 1), grad_sides[:, 0]))
    dub = (dtile.reshape(tokens, channels).astype(jnp.bfloat16).astype(jnp.float32) * maskf).astype(
        jnp.bfloat16
    )
    grad_b_fc1 = jnp.sum(dub.astype(jnp.float32), axis=0)
    grad_w_fc1 = mat(n2b.T, dub)
    dn2_part = mat(dub, w_fc1.T)
    zero_vector = jnp.zeros((width,), jnp.float32)
    dn2 = lax.psum(dn2_part.astype(jnp.bfloat16), "mp").astype(jnp.float32)
    dh1_norm, shared_gain, shared_bias = ln2_back(dn2)
    dh1 = dy + dh1_norm
    split_gain = zero_vector
    split_bias = zero_vector
    dattn = dh1 * maskf
    grad_b_out = jnp.sum(dattn, axis=0)
    dab = dattn.astype(jnp.bfloat16)
    grad_wo = mat(ob.T, dab)
    dob = mat(dab, wo.T).astype(jnp.bfloat16)
    dout = dob.reshape(tokens, slots, HEAD_FEATURES)
    drow = jnp.sum(dout.astype(jnp.float32) * acc, axis=-1).T

    def back_step(dq_acc, blocks):
        key_block, value_block, usable_block = blocks
        prob = jnp.exp(block_scores(key_block, usable_block) - lse[..., None])
        dv_block = jnp.einsum(
            "sqk,qsd->ksd", prob.astype(jnp.bfloat16), dout, preferred_element_type=jnp.float32
        )
        dprob = jnp.einsum("qsd,ksd->sqk", dout, value_block, preferred_element_type=jnp.float32)
        dscore = (prob * (dprob - drow[..., None])).astype(jnp.bfloat16)
        dq_acc = dq_acc + jnp.einsum(
            "sqk,ksd->qsd", dscore, key_block, preferred_element_type=jnp.float32
        )
        dk_block = (
            jnp.einsum("sqk,qsd->ksd", dscore, queries, preferred_element_type=jnp.float32) * scale
        )
        return (dq_acc, (dk_block, dv_block))

    dq_acc, (dk_blocks, dv_blocks) = lax.scan(
        back_step, empty, (key_blocks, value_blocks, usable_blocks)
    )
    zero_keys = jnp.zeros((n_dp, per_key, slots * HEAD_FEATURES), jnp.float32)
    dk_full = (
        zero_keys.at[crop_devices]
        .set(dk_blocks.reshape(per_frame, per_key, -1))
        .reshape(n_dp * per_key, -1)
    )
    dv_full = (
        zero_keys.at[crop_devices]
        .set(dv_blocks.reshape(per_frame, per_key, -1))
        .reshape(n_dp * per_key, -1)
    )
    dk_mine, dv_mine = (
        lax.psum_scatter(dk_full, "dp", scatter_dimension=0, tiled=True),
        lax.psum_scatter(dv_full, "dp", scatter_dimension=0, tiled=True),
    )
    dkb = dk_mine.astype(jnp.bfloat16)
    dvb = dv_mine.astype(jnp.bfloat16)
    dqb = (dq_acc * scale).reshape(tokens, -1).astype(jnp.bfloat16)
    grad_wq = mat(n1b.T, dqb)
    grad_bq = jnp.sum(dqb.astype(jnp.float32), axis=0)
    grad_wk = mat(xrb.T, dkb)
    grad_wv = mat(xrb.T, dvb)
    grad_bv = jnp.sum(dvb.astype(jnp.float32), axis=0)
    dxr, dn1_query = (
        lax.psum((mat(dkb, wk.T) + mat(dvb, wv.T)).astype(jnp.bfloat16), "mp").astype(jnp.float32),
        lax.psum(mat(dqb, wq.T).astype(jnp.bfloat16), "mp").astype(jnp.float32),
    )
    dreduced, grad_lnr_gain, grad_lnr_bias = lnr_back(dxr)
    drb = dreduced.astype(jnp.bfloat16)
    grad_w_reduce = mat(patches.T, drb)
    grad_b_reduce = jnp.sum(drb.astype(jnp.float32), axis=0)
    dpatch = (
        mat(drb, w_reduce.T)
        .reshape(rows // 2, cols // 2, 2, 2, width)
        .transpose(0, 2, 1, 3, 4)
        .reshape(tokens, width)
    )
    dxm, grad_ln1_gain, grad_ln1_bias = first_norm_backward(dn1_query + dpatch)
    grad_whole = (dxm + dh1) * maskf
    grad_input = lax.dynamic_slice_in_dim(grad_whole, part * share, share, 1)
    (
        grad_w_reduce,
        grad_b_reduce,
        grad_lnr_gain,
        grad_lnr_bias,
        grad_ln1_gain,
        grad_ln1_bias,
        shared_gain,
        shared_bias,
        grad_b_out,
        grad_b_fc2,
        grad_w_fc1,
        grad_b_fc1,
        grad_w_depth,
        grad_b_depth,
        grad_w_fc2,
    ) = lax.psum(
        (
            grad_w_reduce,
            grad_b_reduce,
            grad_lnr_gain,
            grad_lnr_bias,
            grad_ln1_gain,
            grad_ln1_bias,
            shared_gain,
            shared_bias,
            grad_b_out,
            grad_b_fc2,
            grad_w_fc1,
            grad_b_fc1,
            grad_w_depth,
            grad_b_depth,
            grad_w_fc2,
        ),
        "dp",
    )
    (
        grad_w_query,
        grad_b_query,
        grad_w_key,
        grad_w_value,
        grad_b_value,
        output_weight_gradient,
        split_gain,
        split_bias,
    ) = lax.psum(
        (
            spread_columns(grad_wq, select_where),
            spread_vector(grad_bq, select_where),
            spread_columns(grad_wk, select_where),
            spread_columns(grad_wv, select_where),
            spread_vector(grad_bv, select_where),
            spread_rows(grad_wo, select_where),
            split_gain,
            split_bias,
        ),
        ("dp", "mp"),
    )
    grad_ln2_gain = shared_gain + split_gain
    grad_ln2_bias = shared_bias + split_bias
    return (
        block_result,
        grad_input,
        grad_ln1_gain,
        grad_ln1_bias,
        grad_w_query,
        grad_b_query,
        grad_w_key,
        grad_w_value,
        grad_b_value,
        grad_w_reduce,
        grad_b_reduce,
        grad_lnr_gain,
        grad_lnr_bias,
        output_weight_gradient,
        grad_b_out,
        grad_ln2_gain,
        grad_ln2_bias,
        grad_w_fc1,
        grad_b_fc1,
        grad_w_depth,
        grad_b_depth,
        grad_w_fc2,
        grad_b_fc2,
    )


BF = jnp.bfloat16
F32 = jnp.float32
LANES = 128
SIDE_SMALL = 64
VMEM_MB = 52


def nn(a, b):
    return lax.dot_general(a, b, (((1,), (0,)), ((), ())), preferred_element_type=F32)


def nt(a, b):
    return lax.dot_general(a, b, (((1,), (1,)), ((), ())), preferred_element_type=F32)


def tn(a, b):
    return lax.dot_general(a, b, (((0,), (0,)), ((), ())), preferred_element_type=F32)


def iota(shape, axis):
    return lax.broadcasted_iota(jnp.int32, shape, axis)


def hot(cond):
    return jnp.where(cond, 1.0, 0.0).astype(BF)


def spread(value):
    mean = jnp.sum(value, axis=-1, keepdims=True) * (1.0 / value.shape[-1])
    centred = value - mean
    var = jnp.sum(centred * centred, axis=-1, keepdims=True) * (1.0 / value.shape[-1])
    rstd = lax.rsqrt(var + EPS)
    return centred * rstd, rstd


def norm_back(dn, gain, xhat, rstd):
    e = dn * gain
    scale = 1.0 / dn.shape[-1]
    mean_e = jnp.sum(e, axis=-1, keepdims=True) * scale
    mean_ex = jnp.sum(e * xhat, axis=-1, keepdims=True) * scale
    return rstd * (e - mean_e - xhat * mean_ex)


def rowsum(value):
    return jnp.sum(value, axis=0, keepdims=True)


class Sizes:
    def __init__(self, n_dp, n_mp, tokens, width, hidden):
        self.n_dp, self.n_mp = n_dp, n_mp
        self.tokens, self.width, self.hidden = tokens, width, hidden
        self.share = width // n_mp
        self.rows = FRAME // TILE_ROWS
        self.cols = tokens // self.rows
        self.pa, self.pb = self.rows // 2, self.cols // 2
        self.keys = self.pa * self.pb
        self.plane = -(-self.keys // 16) * 16
        self.all = 4 * self.plane
        self.step = self.plane // 16 // n_mp * 16
        self.quarter = self.plane - (n_mp - 1) * self.step
        self.wide = -(-width // LANES) * LANES
        self.kvrows = self.plane + self.quarter
        self.top = 8 + self.pb
        self.ext = self.top + self.keys + self.pb
        self.edge = 4 * 2 * self.pb
        self.edge_q = -(-self.edge // LANES) * LANES
        self.queries = -(-4 * self.keys // LANES) * LANES
        self.echunk = (width + hidden) // n_dp
        self.prows = -(-(2 * self.plane + self.plane // 2) // 16) * 16
        self.wrows = 2 * width + width // 2
        self.l2rows = -(-(self.wrows + self.share) // (16 * n_dp)) * 16 * n_dp
        self.orows = HEAD_FEATURES + HEAD_FEATURES // n_mp
        self.l1rows = -(-(2 * width + 2 * self.orows + self.orows // 2) // (16 * n_dp)) * 16 * n_dp


class Load:
    def __init__(self, src, dst, sem):
        self.dst, self.shape, self.waiting = dst, dst.shape, True
        self.copy = pltpu.make_async_copy(src, dst, sem)
        self.copy.start()

    def ready(self):
        if self.waiting:
            self.waiting = False
            self.copy.wait()
        return self.dst

    def __getitem__(self, at):
        return self.ready()[at]


def fused_body(
    sz, names,
    mask_ref, slot_ref, *refs,
):
    ins, refs = refs[:23], refs[23:]
    outs, refs = refs[:7], refs[7:]
    s = dict(zip(names, refs))
    blk_ref, gp_ref, eg_ref, lg1_ref, lg2_ref, veg_ref, vlg_ref = outs
    D, HF, PB, PA, KEYS, PL, T = sz.width, HEAD_FEATURES, sz.pb, sz.pa, sz.keys, sz.plane, sz.all
    C, FS, W = sz.hidden, sz.share, sz.wide
    d = lax.axis_index("dp")
    m = lax.axis_index("mp")
    last = sz.n_mp * HF
    ssem, rsem = s["ssem"], s["rsem"]

    def mpx(k):
        if k == 0:
            return m
        if k == 1:
            return m + 1 - 2 * lax.rem(m, 2)
        if k == 2:
            return lax.rem(m + 2, 4)
        return 3 - m

    def dpx(k):
        z, x = d // 2, lax.rem(d, 2)
        if k & 1:
            x = 1 - x
        kz = k >> 1
        if kz == 1:
            z = z + 1 - 2 * lax.rem(z, 2)
        elif kz == 2:
            z = lax.rem(z + 2, 4)
        elif kz == 3:
            z = 3 - z
        return 2 * z + x

    counter = [0]
    pending = []

    def take(n):
        first = counter[0]
        counter[0] += n
        return first

    def copy(src, dst, sem, dev):
        return pltpu.make_async_remote_copy(
            src_ref=src, dst_ref=dst, send_sem=ssem.at[sem], recv_sem=rsem.at[sem],
            device_id=dev, device_id_type=pl.DeviceIdType.MESH,
        )

    def send(src, dst, sem, dev):
        c = copy(src, dst, sem, dev)
        c.start()
        pending.append(c)

    def drain(keep=0):
        while len(pending) > keep:
            pending.pop(0).wait_send()

    def arrived(ref, sem):
        copy(ref, ref, sem, (d, m)).wait_recv()

    opened = []

    def handle(finish):
        state = [False]

        def once(*a):
            if not state[0]:
                state[0] = True
                return finish(*a)

        opened.append(once)
        return once

    def mp_start(buf):
        base = take(3)
        send(buf.at[m], buf.at[m], base, (d, mpx(1)))
        send(buf.at[m], buf.at[m], base + 1, (d, mpx(2)))

        def middle():
            arrived(buf.at[mpx(2)], base + 1)
            send(buf.at[mpx(2)], buf.at[mpx(2)], base + 2, (d, mpx(1)))

        mid = handle(middle)

        def finish():
            mid()
            arrived(buf.at[mpx(1)], base)
            arrived(buf.at[mpx(3)], base + 2)

        return handle(finish), mid

    def dp_start(buf, each=lambda k: None):
        base = take(7)
        for kz in (3, 2, 1):
            send(buf.at[d], buf.at[d], base + kz, (dpx(2 * kz), m))
        send(buf.at[d], buf.at[d], base, (dpx(1), m))

        def along(kz):
            arrived(buf.at[dpx(2 * kz)], base + kz)
            send(buf.at[dpx(2 * kz)], buf.at[dpx(2 * kz)], base + 3 + kz, (dpx(1), m))
            each(2 * kz)

        def across(kz):
            arrived(buf.at[dpx(2 * kz + 1)], base + 3 + kz if kz else base)
            each(2 * kz + 1)

        steps = [handle(lambda kz=kz: along(kz)) for kz in (1, 2, 3)]
        steps += [handle(lambda kz=kz: across(kz)) for kz in range(4)]

        def mid():
            for step in steps[:4]:
                step()

        def finish():
            for step in steps:
                step()

        return handle(finish), mid, steps

    def dp_pick(buf, chosen, out, came):
        base = take(4)
        z = d // 2
        for kz in (3, 2, 1):
            send(buf.at[z], buf.at[z], base + kz, (dpx(2 * kz), m))

        def middle():
            for kz in (1, 2, 3):
                arrived(buf.at[dpx(2 * kz) // 2], base + kz)
            out[...] = chosen(*beside(dpx(1)))
            send(out, came, base, (dpx(1), m))

        mid = handle(middle)

        def finish():
            mid()
            arrived(came, base)

        return handle(finish), mid

    def mp_scatter(block, dst, landed):
        base = take(4)
        for k in (2, 3, 1):
            send(block(mpx(k)), dst(k), base + k, (d, mpx(k)))

        def finish():
            for k in (1, 2, 3):
                arrived(landed(k), base + k)

        return handle(finish)

    def dp_scatter(block, dst, landed):
        base = take(8)
        for k in (6, 7, 4, 5, 2, 3, 1):
            send(block(dpx(k)), dst(k), base + k, (dpx(k), m))

        def finish():
            for k in range(1, sz.n_dp):
                arrived(landed(k), base + k)

        return handle(finish)

    def mp_sum(block, out, near, far):
        base = take(3)
        out[1] = block(mpx(3)).astype(BF)
        send(out.at[1], near.at[1], base + 1, (d, mpx(1)))
        out[0] = block(mpx(1)).astype(BF)
        send(out.at[0], near.at[0], base, (d, mpx(1)))

        def middle():
            value = block(mpx(2))
            arrived(near.at[1], base + 1)
            out[2] = (value + near[1].astype(F32)).astype(BF)
            send(out.at[2], far, base + 2, (d, mpx(2)))

        mid = handle(middle)

        def finish():
            mid()
            value = block(m)
            arrived(near.at[0], base)
            value = value + near[0].astype(F32)
            arrived(far, base + 2)
            return value + far[...].astype(F32)

        return mid, handle(finish)

    def dp_sum(chunk, near, out, far):
        base = take(8)
        for kz in (2, 3, 1, 0):
            send(chunk(dpx(2 * kz + 1)), near.at[kz], base + kz, (dpx(1), m))

        def middle():
            for kz in (2, 3, 1):
                value = chunk(dpx(2 * kz))[...].astype(F32)
                arrived(near.at[kz], base + kz)
                out[kz] = (value + near[kz].astype(F32)).astype(BF)
                send(out.at[kz], far.at[kz], base + 4 + kz, (dpx(2 * kz), m))

        mid = handle(middle)

        def finish():
            mid()
            value = chunk(d)[...].astype(F32)
            arrived(near.at[0], base)
            value = value + near[0].astype(F32)
            for kz in (1, 2, 3):
                arrived(far.at[kz], base + 4 + kz)
                value = value + far[kz].astype(F32)
            return value

        return mid, handle(finish)

    def dp_total(src, near, parts):
        base = take(4)
        z = d // 2
        send(src, near, base, (dpx(1), m))

        def middle():
            arrived(near, base)
            parts[z] = src[...] + near[...]
            for kz in (2, 3, 1):
                send(parts.at[z], parts.at[z], base + kz, (dpx(2 * kz), m))

        mid = handle(middle)

        def finish():
            mid()
            for kz in (1, 2, 3):
                arrived(parts.at[dpx(2 * kz) // 2], base + kz)
            return (parts[0] + parts[1]) + (parts[2] + parts[3])

        return mid, handle(finish)

    peers = [(d, mpx(k)) for k in (1, 2, 3)] + [(dpx(k), m) for k in range(1, 8)]
    bar = pltpu.get_barrier_semaphore()
    for dev in peers:
        pl.semaphore_signal(bar, inc=1, device_id=dev, device_id_type=pl.DeviceIdType.MESH)

    order = (0, 1, 2, 3, 8, 7, 9, 10, 11, 12, 4, 5, 6, 21, 22, 13, 14, 15, 16, 17, 18, 19, 20)
    loads = [None] * 23
    for i in order:
        dst = s["xt"].at[m] if i == 0 else s["in%d" % i]
        loads[i] = Load(ins[i], dst, s["isem"].at[i])
    (
        pix_ref, cot_ref, ln1g_ref, ln1b_ref, wq_ref, bq_ref, wk_ref, wv_ref, bv_ref, wr_ref, br_ref,
        lnrg_ref, lnrb_ref, wo_ref, bo_ref, ln2g_ref, ln2b_ref, w1_ref, b1_ref, wd_ref, bd_ref, w2_ref, b2_ref,
    ) = loads

    side = jnp.where(mask_ref[sz.cols - 1] > 0, FRAME, SIDE_SMALL)
    tile = slot_ref[1, d]
    tiles = [slot_ref[1, k] for k in range(sz.n_dp)]

    def beside(at):
        t = slot_ref[1, at]
        up = sum(jnp.where(tiles[k] == t - 1, k, 0) for k in range(sz.n_dp))
        down = sum(jnp.where(tiles[k] == t + 1, k, 0) for k in range(sz.n_dp))
        return up, down

    above, below = beside(d)

    def same_x(j):
        return lax.rem(j, 2) == lax.rem(d, 2)

    def place(p, count):
        a = sum(jnp.where(p >= PB * k, 1, 0) for k in range(1, count))
        return a, p - PB * a

    def token_mask(i, j):
        p = iota((PL, 1), 0)
        a, b = place(p, PA)
        inside = (p < KEYS) & (sz.rows * tile + 2 * a + i < side) & (2 * b + j < side)
        return jnp.where(inside, 1.0, 0.0)

    def row_mask(i, j, a):
        b = iota((PB, 1), 0)
        row = sz.rows * tile + 2 * a + i
        inside = (row >= 0) & (row < side) & (2 * b + j < side)
        return jnp.where(inside, 1.0, 0.0)

    def key_bias(p, tile_at):
        a, b = place(p, PA)
        usable = (p < KEYS) & (sz.rows * tile_at + 2 * a < side) & (2 * b < side)
        return jnp.where(usable, 0.0, NEG)

    def vec(ref):
        return ref[...].reshape(1, ref.shape[0])

    def own_part(row, size):
        return sum(
            jnp.where(m == h, 1.0, 0.0) * row[:, size * h : size * (h + 1)] for h in range(sz.n_mp)
        )

    def plane_rows(ref, start):
        return ref[pl.ds(pl.multiple_of(start, 16), PL), :]

    def plane(p):
        return slice(PL * p, PL * (p + 1))

    lanes3 = (s["t0"], s["t1"], s["t2"])

    def to_planes(rows_of):
        for n, ref in enumerate(lanes3):
            ref[...] = rows_of(LANES * n, min(D, LANES * (n + 1))).astype(F32).T
        for i in range(2):
            for j in range(2):
                parts = []
                for ref in lanes3:
                    rows = [
                        ref[pl.ds((2 * a + i) * sz.cols + j, PB, stride=2), :] for a in range(PA)
                    ] + [jnp.zeros((PL - KEYS, ref.shape[1]), F32)]
                    parts.append(jnp.concatenate(rows, axis=0))
                yield i, j, jnp.concatenate(parts, axis=1)

    def from_queries(rows, p):
        n = rows.shape[1]
        return jnp.concatenate([rows[KEYS * p : KEYS * (p + 1)], jnp.zeros((PL - KEYS, n), F32)], axis=0)

    def to_queries(planes):
        n = planes[0].shape[1]
        rows = [v[0:KEYS] for v in planes]
        return jnp.concatenate(rows + [jnp.zeros((sz.queries - 4 * KEYS, n), F32)], axis=0)

    xt, dfm = s["xt"], s["dfm"]
    pl.semaphore_wait(bar, len(peers))
    pix_ref.ready()
    x_at, x_mid = mp_start(xt)

    edge, edge_g, EP = s["edge"], s["edge_g"], 4 * PB
    lane_pad = jnp.zeros((FS, sz.edge_q - 2 * EP), BF)
    edge[d // 2] = jnp.concatenate([xt[m, :, 0:EP], xt[m, :, sz.tokens - EP :], lane_pad], axis=1)

    def edge_chosen(up, down):
        return jnp.concatenate([edge[up // 2][:, EP : 2 * EP], edge[down // 2][:, 0:EP], lane_pad], axis=1)

    edge_at, edge_mid = dp_pick(edge, edge_chosen, s["edge_s"], s["edge_x"])

    for i, j, value in to_planes(lambda lo, hi: cot_ref[lo:hi, :]):
        dfm[plane(2 * i + j), :] = (value * token_mask(i, j)).astype(BF)
    dyh, dyh_g = s["dyh"], s["dyh_g"]
    dyh[d // 2, :, :D] = dfm[pl.ds(pl.multiple_of(PL * m + (KEYS - PB) * (m // 2), 16), 48), :]
    dyh[d // 2, :, D:] = jnp.zeros((48, W - D), BF)
    x_mid()

    r2, c2 = iota((D, LANES), 0), iota((D, LANES), 1)
    own_lo = hot((c2 < HF) & (r2 == HF * m + c2))
    own_hi = hot((c2 >= HF) & (r2 == HF * m + c2 - HF))
    last_lo = hot((c2 < HF) & (r2 == last + c2))
    last_hi = hot((c2 >= HF) & (r2 == last + c2 - HF))
    wq, wk, wv = wq_ref[...], wk_ref[...], wv_ref[...]
    wq2 = nn(wq, own_lo + last_hi).astype(BF)
    wkv = (nn(wk, own_lo) + nn(wv, own_hi)).astype(BF)
    wkv5 = (nn(wk, last_lo) + nn(wv, last_hi)).astype(BF)
    bq, bv = vec(bq_ref), vec(bv_ref)
    bq2 = jnp.concatenate([own_part(bq, HF), bq[:, last:]], axis=1)
    nil = jnp.zeros((1, HF), F32)
    bkv = jnp.concatenate([nil, own_part(bv, HF)], axis=1)
    bkv5 = jnp.concatenate([nil, bv[:, last:]], axis=1)
    w2 = w2_ref[...]
    wo_cat = s["wo_cat"]
    wo = wo_ref[...]
    wo_cat[...] = jnp.concatenate(
        [b for h in range(4) for b in (wo[HF * h : HF * (h + 1)], wo[last:])], axis=0
    )
    wr_t = s["wr_t"]
    wr_t[...] = wr_ref[...].T

    xm_r, n1_r = s["xm_r"], s["n1_r"]
    x_at()
    x_all = xt[...].reshape(D, sz.tokens)
    for i, j, value in to_planes(lambda lo, hi: x_all[lo:hi, :]):
        xm = value * token_mask(i, j)
        xm_r[plane(2 * i + j), :] = xm.astype(BF)
        xhat, _ = spread(xm)
        n1_r[plane(2 * i + j), :] = (xhat * vec(ln1g_ref) + vec(ln1b_ref)).astype(BF)

    kva, xr_r = s["kva"], s["xr_r"]
    red = sum(nn(n1_r[plane(p), :], wr_t[D * p : D * (p + 1), :]) for p in range(4)) + vec(br_ref)
    xhr, rsr = spread(red)
    s["xhr_r"][...] = xhr
    s["rsr_r"][...] = jnp.broadcast_to(rsr, (PL, LANES))
    xr_r[...] = (xhr * vec(lnrg_ref) + vec(lnrb_ref)).astype(BF)
    kva[d, 0:PL, :] = (nn(xr_r[...], wkv) + bkv).astype(BF)
    quarter_rows = pl.ds(pl.multiple_of(sz.step * m, 16), sz.quarter)
    kva[d, PL:, :] = (nn(xr_r[quarter_rows, :], wkv5) + bkv5).astype(BF)
    _, _, kv_steps = dp_start(kva)
    edge_mid()

    def dy_chosen(up, down):
        return dyh[jnp.where(m >= 2, up, down) // 2]

    qa_r, qb_r, qc_r, qd_r = s["qa_r"], s["qb_r"], s["qc_r"], s["qd_r"]
    Q = sz.queries

    def feature_major(q_rows, own_r, last_r):
        q2t = q_rows.T
        nil = jnp.zeros((HF, q2t.shape[1]), F32)
        own_r[...] = jnp.concatenate([q2t[0:HF], nil], axis=0).astype(BF)
        last_r[...] = jnp.concatenate([q2t[HF:], nil], axis=0).astype(BF)

    def query(rows):
        return (nn(rows, wq2) + bq2).astype(BF).astype(F32) * HF ** (-0.5)

    q2 = query(n1_r[...])
    feature_major(to_queries([q2[plane(p)] for p in range(4)]), qa_r, qb_r)
    half = jnp.zeros((HF, Q), F32)

    e5buf, ebuf, ot_r = s["e5buf"], s["ebuf"], s["ot_r"]
    limit5 = jnp.where(m == sz.n_mp - 1, KEYS - sz.step * m, sz.step)
    pk, pk5 = iota((PL, 1), 0), iota((sz.quarter, 1), 0)

    def attend(ks, rows, q_r, bias_of, ebuf, o_r):
        js = [dpx(k) for k in ks]
        n = rows.stop - rows.start
        kv = jnp.concatenate([kva[j, rows, :] for j in js], axis=0)
        bias = jnp.concatenate([bias_of(j) for j in js], axis=0)
        v = nn(kv, q_r[...]) + bias
        top = jnp.max(v, axis=0, keepdims=True)
        e = jnp.exp(v - top).astype(BF)
        if ebuf is not None:
            for q, j in enumerate(js):
                ebuf[j] = e[n * q : n * (q + 1)]
        o_r[ks[0]] = tn(kv, e)[HF:]
        return ks, top, rowsum(e.astype(F32))

    def bias_own(j):
        return key_bias(pk, slot_ref[1, j])

    def bias_last(j):
        return jnp.where(pk5 < limit5, key_bias(pk5 + sz.step * m, slot_ref[1, j]), NEG)

    own, five, own_h, five_h = [], [], [], []
    ROWS, LAST = slice(0, PL), slice(PL, sz.kvrows)

    def block(*ks):
        own.append(attend(ks, ROWS, qa_r, bias_own, ebuf, s["o_own"]))
        five.append(attend(ks, LAST, qb_r, bias_last, e5buf, s["o_five"]))

    def block_h(*ks):
        own_h.append(attend(ks, ROWS, qc_r, bias_own, None, s["oh_own"]))
        five_h.append(attend(ks, LAST, qd_r, bias_last, None, s["oh_five"]))

    block(0)
    edge_at()
    up = jnp.where(
        same_x(above), edge[above // 2][:, EP : 2 * EP].astype(F32), s["edge_x"][:, 0:EP].astype(F32)
    )
    down = jnp.where(
        same_x(below), edge[below // 2][:, 0:EP].astype(F32), s["edge_x"][:, EP : 2 * EP].astype(F32)
    )
    edge_g[m] = jnp.concatenate([up, down, lane_pad.astype(F32)], axis=1).astype(BF)
    edgeg_at, edgeg_mid = mp_start(edge_g)
    kv_steps[3]()
    kv_steps[0]()
    edgeg_mid()
    block(1, 2)
    edgeg_at()

    xh_r = s["xh_r"]
    e_all = edge_g[...].reshape(D, sz.edge_q)
    for n, ref in enumerate(lanes3):
        ref[0 : sz.edge_q, :] = e_all[LANES * n : min(D, LANES * (n + 1))].astype(F32).T
    rows = []
    for i in range(2):
        for j in range(2):
            for a, first in ((-1, 0), (PA, EP)):
                at = pl.ds(first + sz.cols * i + j, PB, stride=2)
                value = jnp.concatenate([ref[at, :] for ref in lanes3], axis=1)
                rows.append(value * row_mask(i, j, a))
    xh = jnp.concatenate(rows, axis=0)
    xh_r[...] = xh.astype(BF)
    xhat, _ = spread(xh)
    q2 = query((xhat * vec(ln1g_ref) + vec(ln1b_ref)).astype(BF))
    q2 = jnp.concatenate([q2, jnp.zeros((sz.edge_q - sz.edge, LANES), F32)], axis=0)
    feature_major(q2, qc_r, qd_r)
    kv_steps[1]()
    block_h(0, 1, 2)
    kv_steps[2]()
    dy_at, dy_mid = dp_pick(dyh, dy_chosen, s["dyh_s"], s["dyh_x"])
    block(4, 6)
    block_h(4, 6)
    kv_steps[4]()
    kv_steps[5]()
    block(3, 5)
    block_h(3, 5)
    kv_steps[6]()
    block(7)
    block_h(7)

    def joined(parts, o_r):
        top = functools.reduce(jnp.maximum, [t for _, t, _ in parts])
        scale = [jnp.exp(t - top) for _, t, _ in parts]
        total = sum(f * n for f, (_, _, n) in zip(scale, parts))
        inv = 1.0 / total
        scale = [f * inv for f in scale]
        out = sum(f * o_r[ks[0]] for f, (ks, _, _) in zip(scale, parts))
        return top + jnp.log(total), {k: f for f, (ks, _, _) in zip(scale, parts) for k in ks}, out

    lse_r, LR = s["lse_r"], (Q + sz.edge_q) // LANES
    lse5, scale5, o5_t = joined(five, s["o_five"])
    lse5h, _, o5h_t = joined(five_h, s["oh_five"])
    flat = [lse5[:, LANES * n : LANES * (n + 1)] for n in range(Q // LANES)]
    flat += [lse5h[:, LANES * n : LANES * (n + 1)] for n in range(sz.edge_q // LANES)]
    lse_r[m] = jnp.concatenate(flat + [jnp.zeros((16 - LR, LANES), F32)], axis=0)
    lse_at = mp_scatter(lambda h: lse_r.at[m], lambda k: lse_r.at[m], lambda k: lse_r.at[mpx(k)])
    _, scale, o_t = joined(own, s["o_own"])
    o2 = jnp.concatenate([o_t, o5_t], axis=0).T.astype(BF)
    chunks = ((s["og_a"], s["ow_a"]), (s["og_b"], s["ow_b"]), (s["og_c"], s["ow_c"]))
    ogs = []
    for n in range(2):
        og = chunks[n][0]
        og[m] = o2[2 * KEYS * n : 2 * KEYS * (n + 1)]
        ogs.append(mp_start(og))
    _, _, oh_t = joined(own_h, s["oh_own"])
    s["og_c"][m] = jnp.concatenate([oh_t, o5h_t], axis=0).T[0 : sz.edge].astype(BF)
    ogs.append(mp_start(s["og_c"]))
    drain(12)
    rt, ct = iota((D, 4 * LANES), 0), iota((D, 4 * LANES), 1)
    lane4, head4 = ct & (LANES - 1), ct >> 7
    place_out = hot((lane4 < FS) & (rt == FS * head4 + lane4))
    rk, ck = iota((D, 5 * LANES), 0), iota((D, 5 * LANES), 1)
    lane5, head5 = ck & (LANES - 1), ck >> 7
    w_all, wq_cat, w2_t = s["w_all"], s["wq_cat"], s["w2_t"]
    w_all[...] = (
        nn(wk, hot((lane5 < HF) & (rk == HF * head5 + lane5)))
        + nn(wv, hot((lane5 >= HF) & (rk == HF * head5 + lane5 - HF)))
    ).astype(BF)
    wq_cat[...] = nn(
        wq, hot(rt == jnp.where(lane4 < HF, HF * head4 + lane4, last + lane4 - HF))
    ).astype(BF)
    w2_t[...] = w2.T
    dgx, dzx = s["dgx"], s["dzx"]
    for p in range(4):
        dgx[p, sz.top : sz.top + PL, :] = nt(dfm[plane(p), :], w2).astype(BF).astype(F32)
    dy_mid()

    lse_at()
    lse4 = [
        jnp.concatenate([lse_r[h][n : n + 1] for n in range(LR)], axis=1) for h in range(4)
    ]
    top = functools.reduce(jnp.maximum, lse4)
    whole = top + jnp.log(sum(jnp.exp(v - top) for v in lse4))
    share_all = jnp.exp(jnp.concatenate(lse4 + [jnp.zeros((4, Q + sz.edge_q), F32)], axis=0) - whole).T
    share = jnp.exp(lse5 - whole[:, 0:Q])

    def weighed(n, first):
        og, ow = chunks[n]
        rows = og.shape[1]
        lane = iota((rows, LANES), 1)
        ogs[n][0]()
        for h in range(4):
            part = share_all[first : first + rows, h : h + 1]
            ow[h] = (og[h].astype(F32) * jnp.where(lane < HF, 1.0, part)).astype(BF)
        oc = jnp.concatenate([ow[h] for h in range(4)], axis=1)
        return nn(oc, wo_cat[...]) + vec(bo_ref)

    h1_r, n2_r = s["h1_r"], s["n2_r"]

    def second_norm(h1):
        xhat, _ = spread(h1)
        return (xhat * vec(ln2g_ref) + vec(ln2b_ref)).astype(BF)

    w1, b1 = w1_ref[...], vec(b1_ref)

    def hidden(rows, mask):
        return ((nn(rows, w1) + b1) * mask).astype(BF).astype(F32)

    ux, ul, ur, dzl, dzr = s["ux"], s["ul"], s["ur"], s["dzl"], s["dzr"]
    b40 = iota((PB, 1), 0)

    def shift(src, left, right, i, start):
        at = slice(start, start + PB)
        left[i, at, :] = jnp.where(b40 == 0, 0.0, pltpu.roll(src[2 * i + 1, at, :], 1, 0))
        right[i, at, :] = jnp.where(b40 == PB - 1, 0.0, pltpu.roll(src[2 * i, at, :], PB - 1, 0))

    for n in range(2):
        mixed = weighed(n, 2 * KEYS * n)
        ogs[n + 1][1]()
        for p in (2 * n, 2 * n + 1):
            mask = token_mask(n, p % 2)
            h1 = xm_r[plane(p), :].astype(F32) + mask * from_queries(mixed, p % 2)
            h1_r[plane(p), :] = h1
            n2_r[plane(p), :] = second_norm(h1)
            ux[p, sz.top : sz.top + PL, :] = hidden(n2_r[plane(p), :], mask)
        for a in range(PA):
            shift(ux, ul, ur, n, sz.top + PB * a)

    wd_ref, bd_row = wd_ref.ready(), vec(bd_ref)
    g_r, du_r = s["g_r"], s["du_r"]
    for p in range(4):
        g_r[p, KEYS:PL, :] = jnp.zeros((PL - KEYS, C), F32)
        du_r[p, KEYS:PL, :] = jnp.zeros((PL - KEYS, C), F32)

    def source(refs, i, j, di, dj, start):
        base, left, right = refs
        i2, up = (i + di) % 2, (i + di) // 2
        j2, across = (j + dj) % 2, (j + dj) // 2
        at = pl.ds(pl.multiple_of(start + PB * up, 8), PB)
        if across < 0:
            return left[i2, at, :]
        if across > 0:
            return right[i2, at, :]
        return base[2 * i2 + j2, at, :]

    TAPS = [(di, dj) for di in (-1, 0, 1) for dj in (-1, 0, 1)]

    def activation(i, j, start):
        p = 2 * i + j
        z = bd_row + sum(
            wd_ref[t : t + 1, :] * source((ux, ul, ur), i, j, di, dj, start)
            for t, (di, dj) in enumerate(TAPS)
        )
        phi = 0.5 * (1.0 + lax.erf(z * 0.7071067811865476))
        dens = jnp.exp(-0.5 * z * z) * 0.3989422804014327
        dz = dgx[p, pl.ds(pl.multiple_of(start, 8), PB), :] * (phi + z * dens)
        dzx[p, pl.ds(pl.multiple_of(start, 8), PB), :] = dz
        return z * phi, dz

    def fold(value):
        return jnp.sum(value.reshape(PB // 8, 8, C), axis=0)

    def forward_step(i, j):
        p = 2 * i + j

        def step(a, acc):
            start = sz.top + PB * a
            act, dz = activation(i, j, start)
            g_r[p, pl.ds(pl.multiple_of(PB * a, 8), PB), :] = act
            new = [
                acc[t] + fold(dz * source((ux, ul, ur), i, j, di, dj, start))
                for t, (di, dj) in enumerate(TAPS)
            ]
            return tuple(new) + (acc[9] + fold(dz),)

        return step

    dy_at()
    beside_j = jnp.where(m >= 2, above, below)
    dyh_g[m] = jnp.where(
        same_x(beside_j), dyh[beside_j // 2].astype(F32), s["dyh_x"][...].astype(F32)
    ).astype(BF)
    dyg_at, dyg_mid = mp_start(dyh_g)

    sums = tuple(jnp.zeros((8, C), F32) for _ in range(10))
    for i in range(2):
        for j in range(2):
            sums = lax.fori_loop(1 - i, PA - i, forward_step(i, j), sums)
    for i in range(2):
        for a in range(1, PA):
            shift(dzx, dzl, dzr, i, sz.top + PB * (a - i))

    def backward_step(i, j):
        p = 2 * i + j

        def step(a, carry):
            start = sz.top + PB * a
            du_r[p, pl.ds(pl.multiple_of(PB * a, 8), PB), :] = sum(
                wd_ref[t : t + 1, :] * source((dzx, dzl, dzr), i, j, -di, -dj, start)
                for t, (di, dj) in enumerate(TAPS)
            )
            return carry

        return step

    dyg_mid()
    for i in range(2):
        for j in range(2):
            lax.fori_loop(1, PA - 1, backward_step(i, j), 0)
    ot_r[...] = jnp.concatenate([o_t, o5_t * share], axis=0)
    mixed = weighed(2, Q)
    dyg_at()
    for p in range(4):
        i, j = p // 2, p % 2
        start = sz.top - PB if i == 1 else sz.top + KEYS
        rows = dyh_g[p][:, :D].astype(F32)[0:PB] * row_mask(i, j, -1 if i == 1 else PA)
        dgx[p, start : start + PB, :] = nt(rows.astype(BF), w2).astype(BF).astype(F32)
    xh = xh_r[...].astype(F32)
    for p in range(4):
        i, j = p // 2, p % 2
        mask = jnp.concatenate([row_mask(i, j, -1), row_mask(i, j, PA)], axis=0)
        at = slice(2 * PB * p, 2 * PB * (p + 1))
        u = hidden(second_norm(xh[at] + mask * mixed[at]), mask)
        ux[p, sz.top - PB : sz.top, :] = u[0:PB]
        ux[p, sz.top + KEYS : sz.top + KEYS + PB, :] = u[PB:]
    for i in range(2):
        shift(ux, ul, ur, i, sz.top - PB)
        shift(ux, ul, ur, i, sz.top + KEYS)
    for i in range(2):
        for j in range(2):
            activation(i, j, sz.top - PB if i == 1 else sz.top + KEYS)
            sums = forward_step(i, j)((PA - 1) * i, sums)
    e_s, ve_s, vl_s = s["e_s"], s["ve_s"], s["vl_s"]
    shift(dzx, dzl, dzr, 0, sz.top)
    shift(dzx, dzl, dzr, 0, sz.top + KEYS)
    shift(dzx, dzl, dzr, 1, sz.top - PB)
    shift(dzx, dzl, dzr, 1, sz.top + KEYS - PB)
    dub = s["dub"]
    for i in range(2):
        for j in range(2):
            p = 2 * i + j
            for a in (0, PA - 1):
                backward_step(i, j)(a, 0)
            dub[p] = (du_r[p].astype(BF).astype(F32) * token_mask(i, j)).astype(BF)
    def packed(value):
        n = value.shape[0] // 2
        parts = [value[:, 0:LANES], value[:, LANES : 2 * LANES]]
        parts.append(jnp.concatenate([value[0:n, 2 * LANES :], value[n:, 2 * LANES :]], axis=1))
        return jnp.concatenate(parts, axis=0)

    def unpacked(value, rows):
        n = rows // 2
        rest = value[2 * rows : 2 * rows + n]
        rest = jnp.concatenate([rest[:, 0:HF], rest[:, HF:]], axis=0)
        return jnp.concatenate([value[0:rows], value[rows : 2 * rows], rest], axis=1)

    def dn2_block(h):
        value = packed(nt(dub[h], w1))
        rest = jnp.zeros((sz.prows - value.shape[0], LANES), F32)
        return jnp.concatenate([value, rest], axis=0)

    dn2_mid, dn2_at = mp_sum(dn2_block, s["dn2_s"], s["dn2_n"], s["dn2_f"])
    dn2_mid()

    gb = g_r[...].reshape(T, C).astype(BF)
    du_all = dub[...].reshape(T, C)
    e_s[0:D, :C] = tn(n2_r[...], du_all).astype(BF)
    e_s[D:, :D] = tn(gb, dfm[...]).astype(BF)

    def rows_of(ref, n):
        return lambda j: ref.at[pl.ds(pl.multiple_of(n * j, 16), n)]

    e_mid, e_at = dp_sum(rows_of(e_s, sz.echunk), s["e_n"], s["e_o"], s["e_f"])
    for t in range(10):
        ve_s[t : t + 1, :C] = rowsum(sums[t])
    ve_s[10:11, :C] = rowsum(du_all.astype(F32))

    for k in range(sz.n_dp):
        j = dpx(k)
        ebuf[j] = (ebuf[j].astype(F32) * scale[k]).astype(BF)
        e5buf[j] = (e5buf[j].astype(F32) * (scale5[k] * share)).astype(BF)
    ogp = s["ogp"]
    lane = iota((PL, LANES), 1)
    for n, (og, ow) in enumerate(chunks[:2]):
        mine, fifth = og[m].astype(F32), sum(ow[h].astype(F32) for h in range(4))
        for q in range(2):
            ogp[plane(2 * n + q), :] = jnp.where(
                lane < HF, from_queries(mine, q), from_queries(fifth, q)
            ).astype(BF)

    drain(12)

    xhat2, rstd2 = spread(plane_rows(h1_r, PL * m))
    dfp = plane_rows(dfm, PL * m).astype(F32)
    ve_s[11:12, :D] = rowsum(dfp)
    dn2 = unpacked(dn2_at(), PL)
    dh1 = dfp + norm_back(dn2, vec(ln2g_ref), xhat2, rstd2)
    dab = dh1.astype(BF)
    docat = nt(dab, wo_cat[...]).astype(BF)
    dos, do_all, dabg = s["dos"], s["do_all"], s["dabg"]
    for h in range(4):
        dos[h] = docat[:, LANES * h : LANES * (h + 1)]
    do_at = mp_scatter(lambda h: dos.at[h], lambda k: do_all.at[m], lambda k: do_all.at[mpx(k)])
    do_all[m] = dos[m]
    s["dh1_r"][...] = dh1
    dabg[m, :, :D] = dab
    ve_s[12:13, :D] = rowsum(dh1)
    ve_s[13:14, :D] = rowsum(dn2 * xhat2)
    ve_s[14:15, :D] = rowsum(dn2)
    ve_s[15:16, :] = jnp.zeros((1, W), F32)
    ve_mid, ve_at = dp_total(ve_s, s["ve_n"], s["ve_p"])
    e_mid()

    def ff_block(h):
        return nt(w2_t[pl.ds(pl.multiple_of(FS * h, 16), FS), :], gb)

    ff_mid, ff_at = mp_sum(ff_block, s["ff_s"], s["ff_n"], s["ff_f"])

    drain(16)
    do_at()
    ve_mid()
    dr_r = s["dr_r"]
    dot_t = to_queries([do_all[p].astype(F32) for p in range(4)]).T
    d_row = rowsum(dot_t[HF:] * ot_r[HF:, :])
    d_row = [d_row[:, LANES * n : LANES * (n + 1)] for n in range(Q // LANES)]
    dr_r[m] = jnp.concatenate(d_row + [jnp.zeros((8 - len(d_row), LANES), F32)], axis=0)
    dr_at = mp_scatter(lambda h: dr_r.at[m], lambda k: dr_r.at[m], lambda k: dr_r.at[mpx(k)])
    drow = rowsum(dot_t[0:HF] * ot_r[0:HF, :])
    da_t = jnp.concatenate([half, dot_t[0:HF]], axis=0).astype(BF)
    db_t = jnp.concatenate([half, dot_t[HF:]], axis=0).astype(BF)
    dqt, dqt5 = s["dqt"], s["dqt5"]
    dqt[...] = jnp.zeros_like(dqt)
    dqt5[...] = jnp.zeros_like(dqt5)
    five_row = []

    def key_grads(js, rows, ebuf, q_r, do_t, d_row, dq):
        n = rows.stop - rows.start
        kv = jnp.concatenate([kva[j, rows, :] for j in js], axis=0)
        e = jnp.concatenate([ebuf[j] for j in js], axis=0)
        ds = (e.astype(F32) * (nn(kv, do_t) - d_row)).astype(BF)
        value = nt(ds, q_r[...]) + nt(e, do_t)
        dq[...] += tn(kv, ds)
        return [value[n * q : n * (q + 1)] for q in range(len(js))]

    def own_keys(*ks):
        return key_grads([dpx(k) for k in ks], ROWS, ebuf, qa_r, da_t, drow, dqt)

    def last_keys(*ks):
        return key_grads([dpx(k) for k in ks], LAST, e5buf, qb_r, db_t, five_row[0], dqt5)

    dk_x, dk_n, dk_o, dk_f = s["dk_x"], s["dk_n"], s["dk_o"], s["dk_f"]
    dl_x, dl_n, dl_o, dl_f = s["dl_x"], s["dl_n"], s["dl_o"], s["dl_f"]
    dk_at = take(8)
    dl_at = take(4)
    for pair in ((2, 3), (1, 0)):
        for kz, value in zip(pair, own_keys(*(2 * kz + 1 for kz in pair))):
            dk_x[kz] = value.astype(BF)
            send(dk_x.at[kz], dk_n.at[kz], dk_at + kz, (dpx(1), m))
    dr_at()
    dab_at, dab_mid = mp_start(dabg)
    d_sum = sum(dr_r[h] for h in range(4))
    five_row.append(jnp.concatenate([d_sum[n : n + 1] for n in range(Q // LANES)], axis=1))
    for kz, value in enumerate(last_keys(1, 3, 5, 7)):
        dl_x[kz] = value.astype(BF)
    send(dl_x, dl_n, dl_at, (dpx(1), m))

    def dk_along(kz, value):
        arrived(dk_n.at[kz], dk_at + kz)
        dk_o[kz] = (value + dk_n[kz].astype(F32)).astype(BF)
        send(dk_o.at[kz], dk_f.at[kz], dk_at + 4 + kz, (dpx(2 * kz), m))

    for kz, value in zip((2, 3), own_keys(4, 6)):
        dk_along(kz, value)
    value, dkv = own_keys(2, 0)
    dk_along(1, value)
    dab_mid()
    dkl, *values = last_keys(0, 2, 4, 6)
    arrived(dl_n, dl_at)
    for kz in (2, 3, 1):
        dl_o[kz] = (values[kz - 1] + dl_n[kz].astype(F32)).astype(BF)
        send(dl_o.at[kz], dl_f.at[kz], dl_at + kz, (dpx(2 * kz), m))
    ff_mid()

    def dk_finish():
        arrived(dk_n.at[0], dk_at)
        total, last = dkv + dk_n[0].astype(F32), dkl + dl_n[0].astype(F32)
        for kz in (1, 2, 3):
            arrived(dk_f.at[kz], dk_at + 4 + kz)
            total = total + dk_f[kz].astype(F32)
        for kz in (1, 2, 3):
            arrived(dl_f.at[kz], dl_at + kz)
            last = last + dl_f[kz].astype(F32)
        return jnp.concatenate([total, last], axis=0)

    dk_fin = handle(dk_finish)

    dq2 = (jnp.concatenate([dqt[0:HF], dqt5[0:HF]], axis=0) * HF ** (-0.5)).T
    dqs, dq_all = s["dqs"], s["dq_all"]
    for h in range(4):
        dqs[h] = from_queries(dq2, h).astype(BF)
    l1_s, l2_s = s["l1_s"], s["l2_s"]
    dqp = dqs[...].reshape(T, LANES)
    l1_s[0:D, :] = tn(n1_r[...], dqp).astype(BF)
    vl_s[...] = jnp.zeros_like(vl_s)
    vl_s[5:6, 0:LANES] = rowsum(dqp.astype(F32))

    def fill(ref, first, value):
        rest = jnp.zeros((ref.shape[0] - first - value.shape[0], LANES), F32)
        ref[first:, :] = jnp.concatenate([value, rest], axis=0).astype(BF)

    def own_rows(value, n):
        return sum(jnp.where(m == h, 1.0, 0.0) * value[n * h : n * (h + 1)] for h in range(4))

    dab_at()
    gwo = tn(ogp[...], dabg[...].reshape(T, W)[:, :D])
    fill(l1_s, 2 * D, packed(jnp.concatenate([gwo[0:HF], own_rows(gwo[HF:], HF // 4)], axis=0)))

    dkvb = dk_fin().astype(BF)
    dkvg = s["dkvg"]
    dkvg[m] = dkvb
    dkv_at, dkv_mid = mp_start(dkvg)
    l1_s[D : 2 * D, :] = tn(xr_r[...], dkvb[0:PL]).astype(BF)
    l1_mid, l1_at = dp_sum(rows_of(l1_s, sz.l1rows // sz.n_dp), s["l1_n"], s["l1_o"], s["l1_f"])
    eg_ref[d] = e_at().astype(BF)
    eg_at, eg_mid, _ = dp_start(eg_ref)
    vl_s[6:7, 0:LANES] = jnp.concatenate(
        [rowsum(dkvb[0:PL].astype(F32))[:, HF:], rowsum(dkvb[PL:].astype(F32))[:, HF:]], axis=1
    )
    dkv_mid()
    dq_at = mp_scatter(lambda h: dqs.at[h], lambda k: dq_all.at[m], lambda k: dq_all.at[mpx(k)])
    dq_all[m] = dqs[m]
    drain(12)
    dkv_mid()
    dkv_at()
    l1_mid()
    rest = jnp.concatenate(
        [dkvg[h, PL : PL + sz.step, :] for h in range(3)] + [dkvg[3, PL:, :]], axis=0
    )
    dkv_all = jnp.concatenate([dkvg[h, 0:PL, :] for h in range(4)] + [rest], axis=1)
    dxr = nt(dkv_all, w_all[...])
    xhr = s["xhr_r"][...]
    drb = norm_back(dxr, vec(lnrg_ref), xhr, s["rsr_r"][:, 0:1]).astype(BF)
    l2_s[0 : sz.wrows, :] = packed(tn(drb, plane_rows(n1_r, PL * m))).astype(BF)
    fill(l2_s, sz.wrows, own_rows(tn(xr_r[...], rest), FS))
    l2_mid, l2_at = dp_sum(rows_of(l2_s, sz.l2rows // sz.n_dp), s["l2_n"], s["l2_o"], s["l2_f"])
    vl_s[2:3, :D] = rowsum(dxr * xhr)
    vl_s[3:4, :D] = rowsum(dxr)
    vl_s[4:5, :D] = rowsum(drb.astype(F32))

    wr_m = wr_t[pl.ds(pl.multiple_of(D * m, 16), D), :]
    dq_at()
    dq_cat = jnp.concatenate([dq_all[h] for h in range(4)], axis=1)
    dn1 = nt(dq_cat, wq_cat[...])
    xhat1, rstd1 = spread(plane_rows(xm_r, PL * m).astype(F32))
    dn1 = dn1 + nt(drb, wr_m)
    vl_s[0:1, :D] = rowsum(dn1 * xhat1)
    vl_s[1:2, :D] = rowsum(dn1)
    vl_mid, vl_at = dp_total(vl_s, s["vl_n"], s["vl_p"])
    dxm = norm_back(dn1, vec(ln1g_ref), xhat1, rstd1)
    gp = (token_mask(m // 2, lax.rem(m, 2)) * (s["dh1_r"][...] + dxm)).astype(BF)
    gpf = nn(gp, place_out).astype(BF)
    gps = s["gps"]
    for h in range(4):
        gps[h] = gpf[:, LANES * h : LANES * (h + 1)]
    gp_at = mp_scatter(lambda h: gps.at[h], lambda k: gp_ref.at[m], lambda k: gp_ref.at[mpx(k)])
    gp_ref[m] = gps[m]

    veg_ref[m] = ve_at()
    veg_at, _ = mp_start(veg_ref)

    def gather(buf):
        base = take(3 * sz.n_dp)

        def onward(k):
            j = dpx(k)
            send(buf.at[m, j], buf.at[m, j], base + 3 * k, (d, mpx(1)))
            send(buf.at[m, j], buf.at[m, j], base + 3 * k + 1, (d, mpx(2)))

        near, mid, steps = dp_start(buf.at[m], onward)
        onward(0)
        seq = (0, 2, 4, 6, 1, 3, 5, 7)

        def relay(k):
            j = dpx(k)
            arrived(buf.at[mpx(2), j], base + 3 * k + 1)
            send(buf.at[mpx(2), j], buf.at[mpx(2), j], base + 3 * k + 2, (d, mpx(1)))

        relays = [handle(lambda k=k: relay(k)) for k in seq]

        def finish():
            near()
            for r in relays:
                r()
            for k in seq:
                arrived(buf.at[mpx(1), dpx(k)], base + 3 * k)
                arrived(buf.at[mpx(3), dpx(k)], base + 3 * k + 2)

        return near, mid, relays, handle(finish)

    drain(12)
    eg_mid()
    lg1_ref[m, d] = l1_at().astype(BF)
    near1, mid1, relays1, lg1_at = gather(lg1_ref)
    l2_mid()
    vl_mid()
    ff = ff_at().T
    ff = jnp.concatenate([ff, jnp.zeros((T, LANES - FS), F32)], axis=1)
    sel = hot((c2 < FS) & (r2 == FS * m + c2))
    b2q = jnp.concatenate(
        [own_part(vec(b2_ref), FS), jnp.zeros((1, LANES - FS), F32)], axis=1
    )
    for p in range(4):
        h1 = h1_r[plane(p), :]
        hi = h1.astype(BF)
        h1q = nn(hi, sel) + nn((h1 - hi.astype(F32)).astype(BF), sel)
        blk_ref[plane(p), :] = h1q + token_mask(p // 2, p % 2) * (ff[plane(p)] + b2q)
    mid1()
    drain(24)
    lg2_ref[m, d] = l2_at().astype(BF)
    near2, mid2, relays2, lg2_at = gather(lg2_ref)
    near1()
    vlg_ref[m] = vl_at()
    vlg_at, _ = mp_start(vlg_ref)
    for r in relays1[:4]:
        r()
    drain(16)
    mid2()
    for r in relays1[4:]:
        r()
    drain(24)
    near2()
    drain(16)
    for r in relays2:
        r()
        drain(16)
    eg_at()
    gp_at()
    veg_at()
    lg1_at()
    vlg_at()
    lg2_at()
    drain()


def unpack_body(sz, *refs):
    srcs, refs = refs[:7], refs[7:]
    dsts, refs = refs[:23], refs[23:]
    (
        out_ref, gpix_ref, ln1g_ref, ln1b_ref, gwq_ref, gbq_ref, gwk_ref, gwv_ref, gbv_ref, gwr_ref, gbr_ref,
        lnrg_ref, lnrb_ref, gwo_ref, gbo_ref, ln2g_ref, ln2b_ref, gw1_ref, gb1_ref, gwd_ref, gbd_ref,
        gw2_ref, gb2_ref,
    ), outs, refs = refs[:23], refs[:23], refs[23:]
    out32, gp32, osem = refs
    stores = []

    def store(*which):
        for i in which:
            c = pltpu.make_async_copy(outs[i], dsts[i], osem.at[i])
            c.start()
            stores.append(c)

    blk_ref, gp_ref, eg_ref, lg1_ref, lg2_ref, veg_ref, vlg_ref = srcs
    D, HF, PB, PA, PL = sz.width, HEAD_FEATURES, sz.pb, sz.pa, sz.plane
    C, FS = sz.hidden, sz.share
    m = lax.axis_index("mp")

    def row(value):
        return value.reshape(value.shape[1])

    ve = veg_ref[m]
    gwd_ref[...] = ve[0:9, :C]
    gbd_ref[...] = row(ve[9:10, :C])
    gb1_ref[...] = row(ve[10:11, :C])
    vs = sum(veg_ref[h] for h in range(4))
    gb2_ref[...] = row(vs[11:12, :D])
    gbo_ref[...] = row(vs[12:13, :D])
    ln2g_ref[...] = row(vs[13:14, :D])
    ln2b_ref[...] = row(vs[14:15, :D])
    vl = sum(vlg_ref[h] for h in range(4))
    ln1g_ref[...] = row(vl[0:1, :D])
    ln1b_ref[...] = row(vl[1:2, :D])
    lnrg_ref[...] = row(vlg_ref[0][2:3, :D])
    lnrb_ref[...] = row(vlg_ref[0][3:4, :D])
    gbr_ref[...] = row(vlg_ref[0][4:5, :D])

    def head_row(r):
        parts = [vlg_ref[h][r : r + 1, 0:HF] for h in range(4)] + [vl[r : r + 1, HF : 2 * HF]]
        return row(jnp.concatenate(parts, axis=1))

    gbq_ref[...] = head_row(5)
    gbv_ref[...] = head_row(6)
    store(2, 3, 5, 8, 10, 11, 12, 14, 15, 16, 18, 19, 20, 22)
    for i in range(2):
        for j in range(2):
            p = 2 * i + j
            for a in range(PA):
                at = pl.ds((2 * a + i) * sz.cols + j, PB, stride=2)
                out32[at, :] = blk_ref[PL * p + PB * a : PL * p + PB * (a + 1), 0:FS]
                gp32[at, :] = gp_ref[p].astype(F32)[PB * a : PB * (a + 1), 0:FS]
    out_ref[...] = out32[...].T.astype(BF)
    gpix_ref[...] = gp32[...].T
    store(0, 1)
    eg = eg_ref[...].reshape(D + C, sz.wide)
    gw1_ref[...] = eg[0:D, :C].astype(F32)
    gw2_ref[...] = eg[D:, :D].astype(F32)
    store(17, 21)

    def unpacked(value):
        n = value.shape[0] * 2 // 5
        tail = value[2 * n :]
        tail = jnp.concatenate([tail[:, 0:HF], tail[:, HF:]], axis=0)
        return jnp.concatenate([value[0:n], value[n : 2 * n], tail], axis=1)

    lg1 = [lg1_ref[h].reshape(sz.l1rows, LANES).astype(F32) for h in range(4)]
    lg2 = [lg2_ref[h].reshape(sz.l2rows, LANES).astype(F32) for h in range(4)]
    tail = jnp.concatenate([lg2[h][sz.wrows : sz.wrows + FS] for h in range(4)], axis=0)
    fifth = sum(lg1[h][0:D, HF:] for h in range(4))
    gwq_ref[...] = jnp.concatenate([lg1[h][0:D, 0:HF] for h in range(4)] + [fifth], axis=1)
    gwk_ref[...] = jnp.concatenate([lg1[h][D : 2 * D, 0:HF] for h in range(4)] + [tail[:, 0:HF]], axis=1)
    gwv_ref[...] = jnp.concatenate([lg1[h][D : 2 * D, HF:] for h in range(4)] + [tail[:, HF:]], axis=1)
    store(4, 6, 7)
    gwr_ref[...] = jnp.concatenate([unpacked(lg2[h][0 : sz.wrows]) for h in range(4)], axis=1)
    store(9)
    n = HF // 4
    for h in range(4):
        wo = unpacked(lg1[h][2 * D : 2 * D + 5 * sz.orows // 2])
        gwo_ref[HF * h : HF * (h + 1), :] = wo[0:HF]
        gwo_ref[4 * HF + n * h : 4 * HF + n * (h + 1), :] = wo[HF:]
    store(13)
    for c in stores:
        c.wait()


def on_device_fused(*args):
    pixels_in, cotangent, pixel_mask, tile_slot = args[:4]
    w_fc1 = args[19]
    sz = Sizes(
        lax.axis_size("dp"), lax.axis_size("mp"), pixels_in.shape[0], cotangent.shape[1], w_fc1.shape[1]
    )
    D, C, PL, T, W, LN, HF = sz.width, sz.hidden, sz.plane, sz.all, sz.wide, LANES, HEAD_FEATURES
    Q, N, PB = sz.queries, sz.n_dp, sz.pb
    sm = pl.BlockSpec(memory_space=pltpu.SMEM)
    vm = pl.BlockSpec(memory_space=pltpu.VMEM)
    hbm = pl.BlockSpec(memory_space=pltpu.HBM)
    S = jax.ShapeDtypeStruct
    ins = [pixels_in.T, cotangent.T, *args[4:11], args[11].T, *args[12:]]
    mids = [
        S((T, LN), F32), S((4, PL, LN), BF), S((N, sz.echunk, W), BF), S((4, N, sz.l1rows // N, LN), BF),
        S((4, N, sz.l2rows // N, LN), BF), S((4, 16, W), F32), S((4, 8, W), F32),
    ]
    chunks = dict(e=(sz.echunk, W), l1=(sz.l1rows // N, LN), l2=(sz.l2rows // N, LN))
    shapes = {
        BF: dict(
            xt=(4, sz.share, sz.tokens), dfm=(T, D), dyh=(4, 48, W), dyh_s=(48, W), dyh_x=(48, W), dyh_g=(4, 48, W),
            edge=(4, sz.share, sz.edge_q), edge_s=(sz.share, sz.edge_q), edge_x=(sz.share, sz.edge_q),
            edge_g=(4, sz.share, sz.edge_q), xh_r=(sz.edge, D), qc_r=(LN, sz.edge_q), qd_r=(LN, sz.edge_q), xm_r=(T, D), n1_r=(T, D),
            xr_r=(PL, D), kva=(N, sz.kvrows, LN), qa_r=(LN, Q), qb_r=(LN, Q), ebuf=(N, PL, Q),
            e5buf=(N, sz.quarter, Q), og_a=(4, 2 * sz.keys, LN), og_b=(4, 2 * sz.keys, LN), og_c=(4, sz.edge, LN),
            ow_a=(4, 2 * sz.keys, LN), ow_b=(4, 2 * sz.keys, LN), ow_c=(4, sz.edge, LN), n2_r=(T, D),
            dub=(4, PL, C), dn2_s=(3, sz.prows, LN), dn2_n=(2, sz.prows, LN),
            dn2_f=(sz.prows, LN), dos=(4, PL, LN), do_all=(4, PL, LN), dabg=(4, PL, W), ff_s=(3, sz.share, T), ff_n=(2, sz.share, T),
            ff_f=(sz.share, T), **{"dk_" + k: (4, PL, LN) for k in "xnof"}, **{"dl_" + k: (4, sz.quarter, LN) for k in "xnof"}, dkvg=(4, sz.kvrows, LN), dqs=(4, PL, LN), dq_all=(4, PL, LN),
            e_s=(D + C, W), gps=(4, PL, LN), wr_t=(4 * D, D), ogp=(T, LN),
            w2_t=(D, C), w_all=(D, 5 * LN), wq_cat=(D, 4 * LN), wo_cat=(4 * LN, D), l1_s=(sz.l1rows, LN),
            l2_s=(sz.l2rows, LN),
            **{n + "_" + k: (4, *v) for k in "nof" for n, v in chunks.items()},
        ),
        F32: dict(
            t0=(sz.tokens, LN), t1=(sz.tokens, LN), t2=(sz.tokens, D - 2 * LN), xhr_r=(PL, D), rsr_r=(PL, LN),
            o_own=(N, HF, Q), o_five=(N, HF, Q), oh_own=(N, HF, sz.edge_q), oh_five=(N, HF, sz.edge_q),
            lse_r=(4, 16, LN), ot_r=(LN, Q),
            h1_r=(T, D), ux=(4, sz.ext, C), ul=(2, sz.ext, C), ur=(2, sz.ext, C), dgx=(4, sz.ext, C),
            dzx=(4, sz.ext, C), dzl=(2, sz.ext, C), dzr=(2, sz.ext, C), g_r=(4, PL, C), du_r=(4, PL, C),
            dh1_r=(PL, D), dr_r=(4, 8, LN), dqt=(LN, Q), dqt5=(LN, Q), ve_s=(16, W), ve_n=(16, W),
            ve_p=(4, 16, W), vl_s=(8, W), vl_n=(8, W), vl_p=(4, 8, W),
        ),
    }
    scratch = {k: pltpu.VMEM(v, t) for t, group in shapes.items() for k, v in group.items()}
    for i in range(1, len(ins)):
        scratch["in%d" % i] = pltpu.VMEM(ins[i].shape, ins[i].dtype)
    scratch["ssem"] = pltpu.SemaphoreType.DMA((200,))
    scratch["rsem"] = pltpu.SemaphoreType.DMA((200,))
    scratch["isem"] = pltpu.SemaphoreType.DMA((len(ins),))
    mid = pl.pallas_call(
        functools.partial(fused_body, sz, tuple(scratch)),
        out_shape=[pltpu.VMEM(v.shape, v.dtype) for v in mids],
        in_specs=[sm, sm] + [hbm] * len(ins),
        out_specs=[vm] * len(mids),
        scratch_shapes=list(scratch.values()),
        compiler_params=pltpu.CompilerParams(
            collective_id=0, has_side_effects=True, vmem_limit_bytes=VMEM_MB * 2**20
        ),
        name="fused_block",
    )(pixel_mask, tile_slot.T, *(pltpu.with_memory_space_constraint(v, pltpu.HBM) for v in ins))
    outs = [
        S((sz.share, sz.tokens), BF), S((sz.share, sz.tokens), F32), S((D,), F32), S((D,), F32), S((D, D), F32),
        S((D,), F32), S((D, D), F32), S((D, D), F32), S((D,), F32), S((D, 4 * D), F32), S((D,), F32), S((D,), F32),
        S((D,), F32), S((D, D), F32), S((D,), F32), S((D,), F32), S((D,), F32), S((D, C), F32), S((C,), F32),
        S((9, C), F32), S((C,), F32), S((C, D), F32), S((D,), F32),
    ]
    res = list(
        pl.pallas_call(
            functools.partial(unpack_body, sz),
            out_shape=outs,
            in_specs=[vm] * len(mids),
            out_specs=[hbm] * len(outs),
            scratch_shapes=[pltpu.VMEM(v.shape, v.dtype) for v in outs]
            + [pltpu.VMEM((sz.tokens, sz.share), F32)] * 2
            + [pltpu.SemaphoreType.DMA((len(outs),))],
            compiler_params=pltpu.CompilerParams(vmem_limit_bytes=40 * 2**20),
            name="unpack",
        )(*mid)
    )
    for k in (0, 1, 9):
        res[k] = res[k].T
    return tuple(res)


def choose(*args):
    tokens, width = args[1].shape
    whole_rows = tokens == FRAME * (FRAME // TILE_ROWS)
    shape = (lax.axis_size("dp"), lax.axis_size("mp"))
    if whole_rows and shape == (TILE_ROWS, 4) and TILE_ROWS == 8 and HEADS == 5 and width == 320 == args[19].shape[1]:
        return on_device_fused(*args)
    return on_device(*args)


def solution(mesh):
    return jax.shard_map(
        choose,
        mesh=mesh,
        in_specs=(
            P("dp", "mp"),
            P("dp", None),
            P("dp"),
            P(),
            P(),
            P(),
            P(),
            P(),
            P(),
            P(),
            P(),
            P(),
            P(),
            P(),
            P(),
            P(),
            P(),
            P(),
            P(),
            P(None, "mp"),
            P("mp"),
            P(None, "mp"),
            P("mp"),
            P("mp", None),
            P(),
        ),
        out_specs=(
            P("dp", "mp"),
            P("dp", "mp"),
            P(),
            P(),
            P(),
            P(),
            P(),
            P(),
            P(),
            P(),
            P(),
            P(),
            P(),
            P(),
            P(),
            P(),
            P(),
            P(None, "mp"),
            P("mp"),
            P(None, "mp"),
            P("mp"),
            P("mp", None),
            P(),
        ),
        check_vma=False,
    )
```

```python
import functools

import jax
import jax.numpy as jnp
from jax import lax
from jax.experimental import pallas as pl
from jax.experimental.pallas import tpu as pltpu
from jax.sharding import PartitionSpec as P

HEADS = 5
HEAD_FEATURES = 64
FRAME = 80
TILE_ROWS = 8


EPS = 1e-05
NEG = -1e30


def layer_norm(value, gain, shift):
    mean = jnp.mean(value, axis=-1, keepdims=True)
    centred = value - mean
    spread = jnp.mean(centred * centred, axis=-1, keepdims=True)
    return centred * lax.rsqrt(spread + EPS) * gain + shift


def depth_gelu(padded, kernel, shift):
    rows = padded.shape[0] - 2
    cols = padded.shape[1] - 2
    total = jnp.zeros((rows, cols, padded.shape[2]), jnp.float32) + shift
    for row_off in range(3):
        for col_off in range(3):
            total = (
                total
                + kernel[3 * row_off + col_off]
                * padded[row_off : row_off + rows, col_off : col_off + cols]
            )
    return jax.nn.gelu(total, approximate=False)


def mat(left, right):
    return jnp.dot(left, right, preferred_element_type=jnp.float32)


def pick(weights, table):
    return jnp.einsum(
        "j,jab->ab", weights.astype(table.dtype), table, preferred_element_type=jnp.float32
    )


def head_columns(weight_matrix, select_where):
    wide_layout = weight_matrix.astype(jnp.float32).reshape(
        weight_matrix.shape[0], HEADS, HEAD_FEATURES
    )
    return (
        jnp.einsum("uzx,nz->unx", wide_layout, select_where)
        .reshape(weight_matrix.shape[0], -1)
        .astype(jnp.bfloat16)
    )


def head_rows(weight_matrix, select_where):
    wide_layout = weight_matrix.astype(jnp.float32).reshape(
        HEADS, HEAD_FEATURES, weight_matrix.shape[1]
    )
    return (
        jnp.einsum("hed,sh->sed", wide_layout, select_where)
        .reshape(-1, weight_matrix.shape[1])
        .astype(jnp.bfloat16)
    )


def head_vector(vector_entries, select_where):
    return jnp.einsum(
        "he,sh->se", vector_entries.reshape(HEADS, HEAD_FEATURES), select_where
    ).reshape(-1)


def spread_columns(gradient_value, select_where):
    return jnp.einsum(
        "tvm,vq->tqm",
        gradient_value.reshape(gradient_value.shape[0], -1, HEAD_FEATURES),
        select_where,
    ).reshape(gradient_value.shape[0], -1)


def spread_rows(gradient_value, select_where):
    return jnp.einsum(
        "sed,sh->hed",
        gradient_value.reshape(-1, HEAD_FEATURES, gradient_value.shape[1]),
        select_where,
    ).reshape(-1, gradient_value.shape[1])


def spread_vector(gradient_value, select_where):
    return jnp.einsum("se,sh->he", gradient_value.reshape(-1, HEAD_FEATURES), select_where).reshape(
        -1
    )


def on_device(
    pixels_in,
    cotangent,
    pixel_mask,
    tile_slot,
    ln1_gain,
    ln1_bias,
    w_query,
    b_query,
    w_key,
    w_value,
    b_value,
    w_reduce,
    b_reduce,
    lnr_gain,
    lnr_bias,
    w_out,
    b_out,
    ln2_gain,
    ln2_bias,
    w_fc1,
    b_fc1,
    w_depth,
    b_depth,
    w_fc2,
    b_fc2,
):
    n_dp = lax.axis_size("dp")
    n_mp = lax.axis_size("mp")
    device = lax.axis_index("dp")
    part = lax.axis_index("mp")
    rows = FRAME // TILE_ROWS
    tokens = pixels_in.shape[0]
    cols = tokens // rows
    tiles_col = FRAME // cols
    per_frame = TILE_ROWS * tiles_col
    width = ln1_gain.shape[0]
    share = width // n_mp
    slots = -(-HEADS // n_mp)
    scale = HEAD_FEATURES ** (-0.5)
    maskf = pixel_mask.astype(jnp.float32)[:, None]
    head_ids = part + n_mp * jnp.arange(slots)
    select_where = (head_ids[:, None] == jnp.arange(HEADS)[None, :]).astype(jnp.float32)
    crops = tile_slot[:, 0]
    tiles = tile_slot[:, 1]
    is_me = jnp.arange(n_dp) == device
    own_crop = jnp.sum(jnp.where(is_me, crops, 0))
    own_tile = jnp.sum(jnp.where(is_me, tiles, 0))
    own_row = own_tile // tiles_col
    own_col = own_tile % tiles_col
    tile_row = tiles // tiles_col
    tile_col = tiles % tiles_col

    def beside(drow, dcol):
        hit = (crops == own_crop) & (tile_row == own_row + drow) & (tile_col == own_col + dcol)
        return hit.astype(jnp.float32)

    member = (crops[None, :] == own_crop) & (tiles[None, :] == jnp.arange(per_frame)[:, None])
    crop_devices = jnp.sum(jnp.where(member, jnp.arange(n_dp)[None, :], 0), axis=1)
    whole = lax.all_gather(pixels_in, "mp", axis=1, tiled=True)
    xm = whole.astype(jnp.float32) * maskf
    n1, first_norm_backward = jax.vjp(layer_norm, xm, ln1_gain, ln1_bias)
    n1b = n1.astype(jnp.bfloat16)
    wq = head_columns(w_query, select_where)
    wk = head_columns(w_key, select_where)
    wv = head_columns(w_value, select_where)
    wo = head_rows(w_out, select_where)
    qb = (mat(n1b, wq) + head_vector(b_query, select_where)).astype(jnp.bfloat16)
    patches = (
        n1b.reshape(rows // 2, 2, cols // 2, 2, width)
        .transpose(0, 2, 1, 3, 4)
        .reshape(-1, 4 * width)
    )
    reduced = mat(patches, w_reduce) + b_reduce
    xr, lnr_back = jax.vjp(layer_norm, reduced, lnr_gain, lnr_bias)
    xrb = xr.astype(jnp.bfloat16)
    kb = mat(xrb, wk).astype(jnp.bfloat16)
    vb = (mat(xrb, wv) + head_vector(b_value, select_where)).astype(jnp.bfloat16)
    kmask = (
        pixel_mask.reshape(rows // 2, 2, cols // 2, 2)[:, 0, :, 0].reshape(-1).astype(jnp.bfloat16)
    )
    keys_all, values_all, kmask_all = (
        lax.all_gather(kb, "dp", axis=0, tiled=True),
        lax.all_gather(vb, "dp", axis=0, tiled=True),
        lax.all_gather(kmask, "dp", axis=0, tiled=True),
    )
    per_key = kb.shape[0]
    keys_crop = keys_all.reshape(n_dp, per_key, -1)[crop_devices]
    values_crop = values_all.reshape(n_dp, per_key, -1)[crop_devices]
    usable_crop = kmask_all.reshape(n_dp, per_key)[crop_devices].astype(jnp.float32) > 0.5
    n_blocks = 4
    key_blocks = keys_crop.reshape(n_blocks, -1, slots, HEAD_FEATURES)
    value_blocks = values_crop.reshape(n_blocks, -1, slots, HEAD_FEATURES)
    usable_blocks = usable_crop.reshape(n_blocks, -1)
    queries = qb.reshape(tokens, slots, HEAD_FEATURES)

    def block_scores(key_block, usable_block):
        raw = (
            jnp.einsum("qsd,ksd->sqk", queries, key_block, preferred_element_type=jnp.float32)
            * scale
        )
        return jnp.where(usable_block[None, None, :], raw, NEG)

    def top_step(carry, blocks):
        top, total = carry
        key_block, usable_block = blocks
        scores = block_scores(key_block, usable_block)
        new_top = jnp.maximum(top, jnp.max(scores, axis=-1))
        total = total * jnp.exp(top - new_top) + jnp.sum(
            jnp.exp(scores - new_top[..., None]), axis=-1
        )
        return ((new_top, total), None)

    start = (jnp.full((slots, tokens), NEG, jnp.float32), jnp.zeros((slots, tokens), jnp.float32))
    (top, total), _ = lax.scan(top_step, start, (key_blocks, usable_blocks))
    lse = top + jnp.log(total)

    def out_step(acc, blocks):
        key_block, value_block, usable_block = blocks
        prob = jnp.exp(block_scores(key_block, usable_block) - lse[..., None])
        acc = acc + jnp.einsum(
            "sqk,ksd->qsd",
            prob.astype(jnp.bfloat16),
            value_block,
            preferred_element_type=jnp.float32,
        )
        return (acc, None)

    empty = jnp.zeros((tokens, slots, HEAD_FEATURES), jnp.float32)
    acc, _ = lax.scan(out_step, empty, (key_blocks, value_blocks, usable_blocks))
    ob = acc.reshape(tokens, -1).astype(jnp.bfloat16)
    branch = lax.psum(mat(ob, wo).astype(jnp.bfloat16), "mp").astype(jnp.float32) + b_out
    h1 = xm + branch * maskf
    n2, ln2_back = jax.vjp(layer_norm, h1, ln2_gain, ln2_bias)
    n2b = n2.astype(jnp.bfloat16)
    ub = ((mat(n2b, w_fc1) + b_fc1) * maskf).astype(jnp.bfloat16)
    channels = ub.shape[1]
    tile_u = ub.reshape(rows, cols, channels)
    lines, sides = (
        lax.all_gather(jnp.stack([tile_u[0], tile_u[-1]]), "dp", axis=0, tiled=True),
        lax.all_gather(jnp.stack([tile_u[:, 0], tile_u[:, -1]]), "dp", axis=0, tiled=True),
    )
    lines = lines.reshape(n_dp, 2, cols, channels)
    sides = sides.reshape(n_dp, 2, rows, channels)
    top_lines = lines[:, 0]
    bottom_lines = lines[:, 1]
    left_sides = sides[:, 0]
    right_sides = sides[:, 1]
    upper = jnp.concatenate(
        [
            pick(beside(-1, -1), bottom_lines[:, -1:]),
            pick(beside(-1, 0), bottom_lines),
            pick(beside(-1, 1), bottom_lines[:, :1]),
        ],
        axis=0,
    )
    lower = jnp.concatenate(
        [
            pick(beside(1, -1), top_lines[:, -1:]),
            pick(beside(1, 0), top_lines),
            pick(beside(1, 1), top_lines[:, :1]),
        ],
        axis=0,
    )
    middle = jnp.concatenate(
        [
            pick(beside(0, -1), right_sides)[:, None],
            tile_u.astype(jnp.float32),
            pick(beside(0, 1), left_sides)[:, None],
        ],
        axis=1,
    )
    padded = jnp.concatenate([upper[None], middle, lower[None]], axis=0)
    act, depth_back = jax.vjp(depth_gelu, padded, w_depth, b_depth)
    gb = act.reshape(tokens, channels).astype(jnp.bfloat16)
    ffn_mine = lax.psum_scatter(
        mat(gb, w_fc2).astype(jnp.bfloat16), "mp", scatter_dimension=1, tiled=True
    ).astype(jnp.float32)
    h1_mine = lax.dynamic_slice_in_dim(h1, part * share, share, 1)
    bias_mine = lax.dynamic_slice_in_dim(b_fc2, part * share, share, 0)
    block_result = (h1_mine + (ffn_mine + bias_mine) * maskf).astype(jnp.bfloat16)
    dy = cotangent.astype(jnp.float32)
    dff = dy * maskf
    grad_b_fc2 = jnp.sum(dff, axis=0)
    dfb = dff.astype(jnp.bfloat16)
    grad_w_fc2 = mat(gb.T, dfb)
    dgr = mat(dfb, w_fc2.T).astype(jnp.bfloat16).astype(jnp.float32).reshape(rows, cols, channels)
    dpad, grad_w_depth, grad_b_depth = depth_back(dgr)
    grad_lines, grad_sides = (
        lax.all_gather(
            jnp.stack([dpad[0], dpad[-1]]).astype(jnp.bfloat16), "dp", axis=0, tiled=True
        ).astype(jnp.float32),
        lax.all_gather(
            jnp.stack([dpad[1:-1, 0], dpad[1:-1, -1]]).astype(jnp.bfloat16),
            "dp",
            axis=0,
            tiled=True,
        ).astype(jnp.float32),
    )
    grad_lines = grad_lines.reshape(n_dp, 2, cols + 2, channels)
    grad_sides = grad_sides.reshape(n_dp, 2, rows, channels)
    top_grads = grad_lines[:, 0]
    bottom_grads = grad_lines[:, 1]
    dtile = dpad[1:-1, 1:-1]
    dtile = dtile.at[0].add(pick(beside(-1, 0), bottom_grads[:, 1:-1]))
    dtile = dtile.at[0, 0].add(pick(beside(-1, -1), bottom_grads[:, -1:])[0])
    dtile = dtile.at[0, -1].add(pick(beside(-1, 1), bottom_grads[:, :1])[0])
    dtile = dtile.at[-1].add(pick(beside(1, 0), top_grads[:, 1:-1]))
    dtile = dtile.at[-1, 0].add(pick(beside(1, -1), top_grads[:, -1:])[0])
    dtile = dtile.at[-1, -1].add(pick(beside(1, 1), top_grads[:, :1])[0])
    dtile = dtile.at[:, 0].add(pick(beside(0, -1), grad_sides[:, 1]))
    dtile = dtile.at[:, -1].add(pick(beside(0, 1), grad_sides[:, 0]))
    dub = (dtile.reshape(tokens, channels).astype(jnp.bfloat16).astype(jnp.float32) * maskf).astype(
        jnp.bfloat16
    )
    grad_b_fc1 = jnp.sum(dub.astype(jnp.float32), axis=0)
    grad_w_fc1 = mat(n2b.T, dub)
    dn2_part = mat(dub, w_fc1.T)
    zero_vector = jnp.zeros((width,), jnp.float32)
    dn2 = lax.psum(dn2_part.astype(jnp.bfloat16), "mp").astype(jnp.float32)
    dh1_norm, shared_gain, shared_bias = ln2_back(dn2)
    dh1 = dy + dh1_norm
    split_gain = zero_vector
    split_bias = zero_vector
    dattn = dh1 * maskf
    grad_b_out = jnp.sum(dattn, axis=0)
    dab = dattn.astype(jnp.bfloat16)
    grad_wo = mat(ob.T, dab)
    dob = mat(dab, wo.T).astype(jnp.bfloat16)
    dout = dob.reshape(tokens, slots, HEAD_FEATURES)
    drow = jnp.sum(dout.astype(jnp.float32) * acc, axis=-1).T

    def back_step(dq_acc, blocks):
        key_block, value_block, usable_block = blocks
        prob = jnp.exp(block_scores(key_block, usable_block) - lse[..., None])
        dv_block = jnp.einsum(
            "sqk,qsd->ksd", prob.astype(jnp.bfloat16), dout, preferred_element_type=jnp.float32
        )
        dprob = jnp.einsum("qsd,ksd->sqk", dout, value_block, preferred_element_type=jnp.float32)
        dscore = (prob * (dprob - drow[..., None])).astype(jnp.bfloat16)
        dq_acc = dq_acc + jnp.einsum(
            "sqk,ksd->qsd", dscore, key_block, preferred_element_type=jnp.float32
        )
        dk_block = (
            jnp.einsum("sqk,qsd->ksd", dscore, queries, preferred_element_type=jnp.float32) * scale
        )
        return (dq_acc, (dk_block, dv_block))

    dq_acc, (dk_blocks, dv_blocks) = lax.scan(
        back_step, empty, (key_blocks, value_blocks, usable_blocks)
    )
    zero_keys = jnp.zeros((n_dp, per_key, slots * HEAD_FEATURES), jnp.float32)
    dk_full = (
        zero_keys.at[crop_devices]
        .set(dk_blocks.reshape(per_frame, per_key, -1))
        .reshape(n_dp * per_key, -1)
    )
    dv_full = (
        zero_keys.at[crop_devices]
        .set(dv_blocks.reshape(per_frame, per_key, -1))
        .reshape(n_dp * per_key, -1)
    )
    dk_mine, dv_mine = (
        lax.psum_scatter(dk_full, "dp", scatter_dimension=0, tiled=True),
        lax.psum_scatter(dv_full, "dp", scatter_dimension=0, tiled=True),
    )
    dkb = dk_mine.astype(jnp.bfloat16)
    dvb = dv_mine.astype(jnp.bfloat16)
    dqb = (dq_acc * scale).reshape(tokens, -1).astype(jnp.bfloat16)
    grad_wq = mat(n1b.T, dqb)
    grad_bq = jnp.sum(dqb.astype(jnp.float32), axis=0)
    grad_wk = mat(xrb.T, dkb)
    grad_wv = mat(xrb.T, dvb)
    grad_bv = jnp.sum(dvb.astype(jnp.float32), axis=0)
    dxr, dn1_query = (
        lax.psum((mat(dkb, wk.T) + mat(dvb, wv.T)).astype(jnp.bfloat16), "mp").astype(jnp.float32),
        lax.psum(mat(dqb, wq.T).astype(jnp.bfloat16), "mp").astype(jnp.float32),
    )
    dreduced, grad_lnr_gain, grad_lnr_bias = lnr_back(dxr)
    drb = dreduced.astype(jnp.bfloat16)
    grad_w_reduce = mat(patches.T, drb)
    grad_b_reduce = jnp.sum(drb.astype(jnp.float32), axis=0)
    dpatch = (
        mat(drb, w_reduce.T)
        .reshape(rows // 2, cols // 2, 2, 2, width)
        .transpose(0, 2, 1, 3, 4)
        .reshape(tokens, width)
    )
    dxm, grad_ln1_gain, grad_ln1_bias = first_norm_backward(dn1_query + dpatch)
    grad_whole = (dxm + dh1) * maskf
    grad_input = lax.dynamic_slice_in_dim(grad_whole, part * share, share, 1)
    (
        grad_w_reduce,
        grad_b_reduce,
        grad_lnr_gain,
        grad_lnr_bias,
        grad_ln1_gain,
        grad_ln1_bias,
        shared_gain,
        shared_bias,
        grad_b_out,
        grad_b_fc2,
        grad_w_fc1,
        grad_b_fc1,
        grad_w_depth,
        grad_b_depth,
        grad_w_fc2,
    ) = lax.psum(
        (
            grad_w_reduce,
            grad_b_reduce,
            grad_lnr_gain,
            grad_lnr_bias,
            grad_ln1_gain,
            grad_ln1_bias,
            shared_gain,
            shared_bias,
            grad_b_out,
            grad_b_fc2,
            grad_w_fc1,
            grad_b_fc1,
            grad_w_depth,
            grad_b_depth,
            grad_w_fc2,
        ),
        "dp",
    )
    (
        grad_w_query,
        grad_b_query,
        grad_w_key,
        grad_w_value,
        grad_b_value,
        output_weight_gradient,
        split_gain,
        split_bias,
    ) = lax.psum(
        (
            spread_columns(grad_wq, select_where),
            spread_vector(grad_bq, select_where),
            spread_columns(grad_wk, select_where),
            spread_columns(grad_wv, select_where),
            spread_vector(grad_bv, select_where),
            spread_rows(grad_wo, select_where),
            split_gain,
            split_bias,
        ),
        ("dp", "mp"),
    )
    grad_ln2_gain = shared_gain + split_gain
    grad_ln2_bias = shared_bias + split_bias
    return (
        block_result,
        grad_input,
        grad_ln1_gain,
        grad_ln1_bias,
        grad_w_query,
        grad_b_query,
        grad_w_key,
        grad_w_value,
        grad_b_value,
        grad_w_reduce,
        grad_b_reduce,
        grad_lnr_gain,
        grad_lnr_bias,
        output_weight_gradient,
        grad_b_out,
        grad_ln2_gain,
        grad_ln2_bias,
        grad_w_fc1,
        grad_b_fc1,
        grad_w_depth,
        grad_b_depth,
        grad_w_fc2,
        grad_b_fc2,
    )


BF = jnp.bfloat16
F32 = jnp.float32
LANES = 128
SIDE_SMALL = 64
VMEM_MB = 52


def nn(a, b):
    return lax.dot_general(a, b, (((1,), (0,)), ((), ())), preferred_element_type=F32)


def nt(a, b):
    return lax.dot_general(a, b, (((1,), (1,)), ((), ())), preferred_element_type=F32)


def tn(a, b):
    return lax.dot_general(a, b, (((0,), (0,)), ((), ())), preferred_element_type=F32)


def iota(shape, axis):
    return lax.broadcasted_iota(jnp.int32, shape, axis)


def hot(cond):
    return jnp.where(cond, 1.0, 0.0).astype(BF)


def spread(value):
    mean = jnp.sum(value, axis=-1, keepdims=True) * (1.0 / value.shape[-1])
    centred = value - mean
    var = jnp.sum(centred * centred, axis=-1, keepdims=True) * (1.0 / value.shape[-1])
    rstd = lax.rsqrt(var + EPS)
    return centred * rstd, rstd


def norm_back(dn, gain, xhat, rstd):
    e = dn * gain
    scale = 1.0 / dn.shape[-1]
    mean_e = jnp.sum(e, axis=-1, keepdims=True) * scale
    mean_ex = jnp.sum(e * xhat, axis=-1, keepdims=True) * scale
    return rstd * (e - mean_e - xhat * mean_ex)


def rowsum(value):
    return jnp.sum(value, axis=0, keepdims=True)


class Sizes:
    def __init__(self, n_dp, n_mp, tokens, width, hidden):
        self.n_dp, self.n_mp = n_dp, n_mp
        self.tokens, self.width, self.hidden = tokens, width, hidden
        self.share = width // n_mp
        self.rows = FRAME // TILE_ROWS
        self.cols = tokens // self.rows
        self.pa, self.pb = self.rows // 2, self.cols // 2
        self.keys = self.pa * self.pb
        self.plane = -(-self.keys // 16) * 16
        self.all = 4 * self.plane
        self.step = self.plane // 16 // n_mp * 16
        self.quarter = self.plane - (n_mp - 1) * self.step
        self.wide = -(-width // LANES) * LANES
        self.kvrows = self.plane + self.quarter
        self.top = 8 + self.pb
        self.ext = self.top + self.keys + self.pb
        self.edge = 4 * 2 * self.pb
        self.edge_q = -(-self.edge // LANES) * LANES
        self.queries = -(-4 * self.keys // LANES) * LANES
        self.echunk = (width + hidden) // n_dp
        self.prows = -(-(2 * self.plane + self.plane // 2) // 16) * 16
        self.wrows = 2 * width + width // 2
        self.l2rows = -(-(self.wrows + self.share) // (16 * n_dp)) * 16 * n_dp
        self.orows = HEAD_FEATURES + HEAD_FEATURES // n_mp
        self.l1rows = -(-(2 * width + 2 * self.orows + self.orows // 2) // (16 * n_dp)) * 16 * n_dp


class Load:
    def __init__(self, src, dst, sem):
        self.dst, self.shape, self.waiting = dst, dst.shape, True
        self.copy = pltpu.make_async_copy(src, dst, sem)
        self.copy.start()

    def ready(self):
        if self.waiting:
            self.waiting = False
            self.copy.wait()
        return self.dst

    def __getitem__(self, at):
        return self.ready()[at]


def fused_body(
    sz, names,
    mask_ref, slot_ref, *refs,
):
    ins, refs = refs[:23], refs[23:]
    outs, refs = refs[:7], refs[7:]
    s = dict(zip(names, refs))
    blk_ref, gp_ref, eg_ref, lg1_ref, lg2_ref, veg_ref, vlg_ref = outs
    D, HF, PB, PA, KEYS, PL, T = sz.width, HEAD_FEATURES, sz.pb, sz.pa, sz.keys, sz.plane, sz.all
    C, FS, W = sz.hidden, sz.share, sz.wide
    d = lax.axis_index("dp")
    m = lax.axis_index("mp")
    last = sz.n_mp * HF
    ssem, rsem = s["ssem"], s["rsem"]

    def mpx(k):
        if k == 0:
            return m
        if k == 1:
            return m + 1 - 2 * lax.rem(m, 2)
        if k == 2:
            return lax.rem(m + 2, 4)
        return 3 - m

    def dpx(k):
        z, x = d // 2, lax.rem(d, 2)
        if k & 1:
            x = 1 - x
        kz = k >> 1
        if kz == 1:
            z = z + 1 - 2 * lax.rem(z, 2)
        elif kz == 2:
            z = lax.rem(z + 2, 4)
        elif kz == 3:
            z = 3 - z
        return 2 * z + x

    counter = [0]
    pending = []

    def take(n):
        first = counter[0]
        counter[0] += n
        return first

    def copy(src, dst, sem, dev):
        return pltpu.make_async_remote_copy(
            src_ref=src, dst_ref=dst, send_sem=ssem.at[sem], recv_sem=rsem.at[sem],
            device_id=dev, device_id_type=pl.DeviceIdType.MESH,
        )

    def send(src, dst, sem, dev):
        c = copy(src, dst, sem, dev)
        c.start()
        pending.append(c)

    def drain(keep=0):
        while len(pending) > keep:
            pending.pop(0).wait_send()

    def arrived(ref, sem):
        copy(ref, ref, sem, (d, m)).wait_recv()

    opened = []

    def handle(finish):
        state = [False]

        def once(*a):
            if not state[0]:
                state[0] = True
                return finish(*a)

        opened.append(once)
        return once

    def mp_start(buf):
        base = take(3)
        send(buf.at[m], buf.at[m], base, (d, mpx(1)))
        send(buf.at[m], buf.at[m], base + 1, (d, mpx(2)))

        def middle():
            arrived(buf.at[mpx(2)], base + 1)
            send(buf.at[mpx(2)], buf.at[mpx(2)], base + 2, (d, mpx(1)))

        mid = handle(middle)

        def finish():
            mid()
            arrived(buf.at[mpx(1)], base)
            arrived(buf.at[mpx(3)], base + 2)

        return handle(finish), mid

    def mp_direct(buf):
        at = mp_scatter(lambda h: buf.at[m], lambda k: buf.at[m], lambda k: buf.at[mpx(k)])
        return at, lambda: None

    def dp_start(buf, each=lambda k: None):
        base = take(7)
        for kz in (3, 2, 1):
            send(buf.at[d], buf.at[d], base + kz, (dpx(2 * kz), m))
        send(buf.at[d], buf.at[d], base, (dpx(1), m))

        def along(kz):
            arrived(buf.at[dpx(2 * kz)], base + kz)
            send(buf.at[dpx(2 * kz)], buf.at[dpx(2 * kz)], base + 3 + kz, (dpx(1), m))
            each(2 * kz)

        def across(kz):
            arrived(buf.at[dpx(2 * kz + 1)], base + 3 + kz if kz else base)
            each(2 * kz + 1)

        steps = [handle(lambda kz=kz: along(kz)) for kz in (1, 2, 3)]
        steps += [handle(lambda kz=kz: across(kz)) for kz in range(4)]

        def mid():
            for step in steps[:4]:
                step()

        def finish():
            for step in steps:
                step()

        return handle(finish), mid, steps

    def dp_pick(buf, chosen, out, came):
        base = take(4)
        z = d // 2
        for kz in (3, 2, 1):
            send(buf.at[z], buf.at[z], base + kz, (dpx(2 * kz), m))

        def middle():
            for kz in (1, 2, 3):
                arrived(buf.at[dpx(2 * kz) // 2], base + kz)
            out[...] = chosen(*beside(dpx(1)))
            send(out, came, base, (dpx(1), m))

        mid = handle(middle)

        def finish():
            mid()
            arrived(came, base)

        return handle(finish), mid

    def mp_scatter(block, dst, landed):
        base = take(4)
        for k in (2, 3, 1):
            send(block(mpx(k)), dst(k), base + k, (d, mpx(k)))

        def finish():
            for k in (1, 2, 3):
                arrived(landed(k), base + k)

        return handle(finish)

    def dp_scatter(block, dst, landed):
        base = take(8)
        for k in (6, 7, 4, 5, 2, 3, 1):
            send(block(dpx(k)), dst(k), base + k, (dpx(k), m))

        def finish():
            for k in range(1, sz.n_dp):
                arrived(landed(k), base + k)

        return handle(finish)

    def mp_sum(block, out, near, far):
        base = take(3)
        out[1] = block(mpx(3)).astype(BF)
        send(out.at[1], near.at[1], base + 1, (d, mpx(1)))
        out[0] = block(mpx(1)).astype(BF)
        send(out.at[0], near.at[0], base, (d, mpx(1)))

        def middle():
            value = block(mpx(2))
            arrived(near.at[1], base + 1)
            out[2] = (value + near[1].astype(F32)).astype(BF)
            send(out.at[2], far, base + 2, (d, mpx(2)))

        mid = handle(middle)

        def finish():
            mid()
            value = block(m)
            arrived(near.at[0], base)
            value = value + near[0].astype(F32)
            arrived(far, base + 2)
            return value + far[...].astype(F32)

        return mid, handle(finish)

    def dp_sum(chunk, near, out, far):
        base = take(8)
        for kz in (2, 3, 1, 0):
            send(chunk(dpx(2 * kz + 1)), near.at[kz], base + kz, (dpx(1), m))

        def middle():
            for kz in (2, 3, 1):
                value = chunk(dpx(2 * kz))[...].astype(F32)
                arrived(near.at[kz], base + kz)
                out[kz] = (value + near[kz].astype(F32)).astype(BF)
                send(out.at[kz], far.at[kz], base + 4 + kz, (dpx(2 * kz), m))

        mid = handle(middle)

        def finish():
            mid()
            value = chunk(d)[...].astype(F32)
            arrived(near.at[0], base)
            value = value + near[0].astype(F32)
            for kz in (1, 2, 3):
                arrived(far.at[kz], base + 4 + kz)
                value = value + far[kz].astype(F32)
            return value

        return mid, handle(finish)

    def dp_total(src, near, parts):
        base = take(4)
        z = d // 2
        send(src, near, base, (dpx(1), m))

        def middle():
            arrived(near, base)
            parts[z] = src[...] + near[...]
            for kz in (2, 3, 1):
                send(parts.at[z], parts.at[z], base + kz, (dpx(2 * kz), m))

        mid = handle(middle)

        def finish():
            mid()
            for kz in (1, 2, 3):
                arrived(parts.at[dpx(2 * kz) // 2], base + kz)
            return (parts[0] + parts[1]) + (parts[2] + parts[3])

        return mid, handle(finish)

    peers = [(d, mpx(k)) for k in (1, 2, 3)] + [(dpx(k), m) for k in range(1, 8)]
    bar = pltpu.get_barrier_semaphore()
    for dev in peers:
        pl.semaphore_signal(bar, inc=1, device_id=dev, device_id_type=pl.DeviceIdType.MESH)

    order = (0, 1, 2, 3, 8, 7, 9, 10, 11, 12, 4, 5, 6, 21, 22, 13, 14, 15, 16, 17, 18, 19, 20)
    loads = [None] * 23
    for i in order:
        dst = s["xt"].at[m] if i == 0 else s["in%d" % i]
        loads[i] = Load(ins[i], dst, s["isem"].at[i])
    (
        pix_ref, cot_ref, ln1g_ref, ln1b_ref, wq_ref, bq_ref, wk_ref, wv_ref, bv_ref, wr_ref, br_ref,
        lnrg_ref, lnrb_ref, wo_ref, bo_ref, ln2g_ref, ln2b_ref, w1_ref, b1_ref, wd_ref, bd_ref, w2_ref, b2_ref,
    ) = loads

    side = jnp.where(mask_ref[sz.cols - 1] > 0, FRAME, SIDE_SMALL)
    tile = slot_ref[1, d]
    tiles = [slot_ref[1, k] for k in range(sz.n_dp)]

    def beside(at):
        t = slot_ref[1, at]
        up = sum(jnp.where(tiles[k] == t - 1, k, 0) for k in range(sz.n_dp))
        down = sum(jnp.where(tiles[k] == t + 1, k, 0) for k in range(sz.n_dp))
        return up, down

    above, below = beside(d)

    def same_x(j):
        return lax.rem(j, 2) == lax.rem(d, 2)

    def place(p, count):
        a = sum(jnp.where(p >= PB * k, 1, 0) for k in range(1, count))
        return a, p - PB * a

    def token_mask(i, j):
        p = iota((PL, 1), 0)
        a, b = place(p, PA)
        inside = (p < KEYS) & (sz.rows * tile + 2 * a + i < side) & (2 * b + j < side)
        return jnp.where(inside, 1.0, 0.0)

    def row_mask(i, j, a):
        b = iota((PB, 1), 0)
        row = sz.rows * tile + 2 * a + i
        inside = (row >= 0) & (row < side) & (2 * b + j < side)
        return jnp.where(inside, 1.0, 0.0)

    def key_bias(p, tile_at):
        a, b = place(p, PA)
        usable = (p < KEYS) & (sz.rows * tile_at + 2 * a < side) & (2 * b < side)
        return jnp.where(usable, 0.0, NEG)

    def vec(ref):
        return ref[...].reshape(1, ref.shape[0])

    def own_part(row, size):
        return sum(
            jnp.where(m == h, 1.0, 0.0) * row[:, size * h : size * (h + 1)] for h in range(sz.n_mp)
        )

    def plane_rows(ref, start):
        return ref[pl.ds(pl.multiple_of(start, 16), PL), :]

    def plane(p):
        return slice(PL * p, PL * (p + 1))

    lanes3 = (s["t0"], s["t1"], s["t2"])

    def to_planes(rows_of):
        for n, ref in enumerate(lanes3):
            ref[...] = rows_of(LANES * n, min(D, LANES * (n + 1))).astype(F32).T
        for i in range(2):
            for j in range(2):
                parts = []
                for ref in lanes3:
                    rows = [
                        ref[pl.ds((2 * a + i) * sz.cols + j, PB, stride=2), :] for a in range(PA)
                    ] + [jnp.zeros((PL - KEYS, ref.shape[1]), F32)]
                    parts.append(jnp.concatenate(rows, axis=0))
                yield i, j, jnp.concatenate(parts, axis=1)

    def from_queries(rows, p):
        n = rows.shape[1]
        return jnp.concatenate([rows[KEYS * p : KEYS * (p + 1)], jnp.zeros((PL - KEYS, n), F32)], axis=0)

    def to_queries(planes):
        n = planes[0].shape[1]
        rows = [v[0:KEYS] for v in planes]
        return jnp.concatenate(rows + [jnp.zeros((sz.queries - 4 * KEYS, n), F32)], axis=0)

    xt, dfm = s["xt"], s["dfm"]
    pl.semaphore_wait(bar, len(peers))
    pix_ref.ready()
    x_at, x_mid = mp_start(xt)

    edge, edge_g, EP = s["edge"], s["edge_g"], 4 * PB
    lane_pad = jnp.zeros((FS, sz.edge_q - 2 * EP), BF)
    edge[d // 2] = jnp.concatenate([xt[m, :, 0:EP], xt[m, :, sz.tokens - EP :], lane_pad], axis=1)

    def edge_chosen(up, down):
        return jnp.concatenate([edge[up // 2][:, EP : 2 * EP], edge[down // 2][:, 0:EP], lane_pad], axis=1)

    edge_at, edge_mid = dp_pick(edge, edge_chosen, s["edge_s"], s["edge_x"])

    for i, j, value in to_planes(lambda lo, hi: cot_ref[lo:hi, :]):
        dfm[plane(2 * i + j), :] = (value * token_mask(i, j)).astype(BF)
    dyh, dyh_g = s["dyh"], s["dyh_g"]
    dyh[d // 2, :, :D] = dfm[pl.ds(pl.multiple_of(PL * m + (KEYS - PB) * (m // 2), 16), 48), :]
    dyh[d // 2, :, D:] = jnp.zeros((48, W - D), BF)
    x_mid()

    r2, c2 = iota((D, LANES), 0), iota((D, LANES), 1)
    own_lo = hot((c2 < HF) & (r2 == HF * m + c2))
    own_hi = hot((c2 >= HF) & (r2 == HF * m + c2 - HF))
    last_lo = hot((c2 < HF) & (r2 == last + c2))
    last_hi = hot((c2 >= HF) & (r2 == last + c2 - HF))
    wq, wk, wv = wq_ref[...], wk_ref[...], wv_ref[...]
    wq2 = nn(wq, own_lo + last_hi).astype(BF)
    wkv = (nn(wk, own_lo) + nn(wv, own_hi)).astype(BF)
    wkv5 = (nn(wk, last_lo) + nn(wv, last_hi)).astype(BF)
    bq, bv = vec(bq_ref), vec(bv_ref)
    bq2 = jnp.concatenate([own_part(bq, HF), bq[:, last:]], axis=1)
    nil = jnp.zeros((1, HF), F32)
    bkv = jnp.concatenate([nil, own_part(bv, HF)], axis=1)
    bkv5 = jnp.concatenate([nil, bv[:, last:]], axis=1)
    w2 = w2_ref[...]
    wo_cat = s["wo_cat"]
    wo = wo_ref[...]
    wo_cat[...] = jnp.concatenate(
        [b for h in range(4) for b in (wo[HF * h : HF * (h + 1)], wo[last:])], axis=0
    )
    wr_t = s["wr_t"]
    wr_t[...] = wr_ref[...].T

    xm_r, n1_r = s["xm_r"], s["n1_r"]
    x_at()

    def dy_chosen(up, down):
        return dyh[jnp.where(m >= 2, up, down) // 2]
    dy_at, dy_mid = dp_pick(dyh, dy_chosen, s["dyh_s"], s["dyh_x"])

    x_all = xt[...].reshape(D, sz.tokens)
    for i, j, value in to_planes(lambda lo, hi: x_all[lo:hi, :]):
        xm = value * token_mask(i, j)
        xm_r[plane(2 * i + j), :] = xm.astype(BF)
        xhat, _ = spread(xm)
        n1_r[plane(2 * i + j), :] = (xhat * vec(ln1g_ref) + vec(ln1b_ref)).astype(BF)

    kva, xr_r = s["kva"], s["xr_r"]
    red = sum(nn(n1_r[plane(p), :], wr_t[D * p : D * (p + 1), :]) for p in range(4)) + vec(br_ref)
    xhr, rsr = spread(red)
    s["xhr_r"][...] = xhr
    s["rsr_r"][...] = jnp.broadcast_to(rsr, (PL, LANES))
    xr_r[...] = (xhr * vec(lnrg_ref) + vec(lnrb_ref)).astype(BF)
    kva[d, 0:PL, :] = (nn(xr_r[...], wkv) + bkv).astype(BF)
    quarter_rows = pl.ds(pl.multiple_of(sz.step * m, 16), sz.quarter)
    kva[d, PL:, :] = (nn(xr_r[quarter_rows, :], wkv5) + bkv5).astype(BF)
    _, _, kv_steps = dp_start(kva)
    edge_mid()

    qa_r, qb_r, qc_r, qd_r = s["qa_r"], s["qb_r"], s["qc_r"], s["qd_r"]
    Q = sz.queries

    def feature_major(q_rows, own_r, last_r):
        q2t = q_rows.T
        nil = jnp.zeros((HF, q2t.shape[1]), F32)
        own_r[...] = jnp.concatenate([q2t[0:HF], nil], axis=0).astype(BF)
        last_r[...] = jnp.concatenate([q2t[HF:], nil], axis=0).astype(BF)

    def query(rows):
        return (nn(rows, wq2) + bq2).astype(BF).astype(F32) * HF ** (-0.5)

    q2 = query(n1_r[...])
    feature_major(to_queries([q2[plane(p)] for p in range(4)]), qa_r, qb_r)
    half = jnp.zeros((HF, Q), F32)

    e5buf, ebuf, ot_r = s["e5buf"], s["ebuf"], s["ot_r"]
    limit5 = jnp.where(m == sz.n_mp - 1, KEYS - sz.step * m, sz.step)
    pk, pk5 = iota((PL, 1), 0), iota((sz.quarter, 1), 0)

    def attend(ks, rows, q_r, bias_of, ebuf, o_r):
        js = [dpx(k) for k in ks]
        n = rows.stop - rows.start
        kv = jnp.concatenate([kva[j, rows, :] for j in js], axis=0)
        bias = jnp.concatenate([bias_of(j) for j in js], axis=0)
        v = nn(kv, q_r[...]) + bias
        top = jnp.max(v, axis=0, keepdims=True)
        e = jnp.exp(v - top).astype(BF)
        if ebuf is not None:
            for q, j in enumerate(js):
                ebuf[j] = e[n * q : n * (q + 1)]
        o_r[ks[0]] = tn(kv, e)[HF:]
        return ks, top, rowsum(e.astype(F32))

    def bias_own(j):
        return key_bias(pk, slot_ref[1, j])

    def bias_last(j):
        return jnp.where(pk5 < limit5, key_bias(pk5 + sz.step * m, slot_ref[1, j]), NEG)

    own, five, own_h, five_h = [], [], [], []
    ROWS, LAST = slice(0, PL), slice(PL, sz.kvrows)

    def block(*ks):
        own.append(attend(ks, ROWS, qa_r, bias_own, ebuf, s["o_own"]))
        five.append(attend(ks, LAST, qb_r, bias_last, e5buf, s["o_five"]))

    def block_h(*ks):
        own_h.append(attend(ks, ROWS, qc_r, bias_own, None, s["oh_own"]))
        five_h.append(attend(ks, LAST, qd_r, bias_last, None, s["oh_five"]))

    block(0)
    edge_at()
    up = jnp.where(
        same_x(above), edge[above // 2][:, EP : 2 * EP].astype(F32), s["edge_x"][:, 0:EP].astype(F32)
    )
    down = jnp.where(
        same_x(below), edge[below // 2][:, 0:EP].astype(F32), s["edge_x"][:, EP : 2 * EP].astype(F32)
    )
    edge_g[m] = jnp.concatenate([up, down, lane_pad.astype(F32)], axis=1).astype(BF)
    edgeg_at, edgeg_mid = mp_direct(edge_g)
    kv_steps[3]()
    kv_steps[0]()
    edgeg_mid()
    block(1, 2)
    dy_mid()
    edgeg_at()

    xh_r = s["xh_r"]
    e_all = edge_g[...].reshape(D, sz.edge_q)
    for n, ref in enumerate(lanes3):
        ref[0 : sz.edge_q, :] = e_all[LANES * n : min(D, LANES * (n + 1))].astype(F32).T
    rows = []
    for i in range(2):
        for j in range(2):
            for a, first in ((-1, 0), (PA, EP)):
                at = pl.ds(first + sz.cols * i + j, PB, stride=2)
                value = jnp.concatenate([ref[at, :] for ref in lanes3], axis=1)
                rows.append(value * row_mask(i, j, a))
    xh = jnp.concatenate(rows, axis=0)
    xh_r[...] = xh.astype(BF)
    xhat, _ = spread(xh)
    q2 = query((xhat * vec(ln1g_ref) + vec(ln1b_ref)).astype(BF))
    q2 = jnp.concatenate([q2, jnp.zeros((sz.edge_q - sz.edge, LANES), F32)], axis=0)
    feature_major(q2, qc_r, qd_r)
    kv_steps[1]()
    block_h(0, 1, 2)
    kv_steps[2]()
    block(4, 6)
    block_h(4, 6)
    dy_at()
    beside_j = jnp.where(m >= 2, above, below)
    dyh_g[m] = jnp.where(
        same_x(beside_j), dyh[beside_j // 2].astype(F32), s["dyh_x"][...].astype(F32)
    ).astype(BF)
    dyg_at, dyg_mid = mp_direct(dyh_g)
    kv_steps[4]()
    kv_steps[5]()
    block(3, 5)
    block_h(3, 5)
    dyg_mid()
    kv_steps[6]()
    block(7)
    block_h(7)

    def joined(parts, o_r):
        top = functools.reduce(jnp.maximum, [t for _, t, _ in parts])
        scale = [jnp.exp(t - top) for _, t, _ in parts]
        total = sum(f * n for f, (_, _, n) in zip(scale, parts))
        inv = 1.0 / total
        scale = [f * inv for f in scale]
        out = sum(f * o_r[ks[0]] for f, (ks, _, _) in zip(scale, parts))
        return top + jnp.log(total), {k: f for f, (ks, _, _) in zip(scale, parts) for k in ks}, out

    lse_r, LR = s["lse_r"], (Q + sz.edge_q) // LANES
    lse5, scale5, o5_t = joined(five, s["o_five"])
    lse5h, _, o5h_t = joined(five_h, s["oh_five"])
    flat = [lse5[:, LANES * n : LANES * (n + 1)] for n in range(Q // LANES)]
    flat += [lse5h[:, LANES * n : LANES * (n + 1)] for n in range(sz.edge_q // LANES)]
    lse_r[m] = jnp.concatenate(flat + [jnp.zeros((16 - LR, LANES), F32)], axis=0)
    lse_at = mp_scatter(lambda h: lse_r.at[m], lambda k: lse_r.at[m], lambda k: lse_r.at[mpx(k)])
    _, scale, o_t = joined(own, s["o_own"])
    o2 = jnp.concatenate([o_t, o5_t], axis=0).T.astype(BF)
    chunks = ((s["og_a"], s["ow_a"]), (s["og_b"], s["ow_b"]), (s["og_c"], s["ow_c"]))
    ogs = []
    for n in range(2):
        og = chunks[n][0]
        og[m] = o2[2 * KEYS * n : 2 * KEYS * (n + 1)]
        ogs.append(mp_start(og))
    _, _, oh_t = joined(own_h, s["oh_own"])
    s["og_c"][m] = jnp.concatenate([oh_t, o5h_t], axis=0).T[0 : sz.edge].astype(BF)
    ogs.append(mp_start(s["og_c"]))
    drain(12)
    rt, ct = iota((D, 4 * LANES), 0), iota((D, 4 * LANES), 1)
    lane4, head4 = ct & (LANES - 1), ct >> 7
    place_out = hot((lane4 < FS) & (rt == FS * head4 + lane4))
    rk, ck = iota((D, 5 * LANES), 0), iota((D, 5 * LANES), 1)
    lane5, head5 = ck & (LANES - 1), ck >> 7
    w_all, wq_cat, w2_t = s["w_all"], s["wq_cat"], s["w2_t"]
    w_all[...] = (
        nn(wk, hot((lane5 < HF) & (rk == HF * head5 + lane5)))
        + nn(wv, hot((lane5 >= HF) & (rk == HF * head5 + lane5 - HF)))
    ).astype(BF)
    wq_cat[...] = nn(
        wq, hot(rt == jnp.where(lane4 < HF, HF * head4 + lane4, last + lane4 - HF))
    ).astype(BF)
    w2_t[...] = w2.T
    dgx, dzx = s["dgx"], s["dzx"]
    for p in range(4):
        dgx[p, sz.top : sz.top + PL, :] = nt(dfm[plane(p), :], w2).astype(BF).astype(F32)

    lse_at()
    lse4 = [
        jnp.concatenate([lse_r[h][n : n + 1] for n in range(LR)], axis=1) for h in range(4)
    ]
    top = functools.reduce(jnp.maximum, lse4)
    whole = top + jnp.log(sum(jnp.exp(v - top) for v in lse4))
    share_all = jnp.exp(jnp.concatenate(lse4 + [jnp.zeros((4, Q + sz.edge_q), F32)], axis=0) - whole).T
    share = jnp.exp(lse5 - whole[:, 0:Q])

    def weighed(n, first):
        og, ow = chunks[n]
        rows = og.shape[1]
        lane = iota((rows, LANES), 1)
        ogs[n][0]()
        for h in range(4):
            part = share_all[first : first + rows, h : h + 1]
            ow[h] = (og[h].astype(F32) * jnp.where(lane < HF, 1.0, part)).astype(BF)
        oc = jnp.concatenate([ow[h] for h in range(4)], axis=1)
        return nn(oc, wo_cat[...]) + vec(bo_ref)

    h1_r, n2_r = s["h1_r"], s["n2_r"]

    def second_norm(h1):
        xhat, _ = spread(h1)
        return (xhat * vec(ln2g_ref) + vec(ln2b_ref)).astype(BF)

    w1, b1 = w1_ref[...], vec(b1_ref)

    def hidden(rows, mask):
        return ((nn(rows, w1) + b1) * mask).astype(BF).astype(F32)

    ux, ul, ur, dzl, dzr = s["ux"], s["ul"], s["ur"], s["dzl"], s["dzr"]
    b40 = iota((PB, 1), 0)

    def shift(src, left, right, i, start):
        at = slice(start, start + PB)
        left[i, at, :] = jnp.where(b40 == 0, 0.0, pltpu.roll(src[2 * i + 1, at, :], 1, 0))
        right[i, at, :] = jnp.where(b40 == PB - 1, 0.0, pltpu.roll(src[2 * i, at, :], PB - 1, 0))

    for n in range(2):
        mixed = weighed(n, 2 * KEYS * n)
        ogs[n + 1][1]()
        for p in (2 * n, 2 * n + 1):
            mask = token_mask(n, p % 2)
            h1 = xm_r[plane(p), :].astype(F32) + mask * from_queries(mixed, p % 2)
            h1_r[plane(p), :] = h1
            n2_r[plane(p), :] = second_norm(h1)
            ux[p, sz.top : sz.top + PL, :] = hidden(n2_r[plane(p), :], mask)
        for a in range(PA):
            shift(ux, ul, ur, n, sz.top + PB * a)

    wd_ref, bd_row = wd_ref.ready(), vec(bd_ref)
    g_r, du_r = s["g_r"], s["du_r"]
    for p in range(4):
        g_r[p, KEYS:PL, :] = jnp.zeros((PL - KEYS, C), F32)
        du_r[p, KEYS:PL, :] = jnp.zeros((PL - KEYS, C), F32)

    def source(refs, i, j, di, dj, start):
        base, left, right = refs
        i2, up = (i + di) % 2, (i + di) // 2
        j2, across = (j + dj) % 2, (j + dj) // 2
        at = pl.ds(pl.multiple_of(start + PB * up, 8), PB)
        if across < 0:
            return left[i2, at, :]
        if across > 0:
            return right[i2, at, :]
        return base[2 * i2 + j2, at, :]

    TAPS = [(di, dj) for di in (-1, 0, 1) for dj in (-1, 0, 1)]

    def activation(i, j, start):
        p = 2 * i + j
        z = bd_row + sum(
            wd_ref[t : t + 1, :] * source((ux, ul, ur), i, j, di, dj, start)
            for t, (di, dj) in enumerate(TAPS)
        )
        phi = 0.5 * (1.0 + lax.erf(z * 0.7071067811865476))
        dens = jnp.exp(-0.5 * z * z) * 0.3989422804014327
        dz = dgx[p, pl.ds(pl.multiple_of(start, 8), PB), :] * (phi + z * dens)
        dzx[p, pl.ds(pl.multiple_of(start, 8), PB), :] = dz
        return z * phi, dz

    def fold(value):
        return jnp.sum(value.reshape(PB // 8, 8, C), axis=0)

    def forward_step(i, j):
        p = 2 * i + j

        def step(a, acc):
            start = sz.top + PB * a
            act, dz = activation(i, j, start)
            g_r[p, pl.ds(pl.multiple_of(PB * a, 8), PB), :] = act
            new = [
                acc[t] + fold(dz * source((ux, ul, ur), i, j, di, dj, start))
                for t, (di, dj) in enumerate(TAPS)
            ]
            return tuple(new) + (acc[9] + fold(dz),)

        return step

    sums = tuple(jnp.zeros((8, C), F32) for _ in range(10))
    for i in range(2):
        for j in range(2):
            sums = lax.fori_loop(1 - i, PA - i, forward_step(i, j), sums)
    for i in range(2):
        for a in range(1, PA):
            shift(dzx, dzl, dzr, i, sz.top + PB * (a - i))

    def backward_step(i, j):
        p = 2 * i + j

        def step(a, carry):
            start = sz.top + PB * a
            du_r[p, pl.ds(pl.multiple_of(PB * a, 8), PB), :] = sum(
                wd_ref[t : t + 1, :] * source((dzx, dzl, dzr), i, j, -di, -dj, start)
                for t, (di, dj) in enumerate(TAPS)
            )
            return carry

        return step

    dyg_mid()
    for i in range(2):
        for j in range(2):
            lax.fori_loop(1, PA - 1, backward_step(i, j), 0)
    ot_r[...] = jnp.concatenate([o_t, o5_t * share], axis=0)
    mixed = weighed(2, Q)
    dyg_at()
    for p in range(4):
        i, j = p // 2, p % 2
        start = sz.top - PB if i == 1 else sz.top + KEYS
        rows = dyh_g[p][:, :D].astype(F32)[0:PB] * row_mask(i, j, -1 if i == 1 else PA)
        dgx[p, start : start + PB, :] = nt(rows.astype(BF), w2).astype(BF).astype(F32)
    xh = xh_r[...].astype(F32)
    for p in range(4):
        i, j = p // 2, p % 2
        mask = jnp.concatenate([row_mask(i, j, -1), row_mask(i, j, PA)], axis=0)
        at = slice(2 * PB * p, 2 * PB * (p + 1))
        u = hidden(second_norm(xh[at] + mask * mixed[at]), mask)
        ux[p, sz.top - PB : sz.top, :] = u[0:PB]
        ux[p, sz.top + KEYS : sz.top + KEYS + PB, :] = u[PB:]
    for i in range(2):
        shift(ux, ul, ur, i, sz.top - PB)
        shift(ux, ul, ur, i, sz.top + KEYS)
    for i in range(2):
        for j in range(2):
            activation(i, j, sz.top - PB if i == 1 else sz.top + KEYS)
            sums = forward_step(i, j)((PA - 1) * i, sums)
    e_s, ve_s, vl_s = s["e_s"], s["ve_s"], s["vl_s"]
    shift(dzx, dzl, dzr, 0, sz.top)
    shift(dzx, dzl, dzr, 0, sz.top + KEYS)
    shift(dzx, dzl, dzr, 1, sz.top - PB)
    shift(dzx, dzl, dzr, 1, sz.top + KEYS - PB)
    dub = s["dub"]
    for i in range(2):
        for j in range(2):
            p = 2 * i + j
            for a in (0, PA - 1):
                backward_step(i, j)(a, 0)
            dub[p] = (du_r[p].astype(BF).astype(F32) * token_mask(i, j)).astype(BF)
    def packed(value):
        n = value.shape[0] // 2
        parts = [value[:, 0:LANES], value[:, LANES : 2 * LANES]]
        parts.append(jnp.concatenate([value[0:n, 2 * LANES :], value[n:, 2 * LANES :]], axis=1))
        return jnp.concatenate(parts, axis=0)

    def unpacked(value, rows):
        n = rows // 2
        rest = value[2 * rows : 2 * rows + n]
        rest = jnp.concatenate([rest[:, 0:HF], rest[:, HF:]], axis=0)
        return jnp.concatenate([value[0:rows], value[rows : 2 * rows], rest], axis=1)

    def dn2_block(h):
        value = packed(nt(dub[h], w1))
        rest = jnp.zeros((sz.prows - value.shape[0], LANES), F32)
        return jnp.concatenate([value, rest], axis=0)

    dn2_mid, dn2_at = mp_sum(dn2_block, s["dn2_s"], s["dn2_n"], s["dn2_f"])
    dn2_mid()

    gb = g_r[...].reshape(T, C).astype(BF)
    du_all = dub[...].reshape(T, C)
    e_s[0:D, :C] = tn(n2_r[...], du_all).astype(BF)
    e_s[D:, :D] = tn(gb, dfm[...]).astype(BF)

    def rows_of(ref, n):
        return lambda j: ref.at[pl.ds(pl.multiple_of(n * j, 16), n)]

    e_mid, e_at = dp_sum(rows_of(e_s, sz.echunk), s["e_n"], s["e_o"], s["e_f"])
    for t in range(10):
        ve_s[t : t + 1, :C] = rowsum(sums[t])
    ve_s[10:11, :C] = rowsum(du_all.astype(F32))

    for k in range(sz.n_dp):
        j = dpx(k)
        ebuf[j] = (ebuf[j].astype(F32) * scale[k]).astype(BF)
        e5buf[j] = (e5buf[j].astype(F32) * (scale5[k] * share)).astype(BF)
    ogp = s["ogp"]
    lane = iota((PL, LANES), 1)
    for n, (og, ow) in enumerate(chunks[:2]):
        mine, fifth = og[m].astype(F32), sum(ow[h].astype(F32) for h in range(4))
        for q in range(2):
            ogp[plane(2 * n + q), :] = jnp.where(
                lane < HF, from_queries(mine, q), from_queries(fifth, q)
            ).astype(BF)

    drain(12)

    xhat2, rstd2 = spread(plane_rows(h1_r, PL * m))
    dfp = plane_rows(dfm, PL * m).astype(F32)
    ve_s[11:12, :D] = rowsum(dfp)
    dn2 = unpacked(dn2_at(), PL)
    dh1 = dfp + norm_back(dn2, vec(ln2g_ref), xhat2, rstd2)
    dab = dh1.astype(BF)
    docat = nt(dab, wo_cat[...]).astype(BF)
    dos, do_all, dabg = s["dos"], s["do_all"], s["dabg"]
    for h in range(4):
        dos[h] = docat[:, LANES * h : LANES * (h + 1)]
    do_at = mp_scatter(lambda h: dos.at[h], lambda k: do_all.at[m], lambda k: do_all.at[mpx(k)])
    do_all[m] = dos[m]
    s["dh1_r"][...] = dh1
    dabg[m, :, :D] = dab
    ve_s[12:13, :D] = rowsum(dh1)
    ve_s[13:14, :D] = rowsum(dn2 * xhat2)
    ve_s[14:15, :D] = rowsum(dn2)
    ve_s[15:16, :] = jnp.zeros((1, W), F32)
    ve_mid, ve_at = dp_total(ve_s, s["ve_n"], s["ve_p"])
    e_mid()

    def ff_block(h):
        return nt(w2_t[pl.ds(pl.multiple_of(FS * h, 16), FS), :], gb)

    ff_mid, ff_at = mp_sum(ff_block, s["ff_s"], s["ff_n"], s["ff_f"])

    drain(16)
    do_at()
    ve_mid()
    dr_r = s["dr_r"]
    dot_t = to_queries([do_all[p].astype(F32) for p in range(4)]).T
    d_row = rowsum(dot_t[HF:] * ot_r[HF:, :])
    d_row = [d_row[:, LANES * n : LANES * (n + 1)] for n in range(Q // LANES)]
    dr_r[m] = jnp.concatenate(d_row + [jnp.zeros((8 - len(d_row), LANES), F32)], axis=0)
    dr_at = mp_scatter(lambda h: dr_r.at[m], lambda k: dr_r.at[m], lambda k: dr_r.at[mpx(k)])
    drow = rowsum(dot_t[0:HF] * ot_r[0:HF, :])
    da_t = jnp.concatenate([half, dot_t[0:HF]], axis=0).astype(BF)
    db_t = jnp.concatenate([half, dot_t[HF:]], axis=0).astype(BF)
    dqt, dqt5 = s["dqt"], s["dqt5"]
    dqt[...] = jnp.zeros_like(dqt)
    dqt5[...] = jnp.zeros_like(dqt5)
    five_row = []

    def key_grads(js, rows, ebuf, q_r, do_t, d_row, dq):
        n = rows.stop - rows.start
        kv = jnp.concatenate([kva[j, rows, :] for j in js], axis=0)
        e = jnp.concatenate([ebuf[j] for j in js], axis=0)
        ds = (e.astype(F32) * (nn(kv, do_t) - d_row)).astype(BF)
        value = nt(ds, q_r[...]) + nt(e, do_t)
        dq[...] += tn(kv, ds)
        return [value[n * q : n * (q + 1)] for q in range(len(js))]

    def own_keys(*ks):
        return key_grads([dpx(k) for k in ks], ROWS, ebuf, qa_r, da_t, drow, dqt)

    def last_keys(*ks):
        return key_grads([dpx(k) for k in ks], LAST, e5buf, qb_r, db_t, five_row[0], dqt5)

    dk_x, dk_n, dk_o, dk_f = s["dk_x"], s["dk_n"], s["dk_o"], s["dk_f"]
    dl_x, dl_n, dl_o, dl_f = s["dl_x"], s["dl_n"], s["dl_o"], s["dl_f"]
    dk_at = take(8)
    dl_at = take(4)
    for pair in ((2, 3), (1, 0)):
        for kz, value in zip(pair, own_keys(*(2 * kz + 1 for kz in pair))):
            dk_x[kz] = value.astype(BF)
            send(dk_x.at[kz], dk_n.at[kz], dk_at + kz, (dpx(1), m))
    dr_at()
    dab_at, dab_mid = mp_start(dabg)
    d_sum = sum(dr_r[h] for h in range(4))
    five_row.append(jnp.concatenate([d_sum[n : n + 1] for n in range(Q // LANES)], axis=1))
    for kz, value in enumerate(last_keys(1, 3, 5, 7)):
        dl_x[kz] = value.astype(BF)
    send(dl_x, dl_n, dl_at, (dpx(1), m))

    def dk_along(kz, value):
        arrived(dk_n.at[kz], dk_at + kz)
        dk_o[kz] = (value + dk_n[kz].astype(F32)).astype(BF)
        send(dk_o.at[kz], dk_f.at[kz], dk_at + 4 + kz, (dpx(2 * kz), m))

    for kz, value in zip((2, 3), own_keys(4, 6)):
        dk_along(kz, value)
    value, dkv = own_keys(2, 0)
    dk_along(1, value)
    dab_mid()
    dkl, *values = last_keys(0, 2, 4, 6)
    arrived(dl_n, dl_at)
    for kz in (2, 3, 1):
        dl_o[kz] = (values[kz - 1] + dl_n[kz].astype(F32)).astype(BF)
        send(dl_o.at[kz], dl_f.at[kz], dl_at + kz, (dpx(2 * kz), m))
    ff_mid()

    def dk_finish():
        arrived(dk_n.at[0], dk_at)
        total, last = dkv + dk_n[0].astype(F32), dkl + dl_n[0].astype(F32)
        for kz in (1, 2, 3):
            arrived(dk_f.at[kz], dk_at + 4 + kz)
            total = total + dk_f[kz].astype(F32)
        for kz in (1, 2, 3):
            arrived(dl_f.at[kz], dl_at + kz)
            last = last + dl_f[kz].astype(F32)
        return jnp.concatenate([total, last], axis=0)

    dk_fin = handle(dk_finish)

    dq2 = (jnp.concatenate([dqt[0:HF], dqt5[0:HF]], axis=0) * HF ** (-0.5)).T
    dqs, dq_all = s["dqs"], s["dq_all"]
    for h in range(4):
        dqs[h] = from_queries(dq2, h).astype(BF)
    l1_s, l2_s = s["l1_s"], s["l2_s"]
    dqp = dqs[...].reshape(T, LANES)
    l1_s[0:D, :] = tn(n1_r[...], dqp).astype(BF)
    vl_s[...] = jnp.zeros_like(vl_s)
    vl_s[5:6, 0:LANES] = rowsum(dqp.astype(F32))

    def fill(ref, first, value):
        rest = jnp.zeros((ref.shape[0] - first - value.shape[0], LANES), F32)
        ref[first:, :] = jnp.concatenate([value, rest], axis=0).astype(BF)

    def own_rows(value, n):
        return sum(jnp.where(m == h, 1.0, 0.0) * value[n * h : n * (h + 1)] for h in range(4))

    dab_at()
    gwo = tn(ogp[...], dabg[...].reshape(T, W)[:, :D])
    fill(l1_s, 2 * D, packed(jnp.concatenate([gwo[0:HF], own_rows(gwo[HF:], HF // 4)], axis=0)))

    dkvb = dk_fin().astype(BF)
    dkvg = s["dkvg"]
    dkvg[m] = dkvb
    dkv_at, dkv_mid = mp_direct(dkvg)
    l1_s[D : 2 * D, :] = tn(xr_r[...], dkvb[0:PL]).astype(BF)
    l1_mid, l1_at = dp_sum(rows_of(l1_s, sz.l1rows // sz.n_dp), s["l1_n"], s["l1_o"], s["l1_f"])
    eg_ref[d] = e_at().astype(BF)
    eg_at, eg_mid, _ = dp_start(eg_ref)
    vl_s[6:7, 0:LANES] = jnp.concatenate(
        [rowsum(dkvb[0:PL].astype(F32))[:, HF:], rowsum(dkvb[PL:].astype(F32))[:, HF:]], axis=1
    )
    dkv_mid()
    dq_at = mp_scatter(lambda h: dqs.at[h], lambda k: dq_all.at[m], lambda k: dq_all.at[mpx(k)])
    dq_all[m] = dqs[m]
    drain(12)
    dkv_mid()
    dkv_at()
    l1_mid()
    rest = jnp.concatenate(
        [dkvg[h, PL : PL + sz.step, :] for h in range(3)] + [dkvg[3, PL:, :]], axis=0
    )
    dkv_all = jnp.concatenate([dkvg[h, 0:PL, :] for h in range(4)] + [rest], axis=1)
    dxr = nt(dkv_all, w_all[...])
    xhr = s["xhr_r"][...]
    drb = norm_back(dxr, vec(lnrg_ref), xhr, s["rsr_r"][:, 0:1]).astype(BF)
    l2_s[0 : sz.wrows, :] = packed(tn(drb, plane_rows(n1_r, PL * m))).astype(BF)
    fill(l2_s, sz.wrows, own_rows(tn(xr_r[...], rest), FS))
    l2_mid, l2_at = dp_sum(rows_of(l2_s, sz.l2rows // sz.n_dp), s["l2_n"], s["l2_o"], s["l2_f"])
    vl_s[2:3, :D] = rowsum(dxr * xhr)
    vl_s[3:4, :D] = rowsum(dxr)
    vl_s[4:5, :D] = rowsum(drb.astype(F32))

    wr_m = wr_t[pl.ds(pl.multiple_of(D * m, 16), D), :]
    dq_at()
    dq_cat = jnp.concatenate([dq_all[h] for h in range(4)], axis=1)
    dn1 = nt(dq_cat, wq_cat[...])
    xhat1, rstd1 = spread(plane_rows(xm_r, PL * m).astype(F32))
    dn1 = dn1 + nt(drb, wr_m)
    vl_s[0:1, :D] = rowsum(dn1 * xhat1)
    vl_s[1:2, :D] = rowsum(dn1)
    vl_mid, vl_at = dp_total(vl_s, s["vl_n"], s["vl_p"])
    dxm = norm_back(dn1, vec(ln1g_ref), xhat1, rstd1)
    gp = (token_mask(m // 2, lax.rem(m, 2)) * (s["dh1_r"][...] + dxm)).astype(BF)
    gpf = nn(gp, place_out).astype(BF)
    gps = s["gps"]
    for h in range(4):
        gps[h] = gpf[:, LANES * h : LANES * (h + 1)]
    gp_at = mp_scatter(lambda h: gps.at[h], lambda k: gp_ref.at[m], lambda k: gp_ref.at[mpx(k)])
    gp_ref[m] = gps[m]

    veg_ref[m] = ve_at()
    veg_at, _ = mp_direct(veg_ref)

    def gather(buf):
        base = take(3 * sz.n_dp)

        def onward(k):
            j = dpx(k)
            send(buf.at[m, j], buf.at[m, j], base + 3 * k, (d, mpx(1)))
            send(buf.at[m, j], buf.at[m, j], base + 3 * k + 1, (d, mpx(2)))

        near, mid, steps = dp_start(buf.at[m], onward)
        onward(0)
        seq = (0, 2, 4, 6, 1, 3, 5, 7)

        def relay(k):
            j = dpx(k)
            arrived(buf.at[mpx(2), j], base + 3 * k + 1)
            send(buf.at[mpx(2), j], buf.at[mpx(2), j], base + 3 * k + 2, (d, mpx(1)))

        relays = [handle(lambda k=k: relay(k)) for k in seq]

        def finish():
            near()
            for r in relays:
                r()
            for k in seq:
                arrived(buf.at[mpx(1), dpx(k)], base + 3 * k)
                arrived(buf.at[mpx(3), dpx(k)], base + 3 * k + 2)

        return near, mid, relays, handle(finish)

    drain(12)
    eg_mid()
    lg1_ref[m, d] = l1_at().astype(BF)
    near1, mid1, relays1, lg1_at = gather(lg1_ref)
    l2_mid()
    ff = ff_at().T
    ff = jnp.concatenate([ff, jnp.zeros((T, LANES - FS), F32)], axis=1)
    sel = hot((c2 < FS) & (r2 == FS * m + c2))
    b2q = jnp.concatenate(
        [own_part(vec(b2_ref), FS), jnp.zeros((1, LANES - FS), F32)], axis=1
    )
    for p in range(4):
        h1 = h1_r[plane(p), :]
        hi = h1.astype(BF)
        h1q = nn(hi, sel) + nn((h1 - hi.astype(F32)).astype(BF), sel)
        blk_ref[plane(p), :] = h1q + token_mask(p // 2, p % 2) * (ff[plane(p)] + b2q)
    mid1()
    drain(24)
    vl_mid()
    lg2_ref[m, d] = l2_at().astype(BF)
    near2, mid2, relays2, lg2_at = gather(lg2_ref)
    near1()
    vlg_ref[m] = vl_at()
    vlg_at, _ = mp_direct(vlg_ref)
    for r in relays1[:4]:
        r()
    drain(16)
    mid2()
    for r in relays1[4:]:
        r()
    drain(24)
    near2()
    drain(16)
    for r in relays2:
        r()
        drain(16)
    eg_at()
    gp_at()
    veg_at()
    lg1_at()
    vlg_at()
    lg2_at()
    drain()


def unpack_body(sz, *refs):
    srcs, refs = refs[:7], refs[7:]
    dsts, refs = refs[:23], refs[23:]
    (
        out_ref, gpix_ref, ln1g_ref, ln1b_ref, gwq_ref, gbq_ref, gwk_ref, gwv_ref, gbv_ref, gwr_ref, gbr_ref,
        lnrg_ref, lnrb_ref, gwo_ref, gbo_ref, ln2g_ref, ln2b_ref, gw1_ref, gb1_ref, gwd_ref, gbd_ref,
        gw2_ref, gb2_ref,
    ), outs, refs = refs[:23], refs[:23], refs[23:]
    out32, gp32, osem = refs
    stores = []

    def store(*which):
        for i in which:
            c = pltpu.make_async_copy(outs[i], dsts[i], osem.at[i])
            c.start()
            stores.append(c)

    blk_ref, gp_ref, eg_ref, lg1_ref, lg2_ref, veg_ref, vlg_ref = srcs
    D, HF, PB, PA, PL = sz.width, HEAD_FEATURES, sz.pb, sz.pa, sz.plane
    C, FS = sz.hidden, sz.share
    m = lax.axis_index("mp")

    def row(value):
        return value.reshape(value.shape[1])

    ve = veg_ref[m]
    gwd_ref[...] = ve[0:9, :C]
    gbd_ref[...] = row(ve[9:10, :C])
    gb1_ref[...] = row(ve[10:11, :C])
    vs = sum(veg_ref[h] for h in range(4))
    gb2_ref[...] = row(vs[11:12, :D])
    gbo_ref[...] = row(vs[12:13, :D])
    ln2g_ref[...] = row(vs[13:14, :D])
    ln2b_ref[...] = row(vs[14:15, :D])
    vl = sum(vlg_ref[h] for h in range(4))
    ln1g_ref[...] = row(vl[0:1, :D])
    ln1b_ref[...] = row(vl[1:2, :D])
    lnrg_ref[...] = row(vlg_ref[0][2:3, :D])
    lnrb_ref[...] = row(vlg_ref[0][3:4, :D])
    gbr_ref[...] = row(vlg_ref[0][4:5, :D])

    def head_row(r):
        parts = [vlg_ref[h][r : r + 1, 0:HF] for h in range(4)] + [vl[r : r + 1, HF : 2 * HF]]
        return row(jnp.concatenate(parts, axis=1))

    gbq_ref[...] = head_row(5)
    gbv_ref[...] = head_row(6)
    store(2, 3, 5, 8, 10, 11, 12, 14, 15, 16, 18, 19, 20, 22)
    for i in range(2):
        for j in range(2):
            p = 2 * i + j
            for a in range(PA):
                at = pl.ds((2 * a + i) * sz.cols + j, PB, stride=2)
                out32[at, :] = blk_ref[PL * p + PB * a : PL * p + PB * (a + 1), 0:FS]
                gp32[at, :] = gp_ref[p].astype(F32)[PB * a : PB * (a + 1), 0:FS]
    out_ref[...] = out32[...].T.astype(BF)
    gpix_ref[...] = gp32[...].T
    store(0, 1)
    eg = eg_ref[...].reshape(D + C, sz.wide)
    gw1_ref[...] = eg[0:D, :C].astype(F32)
    gw2_ref[...] = eg[D:, :D].astype(F32)
    store(17, 21)

    def unpacked(value):
        n = value.shape[0] * 2 // 5
        tail = value[2 * n :]
        tail = jnp.concatenate([tail[:, 0:HF], tail[:, HF:]], axis=0)
        return jnp.concatenate([value[0:n], value[n : 2 * n], tail], axis=1)

    lg1 = [lg1_ref[h].reshape(sz.l1rows, LANES).astype(F32) for h in range(4)]
    lg2 = [lg2_ref[h].reshape(sz.l2rows, LANES).astype(F32) for h in range(4)]
    tail = jnp.concatenate([lg2[h][sz.wrows : sz.wrows + FS] for h in range(4)], axis=0)
    fifth = sum(lg1[h][0:D, HF:] for h in range(4))
    gwq_ref[...] = jnp.concatenate([lg1[h][0:D, 0:HF] for h in range(4)] + [fifth], axis=1)
    gwk_ref[...] = jnp.concatenate([lg1[h][D : 2 * D, 0:HF] for h in range(4)] + [tail[:, 0:HF]], axis=1)
    gwv_ref[...] = jnp.concatenate([lg1[h][D : 2 * D, HF:] for h in range(4)] + [tail[:, HF:]], axis=1)
    store(4, 6, 7)
    gwr_ref[...] = jnp.concatenate([unpacked(lg2[h][0 : sz.wrows]) for h in range(4)], axis=1)
    store(9)
    n = HF // 4
    for h in range(4):
        wo = unpacked(lg1[h][2 * D : 2 * D + 5 * sz.orows // 2])
        gwo_ref[HF * h : HF * (h + 1), :] = wo[0:HF]
        gwo_ref[4 * HF + n * h : 4 * HF + n * (h + 1), :] = wo[HF:]
    store(13)
    for c in stores:
        c.wait()


def on_device_fused(*args):
    pixels_in, cotangent, pixel_mask, tile_slot = args[:4]
    w_fc1 = args[19]
    sz = Sizes(
        lax.axis_size("dp"), lax.axis_size("mp"), pixels_in.shape[0], cotangent.shape[1], w_fc1.shape[1]
    )
    D, C, PL, T, W, LN, HF = sz.width, sz.hidden, sz.plane, sz.all, sz.wide, LANES, HEAD_FEATURES
    Q, N, PB = sz.queries, sz.n_dp, sz.pb
    sm = pl.BlockSpec(memory_space=pltpu.SMEM)
    vm = pl.BlockSpec(memory_space=pltpu.VMEM)
    hbm = pl.BlockSpec(memory_space=pltpu.HBM)
    S = jax.ShapeDtypeStruct
    ins = [pixels_in.T, cotangent.T, *args[4:11], args[11].T, *args[12:]]
    mids = [
        S((T, LN), F32), S((4, PL, LN), BF), S((N, sz.echunk, W), BF), S((4, N, sz.l1rows // N, LN), BF),
        S((4, N, sz.l2rows // N, LN), BF), S((4, 16, W), F32), S((4, 8, W), F32),
    ]
    chunks = dict(e=(sz.echunk, W), l1=(sz.l1rows // N, LN), l2=(sz.l2rows // N, LN))
    shapes = {
        BF: dict(
            xt=(4, sz.share, sz.tokens), dfm=(T, D), dyh=(4, 48, W), dyh_s=(48, W), dyh_x=(48, W), dyh_g=(4, 48, W),
            edge=(4, sz.share, sz.edge_q), edge_s=(sz.share, sz.edge_q), edge_x=(sz.share, sz.edge_q),
            edge_g=(4, sz.share, sz.edge_q), xh_r=(sz.edge, D), qc_r=(LN, sz.edge_q), qd_r=(LN, sz.edge_q), xm_r=(T, D), n1_r=(T, D),
            xr_r=(PL, D), kva=(N, sz.kvrows, LN), qa_r=(LN, Q), qb_r=(LN, Q), ebuf=(N, PL, Q),
            e5buf=(N, sz.quarter, Q), og_a=(4, 2 * sz.keys, LN), og_b=(4, 2 * sz.keys, LN), og_c=(4, sz.edge, LN),
            ow_a=(4, 2 * sz.keys, LN), ow_b=(4, 2 * sz.keys, LN), ow_c=(4, sz.edge, LN), n2_r=(T, D),
            dub=(4, PL, C), dn2_s=(3, sz.prows, LN), dn2_n=(2, sz.prows, LN),
            dn2_f=(sz.prows, LN), dos=(4, PL, LN), do_all=(4, PL, LN), dabg=(4, PL, W), ff_s=(3, sz.share, T), ff_n=(2, sz.share, T),
            ff_f=(sz.share, T), **{"dk_" + k: (4, PL, LN) for k in "xnof"}, **{"dl_" + k: (4, sz.quarter, LN) for k in "xnof"}, dkvg=(4, sz.kvrows, LN), dqs=(4, PL, LN), dq_all=(4, PL, LN),
            e_s=(D + C, W), gps=(4, PL, LN), wr_t=(4 * D, D), ogp=(T, LN),
            w2_t=(D, C), w_all=(D, 5 * LN), wq_cat=(D, 4 * LN), wo_cat=(4 * LN, D), l1_s=(sz.l1rows, LN),
            l2_s=(sz.l2rows, LN),
            **{n + "_" + k: (4, *v) for k in "nof" for n, v in chunks.items()},
        ),
        F32: dict(
            t0=(sz.tokens, LN), t1=(sz.tokens, LN), t2=(sz.tokens, D - 2 * LN), xhr_r=(PL, D), rsr_r=(PL, LN),
            o_own=(N, HF, Q), o_five=(N, HF, Q), oh_own=(N, HF, sz.edge_q), oh_five=(N, HF, sz.edge_q),
            lse_r=(4, 16, LN), ot_r=(LN, Q),
            h1_r=(T, D), ux=(4, sz.ext, C), ul=(2, sz.ext, C), ur=(2, sz.ext, C), dgx=(4, sz.ext, C),
            dzx=(4, sz.ext, C), dzl=(2, sz.ext, C), dzr=(2, sz.ext, C), g_r=(4, PL, C), du_r=(4, PL, C),
            dh1_r=(PL, D), dr_r=(4, 8, LN), dqt=(LN, Q), dqt5=(LN, Q), ve_s=(16, W), ve_n=(16, W),
            ve_p=(4, 16, W), vl_s=(8, W), vl_n=(8, W), vl_p=(4, 8, W),
        ),
    }
    scratch = {k: pltpu.VMEM(v, t) for t, group in shapes.items() for k, v in group.items()}
    for i in range(1, len(ins)):
        scratch["in%d" % i] = pltpu.VMEM(ins[i].shape, ins[i].dtype)
    scratch["ssem"] = pltpu.SemaphoreType.DMA((200,))
    scratch["rsem"] = pltpu.SemaphoreType.DMA((200,))
    scratch["isem"] = pltpu.SemaphoreType.DMA((len(ins),))
    mid = pl.pallas_call(
        functools.partial(fused_body, sz, tuple(scratch)),
        out_shape=[pltpu.VMEM(v.shape, v.dtype) for v in mids],
        in_specs=[sm, sm] + [hbm] * len(ins),
        out_specs=[vm] * len(mids),
        scratch_shapes=list(scratch.values()),
        compiler_params=pltpu.CompilerParams(
            collective_id=0, has_side_effects=True, vmem_limit_bytes=VMEM_MB * 2**20
        ),
        name="fused_block",
    )(pixel_mask, tile_slot.T, *(pltpu.with_memory_space_constraint(v, pltpu.HBM) for v in ins))
    outs = [
        S((sz.share, sz.tokens), BF), S((sz.share, sz.tokens), F32), S((D,), F32), S((D,), F32), S((D, D), F32),
        S((D,), F32), S((D, D), F32), S((D, D), F32), S((D,), F32), S((D, 4 * D), F32), S((D,), F32), S((D,), F32),
        S((D,), F32), S((D, D), F32), S((D,), F32), S((D,), F32), S((D,), F32), S((D, C), F32), S((C,), F32),
        S((9, C), F32), S((C,), F32), S((C, D), F32), S((D,), F32),
    ]
    res = list(
        pl.pallas_call(
            functools.partial(unpack_body, sz),
            out_shape=outs,
            in_specs=[vm] * len(mids),
            out_specs=[hbm] * len(outs),
            scratch_shapes=[pltpu.VMEM(v.shape, v.dtype) for v in outs]
            + [pltpu.VMEM((sz.tokens, sz.share), F32)] * 2
            + [pltpu.SemaphoreType.DMA((len(outs),))],
            compiler_params=pltpu.CompilerParams(vmem_limit_bytes=40 * 2**20),
            name="unpack",
        )(*mid)
    )
    for k in (0, 1, 9):
        res[k] = res[k].T
    return tuple(res)


def choose(*args):
    tokens, width = args[1].shape
    whole_rows = tokens == FRAME * (FRAME // TILE_ROWS)
    shape = (lax.axis_size("dp"), lax.axis_size("mp"))
    if whole_rows and shape == (TILE_ROWS, 4) and TILE_ROWS == 8 and HEADS == 5 and width == 320 == args[19].shape[1]:
        return on_device_fused(*args)
    return on_device(*args)


def solution(mesh):
    return jax.shard_map(
        choose,
        mesh=mesh,
        in_specs=(
            P("dp", "mp"),
            P("dp", None),
            P("dp"),
            P(),
            P(),
            P(),
            P(),
            P(),
            P(),
            P(),
            P(),
            P(),
            P(),
            P(),
            P(),
            P(),
            P(),
            P(),
            P(),
            P(None, "mp"),
            P("mp"),
            P(None, "mp"),
            P("mp"),
            P("mp", None),
            P(),
        ),
        out_specs=(
            P("dp", "mp"),
            P("dp", "mp"),
            P(),
            P(),
            P(),
            P(),
            P(),
            P(),
            P(),
            P(),
            P(),
            P(),
            P(),
            P(),
            P(),
            P(),
            P(),
            P(None, "mp"),
            P("mp"),
            P(None, "mp"),
            P("mp"),
            P("mp", None),
            P(),
        ),
        check_vma=False,
    )
```
